32 devices in a mesh: parts: 2 (over y), tensor: 4 (over z), dp: 4 (over x, core).
Axes of the slice: x: 2, y: 2, z: 4, core: 2. Of those that a mesh axis runs over, the one named last changes fastest.
Arguments:
- train_input: bfloat16 [32, 64, 8192], P(('parts', 'dp'), None, 'tensor'), parts along dimension 0, may hold values from -6 to 6
- train_gate: bfloat16 [32, 64, 14336], P(('parts', 'dp'), None, 'tensor'), parts along dimension 0, may hold values from -6 to 6
- train_up: bfloat16 [32, 64, 14336], P(('parts', 'dp'), None, 'tensor'), parts along dimension 0, may hold values from -6 to 6
- train_outgrad: bfloat16 [32, 64, 8192], P(('parts', 'dp'), None, 'tensor'), parts along dimension 0, may hold values from -6 to 6
- train_lengths: int32 [32], P(('parts', 'dp')), parts along dimension 0, may hold values from 16 to 64, as said below
- query_input: bfloat16 [16, 64, 8192], P(('parts', 'dp'), None, 'tensor'), parts along dimension 0, may hold values from -6 to 6
- query_gate: bfloat16 [16, 64, 14336], P(('parts', 'dp'), None, 'tensor'), parts along dimension 0, may hold values from -6 to 6
- query_up: bfloat16 [16, 64, 14336], P(('parts', 'dp'), None, 'tensor'), parts along dimension 0, may hold values from -6 to 6
- query_outgrad: bfloat16 [16, 64, 8192], P(('parts', 'dp'), None, 'tensor'), parts along dimension 0, may hold values from -6 to 6
- query_lengths: int32 [16], P(('parts', 'dp')), parts along dimension 0, may hold values from 16 to 64, as said below
- down_weight: bfloat16 [14336, 8192], P('tensor', 'dp'), may hold values from -0.0625 to 0.0625
- proj_input: bfloat16 [64, 8192], P(None, 'tensor'), may hold values from -0.0625 to 0.0625
- proj_outgrad: bfloat16 [64, 8192], P(None, 'tensor'), may hold values from -0.0625 to 0.0625
- proj_hidden: bfloat16 [64, 14336], P(None, 'tensor'), may hold values from -0.046875 to 0.046875
- proj_gate: bfloat16 [64, 14336], P(None, 'tensor'), may hold values from -0.046875 to 0.046875
- proj_up: bfloat16 [64, 14336], P(None, 'tensor'), may hold values from -0.046875 to 0.046875
Outputs:
- scores: float32 [32, 8], P(('parts', 'dp')), parts along dimension 0
The draws below stay inside these ranges and needn't reach their ends.
There are 2 independent parts, one for each index of `parts`. The reference program is written for one: setup_inputs(seed, part) draws one part's arguments, and reference() takes and returns one part's arrays. A program takes and returns all parts, laid end to end along the dimension named above; an argument that names none is the same for every part. Nothing has to cross between parts.
Inputs may be any that keep to these rules, and one draw needn't show every extreme that they name: `train_lengths`: positions from an example's length on are padding; some example has exactly 64 real tokens and some exactly 16. `query_lengths`: positions from an example's length on are padding; some example has exactly 64 real tokens and some exactly 16.
All inputs are finite; a program needn't handle non-finite values.
Results may differ from the reference program's by a relative error of at most 0.0041.
Values may be sent and summed in bfloat16 or wider, within the bound.
No kernel may reach another device: no remote copies, remote signals or barrier semaphores. Data moves between devices by JAX's collectives and lax.ppermute only.
A program may use at most 192 MiB of HBM per device.

```python
import jax
import jax.numpy as jnp
from jax import lax

D = 8192
FF = 14336
RANK = 64
SEQ = 64
TRAIN = 16
QUERY = 8


def draw_lengths(key, number):
    choose, shuffle = jax.random.split(key)
    values = jax.random.randint(choose, (number,), SEQ // 4, SEQ + 1, dtype=jnp.int32)
    ranking = jax.random.permutation(shuffle, number)
    values = jnp.where(ranking == 0, SEQ, values)
    return jnp.where(ranking == 1, SEQ // 4, values).astype(jnp.int32)


def draw_train_lengths(key, part):
    key = jax.random.fold_in(key, 11)
    return draw_lengths(key, TRAIN)


def draw_query_lengths(key, part):
    key = jax.random.fold_in(key, 23)
    return draw_lengths(key, QUERY)


def shard_levels(stream_key, extent, shards, smallest, largest):
    level, own = 1.0, jax.random.fold_in(stream_key, 6)
    for dim, shards_of in shards:
        heights = jnp.exp(jax.random.uniform(jax.random.fold_in(own, dim), (shards_of,), jnp.float32, smallest / len(shards), largest / len(shards)))
        level = level * jnp.repeat(heights, extent[dim] // shards_of).reshape([-1 if axis == dim else 1 for axis in range(len(extent))])
    return level


def normal_values(rng, shape, width, reach, cuts=(), kind=jnp.bfloat16):
    drawn = jax.random.normal(rng, shape, jnp.float32) * width
    if len(cuts) > 0:
        drawn = shard_levels(rng, shape, cuts, -0.22, 0.18) * drawn
    return jnp.clip(drawn, min=-reach, max=reach).astype(kind)


def setup_inputs(seed: int = 0, part: int = 0) -> dict:
    arg_keys = jax.random.split(jax.random.key(seed), 17)
    part_splits = jax.random.split(jax.random.fold_in(arg_keys[16], part), 17)
    return {
        "train_input": normal_values(part_splits[0], (TRAIN, SEQ, D), 1.0, 6.0, ((0, 4), (2, 4))),
        "train_gate": normal_values(part_splits[1], (TRAIN, SEQ, FF), 1.0, 6.0, ((0, 4), (2, 4))),
        "train_up": normal_values(part_splits[2], (TRAIN, SEQ, FF), 1.0, 6.0, ((0, 4), (2, 4))),
        "train_outgrad": normal_values(part_splits[3], (TRAIN, SEQ, D), 1.0, 6.0, ((0, 4), (2, 4))),
        "train_lengths": draw_train_lengths(jax.random.fold_in(jax.random.fold_in(arg_keys[16], part), 71), part),
        "query_input": normal_values(part_splits[5], (QUERY, SEQ, D), 1.0, 6.0, ((0, 4), (2, 4))),
        "query_gate": normal_values(part_splits[6], (QUERY, SEQ, FF), 1.0, 6.0, ((0, 4), (2, 4))),
        "query_up": normal_values(part_splits[7], (QUERY, SEQ, FF), 1.0, 6.0, ((0, 4), (2, 4))),
        "query_outgrad": normal_values(part_splits[8], (QUERY, SEQ, D), 1.0, 6.0, ((0, 4), (2, 4))),
        "query_lengths": draw_query_lengths(jax.random.fold_in(jax.random.fold_in(arg_keys[16], part), 71), part),
        "down_weight": normal_values(arg_keys[10], (FF, D), D ** -0.5, 0.0625, ((0, 4), (1, 4))),
        "proj_input": normal_values(arg_keys[11], (RANK, D), D ** -0.5, 0.0625, ((1, 4),)),
        "proj_outgrad": normal_values(arg_keys[12], (RANK, D), D ** -0.5, 0.0625, ((1, 4),)),
        "proj_hidden": normal_values(arg_keys[13], (RANK, FF), FF ** -0.5, 0.046875, ((1, 4),)),
        "proj_gate": normal_values(arg_keys[14], (RANK, FF), FF ** -0.5, 0.046875, ((1, 4),)),
        "proj_up": normal_values(arg_keys[15], (RANK, FF), FF ** -0.5, 0.046875, ((1, 4),)),
    }


def outer_sums(left_side, right_side, lengths):
    number = lengths.shape[0]
    positions = jnp.arange(SEQ, dtype=jnp.int32)
    weights = (positions[None, :] < lengths[:, None]).astype(jnp.float32)
    left_rows = left_side.reshape(number, SEQ, RANK) * weights[:, :, None]
    right_rows = right_side.reshape(number, SEQ, RANK)
    summed = jnp.einsum("est,esu->etu", left_rows, right_rows, precision=lax.Precision.HIGHEST)
    return summed.reshape(number, RANK * RANK)


def example_features(inputs, gate, up, outgrad, lengths, down_weight, tables):
    proj_input, proj_outgrad, proj_hidden, proj_gate, proj_up = tables
    number = lengths.shape[0]
    input_rows = inputs.reshape(number * SEQ, D)
    outgrad_rows = outgrad.reshape(number * SEQ, D)
    gate_wide = gate.reshape(number * SEQ, FF).astype(jnp.float32)
    up_wide = up.reshape(number * SEQ, FF).astype(jnp.float32)
    sigmoid_gate = jax.nn.sigmoid(gate_wide)
    silu_gate = gate_wide * sigmoid_gate
    hidden = (silu_gate * up_wide).astype(jnp.bfloat16)
    hidden_grad = jnp.dot(outgrad_rows, down_weight.T, preferred_element_type=jnp.float32)
    gate_grad = (hidden_grad * up_wide * sigmoid_gate * (1.0 + gate_wide * (1.0 - sigmoid_gate))).astype(jnp.bfloat16)
    up_grad = (hidden_grad * silu_gate).astype(jnp.bfloat16)
    in_side = jnp.dot(input_rows, proj_input.T, preferred_element_type=jnp.float32)
    hidden_side = jnp.dot(hidden, proj_hidden.T, preferred_element_type=jnp.float32)
    gate_side = jnp.dot(gate_grad, proj_gate.T, preferred_element_type=jnp.float32)
    up_side = jnp.dot(up_grad, proj_up.T, preferred_element_type=jnp.float32)
    out_side = jnp.dot(outgrad_rows, proj_outgrad.T, preferred_element_type=jnp.float32)
    return jnp.concatenate([outer_sums(in_side, gate_side, lengths), outer_sums(in_side, up_side, lengths), outer_sums(hidden_side, out_side, lengths)], axis=1)


def reference(train_input, train_gate, train_up, train_outgrad, train_lengths, query_input, query_gate, query_up, query_outgrad, query_lengths, down_weight, proj_input, proj_outgrad, proj_hidden, proj_gate, proj_up):
    tables = (proj_input, proj_outgrad, proj_hidden, proj_gate, proj_up)
    train_features = example_features(train_input, train_gate, train_up, train_outgrad, train_lengths, down_weight, tables)
    query_features = example_features(query_input, query_gate, query_up, query_outgrad, query_lengths, down_weight, tables)
    scores = jnp.dot(train_features, query_features.T, precision=lax.Precision.HIGHEST)
    return (scores / (RANK * SEQ)).astype(jnp.float32)
```

```python
import jax
import jax.numpy as jnp
from jax import lax
from jax.sharding import PartitionSpec as P

RANK = 64
SEQ = 64


def flatten(array):
    return array.reshape(-1, array.shape[-1])


def project(rows, table):
    return lax.dot_general(
        rows, table, (((1,), (1,)), ((), ())), preferred_element_type=jnp.float32
    )


def inner(left_side, right_side):
    return lax.dot_general(
        left_side,
        right_side,
        (((1,), (1,)), ((), ())),
        precision=lax.Precision.HIGHEST,
        preferred_element_type=jnp.float32,
    )


def gated_hidden(gate, up):
    gate_wide = gate.astype(jnp.float32)
    up_wide = up.astype(jnp.float32)
    return (gate_wide * jax.nn.sigmoid(gate_wide) * up_wide).astype(jnp.bfloat16)


def gradient_sides(gate, up, hidden_grad, proj_gate, proj_up):
    gate_wide = gate.astype(jnp.float32)
    up_wide = up.astype(jnp.float32)
    sigmoid_gate = jax.nn.sigmoid(gate_wide)
    silu_gate = gate_wide * sigmoid_gate
    gate_grad = (
        hidden_grad * up_wide * sigmoid_gate * (1.0 + gate_wide * (1.0 - sigmoid_gate))
    ).astype(jnp.bfloat16)
    up_grad = (hidden_grad * silu_gate).astype(jnp.bfloat16)
    return project(gate_grad, proj_gate), project(up_grad, proj_up)


def outer_sums(left_side, right_side, lengths):
    number = lengths.shape[0]
    length = left_side.shape[0] // number
    positions = lax.broadcasted_iota(jnp.int32, (number, length), 1)
    weights = (positions < lengths[:, None]).astype(jnp.float32)
    left_rows = left_side.reshape(number, length, left_side.shape[1]) * weights[:, :, None]
    right_rows = right_side.reshape(number, length, right_side.shape[1])
    summed = jnp.einsum("est,esu->etu", left_rows, right_rows, precision=lax.Precision.HIGHEST)
    return summed.reshape(number, -1)


def features(in_side, hidden_side, gate_side, up_side, out_side, lengths):
    return jnp.concatenate(
        [
            outer_sums(in_side, gate_side, lengths),
            outer_sums(in_side, up_side, lengths),
            outer_sums(hidden_side, out_side, lengths),
        ],
        axis=1,
    )


def gathering_plan(
    train_input,
    train_gate,
    train_up,
    train_outgrad,
    train_lengths,
    query_input,
    query_gate,
    query_up,
    query_outgrad,
    query_lengths,
    down_weight,
    proj_input,
    proj_outgrad,
    proj_hidden,
    proj_gate,
    proj_up,
):
    weight = lax.all_gather(down_weight, "dp", axis=1, tiled=True)

    def full_features(inputs, gate, up, outgrad, lengths):
        inputs, gate, up, outgrad = [flatten(a) for a in (inputs, gate, up, outgrad)]
        rows = lax.all_gather(outgrad, "tensor", axis=1, tiled=True)
        gate_side, up_side = gradient_sides(gate, up, project(rows, weight), proj_gate, proj_up)
        hidden_side = project(gated_hidden(gate, up), proj_hidden)
        sides = (
            project(inputs, proj_input),
            hidden_side,
            gate_side,
            up_side,
            project(outgrad, proj_outgrad),
        )
        return features(*lax.psum(sides, "tensor"), lengths)

    train_features = full_features(
        train_input, train_gate, train_up, train_outgrad, train_lengths
    )
    query_features = full_features(
        query_input, query_gate, query_up, query_outgrad, query_lengths
    )
    gathered = lax.all_gather(query_features, "dp", axis=0, tiled=True)
    return inner(train_features, gathered) / (RANK * SEQ)


def pick(blocks, index):
    chosen = blocks[0]
    for number in range(1, len(blocks)):
        chosen = jnp.where(index == number, blocks[number], chosen)
    return chosen


def moving_plan(
    tensor,
    train_input,
    train_gate,
    train_up,
    train_outgrad,
    train_lengths,
    query_input,
    query_gate,
    query_up,
    query_outgrad,
    query_lengths,
    down_weight,
    proj_input,
    proj_outgrad,
    proj_hidden,
    proj_gate,
    proj_up,
):
    t = lax.axis_index("tensor")
    d = lax.axis_index("dp")
    x, core = d // 2, d % 2
    to_core = [(i, i ^ 1) for i in range(4)]
    to_chip = [(i, i ^ 2) for i in range(4)]
    upward = [(i, i + 1) for i in range(tensor - 1)]
    downward = [(i + 1, i) for i in range(tensor - 1)]

    weight_own = down_weight
    weight_sib = lax.ppermute(down_weight, "dp", to_core)

    def column_blocks(rows):
        rising, falling = [rows], [rows]
        for _ in range(tensor - 1):
            rising.append(lax.ppermute(rising[-1], "tensor", upward))
            falling.append(lax.ppermute(falling[-1], "tensor", downward))
        blocks = [rows]
        for step in range(1, tensor):
            blocks.append(jnp.where(t >= step, rising[step], falling[tensor - step]))
        return blocks

    def hidden_gradient(rows):
        blocks = column_blocks(rows)

        def column(k):
            return pick(blocks, (t - k) % tensor)

        far_own = lax.ppermute(column(2 * (1 - x) + core), "dp", to_chip)
        far_sib = lax.ppermute(column(2 * (1 - x) + 1 - core), "dp", to_chip)
        far = project(far_own, weight_own) + project(far_sib, weight_sib)
        returned = lax.ppermute(far.astype(jnp.bfloat16), "dp", to_chip)
        near = project(column(2 * x + core), weight_own)
        near = near + project(column(2 * x + 1 - core), weight_sib)
        return near + returned.astype(jnp.float32)

    query_rows = [flatten(a) for a in (query_input, query_gate, query_up, query_outgrad)]
    train_rows = [flatten(a) for a in (train_input, train_gate, train_up, train_outgrad)]

    q_input, q_gate, q_up, q_outgrad = query_rows
    gate_side, up_side = gradient_sides(
        q_gate, q_up, hidden_gradient(q_outgrad), proj_gate, proj_up
    )
    query_sides = lax.psum(
        (
            project(q_input, proj_input),
            project(gated_hidden(q_gate, q_up), proj_hidden),
            gate_side,
            up_side,
            project(q_outgrad, proj_outgrad),
        ),
        "tensor",
    )
    query_features = lax.all_gather(
        features(*query_sides, query_lengths), "dp", axis=0, tiled=True
    )

    t_input, t_gate, t_up, t_outgrad = train_rows
    in_side, out_side = lax.psum(
        (project(t_input, proj_input), project(t_outgrad, proj_outgrad)), "tensor"
    )
    hidden_side = project(gated_hidden(t_gate, t_up), proj_hidden)

    pieces = 2
    examples = train_lengths.shape[0] // pieces
    partial = []
    for piece in range(pieces):
        part = slice(piece * examples * SEQ, (piece + 1) * examples * SEQ)
        gate_side, up_side = gradient_sides(
            t_gate[part], t_up[part], hidden_gradient(t_outgrad[part]), proj_gate, proj_up
        )
        piece_features = features(
            in_side[part],
            hidden_side[part],
            gate_side,
            up_side,
            out_side[part],
            train_lengths[piece * examples : (piece + 1) * examples],
        )
        partial.append(inner(piece_features, query_features))
    scores = jnp.concatenate(partial, axis=0)
    total = scores
    for step in range(1, tensor):
        turn = [(i, (i + step) % tensor) for i in range(tensor)]
        total = total + lax.ppermute(scores, "tensor", turn)
    return total / (RANK * SEQ)


def solution(mesh):
    tensor, dp = mesh.shape["tensor"], mesh.shape["dp"]

    def per_device(*arguments):
        if tensor == 4 and dp == 4:
            return moving_plan(tensor, *arguments)
        return gathering_plan(*arguments)

    in_specs = (
        P(("parts", "dp"), None, "tensor"),
        P(("parts", "dp"), None, "tensor"),
        P(("parts", "dp"), None, "tensor"),
        P(("parts", "dp"), None, "tensor"),
        P(("parts", "dp")),
        P(("parts", "dp"), None, "tensor"),
        P(("parts", "dp"), None, "tensor"),
        P(("parts", "dp"), None, "tensor"),
        P(("parts", "dp"), None, "tensor"),
        P(("parts", "dp")),
        P("tensor", "dp"),
        P(None, "tensor"),
        P(None, "tensor"),
        P(None, "tensor"),
        P(None, "tensor"),
        P(None, "tensor"),
    )
    out_specs = P(("parts", "dp"), None)
    return jax.shard_map(
        per_device, mesh=mesh, in_specs=in_specs, out_specs=out_specs, check_vma=False
    )
```

```python
import functools

import jax
import jax.numpy as jnp
from jax import lax
from jax.experimental import pallas as pl
from jax.experimental.pallas import tpu as pltpu
from jax.sharding import PartitionSpec as P

RANK = 64
SEQ = 64
TILE = 512
VMEM_BYTES = 40 * 1024 * 1024


def flatten(array):
    return array.reshape(-1, array.shape[-1])


def project(rows, table):
    return lax.dot_general(
        rows, table, (((1,), (1,)), ((), ())), preferred_element_type=jnp.float32
    )


def inner(left_side, right_side):
    return lax.dot_general(
        left_side,
        right_side,
        (((1,), (1,)), ((), ())),
        precision=lax.Precision.HIGHEST,
        preferred_element_type=jnp.float32,
    )


def gated_hidden(gate, up):
    gate_wide = gate.astype(jnp.float32)
    up_wide = up.astype(jnp.float32)
    return (gate_wide * jax.nn.sigmoid(gate_wide) * up_wide).astype(jnp.bfloat16)


def gradient_sides(gate, up, hidden_grad, proj_gate, proj_up):
    gate_wide = gate.astype(jnp.float32)
    up_wide = up.astype(jnp.float32)
    sigmoid_gate = jax.nn.sigmoid(gate_wide)
    silu_gate = gate_wide * sigmoid_gate
    gate_grad = (
        hidden_grad * up_wide * sigmoid_gate * (1.0 + gate_wide * (1.0 - sigmoid_gate))
    ).astype(jnp.bfloat16)
    up_grad = (hidden_grad * silu_gate).astype(jnp.bfloat16)
    return project(gate_grad, proj_gate), project(up_grad, proj_up)


def outer_sums(left_side, right_side, lengths):
    number = lengths.shape[0]
    length = left_side.shape[0] // number
    positions = lax.broadcasted_iota(jnp.int32, (number, length), 1)
    weights = (positions < lengths[:, None]).astype(jnp.float32)
    left_rows = left_side.reshape(number, length, left_side.shape[1]) * weights[:, :, None]
    right_rows = right_side.reshape(number, length, right_side.shape[1])
    summed = jnp.einsum("est,esu->etu", left_rows, right_rows, precision=lax.Precision.HIGHEST)
    return summed.reshape(number, -1)


def features(in_side, hidden_side, gate_side, up_side, out_side, lengths):
    return jnp.concatenate(
        [
            outer_sums(in_side, gate_side, lengths),
            outer_sums(in_side, up_side, lengths),
            outer_sums(hidden_side, out_side, lengths),
        ],
        axis=1,
    )


def gathering_plan(
    train_input,
    train_gate,
    train_up,
    train_outgrad,
    train_lengths,
    query_input,
    query_gate,
    query_up,
    query_outgrad,
    query_lengths,
    down_weight,
    proj_input,
    proj_outgrad,
    proj_hidden,
    proj_gate,
    proj_up,
):
    weight = lax.all_gather(down_weight, "dp", axis=1, tiled=True)

    def full_features(inputs, gate, up, outgrad, lengths):
        inputs, gate, up, outgrad = [flatten(a) for a in (inputs, gate, up, outgrad)]
        rows = lax.all_gather(outgrad, "tensor", axis=1, tiled=True)
        gate_side, up_side = gradient_sides(gate, up, project(rows, weight), proj_gate, proj_up)
        hidden_side = project(gated_hidden(gate, up), proj_hidden)
        sides = (
            project(inputs, proj_input),
            hidden_side,
            gate_side,
            up_side,
            project(outgrad, proj_outgrad),
        )
        return features(*lax.psum(sides, "tensor"), lengths)

    train_features = full_features(
        train_input, train_gate, train_up, train_outgrad, train_lengths
    )
    query_features = full_features(
        query_input, query_gate, query_up, query_outgrad, query_lengths
    )
    gathered = lax.all_gather(query_features, "dp", axis=0, tiled=True)
    return inner(train_features, gathered) / (RANK * SEQ)


def stacked_products(near, far, weight_own, weight_sib, stacked):
    number = near.shape[0]

    @pl.when(pl.program_id(0) == 0)
    def _():
        stacked[:number, :] = near[...]
        stacked[number:, :] = far[...]

    half = weight_own.shape[1]
    return project(stacked[:, :half], weight_own[...]) + project(
        stacked[:, half:], weight_sib[...]
    )


def add_sides(hidden_grad, gate, up, proj_gate, proj_up, gate_side, up_side):
    gate_part, up_part = gradient_sides(gate, up, hidden_grad, proj_gate, proj_up)
    first = pl.program_id(0) == 0

    @pl.when(first)
    def _():
        gate_side[...] = gate_part
        up_side[...] = up_part

    @pl.when(jnp.logical_not(first))
    def _():
        gate_side[...] += gate_part
        up_side[...] += up_part


def partial_kernel(near, far, weight_own, weight_sib, near_sum, far_sum, stacked):
    total = stacked_products(near, far, weight_own, weight_sib, stacked)
    number = near.shape[0]
    near_sum[...] = total[:number]
    far_sum[...] = total[number:].astype(jnp.bfloat16)


def finish_kernel(near_sum, returned, gate, up, proj_gate, proj_up, gate_side, up_side):
    hidden_grad = near_sum[...] + returned[...].astype(jnp.float32)
    add_sides(hidden_grad, gate[...], up[...], proj_gate[...], proj_up[...], gate_side, up_side)


def lent_kernel(
    near,
    far,
    weight_own,
    weight_sib,
    gate,
    up,
    far_gate,
    far_up,
    proj_gate,
    proj_up,
    gate_side,
    up_side,
    stacked,
):
    hidden_grad = stacked_products(near, far, weight_own, weight_sib, stacked)
    gates = jnp.concatenate([gate[...], far_gate[...]], axis=0)
    ups = jnp.concatenate([up[...], far_up[...]], axis=0)
    add_sides(hidden_grad, gates, ups, proj_gate[...], proj_up[...], gate_side, up_side)


def whole(shape):
    return pl.BlockSpec(shape, lambda i: (0, 0))


def columns(number):
    return pl.BlockSpec((number, TILE), lambda i: (0, i))


def rows(width):
    return pl.BlockSpec((TILE, width), lambda i: (i, 0))


def cost(flops, arrays):
    moved = sum(array.size * array.dtype.itemsize for array in arrays)
    return pl.CostEstimate(flops=flops, bytes_accessed=moved, transcendentals=0)


def partial_sums(near, far, weight_own, weight_sib):
    number, width = near.shape
    units, half = weight_own.shape
    return pl.pallas_call(
        partial_kernel,
        grid=(units // TILE,),
        in_specs=[whole(near.shape), whole(near.shape), rows(half), rows(half)],
        out_specs=[columns(number), columns(number)],
        out_shape=[
            jax.ShapeDtypeStruct((number, units), jnp.float32),
            jax.ShapeDtypeStruct((number, units), jnp.bfloat16),
        ],
        scratch_shapes=[pltpu.VMEM((2 * number, width), jnp.bfloat16)],
        compiler_params=pltpu.CompilerParams(vmem_limit_bytes=VMEM_BYTES),
        cost_estimate=cost(
            4 * number * width * units, (near, far, weight_own, weight_sib)
        ),
    )(near, far, weight_own, weight_sib)


def finished_sides(near_sum, returned, gate, up, proj_gate, proj_up):
    number, units = near_sum.shape
    side = jax.ShapeDtypeStruct((number, RANK), jnp.float32)
    return pl.pallas_call(
        finish_kernel,
        grid=(units // TILE,),
        in_specs=[columns(number)] * 4 + [columns(RANK)] * 2,
        out_specs=[whole(side.shape)] * 2,
        out_shape=[side] * 2,
        compiler_params=pltpu.CompilerParams(vmem_limit_bytes=VMEM_BYTES),
        cost_estimate=cost(
            4 * number * RANK * units, (near_sum, returned, gate, up, proj_gate, proj_up)
        ),
    )(near_sum, returned, gate, up, proj_gate, proj_up)


def lent_sides(near, far, weight_own, weight_sib, gate, up, far_gate, far_up, proj_gate, proj_up):
    number, width = near.shape
    units, half = weight_own.shape
    side = jax.ShapeDtypeStruct((2 * number, RANK), jnp.float32)
    operands = (
        near, far, weight_own, weight_sib, gate, up, far_gate, far_up, proj_gate, proj_up
    )
    return pl.pallas_call(
        lent_kernel,
        grid=(units // TILE,),
        in_specs=[whole(near.shape)] * 2
        + [rows(half)] * 2
        + [columns(number)] * 4
        + [columns(RANK)] * 2,
        out_specs=[whole(side.shape)] * 2,
        out_shape=[side] * 2,
        scratch_shapes=[pltpu.VMEM((2 * number, width), jnp.bfloat16)],
        compiler_params=pltpu.CompilerParams(vmem_limit_bytes=VMEM_BYTES),
        cost_estimate=cost(4 * number * width * units, operands),
    )(*operands)


def after(value, *others):
    return lax.optimization_barrier((value, *others))[0]


def moving_plan(
    train_input,
    train_gate,
    train_up,
    train_outgrad,
    train_lengths,
    query_input,
    query_gate,
    query_up,
    query_outgrad,
    query_lengths,
    down_weight,
    proj_input,
    proj_outgrad,
    proj_hidden,
    proj_gate,
    proj_up,
):
    t = lax.axis_index("tensor")
    d = lax.axis_index("dp")
    x, core = d // 2, d % 2
    upper, inner_chip = t // 2, (t == 1) | (t == 2)
    to_core = functools.partial(lax.ppermute, axis_name="dp", perm=[(i, i ^ 1) for i in range(4)])
    to_chip = functools.partial(lax.ppermute, axis_name="dp", perm=[(i, i ^ 2) for i in range(4)])
    outer = functools.partial(
        lax.ppermute, axis_name="tensor", perm=[(0, 1), (1, 0), (2, 3), (3, 2)]
    )
    middle = functools.partial(
        lax.ppermute, axis_name="tensor", perm=[(0, 0), (1, 2), (2, 1), (3, 3)]
    )
    across = functools.partial(
        lax.ppermute, axis_name="tensor", perm=[(0, 2), (1, 3), (2, 0), (3, 1)]
    )

    def tensor_sum(values):
        values = values + outer(values)
        return values + across(values)

    def hop_one(piece):
        return piece, outer(piece), middle(piece)

    def hop_two(piece, first, second_inner):
        return piece, first, second_inner, outer(second_inner), middle(first)

    def hop_three(piece, first, second_inner, second_outer, third_inner):
        second = jnp.where(inner_chip, second_inner, second_outer)
        third = jnp.where(inner_chip, third_inner, outer(third_inner))

        def column(chip, low):
            within = jnp.where(t % 2 == low, piece, first)
            beyond = jnp.where((t < 2) == (low == 0), second, third)
            return jnp.where(chip == upper, within, beyond)

        def wide(chip):
            return jnp.concatenate([column(chip, core), column(chip, 1 - core)], axis=1)

        return wide(x), wide(1 - x)

    q_input, q_gate, q_up, q_outgrad = [
        flatten(a) for a in (query_input, query_gate, query_up, query_outgrad)
    ]
    t_input, t_gate, t_up, t_outgrad = [
        flatten(a) for a in (train_input, train_gate, train_up, train_outgrad)
    ]
    examples = train_lengths.shape[0] // 2
    cut = examples * SEQ

    weight_own, weight_sib = down_weight, to_core(down_weight)

    far_gate, far_up = to_chip(t_gate[cut:]), to_chip(t_up[cut:])
    q_hops = hop_two(*hop_one(q_outgrad))
    a_hops = hop_one(after(t_outgrad[:cut], q_hops[3], far_gate))
    q_near, q_send = hop_three(*q_hops)
    q_far = to_chip(q_send)
    a_hops = hop_two(a_hops[0], after(a_hops[1], q_send, far_up), a_hops[2])
    b_hops = hop_one(after(t_outgrad[cut:], a_hops[3]))
    a_near, a_send = hop_three(*a_hops)
    a_far = to_chip(a_send)
    q_near_sum, q_far_sum = partial_sums(q_near, q_far, weight_own, weight_sib)
    b_hops = hop_two(b_hops[0], after(b_hops[1], a_send, q_far_sum), b_hops[2])
    b_near, b_send = hop_three(*b_hops)
    b_far = to_chip(b_send)

    in_side, out_side, q_in_side, q_hidden_side, q_out_side = lax.psum(
        (
            project(t_input, proj_input),
            project(t_outgrad, proj_outgrad),
            project(q_input, proj_input),
            project(gated_hidden(q_gate, q_up), proj_hidden),
            project(q_outgrad, proj_outgrad),
        ),
        "tensor",
    )
    hidden_side = project(gated_hidden(t_gate, t_up), proj_hidden)
    far_in_side = to_chip(in_side[cut:])
    far_lengths = to_chip(train_lengths[examples:])

    query_sides = finished_sides(
        q_near_sum, to_chip(q_far_sum), q_gate, q_up, proj_gate, proj_up
    )
    q_gate_side, q_up_side = jnp.split(
        tensor_sum(jnp.concatenate(query_sides, axis=1)), 2, axis=1
    )
    own_query_features = features(
        q_in_side, q_hidden_side, q_gate_side, q_up_side, q_out_side, query_lengths
    )
    query_features = lax.all_gather(own_query_features, "dp", axis=0, tiled=True)

    a_near_sum, a_far_sum = partial_sums(
        a_near, after(a_far, *query_sides), weight_own, weight_sib
    )
    a_gate_side, a_up_side = finished_sides(
        a_near_sum, to_chip(a_far_sum), t_gate[:cut], t_up[:cut], proj_gate, proj_up
    )
    b_gate_side, b_up_side = lent_sides(
        b_near,
        after(b_far, own_query_features),
        weight_own,
        weight_sib,
        t_gate[cut:],
        t_up[cut:],
        far_gate,
        far_up,
        proj_gate,
        proj_up,
    )
    a_features = features(
        in_side[:cut], hidden_side[:cut], a_gate_side, a_up_side, out_side[:cut],
        train_lengths[:examples],
    )
    b_features = features(
        in_side[cut:], hidden_side[cut:], b_gate_side[:cut], b_up_side[:cut], out_side[cut:],
        train_lengths[examples:],
    )
    far_features = jnp.concatenate(
        [
            outer_sums(far_in_side, b_gate_side[cut:], far_lengths),
            outer_sums(far_in_side, b_up_side[cut:], far_lengths),
        ],
        axis=1,
    )
    far_scores = inner(far_features, query_features[:, : far_features.shape[1]])
    a_scores = inner(a_features, query_features)
    b_scores = inner(b_features, query_features) + to_chip(far_scores)
    scores = tensor_sum(jnp.concatenate([a_scores, b_scores], axis=0))
    return scores / (RANK * SEQ)


def solution(mesh):
    tensor, dp = mesh.shape["tensor"], mesh.shape["dp"]

    def per_device(*arguments):
        if tensor == 4 and dp == 4:
            return moving_plan(*arguments)
        return gathering_plan(*arguments)

    in_specs = (
        P(("parts", "dp"), None, "tensor"),
        P(("parts", "dp"), None, "tensor"),
        P(("parts", "dp"), None, "tensor"),
        P(("parts", "dp"), None, "tensor"),
        P(("parts", "dp")),
        P(("parts", "dp"), None, "tensor"),
        P(("parts", "dp"), None, "tensor"),
        P(("parts", "dp"), None, "tensor"),
        P(("parts", "dp"), None, "tensor"),
        P(("parts", "dp")),
        P("tensor", "dp"),
        P(None, "tensor"),
        P(None, "tensor"),
        P(None, "tensor"),
        P(None, "tensor"),
        P(None, "tensor"),
    )
    out_specs = P(("parts", "dp"), None)
    return jax.shard_map(
        per_device, mesh=mesh, in_specs=in_specs, out_specs=out_specs, check_vma=False
    )
```

```python
import functools

import jax
import jax.numpy as jnp
from jax import lax
from jax.experimental import pallas as pl
from jax.experimental.pallas import tpu as pltpu
from jax.sharding import PartitionSpec as P

RANK = 64
SEQ = 64
TILE = 512
VMEM_BYTES = 40 * 1024 * 1024


def flatten(array):
    return array.reshape(-1, array.shape[-1])


def project(rows, table):
    return lax.dot_general(
        rows, table, (((1,), (1,)), ((), ())), preferred_element_type=jnp.float32
    )


def inner(left_side, right_side):
    return lax.dot_general(
        left_side,
        right_side,
        (((1,), (1,)), ((), ())),
        precision=lax.Precision.HIGHEST,
        preferred_element_type=jnp.float32,
    )


def gated_hidden(gate, up):
    gate_wide = gate.astype(jnp.float32)
    up_wide = up.astype(jnp.float32)
    return (gate_wide * jax.nn.sigmoid(gate_wide) * up_wide).astype(jnp.bfloat16)


def gradient_sides(gate, up, hidden_grad, proj_gate, proj_up):
    gate_wide = gate.astype(jnp.float32)
    up_wide = up.astype(jnp.float32)
    sigmoid_gate = jax.nn.sigmoid(gate_wide)
    silu_gate = gate_wide * sigmoid_gate
    gate_grad = (
        hidden_grad * up_wide * sigmoid_gate * (1.0 + gate_wide * (1.0 - sigmoid_gate))
    ).astype(jnp.bfloat16)
    up_grad = (hidden_grad * silu_gate).astype(jnp.bfloat16)
    return project(gate_grad, proj_gate), project(up_grad, proj_up)


def outer_sums(left_side, right_side, lengths):
    number = lengths.shape[0]
    length = left_side.shape[0] // number
    positions = lax.broadcasted_iota(jnp.int32, (number, length), 1)
    weights = (positions < lengths[:, None]).astype(jnp.float32)
    left_rows = left_side.reshape(number, length, left_side.shape[1]) * weights[:, :, None]
    right_rows = right_side.reshape(number, length, right_side.shape[1])
    summed = jnp.einsum("est,esu->etu", left_rows, right_rows, precision=lax.Precision.HIGHEST)
    return summed.reshape(number, -1)


def features(in_side, hidden_side, gate_side, up_side, out_side, lengths):
    return jnp.concatenate(
        [
            outer_sums(in_side, gate_side, lengths),
            outer_sums(in_side, up_side, lengths),
            outer_sums(hidden_side, out_side, lengths),
        ],
        axis=1,
    )


def gathering_plan(
    train_input,
    train_gate,
    train_up,
    train_outgrad,
    train_lengths,
    query_input,
    query_gate,
    query_up,
    query_outgrad,
    query_lengths,
    down_weight,
    proj_input,
    proj_outgrad,
    proj_hidden,
    proj_gate,
    proj_up,
):
    weight = lax.all_gather(down_weight, "dp", axis=1, tiled=True)

    def full_features(inputs, gate, up, outgrad, lengths):
        inputs, gate, up, outgrad = [flatten(a) for a in (inputs, gate, up, outgrad)]
        rows = lax.all_gather(outgrad, "tensor", axis=1, tiled=True)
        gate_side, up_side = gradient_sides(gate, up, project(rows, weight), proj_gate, proj_up)
        hidden_side = project(gated_hidden(gate, up), proj_hidden)
        sides = (
            project(inputs, proj_input),
            hidden_side,
            gate_side,
            up_side,
            project(outgrad, proj_outgrad),
        )
        return features(*lax.psum(sides, "tensor"), lengths)

    train_features = full_features(
        train_input, train_gate, train_up, train_outgrad, train_lengths
    )
    query_features = full_features(
        query_input, query_gate, query_up, query_outgrad, query_lengths
    )
    gathered = lax.all_gather(query_features, "dp", axis=0, tiled=True)
    return inner(train_features, gathered) / (RANK * SEQ)


ANYWHERE = pl.BlockSpec(memory_space=pl.ANY)
SCALARS = pl.BlockSpec(memory_space=pltpu.SMEM)
IN_VMEM = pl.BlockSpec(memory_space=pltpu.VMEM)


def params():
    return pltpu.CompilerParams(vmem_limit_bytes=VMEM_BYTES)


def cost(flops, arrays):
    moved = sum(array.size * array.dtype.itemsize for array in arrays)
    return pl.CostEstimate(flops=flops, bytes_accessed=moved, transcendentals=0)


def tile_columns(number, block=0):
    return pl.BlockSpec((number, TILE), lambda i: (block, i))


def tile_rows(width):
    return pl.BlockSpec((TILE, width), lambda i: (i, 0))


def whole(shape):
    return pl.BlockSpec(shape, lambda i: tuple(0 for _ in shape))


def stacked_products(flags, pairs, far, weight_own, weight_sib, stacked, semaphores):
    number = far.shape[1]

    @pl.when(pl.program_id(0) == 0)
    def _():
        slot = flags[1]
        far_copies = [
            pltpu.make_async_copy(
                far.at[i], stacked.at[jnp.bitwise_xor(slot, i), pl.ds(number, number)],
                semaphores.at[2 + i],
            )
            for i in range(2)
        ]
        for copy in far_copies:
            copy.start()
        for code, pair in enumerate(pairs):

            @pl.when(flags[0] == code)
            def _():
                copies = [
                    pltpu.make_async_copy(
                        pair[i], stacked.at[jnp.bitwise_xor(slot, i), pl.ds(0, number)],
                        semaphores.at[i],
                    )
                    for i in range(2)
                ]
                for copy in copies:
                    copy.start()
                for copy in copies:
                    copy.wait()

        for copy in far_copies:
            copy.wait()

    return project(weight_own[...], stacked[0]) + project(weight_sib[...], stacked[1])


def add_sides(hidden_grad, gate, up, proj_gate, proj_up, sides):
    gate_part, up_part = gradient_sides(gate, up, hidden_grad, proj_gate, proj_up)
    part = jnp.concatenate([gate_part, up_part], axis=1)
    first = pl.program_id(0) == 0

    @pl.when(first)
    def _():
        sides[...] = part

    @pl.when(jnp.logical_not(first))
    def _():
        sides[...] += part


def partial_kernel(
    flags, b0, b1, b2, b3, b4, b5, far, weight_own, weight_sib, near_sum, far_sum, stacked, sems
):
    pairs = ((b0, b1), (b2, b3), (b4, b5))
    total = stacked_products(flags, pairs, far, weight_own, weight_sib, stacked, sems)
    number = far.shape[1]
    near_sum[...] = total[:, :number]
    far_sum[...] = total[:, number:].astype(jnp.bfloat16)


def partial_sums(flags, blocks, far, weight_own, weight_sib):
    number, half = blocks[0].shape
    units = weight_own.shape[0]
    return pl.pallas_call(
        partial_kernel,
        grid=(units // TILE,),
        in_specs=[SCALARS] + [ANYWHERE] * 7 + [tile_rows(half)] * 2,
        out_specs=[tile_rows(number)] * 2,
        out_shape=[
            jax.ShapeDtypeStruct((units, number), jnp.float32),
            jax.ShapeDtypeStruct((units, number), jnp.bfloat16),
        ],
        scratch_shapes=[
            pltpu.VMEM((2, 2 * number, half), jnp.bfloat16),
            pltpu.SemaphoreType.DMA((4,)),
        ],
        compiler_params=params(),
        cost_estimate=cost(8 * number * half * units, (far, weight_own, weight_sib)),
    )(flags, *blocks, far, weight_own, weight_sib)


def finish_kernel(near_sum, returned, gate, up, proj_gate, proj_up, sides):
    hidden_grad = (near_sum[...] + returned[...].astype(jnp.float32)).T
    add_sides(hidden_grad, gate[...], up[...], proj_gate[...], proj_up[...], sides)


def finished_sides(near_sum, returned, gate, up, proj_gate, proj_up):
    units, number = near_sum.shape
    return pl.pallas_call(
        finish_kernel,
        grid=(units // TILE,),
        in_specs=[tile_rows(number)] * 2 + [tile_columns(number)] * 2 + [tile_columns(RANK)] * 2,
        out_specs=whole((number, 2 * RANK)),
        out_shape=jax.ShapeDtypeStruct((number, 2 * RANK), jnp.float32),
        compiler_params=params(),
        cost_estimate=cost(4 * number * RANK * units, (near_sum, returned, gate, up)),
    )(near_sum, returned, gate, up, proj_gate, proj_up)


def lent_kernel(
    flags, b0, b1, b2, b3, b4, b5, far, weight_own, weight_sib, gate, up, far_gate, far_up,
    proj_gate, proj_up, sides, stacked, sems,
):
    pairs = ((b0, b1), (b2, b3), (b4, b5))
    total = stacked_products(flags, pairs, far, weight_own, weight_sib, stacked, sems)
    gates = jnp.concatenate([gate[...], far_gate[...]], axis=0)
    ups = jnp.concatenate([up[...], far_up[...]], axis=0)
    add_sides(total.T, gates, ups, proj_gate[...], proj_up[...], sides)


def lent_sides(
    flags, blocks, far, weight_own, weight_sib, gate, up, far_gate, far_up, proj_gate, proj_up
):
    number, half = blocks[0].shape
    units = weight_own.shape[0]
    return pl.pallas_call(
        lent_kernel,
        grid=(units // TILE,),
        in_specs=[SCALARS]
        + [ANYWHERE] * 7
        + [tile_rows(half)] * 2
        + [tile_columns(number, 1)] * 2
        + [tile_columns(number)] * 2
        + [tile_columns(RANK)] * 2,
        out_specs=whole((2 * number, 2 * RANK)),
        out_shape=jax.ShapeDtypeStruct((2 * number, 2 * RANK), jnp.float32),
        scratch_shapes=[
            pltpu.VMEM((2, 2 * number, half), jnp.bfloat16),
            pltpu.SemaphoreType.DMA((4,)),
        ],
        compiler_params=params(),
        cost_estimate=cost(8 * number * half * units, (far, weight_own, weight_sib)),
    )(
        flags, *blocks, far, weight_own, weight_sib, gate, up, far_gate, far_up, proj_gate, proj_up
    )


def early_kernel(
    t_input, q_input, t_outgrad, q_outgrad, proj_input, proj_outgrad, t_gate, t_up, q_gate, q_up,
    proj_hidden, sides,
):
    number = t_input.shape[0]
    middle = pl.ds(RANK, RANK)
    t_hidden = project(gated_hidden(t_gate[...], t_up[...]), proj_hidden[...])
    q_hidden = project(gated_hidden(q_gate[...], q_up[...]), proj_hidden[...])
    first = pl.program_id(0) == 0

    @pl.when(first)
    def _():
        for inputs, outgrad, hidden, part in (
            (t_input, t_outgrad, t_hidden, slice(0, number)),
            (q_input, q_outgrad, q_hidden, slice(number, None)),
        ):
            sides[part, :] = jnp.concatenate(
                [
                    project(inputs[...], proj_input[...]),
                    hidden,
                    project(outgrad[...], proj_outgrad[...]),
                ],
                axis=1,
            )

    @pl.when(jnp.logical_not(first))
    def _():
        sides[:number, middle] += t_hidden
        sides[number:, middle] += q_hidden


def early_sides(
    t_input, q_input, t_outgrad, q_outgrad, proj_input, proj_outgrad, t_gate, t_up, q_gate, q_up,
    proj_hidden,
):
    train, query, units = t_gate.shape[0], q_gate.shape[0], t_gate.shape[1]
    wide = (t_input, q_input, t_outgrad, q_outgrad, proj_input, proj_outgrad)
    tiled = (t_gate, t_up, q_gate, q_up, proj_hidden)
    return pl.pallas_call(
        early_kernel,
        grid=(units // TILE,),
        in_specs=[whole(a.shape) for a in wide] + [tile_columns(a.shape[0]) for a in tiled],
        out_specs=whole((train + query, 3 * RANK)),
        out_shape=jax.ShapeDtypeStruct((train + query, 3 * RANK), jnp.float32),
        compiler_params=params(),
        cost_estimate=cost(2 * (train + query) * RANK * units, wide + tiled),
    )(*wide, *tiled)


def outer_sum(left_side, right_side, weight):
    return lax.dot_general(
        left_side * weight,
        right_side,
        (((0,), (0,)), ((), ())),
        precision=lax.Precision.HIGHEST,
        preferred_element_type=jnp.float32,
    )


def example_features(in_side, hidden_side, gate_side, up_side, out_side, length):
    positions = lax.broadcasted_iota(jnp.int32, (SEQ, RANK), 0)
    weight = (positions < length).astype(jnp.float32)
    return (
        outer_sum(in_side, gate_side, weight),
        outer_sum(in_side, up_side, weight),
        outer_sum(hidden_side, out_side, weight),
    )


def query_kernel(lengths, sides, gradient, found):
    for e in range(found.shape[0]):
        part = slice(e * SEQ, (e + 1) * SEQ)
        three = example_features(
            sides[part, :RANK],
            sides[part, RANK : 2 * RANK],
            gradient[part, :RANK],
            gradient[part, RANK:],
            sides[part, 2 * RANK :],
            lengths[e],
        )
        for segment in range(3):
            found[e, segment * RANK : (segment + 1) * RANK, :] = three[segment]


def query_features(lengths, sides, gradient):
    return pl.pallas_call(
        query_kernel,
        in_specs=[SCALARS, IN_VMEM, IN_VMEM],
        out_specs=IN_VMEM,
        out_shape=jax.ShapeDtypeStruct((lengths.shape[0], 3 * RANK, RANK), jnp.float32),
        compiler_params=params(),
    )(lengths, sides, gradient)


def score_kernel(
    lengths, place, whole_sides, own_sides, near, far, q0, q1, q2, q3, scores
):
    queries = q0.shape[0]
    shape = scores.shape
    row = lax.broadcasted_iota(jnp.int32, shape, 0)
    column = lax.broadcasted_iota(jnp.int32, shape, 1)
    total = jnp.zeros(shape, jnp.float32)
    for e in range(shape[0]):
        part = slice(e * SEQ, (e + 1) * SEQ)
        gradient = near[part, :] + far[part, :]
        three = jnp.concatenate(
            example_features(
                whole_sides[part, :RANK],
                own_sides[part, RANK : 2 * RANK],
                gradient[:, :RANK],
                gradient[:, RANK:],
                whole_sides[part, 2 * RANK :],
                lengths[e],
            ),
            axis=0,
        )
        for step, found in enumerate((q0, q1, q2, q3)):
            for j in range(queries):
                value = jnp.sum(three * found[j], keepdims=True)
                here = (row == e) & (
                    column == queries * jnp.bitwise_xor(place[0], step) + j
                )
                total = total + jnp.where(here, value, 0.0)
    scores[...] = total


def partial_scores(lengths, place, whole_sides, own_sides, near, far, found):
    number = lengths.shape[0]
    return pl.pallas_call(
        score_kernel,
        in_specs=[SCALARS] * 2 + [IN_VMEM] * 8,
        out_specs=IN_VMEM,
        out_shape=jax.ShapeDtypeStruct((number, 4 * found[0].shape[0]), jnp.float32),
        compiler_params=params(),
    )(lengths, place, whole_sides, own_sides, near, far, *found)


def after(value, *others):
    return lax.optimization_barrier((value, *others))[0]


def moving_plan(
    train_input,
    train_gate,
    train_up,
    train_outgrad,
    train_lengths,
    query_input,
    query_gate,
    query_up,
    query_outgrad,
    query_lengths,
    down_weight,
    proj_input,
    proj_outgrad,
    proj_hidden,
    proj_gate,
    proj_up,
):
    t = lax.axis_index("tensor")
    d = lax.axis_index("dp")
    x, core, upper = d // 2, d % 2, t // 2
    at_home = x == upper
    inner_chip = (t == 1) | (t == 2)
    near_code = jnp.where(at_home, 0, jnp.where(inner_chip, 1, 2))
    first_parity = jnp.where(at_home, t % 2, upper)
    flags = jnp.stack([near_code, first_parity ^ core]).astype(jnp.int32)
    place = jnp.stack([d]).astype(jnp.int32)

    to_core = functools.partial(lax.ppermute, axis_name="dp", perm=[(i, i ^ 1) for i in range(4)])
    to_chip = functools.partial(lax.ppermute, axis_name="dp", perm=[(i, i ^ 2) for i in range(4)])
    outer = functools.partial(
        lax.ppermute, axis_name="tensor", perm=[(i, i ^ 1) for i in range(4)]
    )
    across = functools.partial(
        lax.ppermute, axis_name="tensor", perm=[(i, i ^ 2) for i in range(4)]
    )
    middle = functools.partial(
        lax.ppermute,
        axis_name=("tensor", "dp"),
        perm=[
            (4 * i + j, 4 * (3 - i) + j) if i in (1, 2) else (4 * i + j, 4 * i + (j ^ 1))
            for i in range(4)
            for j in range(4)
        ],
    )

    def tensor_sum(values):
        values = values + outer(values)
        return values + across(values)

    def crossing_pair(piece, first, second_inner, third_inner, second_outer, third_outer):
        def choose(within, beyond_inner, beyond_outer):
            beyond = jnp.where(inner_chip, beyond_inner, beyond_outer)
            return jnp.where(at_home, beyond, within)

        return jnp.stack(
            [choose(piece, second_inner, second_outer), choose(first, third_inner, third_outer)]
        )

    q_input, q_gate, q_up, q_outgrad = [
        flatten(a) for a in (query_input, query_gate, query_up, query_outgrad)
    ]
    t_input, t_gate, t_up, t_outgrad = [
        flatten(a) for a in (train_input, train_gate, train_up, train_outgrad)
    ]
    examples = train_lengths.shape[0] // 2
    cut = examples * SEQ

    weight_own, weight_sib = down_weight, to_core(down_weight)

    q_one, q_mid = outer(q_outgrad), middle(q_outgrad)
    lent = to_chip(jnp.stack([t_gate[cut:], t_up[cut:]]))
    own_sides = early_sides(
        t_input, q_input, t_outgrad, q_outgrad, proj_input, proj_outgrad, t_gate, t_up, q_gate,
        q_up, proj_hidden,
    )
    q_two, q_last = outer(q_mid), middle(q_one)
    whole_sides = lax.psum(own_sides, "tensor")
    q_three = outer(after(q_last, own_sides))
    q_blocks = (q_outgrad, q_one, q_mid, q_last, q_two, q_three)

    a_rows = after(t_outgrad[:cut], q_two)
    a_one, a_mid = outer(a_rows), middle(a_rows)
    q_send = crossing_pair(*q_blocks)
    q_far = to_chip(q_send)
    a_one, a_mid = lax.optimization_barrier((a_one, a_mid, q_send, lent))[:2]
    a_two, a_last = outer(a_mid), middle(a_one)
    a_three = outer(a_last)
    a_blocks = (a_rows, a_one, a_mid, a_last, a_two, a_three)

    b_rows = after(t_outgrad[cut:], a_two, q_far)
    b_one, b_mid = outer(b_rows), middle(b_rows)
    a_send = crossing_pair(*a_blocks)
    a_far = to_chip(a_send)
    q_near_sum, q_far_sum = partial_sums(
        flags, q_blocks, after(q_far, a_send), weight_own, weight_sib
    )
    b_one, b_mid = lax.optimization_barrier((b_one, b_mid, q_far_sum))[:2]
    b_two, b_last = outer(b_mid), middle(b_one)
    b_three = outer(b_last)
    b_blocks = (b_rows, b_one, b_mid, b_last, b_two, b_three)

    q_gradient = finished_sides(
        q_near_sum, after(to_chip(q_far_sum), a_far), q_gate, q_up, proj_gate, proj_up
    )
    b_send = crossing_pair(*b_blocks)
    b_far = to_chip(b_send)
    a_near_sum, a_far_sum = partial_sums(
        flags, a_blocks, after(a_far, q_gradient, b_send), weight_own, weight_sib
    )
    own_found = query_features(
        query_lengths, whole_sides[2 * cut :], tensor_sum(q_gradient)
    )
    core_found = to_core(own_found)
    found = (own_found, core_found, to_chip(own_found), to_chip(core_found))

    b_gradient = lent_sides(
        flags, b_blocks, after(b_far, own_found), weight_own, weight_sib, t_gate, t_up, lent[0],
        lent[1], proj_gate, proj_up,
    )
    a_gradient = finished_sides(
        a_near_sum, to_chip(a_far_sum), t_gate, t_up, proj_gate, proj_up
    )
    a_scores = partial_scores(
        train_lengths[:examples], place, whole_sides[:cut], own_sides[:cut], a_gradient,
        jnp.zeros_like(a_gradient), found,
    )
    b_scores = partial_scores(
        train_lengths[examples:], place, whole_sides[cut : 2 * cut], own_sides[cut : 2 * cut],
        b_gradient[:cut], to_chip(b_gradient[cut:]), found,
    )
    scores = tensor_sum(jnp.concatenate([a_scores, b_scores], axis=0))
    return scores / (RANK * SEQ)


def solution(mesh):
    tensor, dp = mesh.shape["tensor"], mesh.shape["dp"]

    def per_device(*arguments):
        if tensor == 4 and dp == 4:
            return moving_plan(*arguments)
        return gathering_plan(*arguments)

    in_specs = (
        P(("parts", "dp"), None, "tensor"),
        P(("parts", "dp"), None, "tensor"),
        P(("parts", "dp"), None, "tensor"),
        P(("parts", "dp"), None, "tensor"),
        P(("parts", "dp")),
        P(("parts", "dp"), None, "tensor"),
        P(("parts", "dp"), None, "tensor"),
        P(("parts", "dp"), None, "tensor"),
        P(("parts", "dp"), None, "tensor"),
        P(("parts", "dp")),
        P("tensor", "dp"),
        P(None, "tensor"),
        P(None, "tensor"),
        P(None, "tensor"),
        P(None, "tensor"),
        P(None, "tensor"),
    )
    out_specs = P(("parts", "dp"), None)
    return jax.shard_map(
        per_device, mesh=mesh, in_specs=in_specs, out_specs=out_specs, check_vma=False
    )
```

```python
import functools

import jax
import jax.numpy as jnp
from jax import lax
from jax.experimental import pallas as pl
from jax.experimental.pallas import tpu as pltpu
from jax.sharding import PartitionSpec as P

RANK = 64
SEQ = 64
TILE = 512
VMEM_BYTES = 58 * 1024 * 1024


def flatten(array):
    return array.reshape(-1, array.shape[-1])


def project(rows, table):
    return lax.dot_general(
        rows, table, (((1,), (1,)), ((), ())), preferred_element_type=jnp.float32
    )


def inner(left_side, right_side):
    return lax.dot_general(
        left_side,
        right_side,
        (((1,), (1,)), ((), ())),
        precision=lax.Precision.HIGHEST,
        preferred_element_type=jnp.float32,
    )


def gated_hidden(gate, up):
    gate_wide = gate.astype(jnp.float32)
    up_wide = up.astype(jnp.float32)
    return (gate_wide * jax.nn.sigmoid(gate_wide) * up_wide).astype(jnp.bfloat16)


def gradient_sides(gate, up, hidden_grad, proj_gate, proj_up):
    gate_wide = gate.astype(jnp.float32)
    up_wide = up.astype(jnp.float32)
    sigmoid_gate = jax.nn.sigmoid(gate_wide)
    silu_gate = gate_wide * sigmoid_gate
    gate_grad = (
        hidden_grad * up_wide * sigmoid_gate * (1.0 + gate_wide * (1.0 - sigmoid_gate))
    ).astype(jnp.bfloat16)
    up_grad = (hidden_grad * silu_gate).astype(jnp.bfloat16)
    return project(gate_grad, proj_gate), project(up_grad, proj_up)


def outer_sums(left_side, right_side, lengths):
    number = lengths.shape[0]
    length = left_side.shape[0] // number
    positions = lax.broadcasted_iota(jnp.int32, (number, length), 1)
    weights = (positions < lengths[:, None]).astype(jnp.float32)
    left_rows = left_side.reshape(number, length, left_side.shape[1]) * weights[:, :, None]
    right_rows = right_side.reshape(number, length, right_side.shape[1])
    summed = jnp.einsum("est,esu->etu", left_rows, right_rows, precision=lax.Precision.HIGHEST)
    return summed.reshape(number, -1)


def features(in_side, hidden_side, gate_side, up_side, out_side, lengths):
    return jnp.concatenate(
        [
            outer_sums(in_side, gate_side, lengths),
            outer_sums(in_side, up_side, lengths),
            outer_sums(hidden_side, out_side, lengths),
        ],
        axis=1,
    )


def gathering_plan(
    train_input,
    train_gate,
    train_up,
    train_outgrad,
    train_lengths,
    query_input,
    query_gate,
    query_up,
    query_outgrad,
    query_lengths,
    down_weight,
    proj_input,
    proj_outgrad,
    proj_hidden,
    proj_gate,
    proj_up,
):
    weight = lax.all_gather(down_weight, "dp", axis=1, tiled=True)

    def full_features(inputs, gate, up, outgrad, lengths):
        inputs, gate, up, outgrad = [flatten(a) for a in (inputs, gate, up, outgrad)]
        rows = lax.all_gather(outgrad, "tensor", axis=1, tiled=True)
        gate_side, up_side = gradient_sides(gate, up, project(rows, weight), proj_gate, proj_up)
        hidden_side = project(gated_hidden(gate, up), proj_hidden)
        sides = (
            project(inputs, proj_input),
            hidden_side,
            gate_side,
            up_side,
            project(outgrad, proj_outgrad),
        )
        return features(*lax.psum(sides, "tensor"), lengths)

    train_features = full_features(
        train_input, train_gate, train_up, train_outgrad, train_lengths
    )
    query_features = full_features(
        query_input, query_gate, query_up, query_outgrad, query_lengths
    )
    gathered = lax.all_gather(query_features, "dp", axis=0, tiled=True)
    return inner(train_features, gathered) / (RANK * SEQ)


ANYWHERE = pl.BlockSpec(memory_space=pl.ANY)
SCALARS = pl.BlockSpec(memory_space=pltpu.SMEM)
IN_VMEM = pl.BlockSpec(memory_space=pltpu.VMEM)


def params():
    return pltpu.CompilerParams(vmem_limit_bytes=VMEM_BYTES)


def cost(flops, arrays):
    moved = sum(array.size * array.dtype.itemsize for array in arrays)
    return pl.CostEstimate(flops=flops, bytes_accessed=moved, transcendentals=0)


def tile_columns(number, block=0):
    return pl.BlockSpec((number, TILE), lambda i: (block, i))


def tile_rows(width):
    return pl.BlockSpec((TILE, width), lambda i: (i, 0))


def whole(shape):
    return pl.BlockSpec(shape, lambda i: tuple(0 for _ in shape))


def stacked_products(flags, blocks, weights, stacked, held, row_sems, weight_sems):
    own, pa, cross, pb, qa, qb, qc, pc, next_cross, next_pa = blocks
    picks = (
        (own, pa, cross, pb),
        (pa, own, pb, cross),
        (qb, qa, next_cross, qc),
        (pc, pb, next_cross, next_pa),
    )
    number = own.shape[0]
    step = pl.program_id(0)

    def weight_copies(tile):
        part = pl.ds(pl.multiple_of(tile * TILE, TILE), TILE)
        return [
            pltpu.make_async_copy(
                weights[side].at[part], held.at[side, part], weight_sems.at[side, tile]
            )
            for side in range(2)
        ]

    @pl.when(step == 0)
    def _():
        for code, pick in enumerate(picks):

            @pl.when(flags[0] == code)
            def _():
                copies = [
                    pltpu.make_async_copy(
                        block,
                        stacked.at[
                            jnp.bitwise_xor(flags[1], i % 2), pl.ds((i // 2) * number, number)
                        ],
                        row_sems.at[i],
                    )
                    for i, block in enumerate(pick)
                ]
                for copy in copies:
                    copy.start()
                for tile in range(held.shape[1] // TILE):
                    for copy in weight_copies(tile):
                        copy.start()
                for copy in copies:
                    copy.wait()

    for copy in weight_copies(step):
        copy.wait()
    part = pl.ds(pl.multiple_of(step * TILE, TILE), TILE)
    return project(held[0, part, :], stacked[0]) + project(held[1, part, :], stacked[1])


def product_scratch(number, half, units):
    return [
        pltpu.VMEM((2, 2 * number, half), jnp.bfloat16),
        pltpu.VMEM((2, units, half), jnp.bfloat16),
        pltpu.SemaphoreType.DMA((4,)),
        pltpu.SemaphoreType.DMA((2, units // TILE)),
    ]


def add_sides(hidden_grad, gate, up, proj_gate, proj_up, sides):
    gate_part, up_part = gradient_sides(gate, up, hidden_grad, proj_gate, proj_up)
    part = jnp.concatenate([gate_part, up_part], axis=1)
    first = pl.program_id(0) == 0

    @pl.when(first)
    def _():
        sides[...] = part

    @pl.when(jnp.logical_not(first))
    def _():
        sides[...] += part


def partial_kernel(*refs):
    flags, blocks, weights, (near_sum, far_sum), scratch = (
        refs[0], refs[1:11], refs[11:13], refs[13:15], refs[15:]
    )
    total = stacked_products(flags, blocks, weights, *scratch)
    number = blocks[0].shape[0]
    near_sum[...] = total[:, :number]
    far_sum[...] = total[:, number:].astype(jnp.bfloat16)


def partial_sums(flags, blocks, weights):
    number, half = blocks[0].shape
    units = weights[0].shape[0]
    return pl.pallas_call(
        partial_kernel,
        grid=(units // TILE,),
        in_specs=[SCALARS] + [ANYWHERE] * 12,
        out_specs=[tile_rows(number)] * 2,
        out_shape=[
            jax.ShapeDtypeStruct((units, number), jnp.float32),
            jax.ShapeDtypeStruct((units, number), jnp.bfloat16),
        ],
        scratch_shapes=product_scratch(number, half, units),
        compiler_params=params(),
        cost_estimate=cost(8 * number * half * units, weights),
    )(flags, *blocks, *weights)


def finish_kernel(near_sum, returned, gate, up, proj_gate, proj_up, sides):
    hidden_grad = (near_sum[...] + returned[...].astype(jnp.float32)).T
    add_sides(hidden_grad, gate[...], up[...], proj_gate[...], proj_up[...], sides)


def finished_sides(near_sum, returned, gate, up, proj_gate, proj_up):
    units, number = near_sum.shape
    return pl.pallas_call(
        finish_kernel,
        grid=(units // TILE,),
        in_specs=[tile_rows(number)] * 2 + [tile_columns(number)] * 2 + [tile_columns(RANK)] * 2,
        out_specs=whole((number, 2 * RANK)),
        out_shape=jax.ShapeDtypeStruct((number, 2 * RANK), jnp.float32),
        compiler_params=params(),
        cost_estimate=cost(4 * number * RANK * units, (near_sum, returned, gate, up)),
    )(near_sum, returned, gate, up, proj_gate, proj_up)


def lent_kernel(*refs):
    flags, blocks, weights, operands, sides, scratch = (
        refs[0], refs[1:11], refs[11:13], refs[13:19], refs[19], refs[20:]
    )
    gate, up, far_gate, far_up, proj_gate, proj_up = operands
    total = stacked_products(flags, blocks, weights, *scratch)
    gates = jnp.concatenate([gate[...], far_gate[...]], axis=0)
    ups = jnp.concatenate([up[...], far_up[...]], axis=0)
    add_sides(total.T, gates, ups, proj_gate[...], proj_up[...], sides)


def lent_sides(flags, blocks, weights, gate, up, far_gate, far_up, proj_gate, proj_up):
    number, half = blocks[0].shape
    units = weights[0].shape[0]
    return pl.pallas_call(
        lent_kernel,
        grid=(units // TILE,),
        in_specs=[SCALARS]
        + [ANYWHERE] * 12
        + [tile_columns(number, 1)] * 2
        + [tile_columns(number)] * 2
        + [tile_columns(RANK)] * 2,
        out_specs=whole((2 * number, 2 * RANK)),
        out_shape=jax.ShapeDtypeStruct((2 * number, 2 * RANK), jnp.float32),
        scratch_shapes=product_scratch(number, half, units),
        compiler_params=params(),
        cost_estimate=cost(8 * number * half * units, weights),
    )(flags, *blocks, *weights, gate, up, far_gate, far_up, proj_gate, proj_up)


def early_kernel(
    t_input, q_input, t_outgrad, q_outgrad, proj_input, proj_outgrad, t_gate, t_up, q_gate, q_up,
    proj_hidden, in_out, hidden,
):
    number = t_input.shape[0]
    t_hidden = project(gated_hidden(t_gate[...], t_up[...]), proj_hidden[...])
    q_hidden = project(gated_hidden(q_gate[...], q_up[...]), proj_hidden[...])
    first = pl.program_id(0) == 0

    @pl.when(first)
    def _():
        for inputs, outgrad, part in (
            (t_input, t_outgrad, slice(0, number)),
            (q_input, q_outgrad, slice(number, None)),
        ):
            in_out[part, :] = jnp.concatenate(
                [
                    project(inputs[...], proj_input[...]),
                    project(outgrad[...], proj_outgrad[...]),
                ],
                axis=1,
            )
        hidden[:number, :] = t_hidden
        hidden[number:, :] = q_hidden

    @pl.when(jnp.logical_not(first))
    def _():
        hidden[:number, :] += t_hidden
        hidden[number:, :] += q_hidden


def early_sides(
    t_input, q_input, t_outgrad, q_outgrad, proj_input, proj_outgrad, t_gate, t_up, q_gate, q_up,
    proj_hidden,
):
    total, units = t_gate.shape[0] + q_gate.shape[0], t_gate.shape[1]
    wide = (t_input, q_input, t_outgrad, q_outgrad, proj_input, proj_outgrad)
    tiled = (t_gate, t_up, q_gate, q_up, proj_hidden)
    shapes = ((total, 2 * RANK), (total, RANK))
    return pl.pallas_call(
        early_kernel,
        grid=(units // TILE,),
        in_specs=[whole(a.shape) for a in wide] + [tile_columns(a.shape[0]) for a in tiled],
        out_specs=[whole(shape) for shape in shapes],
        out_shape=[jax.ShapeDtypeStruct(shape, jnp.float32) for shape in shapes],
        compiler_params=params(),
        cost_estimate=cost(2 * total * RANK * units, wide + tiled),
    )(*wide, *tiled)


def outer_sum(left_side, right_side, weight):
    return lax.dot_general(
        left_side * weight,
        right_side,
        (((0,), (0,)), ((), ())),
        precision=lax.Precision.HIGHEST,
        preferred_element_type=jnp.float32,
    )


def example_features(in_side, hidden_side, gate_side, up_side, out_side, length):
    positions = lax.broadcasted_iota(jnp.int32, (SEQ, RANK), 0)
    weight = (positions < length).astype(jnp.float32)
    return (
        outer_sum(in_side, gate_side, weight),
        outer_sum(in_side, up_side, weight),
        outer_sum(hidden_side, out_side, weight),
    )


def query_kernel(lengths, in_out, sums, found):
    for e in range(found.shape[0]):
        part = slice(e * SEQ, (e + 1) * SEQ)
        three = example_features(
            in_out[part, :RANK],
            sums[part, 2 * RANK :],
            sums[part, :RANK],
            sums[part, RANK : 2 * RANK],
            in_out[part, RANK:],
            lengths[e],
        )
        for segment in range(3):
            found[e, segment * RANK : (segment + 1) * RANK, :] = three[segment]


def query_features(lengths, in_out, sums):
    return pl.pallas_call(
        query_kernel,
        in_specs=[SCALARS, IN_VMEM, IN_VMEM],
        out_specs=IN_VMEM,
        out_shape=jax.ShapeDtypeStruct((lengths.shape[0], 3 * RANK, RANK), jnp.float32),
        compiler_params=params(),
    )(lengths, in_out, sums)


def score_kernel(
    lengths, place, in_out, hidden, near, far, q0, q1, q2, q3, scores
):
    queries = q0.shape[0]
    shape = scores.shape
    row = lax.broadcasted_iota(jnp.int32, shape, 0)
    column = lax.broadcasted_iota(jnp.int32, shape, 1)
    total = jnp.zeros(shape, jnp.float32)
    for e in range(shape[0]):
        part = slice(e * SEQ, (e + 1) * SEQ)
        gradient = near[part, :] + far[part, :]
        three = jnp.concatenate(
            example_features(
                in_out[part, :RANK],
                hidden[part, :],
                gradient[:, :RANK],
                gradient[:, RANK:],
                in_out[part, RANK:],
                lengths[e],
            ),
            axis=0,
        )
        for step, found in enumerate((q0, q1, q2, q3)):
            for j in range(queries):
                value = jnp.sum(three * found[j], keepdims=True)
                here = (row == e) & (
                    column == queries * jnp.bitwise_xor(place[0], step) + j
                )
                total = total + jnp.where(here, value, 0.0)
    scores[...] = total


def partial_scores(lengths, place, in_out, hidden, near, far, found):
    number = lengths.shape[0]
    return pl.pallas_call(
        score_kernel,
        in_specs=[SCALARS] * 2 + [IN_VMEM] * 8,
        out_specs=IN_VMEM,
        out_shape=jax.ShapeDtypeStruct((number, 4 * found[0].shape[0]), jnp.float32),
        compiler_params=params(),
    )(lengths, place, in_out, hidden, near, far, *found)


def after(value, *others):
    return lax.optimization_barrier((value, *others))[0]


def moving_plan(
    train_input,
    train_gate,
    train_up,
    train_outgrad,
    train_lengths,
    query_input,
    query_gate,
    query_up,
    query_outgrad,
    query_lengths,
    down_weight,
    proj_input,
    proj_outgrad,
    proj_hidden,
    proj_gate,
    proj_up,
):
    t = lax.axis_index("tensor")
    d = lax.axis_index("dp")
    x, core = d // 2, d % 2
    u = jnp.where(x == 0, t, 3 - t)
    at_home = u < 2
    flags = jnp.stack([u, core ^ x]).astype(jnp.int32)
    place = jnp.stack([d]).astype(jnp.int32)

    to_core = functools.partial(lax.ppermute, axis_name="dp", perm=[(i, i ^ 1) for i in range(4)])
    to_chip = functools.partial(lax.ppermute, axis_name="dp", perm=[(i, i ^ 2) for i in range(4)])
    outer = functools.partial(
        lax.ppermute, axis_name="tensor", perm=[(i, i ^ 1) for i in range(4)]
    )
    across = functools.partial(
        lax.ppermute, axis_name="tensor", perm=[(i, i ^ 2) for i in range(4)]
    )
    middle = functools.partial(
        lax.ppermute,
        axis_name=("tensor", "dp"),
        perm=[
            (4 * i + j, 4 * (3 - i) + j) if i in (1, 2) else (4 * i + j, 4 * i + (j ^ 1))
            for i in range(4)
            for j in range(4)
        ],
    )

    def tensor_sum(values):
        values = values + outer(values)
        return values + across(values)

    q_input, q_gate, q_up, q_outgrad = [
        flatten(a) for a in (query_input, query_gate, query_up, query_outgrad)
    ]
    t_input, t_gate, t_up, t_outgrad = [
        flatten(a) for a in (train_input, train_gate, train_up, train_outgrad)
    ]
    examples = train_lengths.shape[0] // 2
    cut = examples * SEQ

    def begin(own, previous):
        if previous is None:
            return outer(own), to_chip(own), middle(own)
        qb, pc, qc = previous
        transit = jnp.where(u == 1, qb, pc)
        return (
            outer(jnp.where(u == 2, qc, own)),
            to_chip(jnp.where(at_home, transit, own)),
            middle(own),
        )

    def second(pa, cross, qa):
        return outer(jnp.where(u == 2, qa, cross)), middle(pa)

    weights = (down_weight, to_core(down_weight))

    q_pa, q_cross, q_qa = begin(q_outgrad, None)
    q_pb, q_qb = second(q_pa, q_cross, q_qa)
    own_in_out, hidden = early_sides(
        t_input, q_input, t_outgrad, q_outgrad, proj_input, proj_outgrad, t_gate, t_up, q_gate,
        q_up, proj_hidden,
    )
    far_gate = to_chip(after(t_gate[cut:], q_cross))
    q_qb = after(q_qb, own_in_out, q_pb)
    q_pc, q_qc = outer(q_qb), middle(q_cross)
    in_out = tensor_sum(own_in_out)

    a_own = t_outgrad[:cut]
    a_pa, a_cross, a_qa = begin(a_own, (q_qb, q_pc, q_qc))
    a_pb, a_qb = second(a_pa, a_cross, a_qa)
    q_blocks = (q_outgrad, q_pa, q_cross, q_pb, q_qa, q_qb, q_qc, q_pc, a_cross, a_pa)
    q_near_sum, q_far_sum = partial_sums(flags, q_blocks, weights)
    far_up = to_chip(after(t_up[cut:], a_cross, far_gate))
    a_qb = after(a_qb, q_far_sum, a_pb, in_out)
    q_returned = to_chip(q_far_sum)
    a_pc, a_qc = outer(a_qb), middle(a_cross)

    b_own = t_outgrad[cut:]
    b_pa, b_cross, b_qa = begin(b_own, (a_qb, a_pc, after(a_qc, far_up)))
    b_pb, b_qb = second(after(b_pa, q_returned), b_cross, b_qa)
    a_blocks = (a_own, a_pa, a_cross, a_pb, a_qa, a_qb, a_qc, a_pc, b_cross, b_pa)
    a_near_sum, a_far_sum = partial_sums(flags, a_blocks, weights)
    b_qb = after(b_qb, a_far_sum, b_pb)
    b_pc, b_qc = outer(b_qb), middle(b_cross)
    q_gradient = finished_sides(q_near_sum, q_returned, q_gate, q_up, proj_gate, proj_up)
    b_qc = after(b_qc, q_gradient)
    c_pa, c_cross = outer(b_qc), to_chip(jnp.where(u == 1, b_qb, b_pc))
    b_blocks = (b_own, b_pa, b_cross, b_pb, b_qa, b_qb, b_qc, b_pc, c_cross, c_pa)

    own_found = query_features(
        query_lengths,
        in_out[2 * cut :],
        tensor_sum(jnp.concatenate([q_gradient, hidden[2 * cut :]], axis=1)),
    )
    core_found = to_core(own_found)
    found = (own_found, core_found, to_chip(own_found), to_chip(core_found))
    a_gradient = finished_sides(
        a_near_sum, to_chip(a_far_sum), t_gate, t_up, proj_gate, proj_up
    )
    b_gradient = lent_sides(
        after(flags, a_gradient, core_found), b_blocks, weights, t_gate, t_up, far_gate, far_up, proj_gate, proj_up
    )
    a_scores = partial_scores(
        train_lengths[:examples], place, in_out[:cut], hidden[:cut], a_gradient,
        jnp.zeros_like(a_gradient), found,
    )
    b_scores = partial_scores(
        train_lengths[examples:], place, in_out[cut : 2 * cut], hidden[cut : 2 * cut],
        b_gradient[:cut], to_chip(b_gradient[cut:]), found,
    )
    scores = tensor_sum(jnp.concatenate([a_scores, b_scores], axis=0))
    return scores / (RANK * SEQ)


def solution(mesh):
    tensor, dp = mesh.shape["tensor"], mesh.shape["dp"]

    def per_device(*arguments):
        if tensor == 4 and dp == 4:
            return moving_plan(*arguments)
        return gathering_plan(*arguments)

    in_specs = (
        P(("parts", "dp"), None, "tensor"),
        P(("parts", "dp"), None, "tensor"),
        P(("parts", "dp"), None, "tensor"),
        P(("parts", "dp"), None, "tensor"),
        P(("parts", "dp")),
        P(("parts", "dp"), None, "tensor"),
        P(("parts", "dp"), None, "tensor"),
        P(("parts", "dp"), None, "tensor"),
        P(("parts", "dp"), None, "tensor"),
        P(("parts", "dp")),
        P("tensor", "dp"),
        P(None, "tensor"),
        P(None, "tensor"),
        P(None, "tensor"),
        P(None, "tensor"),
        P(None, "tensor"),
    )
    out_specs = P(("parts", "dp"), None)
    return jax.shard_map(
        per_device, mesh=mesh, in_specs=in_specs, out_specs=out_specs, check_vma=False
    )
```

```python
import functools

import jax
import jax.numpy as jnp
from jax import lax
from jax.experimental import pallas as pl
from jax.experimental.pallas import tpu as pltpu
from jax.sharding import PartitionSpec as P

RANK = 64
SEQ = 64
TILE = 512
VMEM_BYTES = 40 * 1024 * 1024


def flatten(array):
    return array.reshape(-1, array.shape[-1])


def project(rows, table):
    return lax.dot_general(
        rows, table, (((1,), (1,)), ((), ())), preferred_element_type=jnp.float32
    )


def inner(left_side, right_side):
    return lax.dot_general(
        left_side,
        right_side,
        (((1,), (1,)), ((), ())),
        precision=lax.Precision.HIGHEST,
        preferred_element_type=jnp.float32,
    )


def gated_hidden(gate, up):
    gate_wide = gate.astype(jnp.float32)
    up_wide = up.astype(jnp.float32)
    return (gate_wide * jax.nn.sigmoid(gate_wide) * up_wide).astype(jnp.bfloat16)


def gradient_sides(gate, up, hidden_grad, proj_gate, proj_up):
    gate_wide = gate.astype(jnp.float32)
    up_wide = up.astype(jnp.float32)
    sigmoid_gate = jax.nn.sigmoid(gate_wide)
    silu_gate = gate_wide * sigmoid_gate
    gate_grad = (
        hidden_grad * up_wide * sigmoid_gate * (1.0 + gate_wide * (1.0 - sigmoid_gate))
    ).astype(jnp.bfloat16)
    up_grad = (hidden_grad * silu_gate).astype(jnp.bfloat16)
    return project(gate_grad, proj_gate), project(up_grad, proj_up)


def outer_sums(left_side, right_side, lengths):
    number = lengths.shape[0]
    length = left_side.shape[0] // number
    positions = lax.broadcasted_iota(jnp.int32, (number, length), 1)
    weights = (positions < lengths[:, None]).astype(jnp.float32)
    left_rows = left_side.reshape(number, length, left_side.shape[1]) * weights[:, :, None]
    right_rows = right_side.reshape(number, length, right_side.shape[1])
    summed = jnp.einsum("est,esu->etu", left_rows, right_rows, precision=lax.Precision.HIGHEST)
    return summed.reshape(number, -1)


def features(in_side, hidden_side, gate_side, up_side, out_side, lengths):
    return jnp.concatenate(
        [
            outer_sums(in_side, gate_side, lengths),
            outer_sums(in_side, up_side, lengths),
            outer_sums(hidden_side, out_side, lengths),
        ],
        axis=1,
    )


def gathering_plan(
    train_input,
    train_gate,
    train_up,
    train_outgrad,
    train_lengths,
    query_input,
    query_gate,
    query_up,
    query_outgrad,
    query_lengths,
    down_weight,
    proj_input,
    proj_outgrad,
    proj_hidden,
    proj_gate,
    proj_up,
):
    weight = lax.all_gather(down_weight, "dp", axis=1, tiled=True)

    def full_features(inputs, gate, up, outgrad, lengths):
        inputs, gate, up, outgrad = [flatten(a) for a in (inputs, gate, up, outgrad)]
        rows = lax.all_gather(outgrad, "tensor", axis=1, tiled=True)
        gate_side, up_side = gradient_sides(gate, up, project(rows, weight), proj_gate, proj_up)
        hidden_side = project(gated_hidden(gate, up), proj_hidden)
        sides = (
            project(inputs, proj_input),
            hidden_side,
            gate_side,
            up_side,
            project(outgrad, proj_outgrad),
        )
        return features(*lax.psum(sides, "tensor"), lengths)

    train_features = full_features(
        train_input, train_gate, train_up, train_outgrad, train_lengths
    )
    query_features = full_features(
        query_input, query_gate, query_up, query_outgrad, query_lengths
    )
    gathered = lax.all_gather(query_features, "dp", axis=0, tiled=True)
    return inner(train_features, gathered) / (RANK * SEQ)


ANYWHERE = pl.BlockSpec(memory_space=pl.ANY)
SCALARS = pl.BlockSpec(memory_space=pltpu.SMEM)
IN_VMEM = pl.BlockSpec(memory_space=pltpu.VMEM)


def params():
    return pltpu.CompilerParams(vmem_limit_bytes=VMEM_BYTES)


def cost(flops, arrays):
    moved = sum(array.size * array.dtype.itemsize for array in arrays)
    return pl.CostEstimate(flops=flops, bytes_accessed=moved, transcendentals=0)


def tile_columns(number, block=0):
    return pl.BlockSpec((number, TILE), lambda i: (block, i))


def tile_rows(width):
    return pl.BlockSpec((TILE, width), lambda i: (i, 0))


def whole(shape):
    return pl.BlockSpec(shape, lambda i: tuple(0 for _ in shape))


def stacked_products(
    flags, pairs, far, weight_own, weight_sib, stacked, semaphores, held, weight_sems
):
    number = far.shape[1]
    step = pl.program_id(0)
    tiles = weight_own.shape[0] // TILE

    def weight_copies(tile):
        part = pl.ds(pl.multiple_of(tile * TILE, TILE), TILE)
        slot = lax.rem(tile, 3)
        return [
            pltpu.make_async_copy(
                weight.at[part], held.at[slot, side], weight_sems.at[slot, side]
            )
            for side, weight in enumerate((weight_own, weight_sib))
        ]

    @pl.when(step == 0)
    def _():
        for tile in range(2):
            for copy in weight_copies(tile):
                copy.start()
        slot = flags[1]
        far_copies = [
            pltpu.make_async_copy(
                far.at[i], stacked.at[jnp.bitwise_xor(slot, i), pl.ds(number, number)],
                semaphores.at[2 + i],
            )
            for i in range(2)
        ]
        for copy in far_copies:
            copy.start()
        for code, pair in enumerate(pairs):

            @pl.when(flags[0] == code)
            def _():
                copies = [
                    pltpu.make_async_copy(
                        pair[i], stacked.at[jnp.bitwise_xor(slot, i), pl.ds(0, number)],
                        semaphores.at[i],
                    )
                    for i in range(2)
                ]
                for copy in copies:
                    copy.start()
                for copy in copies:
                    copy.wait()

        for copy in far_copies:
            copy.wait()

    @pl.when(step + 2 < tiles)
    def _():
        for copy in weight_copies(step + 2):
            copy.start()

    for copy in weight_copies(step):
        copy.wait()
    slot = lax.rem(step, 3)
    return project(held[slot, 0], stacked[0]) + project(held[slot, 1], stacked[1])


def add_sides(hidden_grad, gate, up, proj_gate, proj_up, sides):
    gate_part, up_part = gradient_sides(gate, up, hidden_grad, proj_gate, proj_up)
    part = jnp.concatenate([gate_part, up_part], axis=1)
    first = pl.program_id(0) == 0

    @pl.when(first)
    def _():
        sides[...] = part

    @pl.when(jnp.logical_not(first))
    def _():
        sides[...] += part


def partial_kernel(
    flags, b0, b1, b2, b3, b4, b5, far, weight_own, weight_sib, near_sum, far_sum, *scratch
):
    pairs = ((b0, b1), (b2, b3), (b4, b5))
    total = stacked_products(flags, pairs, far, weight_own, weight_sib, *scratch)
    number = far.shape[1]
    near_sum[...] = total[:, :number]
    far_sum[...] = total[:, number:].astype(jnp.bfloat16)


def partial_sums(flags, blocks, far, weight_own, weight_sib):
    number, half = blocks[0].shape
    units = weight_own.shape[0]
    return pl.pallas_call(
        partial_kernel,
        grid=(units // TILE,),
        in_specs=[SCALARS] + [ANYWHERE] * 9,
        out_specs=[tile_rows(number)] * 2,
        out_shape=[
            jax.ShapeDtypeStruct((units, number), jnp.float32),
            jax.ShapeDtypeStruct((units, number), jnp.bfloat16),
        ],
        scratch_shapes=[
            pltpu.VMEM((2, 2 * number, half), jnp.bfloat16),
            pltpu.SemaphoreType.DMA((4,)),
            pltpu.VMEM((3, 2, TILE, half), jnp.bfloat16),
            pltpu.SemaphoreType.DMA((3, 2)),
        ],
        compiler_params=params(),
        cost_estimate=cost(8 * number * half * units, (far, weight_own, weight_sib)),
    )(flags, *blocks, far, weight_own, weight_sib)


def finish_kernel(near_sum, returned, gate, up, proj_gate, proj_up, sides):
    hidden_grad = (near_sum[...] + returned[...].astype(jnp.float32)).T
    add_sides(hidden_grad, gate[...], up[...], proj_gate[...], proj_up[...], sides)


def finished_sides(near_sum, returned, gate, up, proj_gate, proj_up):
    units, number = near_sum.shape
    return pl.pallas_call(
        finish_kernel,
        grid=(units // TILE,),
        in_specs=[tile_rows(number)] * 2 + [tile_columns(number)] * 2 + [tile_columns(RANK)] * 2,
        out_specs=whole((number, 2 * RANK)),
        out_shape=jax.ShapeDtypeStruct((number, 2 * RANK), jnp.float32),
        compiler_params=params(),
        cost_estimate=cost(4 * number * RANK * units, (near_sum, returned, gate, up)),
    )(near_sum, returned, gate, up, proj_gate, proj_up)


def lent_kernel(
    flags, b0, b1, b2, b3, b4, b5, far, weight_own, weight_sib, gate, up, far_gate, far_up,
    proj_gate, proj_up, sides, *scratch,
):
    pairs = ((b0, b1), (b2, b3), (b4, b5))
    total = stacked_products(flags, pairs, far, weight_own, weight_sib, *scratch)
    gates = jnp.concatenate([gate[...], far_gate[...]], axis=0)
    ups = jnp.concatenate([up[...], far_up[...]], axis=0)
    add_sides(total.T, gates, ups, proj_gate[...], proj_up[...], sides)


def lent_sides(
    flags, blocks, far, weight_own, weight_sib, gate, up, far_gate, far_up, proj_gate, proj_up
):
    number, half = blocks[0].shape
    units = weight_own.shape[0]
    return pl.pallas_call(
        lent_kernel,
        grid=(units // TILE,),
        in_specs=[SCALARS]
        + [ANYWHERE] * 9
        + [tile_columns(number, 1)] * 2
        + [tile_columns(number)] * 2
        + [tile_columns(RANK)] * 2,
        out_specs=whole((2 * number, 2 * RANK)),
        out_shape=jax.ShapeDtypeStruct((2 * number, 2 * RANK), jnp.float32),
        scratch_shapes=[
            pltpu.VMEM((2, 2 * number, half), jnp.bfloat16),
            pltpu.SemaphoreType.DMA((4,)),
            pltpu.VMEM((3, 2, TILE, half), jnp.bfloat16),
            pltpu.SemaphoreType.DMA((3, 2)),
        ],
        compiler_params=params(),
        cost_estimate=cost(8 * number * half * units, (far, weight_own, weight_sib)),
    )(
        flags, *blocks, far, weight_own, weight_sib, gate, up, far_gate, far_up, proj_gate, proj_up
    )


def early_kernel(
    t_input, q_input, t_outgrad, q_outgrad, proj_input, proj_outgrad, t_gate, t_up, q_gate, q_up,
    proj_hidden, in_out, hidden,
):
    number = t_input.shape[0]
    t_hidden = project(gated_hidden(t_gate[...], t_up[...]), proj_hidden[...])
    q_hidden = project(gated_hidden(q_gate[...], q_up[...]), proj_hidden[...])
    first = pl.program_id(0) == 0

    @pl.when(first)
    def _():
        for inputs, outgrad, part in (
            (t_input, t_outgrad, slice(0, number)),
            (q_input, q_outgrad, slice(number, None)),
        ):
            in_out[part, :] = jnp.concatenate(
                [
                    project(inputs[...], proj_input[...]),
                    project(outgrad[...], proj_outgrad[...]),
                ],
                axis=1,
            )
        hidden[:number, :] = t_hidden
        hidden[number:, :] = q_hidden

    @pl.when(jnp.logical_not(first))
    def _():
        hidden[:number, :] += t_hidden
        hidden[number:, :] += q_hidden


def early_sides(
    t_input, q_input, t_outgrad, q_outgrad, proj_input, proj_outgrad, t_gate, t_up, q_gate, q_up,
    proj_hidden,
):
    total, units = t_gate.shape[0] + q_gate.shape[0], t_gate.shape[1]
    wide = (t_input, q_input, t_outgrad, q_outgrad, proj_input, proj_outgrad)
    tiled = (t_gate, t_up, q_gate, q_up, proj_hidden)
    shapes = ((total, 2 * RANK), (total, RANK))
    return pl.pallas_call(
        early_kernel,
        grid=(units // TILE,),
        in_specs=[whole(a.shape) for a in wide] + [tile_columns(a.shape[0]) for a in tiled],
        out_specs=[whole(shape) for shape in shapes],
        out_shape=[jax.ShapeDtypeStruct(shape, jnp.float32) for shape in shapes],
        compiler_params=params(),
        cost_estimate=cost(2 * total * RANK * units, wide + tiled),
    )(*wide, *tiled)


def outer_sum(left_side, right_side, weight):
    return lax.dot_general(
        left_side * weight,
        right_side,
        (((0,), (0,)), ((), ())),
        precision=lax.Precision.HIGHEST,
        preferred_element_type=jnp.float32,
    )


def example_features(in_side, hidden_side, gate_side, up_side, out_side, length):
    positions = lax.broadcasted_iota(jnp.int32, (SEQ, RANK), 0)
    weight = (positions < length).astype(jnp.float32)
    return (
        outer_sum(in_side, gate_side, weight),
        outer_sum(in_side, up_side, weight),
        outer_sum(hidden_side, out_side, weight),
    )


def query_kernel(lengths, in_out, sums, found):
    for e in range(found.shape[0]):
        part = slice(e * SEQ, (e + 1) * SEQ)
        three = example_features(
            in_out[part, :RANK],
            sums[part, 2 * RANK :],
            sums[part, :RANK],
            sums[part, RANK : 2 * RANK],
            in_out[part, RANK:],
            lengths[e],
        )
        for segment in range(3):
            found[e, segment * RANK : (segment + 1) * RANK, :] = three[segment]


def query_features(lengths, in_out, sums):
    return pl.pallas_call(
        query_kernel,
        in_specs=[SCALARS, IN_VMEM, IN_VMEM],
        out_specs=IN_VMEM,
        out_shape=jax.ShapeDtypeStruct((lengths.shape[0], 3 * RANK, RANK), jnp.float32),
        compiler_params=params(),
    )(lengths, in_out, sums)


def score_kernel(
    lengths, place, in_out, hidden, near, far, q0, q1, q2, q3, scores
):
    queries = q0.shape[0]
    shape = scores.shape
    row = lax.broadcasted_iota(jnp.int32, shape, 0)
    column = lax.broadcasted_iota(jnp.int32, shape, 1)
    total = jnp.zeros(shape, jnp.float32)
    for e in range(shape[0]):
        part = slice(e * SEQ, (e + 1) * SEQ)
        gradient = near[part, :] + far[part, :]
        three = jnp.concatenate(
            example_features(
                in_out[part, :RANK],
                hidden[part, :],
                gradient[:, :RANK],
                gradient[:, RANK:],
                in_out[part, RANK:],
                lengths[e],
            ),
            axis=0,
        )
        for step, found in enumerate((q0, q1, q2, q3)):
            for j in range(queries):
                value = jnp.sum(three * found[j], keepdims=True)
                here = (row == e) & (
                    column == queries * jnp.bitwise_xor(place[0], step) + j
                )
                total = total + jnp.where(here, value, 0.0)
    scores[...] = total


def partial_scores(lengths, place, in_out, hidden, near, far, found):
    number = lengths.shape[0]
    return pl.pallas_call(
        score_kernel,
        in_specs=[SCALARS] * 2 + [IN_VMEM] * 8,
        out_specs=IN_VMEM,
        out_shape=jax.ShapeDtypeStruct((number, 4 * found[0].shape[0]), jnp.float32),
        compiler_params=params(),
    )(lengths, place, in_out, hidden, near, far, *found)


def after(value, *others):
    return lax.optimization_barrier((value, *others))[0]


def moving_plan(
    train_input,
    train_gate,
    train_up,
    train_outgrad,
    train_lengths,
    query_input,
    query_gate,
    query_up,
    query_outgrad,
    query_lengths,
    down_weight,
    proj_input,
    proj_outgrad,
    proj_hidden,
    proj_gate,
    proj_up,
):
    t = lax.axis_index("tensor")
    d = lax.axis_index("dp")
    x, core, upper = d // 2, d % 2, t // 2
    at_home = x == upper
    inner_chip = (t == 1) | (t == 2)
    near_code = jnp.where(at_home, 0, jnp.where(inner_chip, 1, 2))
    first_parity = jnp.where(at_home, t % 2, upper)
    flags = jnp.stack([near_code, first_parity ^ core]).astype(jnp.int32)
    place = jnp.stack([d]).astype(jnp.int32)

    to_core = functools.partial(lax.ppermute, axis_name="dp", perm=[(i, i ^ 1) for i in range(4)])
    to_chip = functools.partial(lax.ppermute, axis_name="dp", perm=[(i, i ^ 2) for i in range(4)])
    outer = functools.partial(
        lax.ppermute, axis_name="tensor", perm=[(i, i ^ 1) for i in range(4)]
    )
    across = functools.partial(
        lax.ppermute, axis_name="tensor", perm=[(i, i ^ 2) for i in range(4)]
    )
    middle = functools.partial(
        lax.ppermute,
        axis_name=("tensor", "dp"),
        perm=[
            (4 * i + j, 4 * (3 - i) + j) if i in (1, 2) else (4 * i + j, 4 * i + (j ^ 1))
            for i in range(4)
            for j in range(4)
        ],
    )

    def tensor_sum(values):
        values = values + outer(values)
        return values + across(values)

    q_input, q_gate, q_up, q_outgrad = [
        flatten(a) for a in (query_input, query_gate, query_up, query_outgrad)
    ]
    t_input, t_gate, t_up, t_outgrad = [
        flatten(a) for a in (train_input, train_gate, train_up, train_outgrad)
    ]
    examples = train_lengths.shape[0] // 2
    cut = examples * SEQ

    def direct(own, *others):
        return own, outer(after(own, *others)), middle(own), across(own)

    def last_hop(own, one, mid, two, *others):
        two = after(two, one, mid, *others)
        return own, one, mid, two, two, outer(two)

    def crossing_pair(own, one, second_inner, third_inner, second_outer, third_outer):
        def choose(within, beyond_inner, beyond_outer):
            beyond = jnp.where(inner_chip, beyond_inner, beyond_outer)
            return jnp.where(at_home, beyond, within)

        return jnp.stack(
            [choose(own, second_inner, second_outer), choose(one, third_inner, third_outer)]
        )

    q_direct = direct(q_outgrad)
    far_gate = to_chip(t_gate[cut:])
    own_in_out, hidden = early_sides(
        t_input, after(q_input, *q_direct[1:]), t_outgrad, q_outgrad, proj_input, proj_outgrad, t_gate, t_up, q_gate,
        q_up, proj_hidden,
    )
    weight_own, weight_sib = down_weight, to_core(down_weight)
    q_blocks = last_hop(*q_direct, far_gate)

    far_up = to_chip(after(t_up[cut:], far_gate))
    q_send = after(crossing_pair(*q_blocks), far_up, own_in_out)
    a_direct = direct(after(t_outgrad[:cut], q_direct[3]), q_send)
    pair_in_out = own_in_out + outer(own_in_out)
    pair_in_out = after(pair_in_out, a_direct[2], a_direct[3])
    in_out = pair_in_out + across(pair_in_out)
    q_far = to_chip(q_send)
    a_blocks = last_hop(*a_direct, in_out, q_far)

    b_direct = direct(after(t_outgrad[cut:], a_blocks[3]))
    a_send = crossing_pair(*a_blocks)
    a_far = to_chip(a_send)
    q_near_sum, q_far_sum = partial_sums(
        flags, q_blocks, after(q_far, a_send), weight_own, weight_sib
    )
    q_returned = to_chip(after(q_far_sum, a_far))
    b_blocks = last_hop(*b_direct, q_far_sum)
    a_near_sum, a_far_sum = partial_sums(flags, a_blocks, a_far, weight_own, weight_sib)
    a_returned = to_chip(a_far_sum)
    b_blocks = b_blocks[:5] + (after(b_blocks[5], a_far_sum),)
    b_send = crossing_pair(*b_blocks)
    b_far = to_chip(b_send)
    q_gradient = finished_sides(
        q_near_sum, after(q_returned, b_send), q_gate, q_up, proj_gate, proj_up
    )
    own_found = query_features(
        query_lengths,
        in_out[2 * cut :],
        tensor_sum(jnp.concatenate([q_gradient, hidden[2 * cut :]], axis=1)),
    )
    core_found = to_core(own_found)
    found = (own_found, core_found, to_chip(own_found), to_chip(core_found))
    b_gradient = lent_sides(
        flags, b_blocks, after(b_far, core_found), weight_own, weight_sib, t_gate, t_up, far_gate,
        far_up, proj_gate, proj_up,
    )
    a_gradient = finished_sides(a_near_sum, a_returned, t_gate, t_up, proj_gate, proj_up)
    a_scores = partial_scores(
        train_lengths[:examples], place, in_out[:cut], hidden[:cut], a_gradient,
        jnp.zeros_like(a_gradient), found,
    )
    b_scores = partial_scores(
        train_lengths[examples:], place, in_out[cut : 2 * cut], hidden[cut : 2 * cut],
        b_gradient[:cut], to_chip(b_gradient[cut:]), found,
    )
    scores = tensor_sum(jnp.concatenate([a_scores, b_scores], axis=0))
    return scores / (RANK * SEQ)


def solution(mesh):
    tensor, dp = mesh.shape["tensor"], mesh.shape["dp"]

    def per_device(*arguments):
        if tensor == 4 and dp == 4:
            return moving_plan(*arguments)
        return gathering_plan(*arguments)

    in_specs = (
        P(("parts", "dp"), None, "tensor"),
        P(("parts", "dp"), None, "tensor"),
        P(("parts", "dp"), None, "tensor"),
        P(("parts", "dp"), None, "tensor"),
        P(("parts", "dp")),
        P(("parts", "dp"), None, "tensor"),
        P(("parts", "dp"), None, "tensor"),
        P(("parts", "dp"), None, "tensor"),
        P(("parts", "dp"), None, "tensor"),
        P(("parts", "dp")),
        P("tensor", "dp"),
        P(None, "tensor"),
        P(None, "tensor"),
        P(None, "tensor"),
        P(None, "tensor"),
        P(None, "tensor"),
    )
    out_specs = P(("parts", "dp"), None)
    return jax.shard_map(
        per_device, mesh=mesh, in_specs=in_specs, out_specs=out_specs, check_vma=False
    )
```

```python
import functools

import jax
import jax.numpy as jnp
from jax import lax
from jax.experimental import pallas as pl
from jax.experimental.pallas import tpu as pltpu
from jax.sharding import PartitionSpec as P

RANK = 64
SEQ = 64
TILE = 512
VMEM_BYTES = 40 * 1024 * 1024


def flatten(array):
    return array.reshape(-1, array.shape[-1])


def project(rows, table):
    return lax.dot_general(
        rows, table, (((1,), (1,)), ((), ())), preferred_element_type=jnp.float32
    )


def inner(left_side, right_side):
    return lax.dot_general(
        left_side,
        right_side,
        (((1,), (1,)), ((), ())),
        precision=lax.Precision.HIGHEST,
        preferred_element_type=jnp.float32,
    )


def gated_hidden(gate, up):
    gate_wide = gate.astype(jnp.float32)
    up_wide = up.astype(jnp.float32)
    return (gate_wide * jax.nn.sigmoid(gate_wide) * up_wide).astype(jnp.bfloat16)


def gradient_sides(gate, up, hidden_grad, proj_gate, proj_up):
    gate_wide = gate.astype(jnp.float32)
    up_wide = up.astype(jnp.float32)
    sigmoid_gate = jax.nn.sigmoid(gate_wide)
    silu_gate = gate_wide * sigmoid_gate
    gate_grad = (
        hidden_grad * up_wide * sigmoid_gate * (1.0 + gate_wide * (1.0 - sigmoid_gate))
    ).astype(jnp.bfloat16)
    up_grad = (hidden_grad * silu_gate).astype(jnp.bfloat16)
    return project(gate_grad, proj_gate), project(up_grad, proj_up)


def outer_sums(left_side, right_side, lengths):
    number = lengths.shape[0]
    length = left_side.shape[0] // number
    positions = lax.broadcasted_iota(jnp.int32, (number, length), 1)
    weights = (positions < lengths[:, None]).astype(jnp.float32)
    left_rows = left_side.reshape(number, length, left_side.shape[1]) * weights[:, :, None]
    right_rows = right_side.reshape(number, length, right_side.shape[1])
    summed = jnp.einsum("est,esu->etu", left_rows, right_rows, precision=lax.Precision.HIGHEST)
    return summed.reshape(number, -1)


def features(in_side, hidden_side, gate_side, up_side, out_side, lengths):
    return jnp.concatenate(
        [
            outer_sums(in_side, gate_side, lengths),
            outer_sums(in_side, up_side, lengths),
            outer_sums(hidden_side, out_side, lengths),
        ],
        axis=1,
    )


def gathering_plan(
    train_input,
    train_gate,
    train_up,
    train_outgrad,
    train_lengths,
    query_input,
    query_gate,
    query_up,
    query_outgrad,
    query_lengths,
    down_weight,
    proj_input,
    proj_outgrad,
    proj_hidden,
    proj_gate,
    proj_up,
):
    weight = lax.all_gather(down_weight, "dp", axis=1, tiled=True)

    def full_features(inputs, gate, up, outgrad, lengths):
        inputs, gate, up, outgrad = [flatten(a) for a in (inputs, gate, up, outgrad)]
        rows = lax.all_gather(outgrad, "tensor", axis=1, tiled=True)
        gate_side, up_side = gradient_sides(gate, up, project(rows, weight), proj_gate, proj_up)
        hidden_side = project(gated_hidden(gate, up), proj_hidden)
        sides = (
            project(inputs, proj_input),
            hidden_side,
            gate_side,
            up_side,
            project(outgrad, proj_outgrad),
        )
        return features(*lax.psum(sides, "tensor"), lengths)

    train_features = full_features(
        train_input, train_gate, train_up, train_outgrad, train_lengths
    )
    query_features = full_features(
        query_input, query_gate, query_up, query_outgrad, query_lengths
    )
    gathered = lax.all_gather(query_features, "dp", axis=0, tiled=True)
    return inner(train_features, gathered) / (RANK * SEQ)


ANYWHERE = pl.BlockSpec(memory_space=pl.ANY)
SCALARS = pl.BlockSpec(memory_space=pltpu.SMEM)
IN_VMEM = pl.BlockSpec(memory_space=pltpu.VMEM)


def params():
    return pltpu.CompilerParams(vmem_limit_bytes=VMEM_BYTES)


def cost(flops, arrays):
    return pl.CostEstimate(flops=1024, bytes_accessed=1024, transcendentals=0)


def tile_columns(number, block=0):
    return pl.BlockSpec((number, TILE), lambda i: (block, i))


def tile_rows(width):
    return pl.BlockSpec((TILE, width), lambda i: (i, 0))


def whole(shape):
    return pl.BlockSpec(shape, lambda i: tuple(0 for _ in shape))


def stacked_products(
    flags, pairs, far, weight_own, weight_sib, stacked, semaphores, held, weight_sems
):
    number = far.shape[1]
    step = pl.program_id(0)
    tiles = weight_own.shape[0] // TILE

    def weight_copies(tile):
        part = pl.ds(pl.multiple_of(tile * TILE, TILE), TILE)
        slot = lax.rem(tile, 3)
        return [
            pltpu.make_async_copy(
                weight.at[part], held.at[slot, side], weight_sems.at[slot, side]
            )
            for side, weight in enumerate((weight_own, weight_sib))
        ]

    @pl.when(step == 0)
    def _():
        for tile in range(2):
            for copy in weight_copies(tile):
                copy.start()
        slot = flags[1]
        far_copies = [
            pltpu.make_async_copy(
                far.at[i], stacked.at[jnp.bitwise_xor(slot, i), pl.ds(number, number)],
                semaphores.at[2 + i],
            )
            for i in range(2)
        ]
        for copy in far_copies:
            copy.start()
        for code, pair in enumerate(pairs):

            @pl.when(flags[0] == code)
            def _():
                copies = [
                    pltpu.make_async_copy(
                        pair[i], stacked.at[jnp.bitwise_xor(slot, i), pl.ds(0, number)],
                        semaphores.at[i],
                    )
                    for i in range(2)
                ]
                for copy in copies:
                    copy.start()
                for copy in copies:
                    copy.wait()

        for copy in far_copies:
            copy.wait()

    @pl.when(step + 2 < tiles)
    def _():
        for copy in weight_copies(step + 2):
            copy.start()

    for copy in weight_copies(step):
        copy.wait()
    slot = lax.rem(step, 3)
    return project(held[slot, 0], stacked[0]) + project(held[slot, 1], stacked[1])


def add_sides(hidden_grad, gate, up, proj_gate, proj_up, sides):
    gate_part, up_part = gradient_sides(gate, up, hidden_grad, proj_gate, proj_up)
    part = jnp.concatenate([gate_part, up_part], axis=1)
    first = pl.program_id(0) == 0

    @pl.when(first)
    def _():
        sides[...] = part

    @pl.when(jnp.logical_not(first))
    def _():
        sides[...] += part


def partial_kernel(
    flags, b0, b1, b2, b3, b4, b5, far, weight_own, weight_sib, near_sum, far_sum, *scratch
):
    pairs = ((b0, b1), (b2, b3), (b4, b5))
    total = stacked_products(flags, pairs, far, weight_own, weight_sib, *scratch)
    number = far.shape[1]
    near_sum[...] = total[:, :number]
    far_sum[...] = total[:, number:].astype(jnp.bfloat16)


def partial_sums(flags, blocks, far, weight_own, weight_sib):
    number, half = blocks[0].shape
    units = weight_own.shape[0]
    return pl.pallas_call(
        partial_kernel,
        grid=(units // TILE,),
        in_specs=[SCALARS] + [ANYWHERE] * 9,
        out_specs=[tile_rows(number)] * 2,
        out_shape=[
            jax.ShapeDtypeStruct((units, number), jnp.float32),
            jax.ShapeDtypeStruct((units, number), jnp.bfloat16),
        ],
        scratch_shapes=[
            pltpu.VMEM((2, 2 * number, half), jnp.bfloat16),
            pltpu.SemaphoreType.DMA((4,)),
            pltpu.VMEM((3, 2, TILE, half), jnp.bfloat16),
            pltpu.SemaphoreType.DMA((3, 2)),
        ],
        compiler_params=params(),
        cost_estimate=cost(8 * number * half * units, (far, weight_own, weight_sib)),
    )(flags, *blocks, far, weight_own, weight_sib)


def finish_kernel(near_sum, returned, gate, up, proj_gate, proj_up, sides):
    hidden_grad = (near_sum[...] + returned[...].astype(jnp.float32)).T
    add_sides(hidden_grad, gate[...], up[...], proj_gate[...], proj_up[...], sides)


def finished_sides(near_sum, returned, gate, up, proj_gate, proj_up):
    units, number = near_sum.shape
    return pl.pallas_call(
        finish_kernel,
        grid=(units // TILE,),
        in_specs=[tile_rows(number)] * 2 + [tile_columns(number)] * 2 + [tile_columns(RANK)] * 2,
        out_specs=whole((number, 2 * RANK)),
        out_shape=jax.ShapeDtypeStruct((number, 2 * RANK), jnp.float32),
        compiler_params=params(),
        cost_estimate=cost(4 * number * RANK * units, (near_sum, returned, gate, up)),
    )(near_sum, returned, gate, up, proj_gate, proj_up)


def lent_kernel(
    flags, b0, b1, b2, b3, b4, b5, far, weight_own, weight_sib, gate, up, far_gate, far_up,
    proj_gate, proj_up, sides, *scratch,
):
    pairs = ((b0, b1), (b2, b3), (b4, b5))
    total = stacked_products(flags, pairs, far, weight_own, weight_sib, *scratch)
    gates = jnp.concatenate([gate[...], far_gate[...]], axis=0)
    ups = jnp.concatenate([up[...], far_up[...]], axis=0)
    add_sides(total.T, gates, ups, proj_gate[...], proj_up[...], sides)


def lent_sides(
    flags, blocks, far, weight_own, weight_sib, gate, up, far_gate, far_up, proj_gate, proj_up
):
    number, half = blocks[0].shape
    units = weight_own.shape[0]
    return pl.pallas_call(
        lent_kernel,
        grid=(units // TILE,),
        in_specs=[SCALARS]
        + [ANYWHERE] * 9
        + [tile_columns(number, 1)] * 2
        + [tile_columns(number)] * 2
        + [tile_columns(RANK)] * 2,
        out_specs=whole((2 * number, 2 * RANK)),
        out_shape=jax.ShapeDtypeStruct((2 * number, 2 * RANK), jnp.float32),
        scratch_shapes=[
            pltpu.VMEM((2, 2 * number, half), jnp.bfloat16),
            pltpu.SemaphoreType.DMA((4,)),
            pltpu.VMEM((3, 2, TILE, half), jnp.bfloat16),
            pltpu.SemaphoreType.DMA((3, 2)),
        ],
        compiler_params=params(),
        cost_estimate=cost(8 * number * half * units, (far, weight_own, weight_sib)),
    )(
        flags, *blocks, far, weight_own, weight_sib, gate, up, far_gate, far_up, proj_gate, proj_up
    )


def early_kernel(
    t_input, q_input, t_outgrad, q_outgrad, proj_input, proj_outgrad, t_gate, t_up, q_gate, q_up,
    proj_hidden, in_out, hidden,
):
    number = t_input.shape[0]
    t_hidden = project(gated_hidden(t_gate[...], t_up[...]), proj_hidden[...])
    q_hidden = project(gated_hidden(q_gate[...], q_up[...]), proj_hidden[...])
    first = pl.program_id(0) == 0

    @pl.when(first)
    def _():
        for inputs, outgrad, part in (
            (t_input, t_outgrad, slice(0, number)),
            (q_input, q_outgrad, slice(number, None)),
        ):
            in_out[part, :] = jnp.concatenate(
                [
                    project(inputs[...], proj_input[...]),
                    project(outgrad[...], proj_outgrad[...]),
                ],
                axis=1,
            )
        hidden[:number, :] = t_hidden
        hidden[number:, :] = q_hidden

    @pl.when(jnp.logical_not(first))
    def _():
        hidden[:number, :] += t_hidden
        hidden[number:, :] += q_hidden


def early_sides(
    t_input, q_input, t_outgrad, q_outgrad, proj_input, proj_outgrad, t_gate, t_up, q_gate, q_up,
    proj_hidden,
):
    total, units = t_gate.shape[0] + q_gate.shape[0], t_gate.shape[1]
    wide = (t_input, q_input, t_outgrad, q_outgrad, proj_input, proj_outgrad)
    tiled = (t_gate, t_up, q_gate, q_up, proj_hidden)
    shapes = ((total, 2 * RANK), (total, RANK))
    return pl.pallas_call(
        early_kernel,
        grid=(units // TILE,),
        in_specs=[whole(a.shape) for a in wide] + [tile_columns(a.shape[0]) for a in tiled],
        out_specs=[whole(shape) for shape in shapes],
        out_shape=[jax.ShapeDtypeStruct(shape, jnp.float32) for shape in shapes],
        compiler_params=params(),
        cost_estimate=cost(2 * total * RANK * units, wide + tiled),
    )(*wide, *tiled)


def outer_sum(left_side, right_side, weight):
    return lax.dot_general(
        left_side * weight,
        right_side,
        (((0,), (0,)), ((), ())),
        precision=lax.Precision.HIGHEST,
        preferred_element_type=jnp.float32,
    )


def example_features(in_side, hidden_side, gate_side, up_side, out_side, length):
    positions = lax.broadcasted_iota(jnp.int32, (SEQ, RANK), 0)
    weight = (positions < length).astype(jnp.float32)
    return (
        outer_sum(in_side, gate_side, weight),
        outer_sum(in_side, up_side, weight),
        outer_sum(hidden_side, out_side, weight),
    )


def query_kernel(lengths, in_out, sums, found):
    for e in range(found.shape[0]):
        part = slice(e * SEQ, (e + 1) * SEQ)
        three = example_features(
            in_out[part, :RANK],
            sums[part, 2 * RANK :],
            sums[part, :RANK],
            sums[part, RANK : 2 * RANK],
            in_out[part, RANK:],
            lengths[e],
        )
        for segment in range(3):
            found[e, segment * RANK : (segment + 1) * RANK, :] = three[segment]


def query_features(lengths, in_out, sums):
    return pl.pallas_call(
        query_kernel,
        in_specs=[SCALARS, IN_VMEM, IN_VMEM],
        out_specs=IN_VMEM,
        out_shape=jax.ShapeDtypeStruct((lengths.shape[0], 3 * RANK, RANK), jnp.float32),
        compiler_params=params(),
    )(lengths, in_out, sums)


def score_kernel(
    lengths, place, in_out, hidden, early, near, far, q0, q1, q2, q3, scores
):
    queries = q0.shape[0]
    shape = scores.shape
    row = lax.broadcasted_iota(jnp.int32, shape, 0)
    column = lax.broadcasted_iota(jnp.int32, shape, 1)
    gradient = jnp.concatenate([early[...], near[...] + far[...]], axis=0)
    total = jnp.zeros(shape, jnp.float32)
    for e in range(shape[0]):
        part = slice(e * SEQ, (e + 1) * SEQ)
        three = jnp.concatenate(
            example_features(
                in_out[part, :RANK],
                hidden[part, :],
                gradient[part, :RANK],
                gradient[part, RANK:],
                in_out[part, RANK:],
                lengths[e],
            ),
            axis=0,
        )
        for step, found in enumerate((q0, q1, q2, q3)):
            for j in range(queries):
                value = jnp.sum(three * found[j], keepdims=True)
                here = (row == e) & (
                    column == queries * jnp.bitwise_xor(place[0], step) + j
                )
                total = total + jnp.where(here, value, 0.0)
    scores[...] = total


def partial_scores(lengths, place, in_out, hidden, early, near, far, found):
    number = lengths.shape[0]
    return pl.pallas_call(
        score_kernel,
        in_specs=[SCALARS] * 2 + [IN_VMEM] * 9,
        out_specs=IN_VMEM,
        out_shape=jax.ShapeDtypeStruct((number, 4 * found[0].shape[0]), jnp.float32),
        compiler_params=params(),
    )(lengths, place, in_out, hidden, early, near, far, *found)


def after(value, *others):
    return lax.optimization_barrier((value, *others))[0]


def moving_plan(
    train_input,
    train_gate,
    train_up,
    train_outgrad,
    train_lengths,
    query_input,
    query_gate,
    query_up,
    query_outgrad,
    query_lengths,
    down_weight,
    proj_input,
    proj_outgrad,
    proj_hidden,
    proj_gate,
    proj_up,
):
    t = lax.axis_index("tensor")
    d = lax.axis_index("dp")
    x, core, upper = d // 2, d % 2, t // 2
    at_home = x == upper
    inner_chip = (t == 1) | (t == 2)
    near_code = jnp.where(at_home, 0, jnp.where(inner_chip, 1, 2))
    first_parity = jnp.where(at_home, t % 2, upper)
    flags = jnp.stack([near_code, first_parity ^ core]).astype(jnp.int32)
    place = jnp.stack([d]).astype(jnp.int32)

    to_core = functools.partial(lax.ppermute, axis_name="dp", perm=[(i, i ^ 1) for i in range(4)])
    to_chip = functools.partial(lax.ppermute, axis_name="dp", perm=[(i, i ^ 2) for i in range(4)])
    outer = functools.partial(
        lax.ppermute, axis_name="tensor", perm=[(i, i ^ 1) for i in range(4)]
    )
    across = functools.partial(
        lax.ppermute, axis_name="tensor", perm=[(i, i ^ 2) for i in range(4)]
    )
    opposite = functools.partial(
        lax.ppermute, axis_name="tensor", perm=[(i, 3 - i) for i in range(4)]
    )
    middle = functools.partial(
        lax.ppermute,
        axis_name=("tensor", "dp"),
        perm=[
            (4 * i + j, 4 * (3 - i) + j) if i in (1, 2) else (4 * i + j, 4 * i + (j ^ 1))
            for i in range(4)
            for j in range(4)
        ],
    )

    def tensor_sum(values):
        values = values + outer(values)
        return values + across(values)

    q_input, q_gate, q_up, q_outgrad = [
        flatten(a) for a in (query_input, query_gate, query_up, query_outgrad)
    ]
    t_input, t_gate, t_up, t_outgrad = [
        flatten(a) for a in (train_input, train_gate, train_up, train_outgrad)
    ]
    examples = train_lengths.shape[0] // 2
    cut = examples * SEQ

    def first_hops(own):
        return own, outer(own), across(own)

    def last_hops(own, one, two):
        mid = middle(after(own, two))
        return own, one, mid, two, two, outer(after(two, one))

    def crossing_pair(own, one, second_inner, third_inner, second_outer, third_outer):
        def choose(within, beyond_inner, beyond_outer):
            beyond = jnp.where(inner_chip, beyond_inner, beyond_outer)
            return jnp.where(at_home, beyond, within)

        return jnp.stack(
            [choose(own, second_inner, second_outer), choose(one, third_inner, third_outer)]
        )

    weight_own, weight_sib = down_weight, to_core(down_weight)
    q_hops = first_hops(q_outgrad)
    far_gate = to_chip(t_gate[cut:])
    q_blocks = last_hops(*q_hops)
    own_in_out, hidden = early_sides(
        t_input, q_input, t_outgrad, q_outgrad, proj_input, proj_outgrad, t_gate, t_up, q_gate,
        q_up, proj_hidden,
    )

    a_hops = first_hops(after(t_outgrad[:cut], q_hops[2], far_gate))
    far_up = to_chip(after(t_up[cut:], far_gate))
    q_send = after(crossing_pair(*q_blocks), far_up)
    q_far = to_chip(q_send)
    a_blocks = last_hops(*a_hops[:2], after(a_hops[2], q_send))

    b_hops = first_hops(after(t_outgrad[cut:], a_hops[2]))
    a_send = crossing_pair(*a_blocks[:5], after(a_blocks[5], q_far, own_in_out))
    a_far = to_chip(a_send)
    q_near_sum, q_far_sum = partial_sums(
        flags, q_blocks, after(q_far, a_send), weight_own, weight_sib
    )
    q_returned = to_chip(q_far_sum)
    b_blocks = last_hops(*b_hops[:2], after(b_hops[2], q_far_sum))
    a_near_sum, a_far_sum = partial_sums(flags, a_blocks, a_far, weight_own, weight_sib)
    a_returned = to_chip(a_far_sum)
    b_send = after(crossing_pair(*b_blocks), a_far_sum)
    b_far = to_chip(b_send)
    in_out = tensor_sum(after(own_in_out, b_send))
    q_gradient = finished_sides(
        q_near_sum, after(q_returned, b_send), q_gate, q_up, proj_gate, proj_up
    )
    own_found = query_features(
        query_lengths,
        in_out[2 * cut :],
        tensor_sum(jnp.concatenate([q_gradient, hidden[2 * cut :]], axis=1)),
    )
    core_found = to_core(own_found)
    found = (own_found, core_found, to_chip(own_found), to_chip(core_found))
    b_gradient = lent_sides(
        flags, b_blocks, after(b_far, *found), weight_own, weight_sib, t_gate, t_up, far_gate,
        far_up, proj_gate, proj_up,
    )
    a_gradient = finished_sides(a_near_sum, a_returned, t_gate, t_up, proj_gate, proj_up)
    own_scores = partial_scores(
        train_lengths, place, in_out[: 2 * cut], hidden[: 2 * cut], a_gradient, b_gradient[:cut],
        to_chip(b_gradient[cut:]), found,
    )
    scores = own_scores + outer(own_scores) + across(own_scores) + opposite(own_scores)
    return scores / (RANK * SEQ)


def solution(mesh):
    tensor, dp = mesh.shape["tensor"], mesh.shape["dp"]

    def per_device(*arguments):
        if tensor == 4 and dp == 4:
            return moving_plan(*arguments)
        return gathering_plan(*arguments)

    in_specs = (
        P(("parts", "dp"), None, "tensor"),
        P(("parts", "dp"), None, "tensor"),
        P(("parts", "dp"), None, "tensor"),
        P(("parts", "dp"), None, "tensor"),
        P(("parts", "dp")),
        P(("parts", "dp"), None, "tensor"),
        P(("parts", "dp"), None, "tensor"),
        P(("parts", "dp"), None, "tensor"),
        P(("parts", "dp"), None, "tensor"),
        P(("parts", "dp")),
        P("tensor", "dp"),
        P(None, "tensor"),
        P(None, "tensor"),
        P(None, "tensor"),
        P(None, "tensor"),
        P(None, "tensor"),
    )
    out_specs = P(("parts", "dp"), None)
    return jax.shard_map(
        per_device, mesh=mesh, in_specs=in_specs, out_specs=out_specs, check_vma=False
    )
```

```python
import functools

import jax
import jax.numpy as jnp
from jax import lax
from jax.experimental import pallas as pl
from jax.experimental.pallas import tpu as pltpu
from jax.sharding import PartitionSpec as P

RANK = 64
SEQ = 64
TILE = 512
VMEM_BYTES = 40 * 1024 * 1024
BIG_VMEM_BYTES = 58 * 1024 * 1024


def flatten(array):
    return array.reshape(-1, array.shape[-1])


def project(rows, table):
    return lax.dot_general(
        rows, table, (((1,), (1,)), ((), ())), preferred_element_type=jnp.float32
    )


def inner(left_side, right_side):
    return lax.dot_general(
        left_side,
        right_side,
        (((1,), (1,)), ((), ())),
        precision=lax.Precision.HIGHEST,
        preferred_element_type=jnp.float32,
    )


def gated_hidden(gate, up):
    gate_wide = gate.astype(jnp.float32)
    up_wide = up.astype(jnp.float32)
    return (gate_wide * jax.nn.sigmoid(gate_wide) * up_wide).astype(jnp.bfloat16)


def gradients(gate, up, hidden_grad):
    gate_wide = gate.astype(jnp.float32)
    up_wide = up.astype(jnp.float32)
    sigmoid_gate = jax.nn.sigmoid(gate_wide)
    silu_gate = gate_wide * sigmoid_gate
    gate_grad = (
        hidden_grad * up_wide * sigmoid_gate * (1.0 + gate_wide * (1.0 - sigmoid_gate))
    ).astype(jnp.bfloat16)
    up_grad = (hidden_grad * silu_gate).astype(jnp.bfloat16)
    return gate_grad, up_grad


def gradient_sides(gate, up, hidden_grad, proj_gate, proj_up):
    gate_grad, up_grad = gradients(gate, up, hidden_grad)
    return project(gate_grad, proj_gate), project(up_grad, proj_up)


def outer_sums(left_side, right_side, lengths):
    number = lengths.shape[0]
    length = left_side.shape[0] // number
    positions = lax.broadcasted_iota(jnp.int32, (number, length), 1)
    weights = (positions < lengths[:, None]).astype(jnp.float32)
    left_rows = left_side.reshape(number, length, left_side.shape[1]) * weights[:, :, None]
    right_rows = right_side.reshape(number, length, right_side.shape[1])
    summed = jnp.einsum("est,esu->etu", left_rows, right_rows, precision=lax.Precision.HIGHEST)
    return summed.reshape(number, -1)


def features(in_side, hidden_side, gate_side, up_side, out_side, lengths):
    return jnp.concatenate(
        [
            outer_sums(in_side, gate_side, lengths),
            outer_sums(in_side, up_side, lengths),
            outer_sums(hidden_side, out_side, lengths),
        ],
        axis=1,
    )


def gathering_plan(
    train_input,
    train_gate,
    train_up,
    train_outgrad,
    train_lengths,
    query_input,
    query_gate,
    query_up,
    query_outgrad,
    query_lengths,
    down_weight,
    proj_input,
    proj_outgrad,
    proj_hidden,
    proj_gate,
    proj_up,
):
    weight = lax.all_gather(down_weight, "dp", axis=1, tiled=True)

    def full_features(inputs, gate, up, outgrad, lengths):
        inputs, gate, up, outgrad = [flatten(a) for a in (inputs, gate, up, outgrad)]
        rows = lax.all_gather(outgrad, "tensor", axis=1, tiled=True)
        gate_side, up_side = gradient_sides(gate, up, project(rows, weight), proj_gate, proj_up)
        hidden_side = project(gated_hidden(gate, up), proj_hidden)
        sides = (
            project(inputs, proj_input),
            hidden_side,
            gate_side,
            up_side,
            project(outgrad, proj_outgrad),
        )
        return features(*lax.psum(sides, "tensor"), lengths)

    train_features = full_features(
        train_input, train_gate, train_up, train_outgrad, train_lengths
    )
    query_features = full_features(
        query_input, query_gate, query_up, query_outgrad, query_lengths
    )
    gathered = lax.all_gather(query_features, "dp", axis=0, tiled=True)
    return inner(train_features, gathered) / (RANK * SEQ)


ANYWHERE = pl.BlockSpec(memory_space=pl.ANY)
SCALARS = pl.BlockSpec(memory_space=pltpu.SMEM)
IN_VMEM = pl.BlockSpec(memory_space=pltpu.VMEM)


def params(limit=VMEM_BYTES):
    return pltpu.CompilerParams(vmem_limit_bytes=limit)


def cost(flops, arrays):
    return pl.CostEstimate(flops=1024, bytes_accessed=1024, transcendentals=0)


def tile_columns(number, block=0):
    return pl.BlockSpec((number, TILE), lambda i: (block, i))


def tile_rows(width):
    return pl.BlockSpec((TILE, width), lambda i: (i, 0))


def whole(shape):
    return pl.BlockSpec(shape, lambda i: tuple(0 for _ in shape))


def stacked_products(
    flags, pairs, far, weight_own, weight_sib, stacked, semaphores, held, weight_sems
):
    number = far.shape[1]
    step = pl.program_id(0)
    tiles = weight_own.shape[0] // TILE

    def weight_copies(tile):
        part = pl.ds(pl.multiple_of(tile * TILE, TILE), TILE)
        slot = lax.rem(tile, 3)
        return [
            pltpu.make_async_copy(
                weight.at[part], held.at[slot, side], weight_sems.at[slot, side]
            )
            for side, weight in enumerate((weight_own, weight_sib))
        ]

    @pl.when(step == 0)
    def _():
        for tile in range(2):
            for copy in weight_copies(tile):
                copy.start()
        slot = flags[1]
        far_copies = [
            pltpu.make_async_copy(
                far.at[i], stacked.at[jnp.bitwise_xor(slot, i), pl.ds(number, number)],
                semaphores.at[2 + i],
            )
            for i in range(2)
        ]
        for copy in far_copies:
            copy.start()
        for code, pair in enumerate(pairs):

            @pl.when(flags[0] == code)
            def _():
                copies = [
                    pltpu.make_async_copy(
                        pair[i], stacked.at[jnp.bitwise_xor(slot, i), pl.ds(0, number)],
                        semaphores.at[i],
                    )
                    for i in range(2)
                ]
                for copy in copies:
                    copy.start()
                for copy in copies:
                    copy.wait()

        for copy in far_copies:
            copy.wait()

    @pl.when(step + 2 < tiles)
    def _():
        for copy in weight_copies(step + 2):
            copy.start()

    for copy in weight_copies(step):
        copy.wait()
    slot = lax.rem(step, 3)
    return project(held[slot, 0], stacked[0]) + project(held[slot, 1], stacked[1])


def add_sides(hidden_grad, gate, up, proj_gate, proj_up, sides):
    gate_part, up_part = gradient_sides(gate, up, hidden_grad, proj_gate, proj_up)
    part = jnp.concatenate([gate_part, up_part], axis=1)
    first = pl.program_id(0) == 0

    @pl.when(first)
    def _():
        sides[...] = part

    @pl.when(jnp.logical_not(first))
    def _():
        sides[...] += part


def partial_kernel(
    flags, b0, b1, b2, b3, b4, b5, far, weight_own, weight_sib, near_sum, far_sum, *scratch
):
    pairs = ((b0, b1), (b2, b3), (b4, b5))
    total = stacked_products(flags, pairs, far, weight_own, weight_sib, *scratch)
    number = far.shape[1]
    near_sum[...] = total[:, :number]
    far_sum[...] = total[:, number:].astype(jnp.bfloat16)


def partial_sums(flags, blocks, far, weight_own, weight_sib):
    number, half = blocks[0].shape
    units = weight_own.shape[0]
    return pl.pallas_call(
        partial_kernel,
        grid=(units // TILE,),
        in_specs=[SCALARS] + [ANYWHERE] * 9,
        out_specs=[tile_rows(number)] * 2,
        out_shape=[
            jax.ShapeDtypeStruct((units, number), jnp.float32),
            jax.ShapeDtypeStruct((units, number), jnp.bfloat16),
        ],
        scratch_shapes=[
            pltpu.VMEM((2, 2 * number, half), jnp.bfloat16),
            pltpu.SemaphoreType.DMA((4,)),
            pltpu.VMEM((3, 2, TILE, half), jnp.bfloat16),
            pltpu.SemaphoreType.DMA((3, 2)),
        ],
        compiler_params=params(BIG_VMEM_BYTES),
        cost_estimate=cost(8 * number * half * units, (far, weight_own, weight_sib)),
    )(flags, *blocks, far, weight_own, weight_sib)


def finish_kernel(near_sum, returned, gate, up, proj_gate, proj_up, sides):
    hidden_grad = (near_sum[...] + returned[...].astype(jnp.float32)).T
    add_sides(hidden_grad, gate[...], up[...], proj_gate[...], proj_up[...], sides)


def finished_sides(near_sum, returned, gate, up, proj_gate, proj_up):
    units, number = near_sum.shape
    return pl.pallas_call(
        finish_kernel,
        grid=(units // TILE,),
        in_specs=[tile_rows(number)] * 2 + [tile_columns(number)] * 2 + [tile_columns(RANK)] * 2,
        out_specs=whole((number, 2 * RANK)),
        out_shape=jax.ShapeDtypeStruct((number, 2 * RANK), jnp.float32),
        compiler_params=params(),
        cost_estimate=cost(4 * number * RANK * units, (near_sum, returned, gate, up)),
    )(near_sum, returned, gate, up, proj_gate, proj_up)


def turn_kernel(gate, up, far_gate, far_up, gates, ups):
    number = gate.shape[0]
    for source, target, part in (
        (gate, gates, slice(0, number)),
        (up, ups, slice(0, number)),
        (far_gate, gates, slice(number, None)),
        (far_up, ups, slice(number, None)),
    ):
        target[:, part] = source[...].astype(jnp.float32).T.astype(jnp.bfloat16)


def turned(gate, up, far_gate, far_up):
    number, units = far_gate.shape
    shape = jax.ShapeDtypeStruct((units, 2 * number), jnp.bfloat16)
    return pl.pallas_call(
        turn_kernel,
        grid=(units // TILE,),
        in_specs=[tile_columns(number, 1)] * 2 + [tile_columns(number)] * 2,
        out_specs=[tile_rows(2 * number)] * 2,
        out_shape=[shape] * 2,
        compiler_params=params(),
        cost_estimate=cost(0, (gate, up)),
    )(gate, up, far_gate, far_up)


def lent_kernel(
    flags, b0, b1, b2, b3, b4, b5, far, weight_own, weight_sib, gates, ups, proj_gate, proj_up,
    sides, *scratch,
):
    pairs = ((b0, b1), (b2, b3), (b4, b5))
    hidden_grad = stacked_products(flags, pairs, far, weight_own, weight_sib, *scratch)
    gate_grad, up_grad = gradients(gates[...], ups[...], hidden_grad)
    part = jnp.concatenate(
        [
            jnp.dot(proj_gate[...], gate_grad, preferred_element_type=jnp.float32),
            jnp.dot(proj_up[...], up_grad, preferred_element_type=jnp.float32),
        ],
        axis=0,
    )
    first = pl.program_id(0) == 0

    @pl.when(first)
    def _():
        sides[...] = part

    @pl.when(jnp.logical_not(first))
    def _():
        sides[...] += part


def lent_sides(flags, blocks, far, weight_own, weight_sib, gates, ups, proj_gate, proj_up):
    number, half = blocks[0].shape
    units = weight_own.shape[0]
    return pl.pallas_call(
        lent_kernel,
        grid=(units // TILE,),
        in_specs=[SCALARS]
        + [ANYWHERE] * 9
        + [tile_rows(2 * number)] * 2
        + [tile_columns(RANK)] * 2,
        out_specs=whole((2 * RANK, 2 * number)),
        out_shape=jax.ShapeDtypeStruct((2 * RANK, 2 * number), jnp.float32),
        scratch_shapes=[
            pltpu.VMEM((2, 2 * number, half), jnp.bfloat16),
            pltpu.SemaphoreType.DMA((4,)),
            pltpu.VMEM((3, 2, TILE, half), jnp.bfloat16),
            pltpu.SemaphoreType.DMA((3, 2)),
        ],
        compiler_params=params(BIG_VMEM_BYTES),
        cost_estimate=cost(8 * number * half * units, (far, weight_own, weight_sib)),
    )(flags, *blocks, far, weight_own, weight_sib, gates, ups, proj_gate, proj_up)


def early_kernel(
    t_input, q_input, t_outgrad, q_outgrad, proj_input, proj_outgrad, t_gate, t_up, q_gate, q_up,
    proj_hidden, in_out, hidden,
):
    number = t_input.shape[0]
    t_hidden = project(gated_hidden(t_gate[...], t_up[...]), proj_hidden[...])
    q_hidden = project(gated_hidden(q_gate[...], q_up[...]), proj_hidden[...])
    first = pl.program_id(0) == 0

    @pl.when(first)
    def _():
        for inputs, outgrad, part in (
            (t_input, t_outgrad, slice(0, number)),
            (q_input, q_outgrad, slice(number, None)),
        ):
            in_out[part, :] = jnp.concatenate(
                [
                    project(inputs[...], proj_input[...]),
                    project(outgrad[...], proj_outgrad[...]),
                ],
                axis=1,
            )
        hidden[:number, :] = t_hidden
        hidden[number:, :] = q_hidden

    @pl.when(jnp.logical_not(first))
    def _():
        hidden[:number, :] += t_hidden
        hidden[number:, :] += q_hidden


def early_sides(
    t_input, q_input, t_outgrad, q_outgrad, proj_input, proj_outgrad, t_gate, t_up, q_gate, q_up,
    proj_hidden,
):
    total, units = t_gate.shape[0] + q_gate.shape[0], t_gate.shape[1]
    wide = (t_input, q_input, t_outgrad, q_outgrad, proj_input, proj_outgrad)
    tiled = (t_gate, t_up, q_gate, q_up, proj_hidden)
    shapes = ((total, 2 * RANK), (total, RANK))
    return pl.pallas_call(
        early_kernel,
        grid=(units // TILE,),
        in_specs=[whole(a.shape) for a in wide] + [tile_columns(a.shape[0]) for a in tiled],
        out_specs=[whole(shape) for shape in shapes],
        out_shape=[jax.ShapeDtypeStruct(shape, jnp.float32) for shape in shapes],
        compiler_params=params(),
        cost_estimate=cost(2 * total * RANK * units, wide + tiled),
    )(*wide, *tiled)


def outer_sum(left_side, right_side, weight):
    return lax.dot_general(
        left_side * weight,
        right_side,
        (((0,), (0,)), ((), ())),
        precision=lax.Precision.HIGHEST,
        preferred_element_type=jnp.float32,
    )


def example_features(in_side, hidden_side, gate_side, up_side, out_side, length):
    positions = lax.broadcasted_iota(jnp.int32, (SEQ, RANK), 0)
    weight = (positions < length).astype(jnp.float32)
    return (
        outer_sum(in_side, gate_side, weight),
        outer_sum(in_side, up_side, weight),
        outer_sum(hidden_side, out_side, weight),
    )


def query_kernel(lengths, in_out, sums, found):
    for e in range(found.shape[0]):
        part = slice(e * SEQ, (e + 1) * SEQ)
        three = example_features(
            in_out[part, :RANK],
            sums[part, 2 * RANK :],
            sums[part, :RANK],
            sums[part, RANK : 2 * RANK],
            in_out[part, RANK:],
            lengths[e],
        )
        for segment in range(3):
            found[e, segment * RANK : (segment + 1) * RANK, :] = three[segment]


def query_features(lengths, in_out, sums):
    return pl.pallas_call(
        query_kernel,
        in_specs=[SCALARS, IN_VMEM, IN_VMEM],
        out_specs=IN_VMEM,
        out_shape=jax.ShapeDtypeStruct((lengths.shape[0], 3 * RANK, RANK), jnp.float32),
        compiler_params=params(),
    )(lengths, in_out, sums)


def score_kernel(
    lengths, place, in_out, hidden, early, near, far, q0, q1, q2, q3, scores
):
    queries = q0.shape[0]
    shape = scores.shape
    row = lax.broadcasted_iota(jnp.int32, shape, 0)
    column = lax.broadcasted_iota(jnp.int32, shape, 1)
    gradient = jnp.concatenate([early[...], (near[...] + far[...]).T], axis=0)
    total = jnp.zeros(shape, jnp.float32)
    for e in range(shape[0]):
        part = slice(e * SEQ, (e + 1) * SEQ)
        three = jnp.concatenate(
            example_features(
                in_out[part, :RANK],
                hidden[part, :],
                gradient[part, :RANK],
                gradient[part, RANK:],
                in_out[part, RANK:],
                lengths[e],
            ),
            axis=0,
        )
        for step, found in enumerate((q0, q1, q2, q3)):
            for j in range(queries):
                value = jnp.sum(three * found[j], keepdims=True)
                here = (row == e) & (
                    column == queries * jnp.bitwise_xor(place[0], step) + j
                )
                total = total + jnp.where(here, value, 0.0)
    scores[...] = total


def partial_scores(lengths, place, in_out, hidden, early, near, far, found):
    number = lengths.shape[0]
    return pl.pallas_call(
        score_kernel,
        in_specs=[SCALARS] * 2 + [IN_VMEM] * 9,
        out_specs=IN_VMEM,
        out_shape=jax.ShapeDtypeStruct((number, 4 * found[0].shape[0]), jnp.float32),
        compiler_params=params(),
    )(lengths, place, in_out, hidden, early, near, far, *found)


def after(value, *others):
    return lax.optimization_barrier((value, *others))[0]


def moving_plan(
    train_input,
    train_gate,
    train_up,
    train_outgrad,
    train_lengths,
    query_input,
    query_gate,
    query_up,
    query_outgrad,
    query_lengths,
    down_weight,
    proj_input,
    proj_outgrad,
    proj_hidden,
    proj_gate,
    proj_up,
):
    t = lax.axis_index("tensor")
    d = lax.axis_index("dp")
    x, core, upper = d // 2, d % 2, t // 2
    at_home = x == upper
    inner_chip = (t == 1) | (t == 2)
    near_code = jnp.where(at_home, 0, jnp.where(inner_chip, 1, 2))
    first_parity = jnp.where(at_home, t % 2, upper)
    flags = jnp.stack([near_code, first_parity ^ core]).astype(jnp.int32)
    place = jnp.stack([d]).astype(jnp.int32)

    to_core = functools.partial(lax.ppermute, axis_name="dp", perm=[(i, i ^ 1) for i in range(4)])
    to_chip = functools.partial(lax.ppermute, axis_name="dp", perm=[(i, i ^ 2) for i in range(4)])
    outer = functools.partial(
        lax.ppermute, axis_name="tensor", perm=[(i, i ^ 1) for i in range(4)]
    )
    across = functools.partial(
        lax.ppermute, axis_name="tensor", perm=[(i, i ^ 2) for i in range(4)]
    )
    opposite = functools.partial(
        lax.ppermute, axis_name="tensor", perm=[(i, 3 - i) for i in range(4)]
    )
    middle = functools.partial(
        lax.ppermute,
        axis_name=("tensor", "dp"),
        perm=[
            (4 * i + j, 4 * (3 - i) + j) if i in (1, 2) else (4 * i + j, 4 * i + (j ^ 1))
            for i in range(4)
            for j in range(4)
        ],
    )

    def tensor_sum(values):
        values = values + outer(values)
        return values + across(values)

    q_input, q_gate, q_up, q_outgrad = [
        flatten(a) for a in (query_input, query_gate, query_up, query_outgrad)
    ]
    t_input, t_gate, t_up, t_outgrad = [
        flatten(a) for a in (train_input, train_gate, train_up, train_outgrad)
    ]
    examples = train_lengths.shape[0] // 2
    cut = examples * SEQ

    def first_hops(own):
        return own, outer(own), across(own)

    def last_hops(own, one, two):
        mid = middle(after(own, two))
        return own, one, mid, two, two, outer(after(two, one))

    def crossing_pair(own, one, second_inner, third_inner, second_outer, third_outer):
        def choose(within, beyond_inner, beyond_outer):
            beyond = jnp.where(inner_chip, beyond_inner, beyond_outer)
            return jnp.where(at_home, beyond, within)

        return jnp.stack(
            [choose(own, second_inner, second_outer), choose(one, third_inner, third_outer)]
        )

    weight_own, weight_sib = down_weight, to_core(down_weight)
    q_hops = first_hops(q_outgrad)
    far_gate = to_chip(t_gate[cut:])
    own_in_out, hidden = early_sides(
        t_input, q_input, t_outgrad, q_outgrad, proj_input, proj_outgrad, t_gate, t_up, q_gate,
        q_up, proj_hidden,
    )

    q_blocks = last_hops(*q_hops[:2], after(q_hops[2], own_in_out))
    a_hops = first_hops(after(t_outgrad[:cut], q_hops[2], far_gate))
    far_up = to_chip(after(t_up[cut:], far_gate))
    q_send = after(crossing_pair(*q_blocks), far_up)
    q_far = to_chip(q_send)
    a_blocks = last_hops(*a_hops[:2], after(a_hops[2], q_send))

    b_hops = first_hops(after(t_outgrad[cut:], a_hops[2]))
    a_send = crossing_pair(*a_blocks[:5], after(a_blocks[5], q_far))
    a_far = to_chip(a_send)
    q_near_sum, q_far_sum = partial_sums(
        flags, q_blocks, after(q_far, a_send), weight_own, weight_sib
    )
    q_returned = to_chip(q_far_sum)
    b_blocks = last_hops(*b_hops[:2], after(b_hops[2], q_far_sum))
    a_near_sum, a_far_sum = partial_sums(flags, a_blocks, a_far, weight_own, weight_sib)
    b_send = after(crossing_pair(*b_blocks), a_far_sum)
    b_far = to_chip(b_send)
    in_out = tensor_sum(after(own_in_out, b_send))
    a_returned = to_chip(after(a_far_sum, in_out))
    q_gradient = finished_sides(
        q_near_sum, after(q_returned, b_send), q_gate, q_up, proj_gate, proj_up
    )
    own_found = query_features(
        query_lengths,
        in_out[2 * cut :],
        tensor_sum(jnp.concatenate([q_gradient, hidden[2 * cut :]], axis=1)),
    )
    core_found = to_core(own_found)
    found = (own_found, core_found, to_chip(own_found), to_chip(core_found))
    gates, ups = turned(t_gate, t_up, after(far_gate, b_send), far_up)
    b_gradient = lent_sides(
        flags, b_blocks, after(b_far, core_found), weight_own, weight_sib, gates, ups, proj_gate,
        proj_up,
    )
    a_gradient = finished_sides(a_near_sum, a_returned, t_gate, t_up, proj_gate, proj_up)
    own_scores = partial_scores(
        train_lengths, place, in_out[: 2 * cut], hidden[: 2 * cut], a_gradient, b_gradient[:, :cut],
        to_chip(b_gradient[:, cut:]), found,
    )
    scores = own_scores + outer(own_scores) + across(own_scores) + opposite(own_scores)
    return scores / (RANK * SEQ)


def solution(mesh):
    tensor, dp = mesh.shape["tensor"], mesh.shape["dp"]

    def per_device(*arguments):
        if tensor == 4 and dp == 4:
            return moving_plan(*arguments)
        return gathering_plan(*arguments)

    in_specs = (
        P(("parts", "dp"), None, "tensor"),
        P(("parts", "dp"), None, "tensor"),
        P(("parts", "dp"), None, "tensor"),
        P(("parts", "dp"), None, "tensor"),
        P(("parts", "dp")),
        P(("parts", "dp"), None, "tensor"),
        P(("parts", "dp"), None, "tensor"),
        P(("parts", "dp"), None, "tensor"),
        P(("parts", "dp"), None, "tensor"),
        P(("parts", "dp")),
        P("tensor", "dp"),
        P(None, "tensor"),
        P(None, "tensor"),
        P(None, "tensor"),
        P(None, "tensor"),
        P(None, "tensor"),
    )
    out_specs = P(("parts", "dp"), None)
    return jax.shard_map(
        per_device, mesh=mesh, in_specs=in_specs, out_specs=out_specs, check_vma=False
    )
```

```python
import functools

import jax
import jax.numpy as jnp
from jax import lax
from jax.experimental import pallas as pl
from jax.experimental.pallas import tpu as pltpu
from jax.sharding import PartitionSpec as P

RANK = 64
SEQ = 64
TILE = 512
VMEM_BYTES = 40 * 1024 * 1024
BIG_VMEM_BYTES = 58 * 1024 * 1024


def flatten(array):
    return array.reshape(-1, array.shape[-1])


def project(rows, table):
    return lax.dot_general(
        rows, table, (((1,), (1,)), ((), ())), preferred_element_type=jnp.float32
    )


def inner(left_side, right_side):
    return lax.dot_general(
        left_side,
        right_side,
        (((1,), (1,)), ((), ())),
        precision=lax.Precision.HIGHEST,
        preferred_element_type=jnp.float32,
    )


def gated_hidden(gate, up):
    gate_wide = gate.astype(jnp.float32)
    up_wide = up.astype(jnp.float32)
    return (gate_wide * jax.nn.sigmoid(gate_wide) * up_wide).astype(jnp.bfloat16)


def gradients(gate, up, hidden_grad):
    gate_wide = gate.astype(jnp.float32)
    up_wide = up.astype(jnp.float32)
    sigmoid_gate = jax.nn.sigmoid(gate_wide)
    silu_gate = gate_wide * sigmoid_gate
    gate_grad = (
        hidden_grad * up_wide * sigmoid_gate * (1.0 + gate_wide * (1.0 - sigmoid_gate))
    ).astype(jnp.bfloat16)
    up_grad = (hidden_grad * silu_gate).astype(jnp.bfloat16)
    return gate_grad, up_grad


def gradient_sides(gate, up, hidden_grad, proj_gate, proj_up):
    gate_grad, up_grad = gradients(gate, up, hidden_grad)
    return project(gate_grad, proj_gate), project(up_grad, proj_up)


def outer_sums(left_side, right_side, lengths):
    number = lengths.shape[0]
    length = left_side.shape[0] // number
    positions = lax.broadcasted_iota(jnp.int32, (number, length), 1)
    weights = (positions < lengths[:, None]).astype(jnp.float32)
    left_rows = left_side.reshape(number, length, left_side.shape[1]) * weights[:, :, None]
    right_rows = right_side.reshape(number, length, right_side.shape[1])
    summed = jnp.einsum("est,esu->etu", left_rows, right_rows, precision=lax.Precision.HIGHEST)
    return summed.reshape(number, -1)


def features(in_side, hidden_side, gate_side, up_side, out_side, lengths):
    return jnp.concatenate(
        [
            outer_sums(in_side, gate_side, lengths),
            outer_sums(in_side, up_side, lengths),
            outer_sums(hidden_side, out_side, lengths),
        ],
        axis=1,
    )


def gathering_plan(
    train_input,
    train_gate,
    train_up,
    train_outgrad,
    train_lengths,
    query_input,
    query_gate,
    query_up,
    query_outgrad,
    query_lengths,
    down_weight,
    proj_input,
    proj_outgrad,
    proj_hidden,
    proj_gate,
    proj_up,
):
    weight = lax.all_gather(down_weight, "dp", axis=1, tiled=True)

    def full_features(inputs, gate, up, outgrad, lengths):
        inputs, gate, up, outgrad = [flatten(a) for a in (inputs, gate, up, outgrad)]
        rows = lax.all_gather(outgrad, "tensor", axis=1, tiled=True)
        gate_side, up_side = gradient_sides(gate, up, project(rows, weight), proj_gate, proj_up)
        hidden_side = project(gated_hidden(gate, up), proj_hidden)
        sides = (
            project(inputs, proj_input),
            hidden_side,
            gate_side,
            up_side,
            project(outgrad, proj_outgrad),
        )
        return features(*lax.psum(sides, "tensor"), lengths)

    train_features = full_features(
        train_input, train_gate, train_up, train_outgrad, train_lengths
    )
    query_features = full_features(
        query_input, query_gate, query_up, query_outgrad, query_lengths
    )
    gathered = lax.all_gather(query_features, "dp", axis=0, tiled=True)
    return inner(train_features, gathered) / (RANK * SEQ)


ANYWHERE = pl.BlockSpec(memory_space=pl.ANY)
SCALARS = pl.BlockSpec(memory_space=pltpu.SMEM)
IN_VMEM = pl.BlockSpec(memory_space=pltpu.VMEM)


def params(limit=VMEM_BYTES):
    return pltpu.CompilerParams(vmem_limit_bytes=limit)


def cost(flops, arrays):
    return pl.CostEstimate(flops=1024, bytes_accessed=1024, transcendentals=0)


def tile_columns(number, block=0):
    return pl.BlockSpec((number, TILE), lambda i: (block, i))


def tile_rows(width):
    return pl.BlockSpec((TILE, width), lambda i: (i, 0))


def whole(shape):
    return pl.BlockSpec(shape, lambda i: tuple(0 for _ in shape))


def stacked_products(
    flags, pairs, far, weight_own, weight_sib, stacked, semaphores, held, weight_sems
):
    number = far[0].shape[0]
    step = pl.program_id(0)
    tiles = weight_own.shape[0] // TILE

    def weight_copies(tile):
        part = pl.ds(pl.multiple_of(tile * TILE, TILE), TILE)
        slot = lax.rem(tile, 3)
        return [
            pltpu.make_async_copy(
                weight.at[part], held.at[slot, side], weight_sems.at[slot, side]
            )
            for side, weight in enumerate((weight_own, weight_sib))
        ]

    def row_copies(pair, slot, row, first):
        return [
            pltpu.make_async_copy(
                pair[i], stacked.at[jnp.bitwise_xor(slot, i), pl.ds(row, number)],
                semaphores.at[first + i],
            )
            for i in range(2)
        ]

    @pl.when(step == 0)
    def _():
        far_copies = row_copies(far, flags[2], number, 2)
        for copy in far_copies:
            copy.start()
        for code, pair in enumerate(pairs):

            @pl.when(flags[0] == code)
            def _():
                copies = row_copies(pair, flags[1], 0, 0)
                for copy in copies:
                    copy.start()
                for tile in range(2):
                    for copy in weight_copies(tile):
                        copy.start()
                for copy in copies:
                    copy.wait()

        for copy in far_copies:
            copy.wait()

    @pl.when(step + 2 < tiles)
    def _():
        for copy in weight_copies(step + 2):
            copy.start()

    for copy in weight_copies(step):
        copy.wait()
    slot = lax.rem(step, 3)
    return project(held[slot, 0], stacked[0]) + project(held[slot, 1], stacked[1])


def add_sides(hidden_grad, gate, up, proj_gate, proj_up, sides):
    gate_part, up_part = gradient_sides(gate, up, hidden_grad, proj_gate, proj_up)
    part = jnp.concatenate([gate_part, up_part], axis=1)
    first = pl.program_id(0) == 0

    @pl.when(first)
    def _():
        sides[...] = part

    @pl.when(jnp.logical_not(first))
    def _():
        sides[...] += part


def partial_kernel(
    flags, b0, b1, b2, b3, b4, b5, far_a, far_b, weight_own, weight_sib, near_sum, far_sum,
    *scratch,
):
    pairs = ((b0, b1), (b2, b3), (b4, b5))
    far = (far_a, far_b)
    total = stacked_products(flags, pairs, far, weight_own, weight_sib, *scratch)
    number = far_a.shape[0]
    near_sum[...] = total[:, :number]
    far_sum[...] = total[:, number:].astype(jnp.bfloat16)


def product_scratch(number, half):
    return [
        pltpu.VMEM((2, 2 * number, half), jnp.bfloat16),
        pltpu.SemaphoreType.DMA((4,)),
        pltpu.VMEM((3, 2, TILE, half), jnp.bfloat16),
        pltpu.SemaphoreType.DMA((3, 2)),
    ]


def partial_sums(flags, blocks, far, weight_own, weight_sib):
    number, half = blocks[0].shape
    units = weight_own.shape[0]
    return pl.pallas_call(
        partial_kernel,
        grid=(units // TILE,),
        in_specs=[SCALARS] + [ANYWHERE] * 10,
        out_specs=[tile_rows(number)] * 2,
        out_shape=[
            jax.ShapeDtypeStruct((units, number), jnp.float32),
            jax.ShapeDtypeStruct((units, number), jnp.bfloat16),
        ],
        scratch_shapes=product_scratch(number, half),
        compiler_params=params(BIG_VMEM_BYTES),
        cost_estimate=cost(8 * number * half * units, (weight_own, weight_sib)),
    )(flags, *blocks, *far, weight_own, weight_sib)


def finish_kernel(near_sum, returned, gate, up, proj_gate, proj_up, sides):
    hidden_grad = (near_sum[...] + returned[...].astype(jnp.float32)).T
    add_sides(hidden_grad, gate[...], up[...], proj_gate[...], proj_up[...], sides)


def finished_sides(near_sum, returned, gate, up, proj_gate, proj_up):
    units, number = near_sum.shape
    return pl.pallas_call(
        finish_kernel,
        grid=(units // TILE,),
        in_specs=[tile_rows(number)] * 2 + [tile_columns(number)] * 2 + [tile_columns(RANK)] * 2,
        out_specs=whole((number, 2 * RANK)),
        out_shape=jax.ShapeDtypeStruct((number, 2 * RANK), jnp.float32),
        compiler_params=params(),
        cost_estimate=cost(4 * number * RANK * units, (near_sum, returned, gate, up)),
    )(near_sum, returned, gate, up, proj_gate, proj_up)


def turn_kernel(gate, up, far_gate, far_up, gates, ups):
    number = gate.shape[0]
    for source, target, part in (
        (gate, gates, slice(0, number)),
        (up, ups, slice(0, number)),
        (far_gate, gates, slice(number, None)),
        (far_up, ups, slice(number, None)),
    ):
        target[:, part] = source[...].astype(jnp.float32).T.astype(jnp.bfloat16)


def turned(gate, up, far_gate, far_up):
    number, units = far_gate.shape
    shape = jax.ShapeDtypeStruct((units, 2 * number), jnp.bfloat16)
    return pl.pallas_call(
        turn_kernel,
        grid=(units // TILE,),
        in_specs=[tile_columns(number, 1)] * 2 + [tile_columns(number)] * 2,
        out_specs=[tile_rows(2 * number)] * 2,
        out_shape=[shape] * 2,
        compiler_params=params(),
        cost_estimate=cost(0, (gate, up)),
    )(gate, up, far_gate, far_up)


def lent_kernel(
    flags, b0, b1, b2, b3, b4, b5, far_a, far_b, weight_own, weight_sib, gates, ups, proj_gate,
    proj_up, near, away, *scratch,
):
    pairs = ((b0, b1), (b2, b3), (b4, b5))
    far = (far_a, far_b)
    hidden_grad = stacked_products(flags, pairs, far, weight_own, weight_sib, *scratch)
    gate_grad, up_grad = gradients(gates[...], ups[...], hidden_grad)
    part = jnp.concatenate(
        [
            jnp.dot(proj_gate[...], gate_grad, preferred_element_type=jnp.float32),
            jnp.dot(proj_up[...], up_grad, preferred_element_type=jnp.float32),
        ],
        axis=0,
    )
    number = near.shape[1]
    first = pl.program_id(0) == 0

    @pl.when(first)
    def _():
        near[...] = part[:, :number]
        away[...] = part[:, number:]

    @pl.when(jnp.logical_not(first))
    def _():
        near[...] += part[:, :number]
        away[...] += part[:, number:]


def lent_sides(flags, blocks, far, weight_own, weight_sib, gates, ups, proj_gate, proj_up):
    number, half = blocks[0].shape
    units = weight_own.shape[0]
    side = jax.ShapeDtypeStruct((2 * RANK, number), jnp.float32)
    return pl.pallas_call(
        lent_kernel,
        grid=(units // TILE,),
        in_specs=[SCALARS]
        + [ANYWHERE] * 10
        + [tile_rows(2 * number)] * 2
        + [tile_columns(RANK)] * 2,
        out_specs=[whole(side.shape)] * 2,
        out_shape=[side] * 2,
        scratch_shapes=product_scratch(number, half),
        compiler_params=params(BIG_VMEM_BYTES),
        cost_estimate=cost(8 * number * half * units, (weight_own, weight_sib)),
    )(flags, *blocks, *far, weight_own, weight_sib, gates, ups, proj_gate, proj_up)


def early_kernel(
    t_input, q_input, t_outgrad, q_outgrad, proj_input, proj_outgrad, t_gate, t_up, q_gate, q_up,
    proj_hidden, in_out, hidden,
):
    number = t_input.shape[0]
    t_hidden = project(gated_hidden(t_gate[...], t_up[...]), proj_hidden[...])
    q_hidden = project(gated_hidden(q_gate[...], q_up[...]), proj_hidden[...])
    first = pl.program_id(0) == 0

    @pl.when(first)
    def _():
        for inputs, outgrad, part in (
            (t_input, t_outgrad, slice(0, number)),
            (q_input, q_outgrad, slice(number, None)),
        ):
            in_out[part, :] = jnp.concatenate(
                [
                    project(inputs[...], proj_input[...]),
                    project(outgrad[...], proj_outgrad[...]),
                ],
                axis=1,
            )
        hidden[:number, :] = t_hidden
        hidden[number:, :] = q_hidden

    @pl.when(jnp.logical_not(first))
    def _():
        hidden[:number, :] += t_hidden
        hidden[number:, :] += q_hidden


def early_sides(
    t_input, q_input, t_outgrad, q_outgrad, proj_input, proj_outgrad, t_gate, t_up, q_gate, q_up,
    proj_hidden,
):
    total, units = t_gate.shape[0] + q_gate.shape[0], t_gate.shape[1]
    wide = (t_input, q_input, t_outgrad, q_outgrad, proj_input, proj_outgrad)
    tiled = (t_gate, t_up, q_gate, q_up, proj_hidden)
    shapes = ((total, 2 * RANK), (total, RANK))
    return pl.pallas_call(
        early_kernel,
        grid=(units // TILE,),
        in_specs=[whole(a.shape) for a in wide] + [tile_columns(a.shape[0]) for a in tiled],
        out_specs=[whole(shape) for shape in shapes],
        out_shape=[jax.ShapeDtypeStruct(shape, jnp.float32) for shape in shapes],
        compiler_params=params(),
        cost_estimate=cost(2 * total * RANK * units, wide + tiled),
    )(*wide, *tiled)


def outer_sum(left_side, right_side, weight):
    return lax.dot_general(
        left_side * weight,
        right_side,
        (((0,), (0,)), ((), ())),
        precision=lax.Precision.HIGHEST,
        preferred_element_type=jnp.float32,
    )


def example_features(in_side, hidden_side, gate_side, up_side, out_side, length):
    positions = lax.broadcasted_iota(jnp.int32, (SEQ, RANK), 0)
    weight = (positions < length).astype(jnp.float32)
    return (
        outer_sum(in_side, gate_side, weight),
        outer_sum(in_side, up_side, weight),
        outer_sum(hidden_side, out_side, weight),
    )


def query_kernel(lengths, sums, found):
    for e in range(found.shape[0]):
        part = slice(e * SEQ, (e + 1) * SEQ)
        gate_side, up_side, hidden_side, in_side, out_side = [
            sums[part, i * RANK : (i + 1) * RANK] for i in range(5)
        ]
        three = example_features(
            in_side, hidden_side, gate_side, up_side, out_side, lengths[e]
        )
        for segment in range(3):
            found[e, segment * RANK : (segment + 1) * RANK, :] = three[segment]


def query_features(lengths, sums):
    return pl.pallas_call(
        query_kernel,
        in_specs=[SCALARS, IN_VMEM],
        out_specs=IN_VMEM,
        out_shape=jax.ShapeDtypeStruct((lengths.shape[0], 3 * RANK, RANK), jnp.float32),
        compiler_params=params(),
    )(lengths, sums)


def score_kernel(
    lengths, place, in_out, hidden, early, near, far, q0, q1, q2, q3, scores
):
    queries = q0.shape[0]
    shape = scores.shape
    row = lax.broadcasted_iota(jnp.int32, shape, 0)
    column = lax.broadcasted_iota(jnp.int32, shape, 1)
    gradient = jnp.concatenate([early[...], (near[...] + far[...]).T], axis=0)
    total = jnp.zeros(shape, jnp.float32)
    for e in range(shape[0]):
        part = slice(e * SEQ, (e + 1) * SEQ)
        three = jnp.concatenate(
            example_features(
                in_out[part, :RANK],
                hidden[part, :],
                gradient[part, :RANK],
                gradient[part, RANK:],
                in_out[part, RANK:],
                lengths[e],
            ),
            axis=0,
        )
        for step, found in enumerate((q0, q1, q2, q3)):
            for j in range(queries):
                value = jnp.sum(three * found[j], keepdims=True)
                here = (row == e) & (
                    column == queries * jnp.bitwise_xor(place[0], step) + j
                )
                total = total + jnp.where(here, value, 0.0)
    scores[...] = total


def partial_scores(lengths, place, in_out, hidden, early, near, far, found):
    number = lengths.shape[0]
    return pl.pallas_call(
        score_kernel,
        in_specs=[SCALARS] * 2 + [IN_VMEM] * 9,
        out_specs=IN_VMEM,
        out_shape=jax.ShapeDtypeStruct((number, 4 * found[0].shape[0]), jnp.float32),
        compiler_params=params(),
    )(lengths, place, in_out, hidden, early, near, far, *found)


def after(value, *others):
    return lax.optimization_barrier((value, *others))[0]


def moving_plan(
    train_input,
    train_gate,
    train_up,
    train_outgrad,
    train_lengths,
    query_input,
    query_gate,
    query_up,
    query_outgrad,
    query_lengths,
    down_weight,
    proj_input,
    proj_outgrad,
    proj_hidden,
    proj_gate,
    proj_up,
):
    t = lax.axis_index("tensor")
    d = lax.axis_index("dp")
    x, core, upper = d // 2, d % 2, t // 2
    at_home = x == upper
    inner_chip = (t == 1) | (t == 2)
    near_code = jnp.where(at_home, 0, jnp.where(inner_chip, 1, 2))
    first_parity = jnp.where(at_home, t % 2, upper)
    near_slot = first_parity ^ core
    far_slot = jnp.where(inner_chip & ~at_home, 1 - near_slot, near_slot)
    flags = jnp.stack([near_code, near_slot, far_slot]).astype(jnp.int32)
    place = jnp.stack([d]).astype(jnp.int32)

    to_core = functools.partial(lax.ppermute, axis_name="dp", perm=[(i, i ^ 1) for i in range(4)])
    to_chip = functools.partial(lax.ppermute, axis_name="dp", perm=[(i, i ^ 2) for i in range(4)])
    to_other = functools.partial(lax.ppermute, axis_name="dp", perm=[(i, i ^ 3) for i in range(4)])
    outer = functools.partial(
        lax.ppermute, axis_name="tensor", perm=[(i, i ^ 1) for i in range(4)]
    )
    across = functools.partial(
        lax.ppermute, axis_name="tensor", perm=[(i, i ^ 2) for i in range(4)]
    )
    opposite = functools.partial(
        lax.ppermute, axis_name="tensor", perm=[(i, 3 - i) for i in range(4)]
    )
    middle = functools.partial(
        lax.ppermute,
        axis_name=("tensor", "dp"),
        perm=[
            (4 * i + j, 4 * (3 - i) + j) if i in (1, 2) else (4 * i + j, 4 * i + (j ^ 1))
            for i in range(4)
            for j in range(4)
        ],
    )

    def tensor_sum(values):
        return values + outer(values) + across(values) + opposite(values)

    def first_hops(own):
        return own, outer(own), across(own)

    def last_hops(own, one, two):
        mid = middle(after(own, two))
        return own, one, mid, two, two, outer(after(two, one))

    def crossing_first(own, two):
        return jnp.where(at_home, two, own)

    def crossing_second(one, mid, last):
        return jnp.where(at_home, jnp.where(inner_chip, mid, last), one)

    q_input, q_gate, q_up, q_outgrad = [
        flatten(a) for a in (query_input, query_gate, query_up, query_outgrad)
    ]
    t_input, t_gate, t_up, t_outgrad = [
        flatten(a) for a in (train_input, train_gate, train_up, train_outgrad)
    ]
    examples = train_lengths.shape[0] // 2
    cut = examples * SEQ

    def first_hops(own):
        return own, outer(own), across(own)

    def last_hops(own, one, two):
        mid = middle(after(own, two))
        return own, one, mid, two, two, outer(after(two, one))

    def crossing_pair(own, one, second_inner, third_inner, second_outer, third_outer):
        def choose(within, beyond_inner, beyond_outer):
            beyond = jnp.where(inner_chip, beyond_inner, beyond_outer)
            return jnp.where(at_home, beyond, within)

        return jnp.stack(
            [choose(own, second_inner, second_outer), choose(one, third_inner, third_outer)]
        )

    weight_own, weight_sib = down_weight, to_core(down_weight)
    q_own, q_one, q_two = first_hops(q_outgrad)
    far_gate = to_chip(t_gate[cut:])
    own_in_out, hidden = early_sides(
        t_input, q_input, t_outgrad, q_outgrad, proj_input, proj_outgrad, t_gate, t_up, q_gate,
        q_up, proj_hidden,
    )
    q_blocks = last_hops(q_own, q_one, after(q_two, own_in_out, far_gate))
    far_up = to_chip(after(t_up[cut:], far_gate))
    q_first = to_chip(crossing_first(q_own, q_blocks[3]))
    q_send = after(crossing_second(q_one, q_blocks[2], q_blocks[5]), far_up)
    q_far = (q_first, to_chip(q_send))

    a_own, a_one, a_two = first_hops(after(t_outgrad[:cut], q_send))
    a_two = after(a_two, a_one)
    a_cross = crossing_first(a_own, a_two)
    a_first = to_chip(a_cross)
    a_blocks = last_hops(a_own, a_one, a_two)
    q_near_sum, q_far_sum = partial_sums(
        after(flags, a_cross), q_blocks, q_far, weight_own, weight_sib
    )
    a_send = crossing_second(a_one, a_blocks[2], after(a_blocks[5], q_far_sum))
    a_far = (a_first, to_chip(a_send))
    q_returned = to_chip(after(q_far_sum, *a_far))

    b_own, b_one, b_two = first_hops(after(t_outgrad[cut:], a_send))
    a_near_sum, a_far_sum = partial_sums(flags, a_blocks, a_far, weight_own, weight_sib)
    b_two = after(b_two, b_one, a_far_sum)
    b_first = to_chip(crossing_first(b_own, b_two))
    b_blocks = last_hops(b_own, b_one, b_two)
    q_gradient = finished_sides(q_near_sum, q_returned, q_gate, q_up, proj_gate, proj_up)
    gates, ups = turned(t_gate, t_up, after(far_gate, a_far_sum), far_up)
    b_send = crossing_second(
        after(b_one, q_gradient, b_first, gates), b_blocks[2], b_blocks[5]
    )
    b_far = (b_first, to_chip(b_send))
    q_sums = jnp.concatenate([q_gradient, hidden[2 * cut :], own_in_out[2 * cut :]], axis=1)
    q_sums = tensor_sum(after(q_sums, b_send))
    a_returned = to_chip(after(a_far_sum, q_sums, *b_far))
    in_out = tensor_sum(after(own_in_out[: 2 * cut], b_send))
    own_found = query_features(query_lengths, q_sums)
    found = (own_found, to_core(own_found), to_chip(own_found), to_other(own_found))
    b_near, b_away = lent_sides(
        flags, b_blocks, b_far, weight_own, weight_sib, gates, ups, proj_gate,
        proj_up,
    )
    a_gradient = finished_sides(a_near_sum, a_returned, t_gate, t_up, proj_gate, proj_up)
    own_scores = partial_scores(
        train_lengths, place, in_out, hidden[: 2 * cut], a_gradient, b_near,
        to_chip(b_away), found,
    )
    return tensor_sum(own_scores) / (RANK * SEQ)


def solution(mesh):
    tensor, dp = mesh.shape["tensor"], mesh.shape["dp"]

    def per_device(*arguments):
        if tensor == 4 and dp == 4:
            return moving_plan(*arguments)
        return gathering_plan(*arguments)

    in_specs = (
        P(("parts", "dp"), None, "tensor"),
        P(("parts", "dp"), None, "tensor"),
        P(("parts", "dp"), None, "tensor"),
        P(("parts", "dp"), None, "tensor"),
        P(("parts", "dp")),
        P(("parts", "dp"), None, "tensor"),
        P(("parts", "dp"), None, "tensor"),
        P(("parts", "dp"), None, "tensor"),
        P(("parts", "dp"), None, "tensor"),
        P(("parts", "dp")),
        P("tensor", "dp"),
        P(None, "tensor"),
        P(None, "tensor"),
        P(None, "tensor"),
        P(None, "tensor"),
        P(None, "tensor"),
    )
    out_specs = P(("parts", "dp"), None)
    return jax.shard_map(
        per_device, mesh=mesh, in_specs=in_specs, out_specs=out_specs, check_vma=False
    )
```

```python
import functools

import jax
import jax.numpy as jnp
from jax import lax
from jax.experimental import pallas as pl
from jax.experimental.pallas import tpu as pltpu
from jax.sharding import PartitionSpec as P

RANK = 64
SEQ = 64
TILE = 512
VMEM_BYTES = 40 * 1024 * 1024
BIG_VMEM_BYTES = 58 * 1024 * 1024


def flatten(array):
    return array.reshape(-1, array.shape[-1])


def project(rows, table):
    return lax.dot_general(
        rows, table, (((1,), (1,)), ((), ())), preferred_element_type=jnp.float32
    )


def inner(left_side, right_side):
    return lax.dot_general(
        left_side,
        right_side,
        (((1,), (1,)), ((), ())),
        precision=lax.Precision.HIGHEST,
        preferred_element_type=jnp.float32,
    )


def gated_hidden(gate, up):
    gate_wide = gate.astype(jnp.float32)
    up_wide = up.astype(jnp.float32)
    return (gate_wide * jax.nn.sigmoid(gate_wide) * up_wide).astype(jnp.bfloat16)


def gradients(gate, up, hidden_grad):
    gate_wide = gate.astype(jnp.float32)
    up_wide = up.astype(jnp.float32)
    sigmoid_gate = jax.nn.sigmoid(gate_wide)
    silu_gate = gate_wide * sigmoid_gate
    gate_grad = (
        hidden_grad * up_wide * sigmoid_gate * (1.0 + gate_wide * (1.0 - sigmoid_gate))
    ).astype(jnp.bfloat16)
    up_grad = (hidden_grad * silu_gate).astype(jnp.bfloat16)
    return gate_grad, up_grad


def gradient_sides(gate, up, hidden_grad, proj_gate, proj_up):
    gate_grad, up_grad = gradients(gate, up, hidden_grad)
    return project(gate_grad, proj_gate), project(up_grad, proj_up)


def outer_sums(left_side, right_side, lengths):
    number = lengths.shape[0]
    length = left_side.shape[0] // number
    positions = lax.broadcasted_iota(jnp.int32, (number, length), 1)
    weights = (positions < lengths[:, None]).astype(jnp.float32)
    left_rows = left_side.reshape(number, length, left_side.shape[1]) * weights[:, :, None]
    right_rows = right_side.reshape(number, length, right_side.shape[1])
    summed = jnp.einsum("est,esu->etu", left_rows, right_rows, precision=lax.Precision.HIGHEST)
    return summed.reshape(number, -1)


def features(in_side, hidden_side, gate_side, up_side, out_side, lengths):
    return jnp.concatenate(
        [
            outer_sums(in_side, gate_side, lengths),
            outer_sums(in_side, up_side, lengths),
            outer_sums(hidden_side, out_side, lengths),
        ],
        axis=1,
    )


def gathering_plan(
    train_input,
    train_gate,
    train_up,
    train_outgrad,
    train_lengths,
    query_input,
    query_gate,
    query_up,
    query_outgrad,
    query_lengths,
    down_weight,
    proj_input,
    proj_outgrad,
    proj_hidden,
    proj_gate,
    proj_up,
):
    weight = lax.all_gather(down_weight, "dp", axis=1, tiled=True)

    def full_features(inputs, gate, up, outgrad, lengths):
        inputs, gate, up, outgrad = [flatten(a) for a in (inputs, gate, up, outgrad)]
        rows = lax.all_gather(outgrad, "tensor", axis=1, tiled=True)
        gate_side, up_side = gradient_sides(gate, up, project(rows, weight), proj_gate, proj_up)
        hidden_side = project(gated_hidden(gate, up), proj_hidden)
        sides = (
            project(inputs, proj_input),
            hidden_side,
            gate_side,
            up_side,
            project(outgrad, proj_outgrad),
        )
        return features(*lax.psum(sides, "tensor"), lengths)

    train_features = full_features(
        train_input, train_gate, train_up, train_outgrad, train_lengths
    )
    query_features = full_features(
        query_input, query_gate, query_up, query_outgrad, query_lengths
    )
    gathered = lax.all_gather(query_features, "dp", axis=0, tiled=True)
    return inner(train_features, gathered) / (RANK * SEQ)


ANYWHERE = pl.BlockSpec(memory_space=pl.ANY)
SCALARS = pl.BlockSpec(memory_space=pltpu.SMEM)
IN_VMEM = pl.BlockSpec(memory_space=pltpu.VMEM)


def params(limit=VMEM_BYTES):
    return pltpu.CompilerParams(vmem_limit_bytes=limit)


def cost(flops, arrays):
    return pl.CostEstimate(flops=1024, bytes_accessed=1024, transcendentals=0)


def tile_columns(number, block=0):
    return pl.BlockSpec((number, TILE), lambda i: (block, i))


def tile_rows(width):
    return pl.BlockSpec((TILE, width), lambda i: (i, 0))


def whole(shape):
    return pl.BlockSpec(shape, lambda i: tuple(0 for _ in shape))


def stacked_products(
    flags, pairs, far, weight_own, weight_sib, stacked, semaphores, held, weight_sems
):
    number = far[0].shape[0]
    step = pl.program_id(0)
    tiles = weight_own.shape[0] // TILE

    def weight_copies(tile):
        part = pl.ds(pl.multiple_of(tile * TILE, TILE), TILE)
        slot = lax.rem(tile, 3)
        return [
            pltpu.make_async_copy(
                weight.at[part], held.at[slot, side], weight_sems.at[slot, side]
            )
            for side, weight in enumerate((weight_own, weight_sib))
        ]

    def row_copies(pair, slot, row, first):
        return [
            pltpu.make_async_copy(
                pair[i], stacked.at[jnp.bitwise_xor(slot, i), pl.ds(row, number)],
                semaphores.at[first + i],
            )
            for i in range(2)
        ]

    @pl.when(step == 0)
    def _():
        far_copies = row_copies(far, flags[2], number, 2)
        for copy in far_copies:
            copy.start()
        for code, pair in enumerate(pairs):

            @pl.when(flags[0] == code)
            def _():
                copies = row_copies(pair, flags[1], 0, 0)
                for copy in copies:
                    copy.start()
                for tile in range(2):
                    for copy in weight_copies(tile):
                        copy.start()
                for copy in copies:
                    copy.wait()

        for copy in far_copies:
            copy.wait()

    @pl.when(step + 2 < tiles)
    def _():
        for copy in weight_copies(step + 2):
            copy.start()

    for copy in weight_copies(step):
        copy.wait()
    slot = lax.rem(step, 3)
    return project(held[slot, 0], stacked[0]) + project(held[slot, 1], stacked[1])


def add_sides(hidden_grad, gate, up, proj_gate, proj_up, sides):
    gate_part, up_part = gradient_sides(gate, up, hidden_grad, proj_gate, proj_up)
    part = jnp.concatenate([gate_part, up_part], axis=1)
    first = pl.program_id(0) == 0

    @pl.when(first)
    def _():
        sides[...] = part

    @pl.when(jnp.logical_not(first))
    def _():
        sides[...] += part


def partial_kernel(
    flags, b0, b1, b2, b3, b4, b5, far_a, far_b, weight_own, weight_sib, near_sum, far_sum,
    *scratch,
):
    pairs = ((b0, b1), (b2, b3), (b4, b5))
    far = (far_a, far_b)
    total = stacked_products(flags, pairs, far, weight_own, weight_sib, *scratch)
    number = far_a.shape[0]
    near_sum[...] = total[:, :number]
    far_sum[...] = total[:, number:].astype(jnp.bfloat16)


def product_scratch(number, half):
    return [
        pltpu.VMEM((2, 2 * number, half), jnp.bfloat16),
        pltpu.SemaphoreType.DMA((4,)),
        pltpu.VMEM((3, 2, TILE, half), jnp.bfloat16),
        pltpu.SemaphoreType.DMA((3, 2)),
    ]


def partial_sums(flags, blocks, far, weight_own, weight_sib):
    number, half = blocks[0].shape
    units = weight_own.shape[0]
    return pl.pallas_call(
        partial_kernel,
        grid=(units // TILE,),
        in_specs=[SCALARS] + [ANYWHERE] * 10,
        out_specs=[tile_rows(number)] * 2,
        out_shape=[
            jax.ShapeDtypeStruct((units, number), jnp.float32),
            jax.ShapeDtypeStruct((units, number), jnp.bfloat16),
        ],
        scratch_shapes=product_scratch(number, half),
        compiler_params=params(BIG_VMEM_BYTES),
        cost_estimate=cost(8 * number * half * units, (weight_own, weight_sib)),
    )(flags, *blocks, *far, weight_own, weight_sib)


def finish_kernel(near_sum, returned, gate, up, proj_gate, proj_up, sides):
    hidden_grad = (near_sum[...] + returned[...].astype(jnp.float32)).T
    add_sides(hidden_grad, gate[...], up[...], proj_gate[...], proj_up[...], sides)


def finished_sides(near_sum, returned, gate, up, proj_gate, proj_up):
    units, number = near_sum.shape
    return pl.pallas_call(
        finish_kernel,
        grid=(units // TILE,),
        in_specs=[tile_rows(number)] * 2 + [tile_columns(number)] * 2 + [tile_columns(RANK)] * 2,
        out_specs=whole((number, 2 * RANK)),
        out_shape=jax.ShapeDtypeStruct((number, 2 * RANK), jnp.float32),
        compiler_params=params(),
        cost_estimate=cost(4 * number * RANK * units, (near_sum, returned, gate, up)),
    )(near_sum, returned, gate, up, proj_gate, proj_up)


def turn_kernel(gate, up, far_gate, far_up, gates, ups):
    number = gate.shape[0]
    for source, target, part in (
        (gate, gates, slice(0, number)),
        (up, ups, slice(0, number)),
        (far_gate, gates, slice(number, None)),
        (far_up, ups, slice(number, None)),
    ):
        target[:, part] = source[...].astype(jnp.float32).T.astype(jnp.bfloat16)


def turned(gate, up, far_gate, far_up):
    number, units = far_gate.shape
    shape = jax.ShapeDtypeStruct((units, 2 * number), jnp.bfloat16)
    return pl.pallas_call(
        turn_kernel,
        grid=(units // TILE,),
        in_specs=[tile_columns(number, 1)] * 2 + [tile_columns(number)] * 2,
        out_specs=[tile_rows(2 * number)] * 2,
        out_shape=[shape] * 2,
        compiler_params=params(),
        cost_estimate=cost(0, (gate, up)),
    )(gate, up, far_gate, far_up)


def lent_kernel(
    flags, b0, b1, b2, b3, b4, b5, far_a, far_b, weight_own, weight_sib, gates, ups, proj_gate,
    proj_up, near, away, *scratch,
):
    pairs = ((b0, b1), (b2, b3), (b4, b5))
    far = (far_a, far_b)
    hidden_grad = stacked_products(flags, pairs, far, weight_own, weight_sib, *scratch)
    gate_grad, up_grad = gradients(gates[...], ups[...], hidden_grad)
    part = jnp.concatenate(
        [
            jnp.dot(proj_gate[...], gate_grad, preferred_element_type=jnp.float32),
            jnp.dot(proj_up[...], up_grad, preferred_element_type=jnp.float32),
        ],
        axis=0,
    )
    number = near.shape[1]
    first = pl.program_id(0) == 0

    @pl.when(first)
    def _():
        near[...] = part[:, :number]
        away[...] = part[:, number:]

    @pl.when(jnp.logical_not(first))
    def _():
        near[...] += part[:, :number]
        away[...] += part[:, number:]


def lent_sides(flags, blocks, far, weight_own, weight_sib, gates, ups, proj_gate, proj_up):
    number, half = blocks[0].shape
    units = weight_own.shape[0]
    side = jax.ShapeDtypeStruct((2 * RANK, number), jnp.float32)
    return pl.pallas_call(
        lent_kernel,
        grid=(units // TILE,),
        in_specs=[SCALARS]
        + [ANYWHERE] * 10
        + [tile_rows(2 * number)] * 2
        + [tile_columns(RANK)] * 2,
        out_specs=[whole(side.shape)] * 2,
        out_shape=[side] * 2,
        scratch_shapes=product_scratch(number, half),
        compiler_params=params(BIG_VMEM_BYTES),
        cost_estimate=cost(8 * number * half * units, (weight_own, weight_sib)),
    )(flags, *blocks, *far, weight_own, weight_sib, gates, ups, proj_gate, proj_up)


def early_kernel(
    t_input, q_input, t_outgrad, q_outgrad, proj_input, proj_outgrad, t_gate, t_up, q_gate, q_up,
    proj_hidden, in_out, hidden,
):
    number = t_input.shape[0]
    t_hidden = project(gated_hidden(t_gate[...], t_up[...]), proj_hidden[...])
    q_hidden = project(gated_hidden(q_gate[...], q_up[...]), proj_hidden[...])
    first = pl.program_id(0) == 0

    @pl.when(first)
    def _():
        for inputs, outgrad, part in (
            (t_input, t_outgrad, slice(0, number)),
            (q_input, q_outgrad, slice(number, None)),
        ):
            in_out[part, :] = jnp.concatenate(
                [
                    project(inputs[...], proj_input[...]),
                    project(outgrad[...], proj_outgrad[...]),
                ],
                axis=1,
            )
        hidden[:number, :] = t_hidden
        hidden[number:, :] = q_hidden

    @pl.when(jnp.logical_not(first))
    def _():
        hidden[:number, :] += t_hidden
        hidden[number:, :] += q_hidden


def early_sides(
    t_input, q_input, t_outgrad, q_outgrad, proj_input, proj_outgrad, t_gate, t_up, q_gate, q_up,
    proj_hidden,
):
    total, units = t_gate.shape[0] + q_gate.shape[0], t_gate.shape[1]
    wide = (t_input, q_input, t_outgrad, q_outgrad, proj_input, proj_outgrad)
    tiled = (t_gate, t_up, q_gate, q_up, proj_hidden)
    shapes = ((total, 2 * RANK), (total, RANK))
    return pl.pallas_call(
        early_kernel,
        grid=(units // TILE,),
        in_specs=[whole(a.shape) for a in wide] + [tile_columns(a.shape[0]) for a in tiled],
        out_specs=[whole(shape) for shape in shapes],
        out_shape=[jax.ShapeDtypeStruct(shape, jnp.float32) for shape in shapes],
        compiler_params=params(),
        cost_estimate=cost(2 * total * RANK * units, wide + tiled),
    )(*wide, *tiled)


def outer_sum(left_side, right_side, weight):
    return lax.dot_general(
        left_side * weight,
        right_side,
        (((0,), (0,)), ((), ())),
        precision=lax.Precision.HIGHEST,
        preferred_element_type=jnp.float32,
    )


def example_features(in_side, hidden_side, gate_side, up_side, out_side, length):
    positions = lax.broadcasted_iota(jnp.int32, (SEQ, RANK), 0)
    weight = (positions < length).astype(jnp.float32)
    return (
        outer_sum(in_side, gate_side, weight),
        outer_sum(in_side, up_side, weight),
        outer_sum(hidden_side, out_side, weight),
    )


def query_kernel(lengths, sums, found):
    for e in range(found.shape[0]):
        part = slice(e * SEQ, (e + 1) * SEQ)
        gate_side, up_side, hidden_side, in_side, out_side = [
            sums[part, i * RANK : (i + 1) * RANK] for i in range(5)
        ]
        three = example_features(
            in_side, hidden_side, gate_side, up_side, out_side, lengths[e]
        )
        for segment in range(3):
            found[e, segment * RANK : (segment + 1) * RANK, :] = three[segment]


def query_features(lengths, sums):
    return pl.pallas_call(
        query_kernel,
        in_specs=[SCALARS, IN_VMEM],
        out_specs=IN_VMEM,
        out_shape=jax.ShapeDtypeStruct((lengths.shape[0], 3 * RANK, RANK), jnp.float32),
        compiler_params=params(),
    )(lengths, sums)


def score_kernel(
    lengths, place, in_out, hidden, early, near, far, q0, q1, q2, q3, scores
):
    queries = q0.shape[0]
    shape = scores.shape
    row = lax.broadcasted_iota(jnp.int32, shape, 0)
    column = lax.broadcasted_iota(jnp.int32, shape, 1)
    gradient = jnp.concatenate([early[...], (near[...] + far[...]).T], axis=0)
    total = jnp.zeros(shape, jnp.float32)
    for e in range(shape[0]):
        part = slice(e * SEQ, (e + 1) * SEQ)
        three = jnp.concatenate(
            example_features(
                in_out[part, :RANK],
                hidden[part, :],
                gradient[part, :RANK],
                gradient[part, RANK:],
                in_out[part, RANK:],
                lengths[e],
            ),
            axis=0,
        )
        for step, found in enumerate((q0, q1, q2, q3)):
            for j in range(queries):
                value = jnp.sum(three * found[j], keepdims=True)
                here = (row == e) & (
                    column == queries * jnp.bitwise_xor(place[0], step) + j
                )
                total = total + jnp.where(here, value, 0.0)
    scores[...] = total


def partial_scores(lengths, place, in_out, hidden, early, near, far, found):
    number = lengths.shape[0]
    return pl.pallas_call(
        score_kernel,
        in_specs=[SCALARS] * 2 + [IN_VMEM] * 9,
        out_specs=IN_VMEM,
        out_shape=jax.ShapeDtypeStruct((number, 4 * found[0].shape[0]), jnp.float32),
        compiler_params=params(),
    )(lengths, place, in_out, hidden, early, near, far, *found)


def after(value, *others):
    return lax.optimization_barrier((value, *others))[0]


def moving_plan(
    train_input,
    train_gate,
    train_up,
    train_outgrad,
    train_lengths,
    query_input,
    query_gate,
    query_up,
    query_outgrad,
    query_lengths,
    down_weight,
    proj_input,
    proj_outgrad,
    proj_hidden,
    proj_gate,
    proj_up,
):
    t = lax.axis_index("tensor")
    d = lax.axis_index("dp")
    x, core, upper = d // 2, d % 2, t // 2
    at_home = x == upper
    inner_chip = (t == 1) | (t == 2)
    near_code = jnp.where(at_home, 0, jnp.where(inner_chip, 1, 2))
    first_parity = jnp.where(at_home, t % 2, upper)
    near_slot = first_parity ^ core
    far_slot = jnp.where(inner_chip & ~at_home, 1 - near_slot, near_slot)
    flags = jnp.stack([near_code, near_slot, far_slot]).astype(jnp.int32)
    place = jnp.stack([d]).astype(jnp.int32)

    to_core = functools.partial(lax.ppermute, axis_name="dp", perm=[(i, i ^ 1) for i in range(4)])
    to_chip = functools.partial(lax.ppermute, axis_name="dp", perm=[(i, i ^ 2) for i in range(4)])
    to_other = functools.partial(lax.ppermute, axis_name="dp", perm=[(i, i ^ 3) for i in range(4)])
    outer = functools.partial(
        lax.ppermute, axis_name="tensor", perm=[(i, i ^ 1) for i in range(4)]
    )
    across = functools.partial(
        lax.ppermute, axis_name="tensor", perm=[(i, i ^ 2) for i in range(4)]
    )
    opposite = functools.partial(
        lax.ppermute, axis_name="tensor", perm=[(i, 3 - i) for i in range(4)]
    )
    middle = functools.partial(
        lax.ppermute,
        axis_name=("tensor", "dp"),
        perm=[
            (4 * i + j, 4 * (3 - i) + j) if i in (1, 2) else (4 * i + j, 4 * i + (j ^ 1))
            for i in range(4)
            for j in range(4)
        ],
    )

    def tensor_sum(values):
        return values + outer(values) + across(values) + opposite(values)

    def last_hops(own, one, two):
        mid = middle(after(own, two))
        return own, one, mid, two, two, outer(after(two, one))

    def crossing_first(own, two):
        return jnp.where(at_home, two, own)

    def crossing_second(one, mid, last):
        return jnp.where(at_home, jnp.where(inner_chip, mid, last), one)

    q_input, q_gate, q_up, q_outgrad = [
        flatten(a) for a in (query_input, query_gate, query_up, query_outgrad)
    ]
    t_input, t_gate, t_up, t_outgrad = [
        flatten(a) for a in (train_input, train_gate, train_up, train_outgrad)
    ]
    examples = train_lengths.shape[0] // 2
    cut = examples * SEQ

    def first_hops(own):
        return own, outer(own), across(own)

    def last_hops(own, one, two):
        mid = middle(after(own, two))
        return own, one, mid, two, two, outer(after(two, one))

    def crossing_pair(own, one, second_inner, third_inner, second_outer, third_outer):
        def choose(within, beyond_inner, beyond_outer):
            beyond = jnp.where(inner_chip, beyond_inner, beyond_outer)
            return jnp.where(at_home, beyond, within)

        return jnp.stack(
            [choose(own, second_inner, second_outer), choose(one, third_inner, third_outer)]
        )

    weight_own, weight_sib = down_weight, to_core(down_weight)
    q_own, q_one, q_two = q_outgrad, outer(q_outgrad), across(q_outgrad)
    far_gate = to_chip(t_gate[cut:])
    own_in_out, hidden = early_sides(
        t_input, q_input, t_outgrad, q_outgrad, proj_input, proj_outgrad, t_gate, t_up, q_gate,
        q_up, proj_hidden,
    )
    q_blocks = last_hops(q_own, q_one, after(q_two, own_in_out, far_gate))
    q_first = to_chip(crossing_first(q_own, q_blocks[3]))
    q_send = crossing_second(q_one, q_blocks[2], q_blocks[5])
    q_far = (q_first, to_chip(q_send))

    far_up = to_chip(after(t_up[cut:], far_gate))
    a_own = after(t_outgrad[:cut], q_send)
    a_one, a_two = outer(a_own), across(a_own)
    a_two = after(a_two, a_one, far_up, *q_far)
    a_cross = crossing_first(a_own, a_two)
    a_first = to_chip(a_cross)
    a_blocks = last_hops(a_own, a_one, a_two)
    q_near_sum, q_far_sum = partial_sums(
        after(flags, a_cross), q_blocks, q_far, weight_own, weight_sib
    )
    a_send = crossing_second(a_one, a_blocks[2], after(a_blocks[5], q_far_sum, a_first))
    a_far = (a_first, to_chip(a_send))
    q_returned = to_chip(after(q_far_sum, *a_far))

    b_own = t_outgrad[cut:]
    b_two = across(after(b_own, a_two))
    b_one = outer(after(b_own, a_send))
    q_hidden = hidden[2 * cut :]
    pair_in_out = own_in_out + outer(after(own_in_out, a_send))
    pair_hidden = q_hidden + outer(after(q_hidden, a_send))
    b_two = after(b_two, b_one, pair_in_out, pair_hidden)
    b_cross = crossing_first(b_own, b_two)
    b_first = to_chip(b_cross)
    b_blocks = last_hops(b_own, b_one, b_two)
    a_near_sum, a_far_sum = partial_sums(
        after(flags, b_cross), a_blocks, a_far, weight_own, weight_sib
    )
    in_out = pair_in_out + across(after(pair_in_out, a_far_sum))
    whole_hidden = pair_hidden + across(after(pair_hidden, a_far_sum))
    q_gradient = finished_sides(q_near_sum, q_returned, q_gate, q_up, proj_gate, proj_up)
    gates, ups = turned(t_gate, t_up, after(far_gate, a_far_sum), far_up)
    b_send = crossing_second(
        after(b_one, q_gradient, b_first, gates, in_out, whole_hidden), b_blocks[2], b_blocks[5]
    )
    b_far = (b_first, to_chip(b_send))
    q_sums = tensor_sum(after(q_gradient, b_send))
    a_returned = to_chip(after(a_far_sum, q_sums, *b_far))
    q_sums = jnp.concatenate([q_sums, whole_hidden, in_out[2 * cut :]], axis=1)
    own_found = query_features(query_lengths, q_sums)
    found = (own_found, to_core(own_found), to_chip(own_found), to_other(own_found))
    b_near, b_away = lent_sides(
        flags, b_blocks, b_far, weight_own, weight_sib, gates, ups, proj_gate,
        proj_up,
    )
    a_gradient = finished_sides(a_near_sum, a_returned, t_gate, t_up, proj_gate, proj_up)
    own_scores = partial_scores(
        train_lengths, place, in_out[: 2 * cut], hidden[: 2 * cut], a_gradient, b_near,
        to_chip(b_away), found,
    )
    return tensor_sum(own_scores) / (RANK * SEQ)


def solution(mesh):
    tensor, dp = mesh.shape["tensor"], mesh.shape["dp"]

    def per_device(*arguments):
        if tensor == 4 and dp == 4:
            return moving_plan(*arguments)
        return gathering_plan(*arguments)

    in_specs = (
        P(("parts", "dp"), None, "tensor"),
        P(("parts", "dp"), None, "tensor"),
        P(("parts", "dp"), None, "tensor"),
        P(("parts", "dp"), None, "tensor"),
        P(("parts", "dp")),
        P(("parts", "dp"), None, "tensor"),
        P(("parts", "dp"), None, "tensor"),
        P(("parts", "dp"), None, "tensor"),
        P(("parts", "dp"), None, "tensor"),
        P(("parts", "dp")),
        P("tensor", "dp"),
        P(None, "tensor"),
        P(None, "tensor"),
        P(None, "tensor"),
        P(None, "tensor"),
        P(None, "tensor"),
    )
    out_specs = P(("parts", "dp"), None)
    return jax.shard_map(
        per_device, mesh=mesh, in_specs=in_specs, out_specs=out_specs, check_vma=False
    )
```

```python
import functools

import jax
import jax.numpy as jnp
from jax import lax
from jax.experimental import pallas as pl
from jax.experimental.pallas import tpu as pltpu
from jax.sharding import PartitionSpec as P

RANK = 64
SEQ = 64
TILE = 512
VMEM_BYTES = 40 * 1024 * 1024
BIG_VMEM_BYTES = 58 * 1024 * 1024


def flatten(array):
    return array.reshape(-1, array.shape[-1])


def project(rows, table):
    return lax.dot_general(
        rows, table, (((1,), (1,)), ((), ())), preferred_element_type=jnp.float32
    )


def inner(left_side, right_side):
    return lax.dot_general(
        left_side,
        right_side,
        (((1,), (1,)), ((), ())),
        precision=lax.Precision.HIGHEST,
        preferred_element_type=jnp.float32,
    )


def gated_hidden(gate, up):
    gate_wide = gate.astype(jnp.float32)
    up_wide = up.astype(jnp.float32)
    return (gate_wide * jax.nn.sigmoid(gate_wide) * up_wide).astype(jnp.bfloat16)


def gradients(gate, up, hidden_grad):
    gate_wide = gate.astype(jnp.float32)
    up_wide = up.astype(jnp.float32)
    sigmoid_gate = jax.nn.sigmoid(gate_wide)
    silu_gate = gate_wide * sigmoid_gate
    gate_grad = (
        hidden_grad * up_wide * sigmoid_gate * (1.0 + gate_wide * (1.0 - sigmoid_gate))
    ).astype(jnp.bfloat16)
    up_grad = (hidden_grad * silu_gate).astype(jnp.bfloat16)
    return gate_grad, up_grad


def gradient_sides(gate, up, hidden_grad, proj_gate, proj_up):
    gate_grad, up_grad = gradients(gate, up, hidden_grad)
    return project(gate_grad, proj_gate), project(up_grad, proj_up)


def outer_sums(left_side, right_side, lengths):
    number = lengths.shape[0]
    length = left_side.shape[0] // number
    positions = lax.broadcasted_iota(jnp.int32, (number, length), 1)
    weights = (positions < lengths[:, None]).astype(jnp.float32)
    left_rows = left_side.reshape(number, length, left_side.shape[1]) * weights[:, :, None]
    right_rows = right_side.reshape(number, length, right_side.shape[1])
    summed = jnp.einsum("est,esu->etu", left_rows, right_rows, precision=lax.Precision.HIGHEST)
    return summed.reshape(number, -1)


def features(in_side, hidden_side, gate_side, up_side, out_side, lengths):
    return jnp.concatenate(
        [
            outer_sums(in_side, gate_side, lengths),
            outer_sums(in_side, up_side, lengths),
            outer_sums(hidden_side, out_side, lengths),
        ],
        axis=1,
    )


def gathering_plan(
    train_input,
    train_gate,
    train_up,
    train_outgrad,
    train_lengths,
    query_input,
    query_gate,
    query_up,
    query_outgrad,
    query_lengths,
    down_weight,
    proj_input,
    proj_outgrad,
    proj_hidden,
    proj_gate,
    proj_up,
):
    weight = lax.all_gather(down_weight, "dp", axis=1, tiled=True)

    def full_features(inputs, gate, up, outgrad, lengths):
        inputs, gate, up, outgrad = [flatten(a) for a in (inputs, gate, up, outgrad)]
        rows = lax.all_gather(outgrad, "tensor", axis=1, tiled=True)
        gate_side, up_side = gradient_sides(gate, up, project(rows, weight), proj_gate, proj_up)
        hidden_side = project(gated_hidden(gate, up), proj_hidden)
        sides = (
            project(inputs, proj_input),
            hidden_side,
            gate_side,
            up_side,
            project(outgrad, proj_outgrad),
        )
        return features(*lax.psum(sides, "tensor"), lengths)

    train_features = full_features(
        train_input, train_gate, train_up, train_outgrad, train_lengths
    )
    query_features = full_features(
        query_input, query_gate, query_up, query_outgrad, query_lengths
    )
    gathered = lax.all_gather(query_features, "dp", axis=0, tiled=True)
    return inner(train_features, gathered) / (RANK * SEQ)


ANYWHERE = pl.BlockSpec(memory_space=pl.ANY)
SCALARS = pl.BlockSpec(memory_space=pltpu.SMEM)
IN_VMEM = pl.BlockSpec(memory_space=pltpu.VMEM)


def params(limit=VMEM_BYTES):
    return pltpu.CompilerParams(vmem_limit_bytes=limit)


def cost(flops, arrays):
    return pl.CostEstimate(flops=1024, bytes_accessed=1024, transcendentals=0)


def tile_columns(number, block=0):
    return pl.BlockSpec((number, TILE), lambda i: (block, i))


def tile_rows(width):
    return pl.BlockSpec((TILE, width), lambda i: (i, 0))


def whole(shape):
    return pl.BlockSpec(shape, lambda i: tuple(0 for _ in shape))


def stacked_products(
    flags, pairs, far, weight_own, weight_sib, stacked, semaphores, held, weight_sems
):
    number = far.shape[1]
    step = pl.program_id(0)
    tiles = weight_own.shape[0] // TILE

    def weight_copies(tile):
        part = pl.ds(pl.multiple_of(tile * TILE, TILE), TILE)
        slot = lax.rem(tile, 3)
        return [
            pltpu.make_async_copy(
                weight.at[part], held.at[slot, side], weight_sems.at[slot, side]
            )
            for side, weight in enumerate((weight_own, weight_sib))
        ]

    @pl.when(step == 0)
    def _():
        slot = flags[1]
        far_copies = [
            pltpu.make_async_copy(
                far.at[i], stacked.at[jnp.bitwise_xor(slot, i), pl.ds(number, number)],
                semaphores.at[2 + i],
            )
            for i in range(2)
        ]
        for copy in far_copies:
            copy.start()
        for code, pair in enumerate(pairs):

            @pl.when(flags[0] == code)
            def _():
                copies = [
                    pltpu.make_async_copy(
                        pair[i], stacked.at[jnp.bitwise_xor(slot, i), pl.ds(0, number)],
                        semaphores.at[i],
                    )
                    for i in range(2)
                ]
                for copy in copies:
                    copy.start()
                for tile in range(2):
                    for copy in weight_copies(tile):
                        copy.start()
                for copy in copies:
                    copy.wait()

        for copy in far_copies:
            copy.wait()

    @pl.when(step + 2 < tiles)
    def _():
        for copy in weight_copies(step + 2):
            copy.start()

    for copy in weight_copies(step):
        copy.wait()
    slot = lax.rem(step, 3)
    return project(held[slot, 0], stacked[0]) + project(held[slot, 1], stacked[1])


def add_sides(hidden_grad, gate, up, proj_gate, proj_up, sides):
    gate_part, up_part = gradient_sides(gate, up, hidden_grad, proj_gate, proj_up)
    part = jnp.concatenate([gate_part, up_part], axis=1)
    first = pl.program_id(0) == 0

    @pl.when(first)
    def _():
        sides[...] = part

    @pl.when(jnp.logical_not(first))
    def _():
        sides[...] += part


def partial_kernel(
    flags, b0, b1, b2, b3, b4, b5, far, weight_own, weight_sib, near_sum, far_sum, *scratch
):
    pairs = ((b0, b1), (b2, b3), (b4, b5))
    total = stacked_products(flags, pairs, far, weight_own, weight_sib, *scratch)
    number = far.shape[1]
    near_sum[...] = total[:, :number]
    far_sum[...] = total[:, number:].astype(jnp.bfloat16)


def partial_sums(flags, blocks, far, weight_own, weight_sib):
    number, half = blocks[0].shape
    units = weight_own.shape[0]
    return pl.pallas_call(
        partial_kernel,
        grid=(units // TILE,),
        in_specs=[SCALARS] + [ANYWHERE] * 9,
        out_specs=[tile_rows(number)] * 2,
        out_shape=[
            jax.ShapeDtypeStruct((units, number), jnp.float32),
            jax.ShapeDtypeStruct((units, number), jnp.bfloat16),
        ],
        scratch_shapes=[
            pltpu.VMEM((2, 2 * number, half), jnp.bfloat16),
            pltpu.SemaphoreType.DMA((4,)),
            pltpu.VMEM((3, 2, TILE, half), jnp.bfloat16),
            pltpu.SemaphoreType.DMA((3, 2)),
        ],
        compiler_params=params(BIG_VMEM_BYTES),
        cost_estimate=cost(8 * number * half * units, (far, weight_own, weight_sib)),
    )(flags, *blocks, far, weight_own, weight_sib)


def finish_kernel(near_sum, returned, gate, up, proj_gate, proj_up, sides):
    hidden_grad = (near_sum[...] + returned[...].astype(jnp.float32)).T
    add_sides(hidden_grad, gate[...], up[...], proj_gate[...], proj_up[...], sides)


def finished_sides(near_sum, returned, gate, up, proj_gate, proj_up):
    units, number = near_sum.shape
    return pl.pallas_call(
        finish_kernel,
        grid=(units // TILE,),
        in_specs=[tile_rows(number)] * 2 + [tile_columns(number)] * 2 + [tile_columns(RANK)] * 2,
        out_specs=whole((number, 2 * RANK)),
        out_shape=jax.ShapeDtypeStruct((number, 2 * RANK), jnp.float32),
        compiler_params=params(),
        cost_estimate=cost(4 * number * RANK * units, (near_sum, returned, gate, up)),
    )(near_sum, returned, gate, up, proj_gate, proj_up)


def turn_kernel(gate, up, far_gate, far_up, gates, ups):
    number = gate.shape[0]
    for source, target, part in (
        (gate, gates, slice(0, number)),
        (up, ups, slice(0, number)),
        (far_gate, gates, slice(number, None)),
        (far_up, ups, slice(number, None)),
    ):
        target[:, part] = source[...].astype(jnp.float32).T.astype(jnp.bfloat16)


def turned(gate, up, far_gate, far_up):
    number, units = far_gate.shape
    shape = jax.ShapeDtypeStruct((units, 2 * number), jnp.bfloat16)
    return pl.pallas_call(
        turn_kernel,
        grid=(units // TILE,),
        in_specs=[tile_columns(number, 1)] * 2 + [tile_columns(number)] * 2,
        out_specs=[tile_rows(2 * number)] * 2,
        out_shape=[shape] * 2,
        compiler_params=params(),
        cost_estimate=cost(0, (gate, up)),
    )(gate, up, far_gate, far_up)


def lent_kernel(
    flags, b0, b1, b2, b3, b4, b5, far, weight_own, weight_sib, gates, ups, proj_gate, proj_up,
    near, away, *scratch,
):
    pairs = ((b0, b1), (b2, b3), (b4, b5))
    hidden_grad = stacked_products(flags, pairs, far, weight_own, weight_sib, *scratch)
    gate_grad, up_grad = gradients(gates[...], ups[...], hidden_grad)
    part = jnp.concatenate(
        [
            jnp.dot(proj_gate[...], gate_grad, preferred_element_type=jnp.float32),
            jnp.dot(proj_up[...], up_grad, preferred_element_type=jnp.float32),
        ],
        axis=0,
    )
    number = near.shape[1]
    first = pl.program_id(0) == 0

    @pl.when(first)
    def _():
        near[...] = part[:, :number]
        away[...] = part[:, number:]

    @pl.when(jnp.logical_not(first))
    def _():
        near[...] += part[:, :number]
        away[...] += part[:, number:]


def lent_sides(flags, blocks, far, weight_own, weight_sib, gates, ups, proj_gate, proj_up):
    number, half = blocks[0].shape
    units = weight_own.shape[0]
    return pl.pallas_call(
        lent_kernel,
        grid=(units // TILE,),
        in_specs=[SCALARS]
        + [ANYWHERE] * 9
        + [tile_rows(2 * number)] * 2
        + [tile_columns(RANK)] * 2,
        out_specs=[whole((2 * RANK, number))] * 2,
        out_shape=[jax.ShapeDtypeStruct((2 * RANK, number), jnp.float32)] * 2,
        scratch_shapes=[
            pltpu.VMEM((2, 2 * number, half), jnp.bfloat16),
            pltpu.SemaphoreType.DMA((4,)),
            pltpu.VMEM((3, 2, TILE, half), jnp.bfloat16),
            pltpu.SemaphoreType.DMA((3, 2)),
        ],
        compiler_params=params(BIG_VMEM_BYTES),
        cost_estimate=cost(8 * number * half * units, (far, weight_own, weight_sib)),
    )(flags, *blocks, far, weight_own, weight_sib, gates, ups, proj_gate, proj_up)


def early_kernel(
    t_input, q_input, t_outgrad, q_outgrad, proj_input, proj_outgrad, t_gate, t_up, q_gate, q_up,
    proj_hidden, in_out, hidden,
):
    number = t_input.shape[0]
    t_hidden = project(gated_hidden(t_gate[...], t_up[...]), proj_hidden[...])
    q_hidden = project(gated_hidden(q_gate[...], q_up[...]), proj_hidden[...])
    first = pl.program_id(0) == 0

    @pl.when(first)
    def _():
        for inputs, outgrad, part in (
            (t_input, t_outgrad, slice(0, number)),
            (q_input, q_outgrad, slice(number, None)),
        ):
            in_out[part, :] = jnp.concatenate(
                [
                    project(inputs[...], proj_input[...]),
                    project(outgrad[...], proj_outgrad[...]),
                ],
                axis=1,
            )
        hidden[:number, :] = t_hidden
        hidden[number:, :] = q_hidden

    @pl.when(jnp.logical_not(first))
    def _():
        hidden[:number, :] += t_hidden
        hidden[number:, :] += q_hidden


def early_sides(
    t_input, q_input, t_outgrad, q_outgrad, proj_input, proj_outgrad, t_gate, t_up, q_gate, q_up,
    proj_hidden,
):
    total, units = t_gate.shape[0] + q_gate.shape[0], t_gate.shape[1]
    wide = (t_input, q_input, t_outgrad, q_outgrad, proj_input, proj_outgrad)
    tiled = (t_gate, t_up, q_gate, q_up, proj_hidden)
    shapes = ((total, 2 * RANK), (total, RANK))
    return pl.pallas_call(
        early_kernel,
        grid=(units // TILE,),
        in_specs=[whole(a.shape) for a in wide] + [tile_columns(a.shape[0]) for a in tiled],
        out_specs=[whole(shape) for shape in shapes],
        out_shape=[jax.ShapeDtypeStruct(shape, jnp.float32) for shape in shapes],
        compiler_params=params(),
        cost_estimate=cost(2 * total * RANK * units, wide + tiled),
    )(*wide, *tiled)


def outer_sum(left_side, right_side, weight):
    return lax.dot_general(
        left_side * weight,
        right_side,
        (((0,), (0,)), ((), ())),
        precision=lax.Precision.HIGHEST,
        preferred_element_type=jnp.float32,
    )


def example_features(in_side, hidden_side, gate_side, up_side, out_side, length):
    positions = lax.broadcasted_iota(jnp.int32, (SEQ, RANK), 0)
    weight = (positions < length).astype(jnp.float32)
    return (
        outer_sum(in_side, gate_side, weight),
        outer_sum(in_side, up_side, weight),
        outer_sum(hidden_side, out_side, weight),
    )


def query_kernel(lengths, in_out, sums, found):
    for e in range(found.shape[0]):
        part = slice(e * SEQ, (e + 1) * SEQ)
        three = example_features(
            in_out[part, :RANK],
            sums[part, 2 * RANK :],
            sums[part, :RANK],
            sums[part, RANK : 2 * RANK],
            in_out[part, RANK:],
            lengths[e],
        )
        for segment in range(3):
            found[e, segment * RANK : (segment + 1) * RANK, :] = three[segment]


def query_features(lengths, in_out, sums):
    return pl.pallas_call(
        query_kernel,
        in_specs=[SCALARS, IN_VMEM, IN_VMEM],
        out_specs=IN_VMEM,
        out_shape=jax.ShapeDtypeStruct((lengths.shape[0], 3 * RANK, RANK), jnp.float32),
        compiler_params=params(),
    )(lengths, in_out, sums)


def score_kernel(
    lengths, place, in_out, hidden, early, near, far, q0, q1, q2, q3, scores
):
    queries = q0.shape[0]
    shape = scores.shape
    row = lax.broadcasted_iota(jnp.int32, shape, 0)
    column = lax.broadcasted_iota(jnp.int32, shape, 1)
    gradient = jnp.concatenate([early[...], (near[...] + far[...]).T], axis=0)
    total = jnp.zeros(shape, jnp.float32)
    for e in range(shape[0]):
        part = slice(e * SEQ, (e + 1) * SEQ)
        three = jnp.concatenate(
            example_features(
                in_out[part, :RANK],
                hidden[part, :],
                gradient[part, :RANK],
                gradient[part, RANK:],
                in_out[part, RANK:],
                lengths[e],
            ),
            axis=0,
        )
        for step, found in enumerate((q0, q1, q2, q3)):
            for j in range(queries):
                value = jnp.sum(three * found[j], keepdims=True)
                here = (row == e) & (
                    column == queries * jnp.bitwise_xor(place[0], step) + j
                )
                total = total + jnp.where(here, value, 0.0)
    scores[...] = total


def partial_scores(lengths, place, in_out, hidden, early, near, far, found):
    number = lengths.shape[0]
    return pl.pallas_call(
        score_kernel,
        in_specs=[SCALARS] * 2 + [IN_VMEM] * 9,
        out_specs=IN_VMEM,
        out_shape=jax.ShapeDtypeStruct((number, 4 * found[0].shape[0]), jnp.float32),
        compiler_params=params(),
    )(lengths, place, in_out, hidden, early, near, far, *found)


def after(value, *others):
    return lax.optimization_barrier((value, *others))[0]


def moving_plan(
    train_input,
    train_gate,
    train_up,
    train_outgrad,
    train_lengths,
    query_input,
    query_gate,
    query_up,
    query_outgrad,
    query_lengths,
    down_weight,
    proj_input,
    proj_outgrad,
    proj_hidden,
    proj_gate,
    proj_up,
):
    t = lax.axis_index("tensor")
    d = lax.axis_index("dp")
    x, core, upper = d // 2, d % 2, t // 2
    at_home = x == upper
    inner_chip = (t == 1) | (t == 2)
    near_code = jnp.where(at_home, 0, jnp.where(inner_chip, 1, 2))
    first_parity = jnp.where(at_home, t % 2, upper)
    flags = jnp.stack([near_code, first_parity ^ core]).astype(jnp.int32)
    place = jnp.stack([d]).astype(jnp.int32)

    to_core = functools.partial(lax.ppermute, axis_name="dp", perm=[(i, i ^ 1) for i in range(4)])
    to_chip = functools.partial(lax.ppermute, axis_name="dp", perm=[(i, i ^ 2) for i in range(4)])
    to_other = functools.partial(lax.ppermute, axis_name="dp", perm=[(i, i ^ 3) for i in range(4)])
    outer = functools.partial(
        lax.ppermute, axis_name="tensor", perm=[(i, i ^ 1) for i in range(4)]
    )
    across = functools.partial(
        lax.ppermute, axis_name="tensor", perm=[(i, i ^ 2) for i in range(4)]
    )
    opposite = functools.partial(
        lax.ppermute, axis_name="tensor", perm=[(i, 3 - i) for i in range(4)]
    )
    middle = functools.partial(
        lax.ppermute,
        axis_name=("tensor", "dp"),
        perm=[
            (4 * i + j, 4 * (3 - i) + j) if i in (1, 2) else (4 * i + j, 4 * i + (j ^ 1))
            for i in range(4)
            for j in range(4)
        ],
    )

    q_input, q_gate, q_up, q_outgrad = [
        flatten(a) for a in (query_input, query_gate, query_up, query_outgrad)
    ]
    t_input, t_gate, t_up, t_outgrad = [
        flatten(a) for a in (train_input, train_gate, train_up, train_outgrad)
    ]
    examples = train_lengths.shape[0] // 2
    cut = examples * SEQ

    def first_hops(own):
        return own, outer(own), across(own)

    def last_hops(own, one, two):
        mid = middle(after(own, two))
        return own, one, mid, two, two, outer(after(two, one))

    def crossing_pair(own, one, second_inner, third_inner, second_outer, third_outer):
        def choose(within, beyond_inner, beyond_outer):
            beyond = jnp.where(inner_chip, beyond_inner, beyond_outer)
            return jnp.where(at_home, beyond, within)

        return jnp.stack(
            [choose(own, second_inner, second_outer), choose(one, third_inner, third_outer)]
        )

    weight_own, weight_sib = down_weight, to_core(down_weight)
    q_hops = first_hops(q_outgrad)
    far_gate = to_chip(t_gate[cut:])
    own_in_out, hidden = early_sides(
        t_input, q_input, t_outgrad, q_outgrad, proj_input, proj_outgrad, t_gate, t_up, q_gate,
        q_up, proj_hidden,
    )

    q_blocks = last_hops(*q_hops[:2], after(q_hops[2], own_in_out))
    a_hops = first_hops(after(t_outgrad[:cut], q_hops[2], far_gate))
    far_up = to_chip(after(t_up[cut:], far_gate))
    q_send = after(crossing_pair(*q_blocks), far_up)
    q_far = to_chip(q_send)
    a_blocks = last_hops(*a_hops[:2], after(a_hops[2], q_send))

    b_hops = first_hops(after(t_outgrad[cut:], a_hops[2]))
    gates, ups = turned(t_gate, t_up, far_gate, far_up)
    a_send = crossing_pair(*a_blocks[:5], after(a_blocks[5], q_far, gates))
    a_far = to_chip(a_send)
    q_near_sum, q_far_sum = partial_sums(
        flags, q_blocks, after(q_far, a_send), weight_own, weight_sib
    )
    q_returned = to_chip(after(q_far_sum, a_far))
    b_blocks = last_hops(*b_hops[:2], after(b_hops[2], q_far_sum))
    b_send = crossing_pair(*b_blocks)
    b_far = to_chip(b_send)
    a_near_sum, a_far_sum = partial_sums(
        flags, a_blocks, after(a_far, b_send), weight_own, weight_sib
    )
    a_returned = to_chip(a_far_sum)
    in_out = own_in_out + outer(after(own_in_out, b_send))
    q_gradient = finished_sides(
        q_near_sum, after(q_returned, a_far_sum), q_gate, q_up, proj_gate, proj_up
    )
    q_sums = jnp.concatenate([q_gradient, hidden[2 * cut :]], axis=1)
    q_sums = q_sums + outer(q_sums)
    b_near, b_away = lent_sides(
        after(flags, q_sums, in_out), b_blocks, b_far, weight_own, weight_sib, gates, ups,
        proj_gate, proj_up,
    )
    in_out = in_out + after(across(in_out), b_near)
    q_sums = q_sums + after(across(q_sums), b_near)
    own_found = query_features(query_lengths, in_out[2 * cut :], q_sums)
    found = (own_found, to_core(own_found), to_chip(own_found), to_other(own_found))
    a_gradient = finished_sides(a_near_sum, a_returned, t_gate, t_up, proj_gate, proj_up)
    own_scores = partial_scores(
        train_lengths, place, in_out[: 2 * cut], hidden[: 2 * cut], a_gradient, b_near,
        to_chip(b_away), found,
    )
    scores = own_scores + outer(own_scores) + across(own_scores) + opposite(own_scores)
    return scores / (RANK * SEQ)


def solution(mesh):
    tensor, dp = mesh.shape["tensor"], mesh.shape["dp"]

    def per_device(*arguments):
        if tensor == 4 and dp == 4:
            return moving_plan(*arguments)
        return gathering_plan(*arguments)

    in_specs = (
        P(("parts", "dp"), None, "tensor"),
        P(("parts", "dp"), None, "tensor"),
        P(("parts", "dp"), None, "tensor"),
        P(("parts", "dp"), None, "tensor"),
        P(("parts", "dp")),
        P(("parts", "dp"), None, "tensor"),
        P(("parts", "dp"), None, "tensor"),
        P(("parts", "dp"), None, "tensor"),
        P(("parts", "dp"), None, "tensor"),
        P(("parts", "dp")),
        P("tensor", "dp"),
        P(None, "tensor"),
        P(None, "tensor"),
        P(None, "tensor"),
        P(None, "tensor"),
        P(None, "tensor"),
    )
    out_specs = P(("parts", "dp"), None)
    return jax.shard_map(
        per_device, mesh=mesh, in_specs=in_specs, out_specs=out_specs, check_vma=False
    )
```

```python
import functools

import jax
import jax.numpy as jnp
from jax import lax
from jax.experimental import pallas as pl
from jax.experimental.pallas import tpu as pltpu
from jax.sharding import PartitionSpec as P

RANK = 64
SEQ = 64
TILE = 512
WIDE = 1792
VMEM_BYTES = 40 * 1024 * 1024
BIG_VMEM_BYTES = 58 * 1024 * 1024


def flatten(array):
    return array.reshape(-1, array.shape[-1])


def project(rows, table):
    return lax.dot_general(
        rows, table, (((1,), (1,)), ((), ())), preferred_element_type=jnp.float32
    )


def inner(left_side, right_side):
    return lax.dot_general(
        left_side,
        right_side,
        (((1,), (1,)), ((), ())),
        precision=lax.Precision.HIGHEST,
        preferred_element_type=jnp.float32,
    )


def gated_hidden(gate, up):
    gate_wide = gate.astype(jnp.float32)
    up_wide = up.astype(jnp.float32)
    return (gate_wide * jax.nn.sigmoid(gate_wide) * up_wide).astype(jnp.bfloat16)


def gradients(gate, up, hidden_grad):
    gate_wide = gate.astype(jnp.float32)
    up_wide = up.astype(jnp.float32)
    sigmoid_gate = jax.nn.sigmoid(gate_wide)
    silu_gate = gate_wide * sigmoid_gate
    gate_grad = (
        hidden_grad * up_wide * sigmoid_gate * (1.0 + gate_wide * (1.0 - sigmoid_gate))
    ).astype(jnp.bfloat16)
    up_grad = (hidden_grad * silu_gate).astype(jnp.bfloat16)
    return gate_grad, up_grad


def gradient_sides(gate, up, hidden_grad, proj_gate, proj_up):
    gate_grad, up_grad = gradients(gate, up, hidden_grad)
    return project(gate_grad, proj_gate), project(up_grad, proj_up)


def outer_sums(left_side, right_side, lengths):
    number = lengths.shape[0]
    length = left_side.shape[0] // number
    positions = lax.broadcasted_iota(jnp.int32, (number, length), 1)
    weights = (positions < lengths[:, None]).astype(jnp.float32)
    left_rows = left_side.reshape(number, length, left_side.shape[1]) * weights[:, :, None]
    right_rows = right_side.reshape(number, length, right_side.shape[1])
    summed = jnp.einsum("est,esu->etu", left_rows, right_rows, precision=lax.Precision.HIGHEST)
    return summed.reshape(number, -1)


def features(in_side, hidden_side, gate_side, up_side, out_side, lengths):
    return jnp.concatenate(
        [
            outer_sums(in_side, gate_side, lengths),
            outer_sums(in_side, up_side, lengths),
            outer_sums(hidden_side, out_side, lengths),
        ],
        axis=1,
    )


def gathering_plan(
    train_input,
    train_gate,
    train_up,
    train_outgrad,
    train_lengths,
    query_input,
    query_gate,
    query_up,
    query_outgrad,
    query_lengths,
    down_weight,
    proj_input,
    proj_outgrad,
    proj_hidden,
    proj_gate,
    proj_up,
):
    weight = lax.all_gather(down_weight, "dp", axis=1, tiled=True)

    def full_features(inputs, gate, up, outgrad, lengths):
        inputs, gate, up, outgrad = [flatten(a) for a in (inputs, gate, up, outgrad)]
        rows = lax.all_gather(outgrad, "tensor", axis=1, tiled=True)
        gate_side, up_side = gradient_sides(gate, up, project(rows, weight), proj_gate, proj_up)
        hidden_side = project(gated_hidden(gate, up), proj_hidden)
        sides = (
            project(inputs, proj_input),
            hidden_side,
            gate_side,
            up_side,
            project(outgrad, proj_outgrad),
        )
        return features(*lax.psum(sides, "tensor"), lengths)

    train_features = full_features(
        train_input, train_gate, train_up, train_outgrad, train_lengths
    )
    query_features = full_features(
        query_input, query_gate, query_up, query_outgrad, query_lengths
    )
    gathered = lax.all_gather(query_features, "dp", axis=0, tiled=True)
    return inner(train_features, gathered) / (RANK * SEQ)


ANYWHERE = pl.BlockSpec(memory_space=pl.ANY)
SCALARS = pl.BlockSpec(memory_space=pltpu.SMEM)
IN_VMEM = pl.BlockSpec(memory_space=pltpu.VMEM)


def params(limit=VMEM_BYTES):
    return pltpu.CompilerParams(vmem_limit_bytes=limit)


def cost(flops, arrays):
    return pl.CostEstimate(flops=1024, bytes_accessed=1024, transcendentals=0)


def tile_columns(number, block=0, tile=TILE):
    return pl.BlockSpec((number, tile), lambda i: (block, i))


def tile_rows(width, tile=TILE):
    return pl.BlockSpec((tile, width), lambda i: (i, 0))


def whole(shape):
    return pl.BlockSpec(shape, lambda i: tuple(0 for _ in shape))


def stacked_products(
    flags, pairs, far, weight_own, weight_sib, stacked, semaphores, held, weight_sems
):
    number = far.shape[1]
    step = pl.program_id(0)
    tiles = weight_own.shape[0] // TILE

    def weight_copies(tile):
        part = pl.ds(pl.multiple_of(tile * TILE, TILE), TILE)
        slot = lax.rem(tile, 3)
        return [
            pltpu.make_async_copy(
                weight.at[part], held.at[slot, side], weight_sems.at[slot, side]
            )
            for side, weight in enumerate((weight_own, weight_sib))
        ]

    @pl.when(step == 0)
    def _():
        slot = flags[1]
        far_copies = [
            pltpu.make_async_copy(
                far.at[i], stacked.at[jnp.bitwise_xor(slot, i), pl.ds(number, number)],
                semaphores.at[2 + i],
            )
            for i in range(2)
        ]
        for copy in far_copies:
            copy.start()
        for code, pair in enumerate(pairs):

            @pl.when(flags[0] == code)
            def _():
                copies = [
                    pltpu.make_async_copy(
                        pair[i], stacked.at[jnp.bitwise_xor(slot, i), pl.ds(0, number)],
                        semaphores.at[i],
                    )
                    for i in range(2)
                ]
                for copy in copies:
                    copy.start()
                for tile in range(2):
                    for copy in weight_copies(tile):
                        copy.start()
                for copy in copies:
                    copy.wait()

        for copy in far_copies:
            copy.wait()

    @pl.when(step + 2 < tiles)
    def _():
        for copy in weight_copies(step + 2):
            copy.start()

    for copy in weight_copies(step):
        copy.wait()
    slot = lax.rem(step, 3)
    return project(held[slot, 0], stacked[0]) + project(held[slot, 1], stacked[1])


def add_sides(hidden_grad, gate, up, proj_gate, proj_up, sides):
    gate_part, up_part = gradient_sides(gate, up, hidden_grad, proj_gate, proj_up)
    part = jnp.concatenate([gate_part, up_part], axis=1)
    first = pl.program_id(0) == 0

    @pl.when(first)
    def _():
        sides[...] = part

    @pl.when(jnp.logical_not(first))
    def _():
        sides[...] += part


def partial_kernel(
    flags, b0, b1, b2, b3, b4, b5, far, weight_own, weight_sib, near_sum, far_sum, *scratch
):
    pairs = ((b0, b1), (b2, b3), (b4, b5))
    total = stacked_products(flags, pairs, far, weight_own, weight_sib, *scratch)
    number = far.shape[1]
    near_sum[...] = total[:, :number]
    far_sum[...] = total[:, number:].astype(jnp.bfloat16)


def partial_sums(flags, blocks, far, weight_own, weight_sib):
    number, half = blocks[0].shape
    units = weight_own.shape[0]
    return pl.pallas_call(
        partial_kernel,
        grid=(units // TILE,),
        in_specs=[SCALARS] + [ANYWHERE] * 9,
        out_specs=[tile_rows(number)] * 2,
        out_shape=[
            jax.ShapeDtypeStruct((units, number), jnp.float32),
            jax.ShapeDtypeStruct((units, number), jnp.bfloat16),
        ],
        scratch_shapes=[
            pltpu.VMEM((2, 2 * number, half), jnp.bfloat16),
            pltpu.SemaphoreType.DMA((4,)),
            pltpu.VMEM((3, 2, TILE, half), jnp.bfloat16),
            pltpu.SemaphoreType.DMA((3, 2)),
        ],
        compiler_params=params(BIG_VMEM_BYTES),
        cost_estimate=cost(8 * number * half * units, (far, weight_own, weight_sib)),
    )(flags, *blocks, far, weight_own, weight_sib)


def finish_kernel(near_sum, returned, gate, up, proj_gate, proj_up, sides):
    hidden_grad = (near_sum[...] + returned[...].astype(jnp.float32)).T
    add_sides(hidden_grad, gate[...], up[...], proj_gate[...], proj_up[...], sides)


def finished_sides(near_sum, returned, gate, up, proj_gate, proj_up):
    units, number = near_sum.shape
    return pl.pallas_call(
        finish_kernel,
        grid=(units // WIDE,),
        in_specs=[tile_rows(number, WIDE)] * 2
        + [tile_columns(number, 0, WIDE)] * 2
        + [tile_columns(RANK, 0, WIDE)] * 2,
        out_specs=whole((number, 2 * RANK)),
        out_shape=jax.ShapeDtypeStruct((number, 2 * RANK), jnp.float32),
        compiler_params=params(),
        cost_estimate=cost(4 * number * RANK * units, (near_sum, returned, gate, up)),
    )(near_sum, returned, gate, up, proj_gate, proj_up)


def turn_kernel(gate, up, far_gate, far_up, gates, ups):
    number = gate.shape[0]
    for source, target, part in (
        (gate, gates, slice(0, number)),
        (up, ups, slice(0, number)),
        (far_gate, gates, slice(number, None)),
        (far_up, ups, slice(number, None)),
    ):
        target[:, part] = source[...].astype(jnp.float32).T.astype(jnp.bfloat16)


def turned(gate, up, far_gate, far_up):
    number, units = far_gate.shape
    shape = jax.ShapeDtypeStruct((units, 2 * number), jnp.bfloat16)
    return pl.pallas_call(
        turn_kernel,
        grid=(units // TILE,),
        in_specs=[tile_columns(number, 1)] * 2 + [tile_columns(number)] * 2,
        out_specs=[tile_rows(2 * number)] * 2,
        out_shape=[shape] * 2,
        compiler_params=params(),
        cost_estimate=cost(0, (gate, up)),
    )(gate, up, far_gate, far_up)


def lent_kernel(
    flags, b0, b1, b2, b3, b4, b5, far, weight_own, weight_sib, gates, ups, proj_gate, proj_up,
    near, away, *scratch,
):
    pairs = ((b0, b1), (b2, b3), (b4, b5))
    hidden_grad = stacked_products(flags, pairs, far, weight_own, weight_sib, *scratch)
    gate_grad, up_grad = gradients(gates[...], ups[...], hidden_grad)
    part = jnp.concatenate(
        [
            jnp.dot(proj_gate[...], gate_grad, preferred_element_type=jnp.float32),
            jnp.dot(proj_up[...], up_grad, preferred_element_type=jnp.float32),
        ],
        axis=0,
    )
    number = near.shape[1]
    first = pl.program_id(0) == 0

    @pl.when(first)
    def _():
        near[...] = part[:, :number]
        away[...] = part[:, number:]

    @pl.when(jnp.logical_not(first))
    def _():
        near[...] += part[:, :number]
        away[...] += part[:, number:]


def lent_sides(flags, blocks, far, weight_own, weight_sib, gates, ups, proj_gate, proj_up):
    number, half = blocks[0].shape
    units = weight_own.shape[0]
    return pl.pallas_call(
        lent_kernel,
        grid=(units // TILE,),
        in_specs=[SCALARS]
        + [ANYWHERE] * 9
        + [tile_rows(2 * number)] * 2
        + [tile_columns(RANK)] * 2,
        out_specs=[whole((2 * RANK, number))] * 2,
        out_shape=[jax.ShapeDtypeStruct((2 * RANK, number), jnp.float32)] * 2,
        scratch_shapes=[
            pltpu.VMEM((2, 2 * number, half), jnp.bfloat16),
            pltpu.SemaphoreType.DMA((4,)),
            pltpu.VMEM((3, 2, TILE, half), jnp.bfloat16),
            pltpu.SemaphoreType.DMA((3, 2)),
        ],
        compiler_params=params(BIG_VMEM_BYTES),
        cost_estimate=cost(8 * number * half * units, (far, weight_own, weight_sib)),
    )(flags, *blocks, far, weight_own, weight_sib, gates, ups, proj_gate, proj_up)


def early_kernel(
    t_input, q_input, t_outgrad, q_outgrad, proj_input, proj_outgrad, t_gate, t_up, q_gate, q_up,
    proj_hidden, in_out, hidden,
):
    number = t_input.shape[0]
    t_hidden = project(gated_hidden(t_gate[...], t_up[...]), proj_hidden[...])
    q_hidden = project(gated_hidden(q_gate[...], q_up[...]), proj_hidden[...])
    first = pl.program_id(0) == 0

    @pl.when(first)
    def _():
        for inputs, outgrad, part in (
            (t_input, t_outgrad, slice(0, number)),
            (q_input, q_outgrad, slice(number, None)),
        ):
            in_out[part, :] = jnp.concatenate(
                [
                    project(inputs[...], proj_input[...]),
                    project(outgrad[...], proj_outgrad[...]),
                ],
                axis=1,
            )
        hidden[:number, :] = t_hidden
        hidden[number:, :] = q_hidden

    @pl.when(jnp.logical_not(first))
    def _():
        hidden[:number, :] += t_hidden
        hidden[number:, :] += q_hidden


def early_sides(
    t_input, q_input, t_outgrad, q_outgrad, proj_input, proj_outgrad, t_gate, t_up, q_gate, q_up,
    proj_hidden,
):
    total, units = t_gate.shape[0] + q_gate.shape[0], t_gate.shape[1]
    wide = (t_input, q_input, t_outgrad, q_outgrad, proj_input, proj_outgrad)
    tiled = (t_gate, t_up, q_gate, q_up, proj_hidden)
    shapes = ((total, 2 * RANK), (total, RANK))
    return pl.pallas_call(
        early_kernel,
        grid=(units // TILE,),
        in_specs=[whole(a.shape) for a in wide] + [tile_columns(a.shape[0]) for a in tiled],
        out_specs=[whole(shape) for shape in shapes],
        out_shape=[jax.ShapeDtypeStruct(shape, jnp.float32) for shape in shapes],
        compiler_params=params(),
        cost_estimate=cost(2 * total * RANK * units, wide + tiled),
    )(*wide, *tiled)


def outer_sum(left_side, right_side, weight):
    return lax.dot_general(
        left_side * weight,
        right_side,
        (((0,), (0,)), ((), ())),
        precision=lax.Precision.HIGHEST,
        preferred_element_type=jnp.float32,
    )


def example_features(in_side, hidden_side, gate_side, up_side, out_side, length):
    positions = lax.broadcasted_iota(jnp.int32, (SEQ, RANK), 0)
    weight = (positions < length).astype(jnp.float32)
    return (
        outer_sum(in_side, gate_side, weight),
        outer_sum(in_side, up_side, weight),
        outer_sum(hidden_side, out_side, weight),
    )


def query_kernel(lengths, in_out, sums, found):
    for e in range(found.shape[0]):
        part = slice(e * SEQ, (e + 1) * SEQ)
        three = example_features(
            in_out[part, :RANK],
            sums[part, 2 * RANK :],
            sums[part, :RANK],
            sums[part, RANK : 2 * RANK],
            in_out[part, RANK:],
            lengths[e],
        )
        for segment in range(3):
            found[e, segment * RANK : (segment + 1) * RANK, :] = three[segment]


def query_features(lengths, in_out, sums):
    return pl.pallas_call(
        query_kernel,
        in_specs=[SCALARS, IN_VMEM, IN_VMEM],
        out_specs=IN_VMEM,
        out_shape=jax.ShapeDtypeStruct((lengths.shape[0], 3 * RANK, RANK), jnp.float32),
        compiler_params=params(),
    )(lengths, in_out, sums)


def score_kernel(
    lengths, place, in_out, hidden, early, near, far, q0, q1, q2, q3, scores
):
    queries = q0.shape[0]
    shape = scores.shape
    row = lax.broadcasted_iota(jnp.int32, shape, 0)
    column = lax.broadcasted_iota(jnp.int32, shape, 1)
    gradient = jnp.concatenate([early[...], (near[...] + far[...]).T], axis=0)
    total = jnp.zeros(shape, jnp.float32)
    for e in range(shape[0]):
        part = slice(e * SEQ, (e + 1) * SEQ)
        three = jnp.concatenate(
            example_features(
                in_out[part, :RANK],
                hidden[part, :],
                gradient[part, :RANK],
                gradient[part, RANK:],
                in_out[part, RANK:],
                lengths[e],
            ),
            axis=0,
        )
        for step, found in enumerate((q0, q1, q2, q3)):
            for j in range(queries):
                value = jnp.sum(three * found[j], keepdims=True)
                here = (row == e) & (
                    column == queries * jnp.bitwise_xor(place[0], step) + j
                )
                total = total + jnp.where(here, value, 0.0)
    scores[...] = total


def partial_scores(lengths, place, in_out, hidden, early, near, far, found):
    number = lengths.shape[0]
    return pl.pallas_call(
        score_kernel,
        in_specs=[SCALARS] * 2 + [IN_VMEM] * 9,
        out_specs=IN_VMEM,
        out_shape=jax.ShapeDtypeStruct((number, 4 * found[0].shape[0]), jnp.float32),
        compiler_params=params(),
    )(lengths, place, in_out, hidden, early, near, far, *found)


def after(value, *others):
    return lax.optimization_barrier((value, *others))[0]


def moving_plan(
    train_input,
    train_gate,
    train_up,
    train_outgrad,
    train_lengths,
    query_input,
    query_gate,
    query_up,
    query_outgrad,
    query_lengths,
    down_weight,
    proj_input,
    proj_outgrad,
    proj_hidden,
    proj_gate,
    proj_up,
):
    t = lax.axis_index("tensor")
    d = lax.axis_index("dp")
    x, core, upper = d // 2, d % 2, t // 2
    at_home = x == upper
    inner_chip = (t == 1) | (t == 2)
    near_code = jnp.where(at_home, 0, jnp.where(inner_chip, 1, 2))
    first_parity = jnp.where(at_home, t % 2, upper)
    flags = jnp.stack([near_code, first_parity ^ core]).astype(jnp.int32)
    place = jnp.stack([d]).astype(jnp.int32)

    to_core = functools.partial(lax.ppermute, axis_name="dp", perm=[(i, i ^ 1) for i in range(4)])
    to_chip = functools.partial(lax.ppermute, axis_name="dp", perm=[(i, i ^ 2) for i in range(4)])
    to_other = functools.partial(lax.ppermute, axis_name="dp", perm=[(i, i ^ 3) for i in range(4)])
    outer = functools.partial(
        lax.ppermute, axis_name="tensor", perm=[(i, i ^ 1) for i in range(4)]
    )
    across = functools.partial(
        lax.ppermute, axis_name="tensor", perm=[(i, i ^ 2) for i in range(4)]
    )
    opposite = functools.partial(
        lax.ppermute, axis_name="tensor", perm=[(i, 3 - i) for i in range(4)]
    )
    middle = functools.partial(
        lax.ppermute,
        axis_name=("tensor", "dp"),
        perm=[
            (4 * i + j, 4 * (3 - i) + j) if i in (1, 2) else (4 * i + j, 4 * i + (j ^ 1))
            for i in range(4)
            for j in range(4)
        ],
    )

    q_input, q_gate, q_up, q_outgrad = [
        flatten(a) for a in (query_input, query_gate, query_up, query_outgrad)
    ]
    t_input, t_gate, t_up, t_outgrad = [
        flatten(a) for a in (train_input, train_gate, train_up, train_outgrad)
    ]
    examples = train_lengths.shape[0] // 2
    cut = examples * SEQ

    def first_hops(own):
        return own, outer(own), across(own)

    def last_hops(own, one, two):
        mid = middle(after(own, two))
        return own, one, mid, two, two, outer(after(two, one))

    def crossing_pair(own, one, second_inner, third_inner, second_outer, third_outer):
        def choose(within, beyond_inner, beyond_outer):
            beyond = jnp.where(inner_chip, beyond_inner, beyond_outer)
            return jnp.where(at_home, beyond, within)

        return jnp.stack(
            [choose(own, second_inner, second_outer), choose(one, third_inner, third_outer)]
        )

    weight_own, weight_sib = down_weight, to_core(down_weight)
    q_hops = first_hops(q_outgrad)
    far_gate = to_chip(t_gate[cut:])
    own_in_out, hidden = early_sides(
        t_input, q_input, t_outgrad, q_outgrad, proj_input, proj_outgrad, t_gate, t_up, q_gate,
        q_up, proj_hidden,
    )

    q_blocks = last_hops(*q_hops[:2], after(q_hops[2], own_in_out))
    a_hops = first_hops(after(t_outgrad[:cut], q_hops[2], far_gate, weight_sib))
    far_up = to_chip(after(t_up[cut:], far_gate))
    q_send = after(crossing_pair(*q_blocks), far_up)
    q_far = to_chip(q_send)
    a_blocks = last_hops(*a_hops[:2], after(a_hops[2], q_send))

    b_hops = first_hops(after(t_outgrad[cut:], a_hops[2]))
    gates, ups = turned(t_gate, t_up, far_gate, far_up)
    a_send = crossing_pair(*a_blocks[:5], after(a_blocks[5], q_far, gates))
    a_far = to_chip(a_send)
    q_near_sum, q_far_sum = partial_sums(
        flags, q_blocks, after(q_far, a_send), weight_own, weight_sib
    )
    q_returned = to_chip(after(q_far_sum, a_far))
    b_blocks = last_hops(*b_hops[:2], after(b_hops[2], q_far_sum))
    b_send = crossing_pair(*b_blocks)
    b_far = to_chip(b_send)
    a_near_sum, a_far_sum = partial_sums(
        flags, a_blocks, after(a_far, b_send), weight_own, weight_sib
    )
    in_out = own_in_out + outer(after(own_in_out, b_send))
    a_returned = to_chip(a_far_sum)
    q_gradient = finished_sides(
        q_near_sum, after(q_returned, a_far_sum), q_gate, q_up, proj_gate, proj_up
    )
    q_sums = jnp.concatenate([q_gradient, hidden[2 * cut :]], axis=1)
    q_sums = q_sums + outer(q_sums)
    b_near, b_away = lent_sides(
        after(flags, q_sums, in_out), b_blocks, b_far, weight_own, weight_sib, gates, ups,
        proj_gate, proj_up,
    )
    in_out = in_out + after(across(in_out), b_near)
    q_sums = q_sums + after(across(q_sums), b_near)
    own_found = query_features(query_lengths, in_out[2 * cut :], q_sums)
    found = (own_found, to_core(own_found), to_chip(own_found), to_other(own_found))
    b_far_sides = to_chip(b_away)
    a_gradient = finished_sides(
        a_near_sum, after(a_returned, b_far_sides), t_gate, t_up, proj_gate, proj_up
    )
    own_scores = partial_scores(
        train_lengths, place, in_out[: 2 * cut], hidden[: 2 * cut], a_gradient, b_near,
        b_far_sides, found,
    )
    scores = own_scores + outer(own_scores) + across(own_scores) + opposite(own_scores)
    return scores / (RANK * SEQ)


def solution(mesh):
    tensor, dp = mesh.shape["tensor"], mesh.shape["dp"]

    def per_device(*arguments):
        if tensor == 4 and dp == 4:
            return moving_plan(*arguments)
        return gathering_plan(*arguments)

    in_specs = (
        P(("parts", "dp"), None, "tensor"),
        P(("parts", "dp"), None, "tensor"),
        P(("parts", "dp"), None, "tensor"),
        P(("parts", "dp"), None, "tensor"),
        P(("parts", "dp")),
        P(("parts", "dp"), None, "tensor"),
        P(("parts", "dp"), None, "tensor"),
        P(("parts", "dp"), None, "tensor"),
        P(("parts", "dp"), None, "tensor"),
        P(("parts", "dp")),
        P("tensor", "dp"),
        P(None, "tensor"),
        P(None, "tensor"),
        P(None, "tensor"),
        P(None, "tensor"),
        P(None, "tensor"),
    )
    out_specs = P(("parts", "dp"), None)
    return jax.shard_map(
        per_device, mesh=mesh, in_specs=in_specs, out_specs=out_specs, check_vma=False
    )
```

```python
import functools

import jax
import jax.numpy as jnp
from jax import lax
from jax.experimental import pallas as pl
from jax.experimental.pallas import tpu as pltpu
from jax.sharding import PartitionSpec as P

RANK = 64
SEQ = 64
TILE = 512
WIDE = 1792
VMEM_BYTES = 40 * 1024 * 1024
BIG_VMEM_BYTES = 58 * 1024 * 1024


def flatten(array):
    return array.reshape(-1, array.shape[-1])


def project(rows, table):
    return lax.dot_general(
        rows, table, (((1,), (1,)), ((), ())), preferred_element_type=jnp.float32
    )


def inner(left_side, right_side):
    return lax.dot_general(
        left_side,
        right_side,
        (((1,), (1,)), ((), ())),
        precision=lax.Precision.HIGHEST,
        preferred_element_type=jnp.float32,
    )


def gated_hidden(gate, up):
    gate_wide = gate.astype(jnp.float32)
    up_wide = up.astype(jnp.float32)
    return (gate_wide * jax.nn.sigmoid(gate_wide) * up_wide).astype(jnp.bfloat16)


def gradients(gate, up, hidden_grad):
    gate_wide = gate.astype(jnp.float32)
    up_wide = up.astype(jnp.float32)
    sigmoid_gate = jax.nn.sigmoid(gate_wide)
    silu_gate = gate_wide * sigmoid_gate
    gate_grad = (
        hidden_grad * up_wide * sigmoid_gate * (1.0 + gate_wide * (1.0 - sigmoid_gate))
    ).astype(jnp.bfloat16)
    up_grad = (hidden_grad * silu_gate).astype(jnp.bfloat16)
    return gate_grad, up_grad


def gradient_sides(gate, up, hidden_grad, proj_gate, proj_up):
    gate_grad, up_grad = gradients(gate, up, hidden_grad)
    return project(gate_grad, proj_gate), project(up_grad, proj_up)


def outer_sums(left_side, right_side, lengths):
    number = lengths.shape[0]
    length = left_side.shape[0] // number
    positions = lax.broadcasted_iota(jnp.int32, (number, length), 1)
    weights = (positions < lengths[:, None]).astype(jnp.float32)
    left_rows = left_side.reshape(number, length, left_side.shape[1]) * weights[:, :, None]
    right_rows = right_side.reshape(number, length, right_side.shape[1])
    summed = jnp.einsum("est,esu->etu", left_rows, right_rows, precision=lax.Precision.HIGHEST)
    return summed.reshape(number, -1)


def features(in_side, hidden_side, gate_side, up_side, out_side, lengths):
    return jnp.concatenate(
        [
            outer_sums(in_side, gate_side, lengths),
            outer_sums(in_side, up_side, lengths),
            outer_sums(hidden_side, out_side, lengths),
        ],
        axis=1,
    )


def gathering_plan(
    train_input,
    train_gate,
    train_up,
    train_outgrad,
    train_lengths,
    query_input,
    query_gate,
    query_up,
    query_outgrad,
    query_lengths,
    down_weight,
    proj_input,
    proj_outgrad,
    proj_hidden,
    proj_gate,
    proj_up,
):
    weight = lax.all_gather(down_weight, "dp", axis=1, tiled=True)

    def full_features(inputs, gate, up, outgrad, lengths):
        inputs, gate, up, outgrad = [flatten(a) for a in (inputs, gate, up, outgrad)]
        rows = lax.all_gather(outgrad, "tensor", axis=1, tiled=True)
        gate_side, up_side = gradient_sides(gate, up, project(rows, weight), proj_gate, proj_up)
        hidden_side = project(gated_hidden(gate, up), proj_hidden)
        sides = (
            project(inputs, proj_input),
            hidden_side,
            gate_side,
            up_side,
            project(outgrad, proj_outgrad),
        )
        return features(*lax.psum(sides, "tensor"), lengths)

    train_features = full_features(
        train_input, train_gate, train_up, train_outgrad, train_lengths
    )
    query_features = full_features(
        query_input, query_gate, query_up, query_outgrad, query_lengths
    )
    gathered = lax.all_gather(query_features, "dp", axis=0, tiled=True)
    return inner(train_features, gathered) / (RANK * SEQ)


ANYWHERE = pl.BlockSpec(memory_space=pl.ANY)
SCALARS = pl.BlockSpec(memory_space=pltpu.SMEM)
IN_VMEM = pl.BlockSpec(memory_space=pltpu.VMEM)


def params(limit=VMEM_BYTES):
    return pltpu.CompilerParams(vmem_limit_bytes=limit)


def cost(flops, arrays):
    return pl.CostEstimate(flops=1024, bytes_accessed=1024, transcendentals=0)


def tile_columns(number, block=0, tile=TILE):
    return pl.BlockSpec((number, tile), lambda i: (block, i))


def tile_rows(width, tile=TILE):
    return pl.BlockSpec((tile, width), lambda i: (i, 0))


def whole(shape):
    return pl.BlockSpec(shape, lambda i: tuple(0 for _ in shape))


def stacked_products(
    flags, pairs, far, weight_own, weight_sib, stacked, semaphores, held, weight_sems
):
    number = far[0].shape[0]
    step = pl.program_id(0)
    tiles = weight_own.shape[0] // TILE

    def weight_copies(tile):
        part = pl.ds(pl.multiple_of(tile * TILE, TILE), TILE)
        slot = lax.rem(tile, 3)
        return [
            pltpu.make_async_copy(
                weight.at[part], held.at[slot, side], weight_sems.at[slot, side]
            )
            for side, weight in enumerate((weight_own, weight_sib))
        ]

    def row_copies(pair, slot, row, first):
        return [
            pltpu.make_async_copy(
                pair[i], stacked.at[jnp.bitwise_xor(slot, i), pl.ds(row, number)],
                semaphores.at[first + i],
            )
            for i in range(2)
        ]

    @pl.when(step == 0)
    def _():
        far_copies = row_copies(far, flags[2], number, 2)
        for copy in far_copies:
            copy.start()
        for code, pair in enumerate(pairs):

            @pl.when(flags[0] == code)
            def _():
                copies = row_copies(pair, flags[1], 0, 0)
                for copy in copies:
                    copy.start()
                for tile in range(2):
                    for copy in weight_copies(tile):
                        copy.start()
                for copy in copies:
                    copy.wait()

        for copy in far_copies:
            copy.wait()

    @pl.when(step + 2 < tiles)
    def _():
        for copy in weight_copies(step + 2):
            copy.start()

    for copy in weight_copies(step):
        copy.wait()
    slot = lax.rem(step, 3)
    return project(held[slot, 0], stacked[0]) + project(held[slot, 1], stacked[1])


def add_sides(hidden_grad, gate, up, proj_gate, proj_up, sides):
    gate_part, up_part = gradient_sides(gate, up, hidden_grad, proj_gate, proj_up)
    part = jnp.concatenate([gate_part, up_part], axis=1)
    first = pl.program_id(0) == 0

    @pl.when(first)
    def _():
        sides[...] = part

    @pl.when(jnp.logical_not(first))
    def _():
        sides[...] += part


def partial_kernel(
    flags, b0, b1, b2, b3, b4, b5, far_a, far_b, weight_own, weight_sib, near_sum, far_sum,
    *scratch,
):
    pairs = ((b0, b1), (b2, b3), (b4, b5))
    far = (far_a, far_b)
    total = stacked_products(flags, pairs, far, weight_own, weight_sib, *scratch)
    number = far_a.shape[0]
    near_sum[...] = total[:, :number]
    far_sum[...] = total[:, number:].astype(jnp.bfloat16)


def product_scratch(number, half):
    return [
        pltpu.VMEM((2, 2 * number, half), jnp.bfloat16),
        pltpu.SemaphoreType.DMA((4,)),
        pltpu.VMEM((3, 2, TILE, half), jnp.bfloat16),
        pltpu.SemaphoreType.DMA((3, 2)),
    ]


def partial_sums(flags, blocks, far, weight_own, weight_sib):
    number, half = blocks[0].shape
    units = weight_own.shape[0]
    return pl.pallas_call(
        partial_kernel,
        grid=(units // TILE,),
        in_specs=[SCALARS] + [ANYWHERE] * 10,
        out_specs=[tile_rows(number)] * 2,
        out_shape=[
            jax.ShapeDtypeStruct((units, number), jnp.float32),
            jax.ShapeDtypeStruct((units, number), jnp.bfloat16),
        ],
        scratch_shapes=product_scratch(number, half),
        compiler_params=params(BIG_VMEM_BYTES),
        cost_estimate=cost(8 * number * half * units, (weight_own, weight_sib)),
    )(flags, *blocks, *far, weight_own, weight_sib)


def finish_kernel(near_sum, returned, gate, up, proj_gate, proj_up, sides):
    hidden_grad = (near_sum[...] + returned[...].astype(jnp.float32)).T
    add_sides(hidden_grad, gate[...], up[...], proj_gate[...], proj_up[...], sides)


def finished_sides(near_sum, returned, gate, up, proj_gate, proj_up):
    units, number = near_sum.shape
    return pl.pallas_call(
        finish_kernel,
        grid=(units // WIDE,),
        in_specs=[tile_rows(number, WIDE)] * 2
        + [tile_columns(number, 0, WIDE)] * 2
        + [tile_columns(RANK, 0, WIDE)] * 2,
        out_specs=whole((number, 2 * RANK)),
        out_shape=jax.ShapeDtypeStruct((number, 2 * RANK), jnp.float32),
        compiler_params=params(),
        cost_estimate=cost(4 * number * RANK * units, (near_sum, returned, gate, up)),
    )(near_sum, returned, gate, up, proj_gate, proj_up)


def turn_kernel(gate, up, far_gate, far_up, gates, ups):
    number = gate.shape[0]
    for source, target, part in (
        (gate, gates, slice(0, number)),
        (up, ups, slice(0, number)),
        (far_gate, gates, slice(number, None)),
        (far_up, ups, slice(number, None)),
    ):
        target[:, part] = source[...].astype(jnp.float32).T.astype(jnp.bfloat16)


def turned(gate, up, far_gate, far_up):
    number, units = far_gate.shape
    shape = jax.ShapeDtypeStruct((units, 2 * number), jnp.bfloat16)
    return pl.pallas_call(
        turn_kernel,
        grid=(units // TILE,),
        in_specs=[tile_columns(number, 1)] * 2 + [tile_columns(number)] * 2,
        out_specs=[tile_rows(2 * number)] * 2,
        out_shape=[shape] * 2,
        compiler_params=params(),
        cost_estimate=cost(0, (gate, up)),
    )(gate, up, far_gate, far_up)


def lent_kernel(
    flags, b0, b1, b2, b3, b4, b5, far_a, far_b, weight_own, weight_sib, gates, ups, proj_gate,
    proj_up, near, away, *scratch,
):
    pairs = ((b0, b1), (b2, b3), (b4, b5))
    far = (far_a, far_b)
    hidden_grad = stacked_products(flags, pairs, far, weight_own, weight_sib, *scratch)
    gate_grad, up_grad = gradients(gates[...], ups[...], hidden_grad)
    part = jnp.concatenate(
        [
            jnp.dot(proj_gate[...], gate_grad, preferred_element_type=jnp.float32),
            jnp.dot(proj_up[...], up_grad, preferred_element_type=jnp.float32),
        ],
        axis=0,
    )
    number = near.shape[1]
    first = pl.program_id(0) == 0

    @pl.when(first)
    def _():
        near[...] = part[:, :number]
        away[...] = part[:, number:]

    @pl.when(jnp.logical_not(first))
    def _():
        near[...] += part[:, :number]
        away[...] += part[:, number:]


def lent_sides(flags, blocks, far, weight_own, weight_sib, gates, ups, proj_gate, proj_up):
    number, half = blocks[0].shape
    units = weight_own.shape[0]
    side = jax.ShapeDtypeStruct((2 * RANK, number), jnp.float32)
    return pl.pallas_call(
        lent_kernel,
        grid=(units // TILE,),
        in_specs=[SCALARS]
        + [ANYWHERE] * 10
        + [tile_rows(2 * number)] * 2
        + [tile_columns(RANK)] * 2,
        out_specs=[whole(side.shape)] * 2,
        out_shape=[side] * 2,
        scratch_shapes=product_scratch(number, half),
        compiler_params=params(BIG_VMEM_BYTES),
        cost_estimate=cost(8 * number * half * units, (weight_own, weight_sib)),
    )(flags, *blocks, *far, weight_own, weight_sib, gates, ups, proj_gate, proj_up)


def early_kernel(
    t_input, q_input, t_outgrad, q_outgrad, proj_input, proj_outgrad, t_gate, t_up, q_gate, q_up,
    proj_hidden, in_out, hidden,
):
    number = t_input.shape[0]
    t_hidden = project(gated_hidden(t_gate[...], t_up[...]), proj_hidden[...])
    q_hidden = project(gated_hidden(q_gate[...], q_up[...]), proj_hidden[...])
    first = pl.program_id(0) == 0

    @pl.when(first)
    def _():
        for inputs, outgrad, part in (
            (t_input, t_outgrad, slice(0, number)),
            (q_input, q_outgrad, slice(number, None)),
        ):
            in_out[part, :] = jnp.concatenate(
                [
                    project(inputs[...], proj_input[...]),
                    project(outgrad[...], proj_outgrad[...]),
                ],
                axis=1,
            )
        hidden[:number, :] = t_hidden
        hidden[number:, :] = q_hidden

    @pl.when(jnp.logical_not(first))
    def _():
        hidden[:number, :] += t_hidden
        hidden[number:, :] += q_hidden


def early_sides(
    t_input, q_input, t_outgrad, q_outgrad, proj_input, proj_outgrad, t_gate, t_up, q_gate, q_up,
    proj_hidden,
):
    total, units = t_gate.shape[0] + q_gate.shape[0], t_gate.shape[1]
    wide = (t_input, q_input, t_outgrad, q_outgrad, proj_input, proj_outgrad)
    tiled = (t_gate, t_up, q_gate, q_up, proj_hidden)
    shapes = ((total, 2 * RANK), (total, RANK))
    return pl.pallas_call(
        early_kernel,
        grid=(units // TILE,),
        in_specs=[whole(a.shape) for a in wide] + [tile_columns(a.shape[0]) for a in tiled],
        out_specs=[whole(shape) for shape in shapes],
        out_shape=[jax.ShapeDtypeStruct(shape, jnp.float32) for shape in shapes],
        compiler_params=params(),
        cost_estimate=cost(2 * total * RANK * units, wide + tiled),
    )(*wide, *tiled)


def outer_sum(left_side, right_side, weight):
    return lax.dot_general(
        left_side * weight,
        right_side,
        (((0,), (0,)), ((), ())),
        precision=lax.Precision.HIGHEST,
        preferred_element_type=jnp.float32,
    )


def example_features(in_side, hidden_side, gate_side, up_side, out_side, length):
    positions = lax.broadcasted_iota(jnp.int32, (SEQ, RANK), 0)
    weight = (positions < length).astype(jnp.float32)
    return (
        outer_sum(in_side, gate_side, weight),
        outer_sum(in_side, up_side, weight),
        outer_sum(hidden_side, out_side, weight),
    )


def query_kernel(lengths, sums, found):
    for e in range(found.shape[0]):
        part = slice(e * SEQ, (e + 1) * SEQ)
        gate_side, up_side, hidden_side, in_side, out_side = [
            sums[part, i * RANK : (i + 1) * RANK] for i in range(5)
        ]
        three = example_features(
            in_side, hidden_side, gate_side, up_side, out_side, lengths[e]
        )
        for segment in range(3):
            found[e, segment * RANK : (segment + 1) * RANK, :] = three[segment]


def query_features(lengths, sums):
    return pl.pallas_call(
        query_kernel,
        in_specs=[SCALARS, IN_VMEM],
        out_specs=IN_VMEM,
        out_shape=jax.ShapeDtypeStruct((lengths.shape[0], 3 * RANK, RANK), jnp.float32),
        compiler_params=params(),
    )(lengths, sums)


def score_kernel(
    lengths, place, in_out, hidden, early, near, far, q0, q1, q2, q3, scores
):
    queries = q0.shape[0]
    shape = scores.shape
    row = lax.broadcasted_iota(jnp.int32, shape, 0)
    column = lax.broadcasted_iota(jnp.int32, shape, 1)
    gradient = jnp.concatenate([early[...], (near[...] + far[...]).T], axis=0)
    total = jnp.zeros(shape, jnp.float32)
    for e in range(shape[0]):
        part = slice(e * SEQ, (e + 1) * SEQ)
        three = jnp.concatenate(
            example_features(
                in_out[part, :RANK],
                hidden[part, :],
                gradient[part, :RANK],
                gradient[part, RANK:],
                in_out[part, RANK:],
                lengths[e],
            ),
            axis=0,
        )
        for step, found in enumerate((q0, q1, q2, q3)):
            for j in range(queries):
                value = jnp.sum(three * found[j], keepdims=True)
                here = (row == e) & (
                    column == queries * jnp.bitwise_xor(place[0], step) + j
                )
                total = total + jnp.where(here, value, 0.0)
    scores[...] = total


def partial_scores(lengths, place, in_out, hidden, early, near, far, found):
    number = lengths.shape[0]
    return pl.pallas_call(
        score_kernel,
        in_specs=[SCALARS] * 2 + [IN_VMEM] * 9,
        out_specs=IN_VMEM,
        out_shape=jax.ShapeDtypeStruct((number, 4 * found[0].shape[0]), jnp.float32),
        compiler_params=params(),
    )(lengths, place, in_out, hidden, early, near, far, *found)


def after(value, *others):
    return lax.optimization_barrier((value, *others))[0]


def moving_plan(
    train_input,
    train_gate,
    train_up,
    train_outgrad,
    train_lengths,
    query_input,
    query_gate,
    query_up,
    query_outgrad,
    query_lengths,
    down_weight,
    proj_input,
    proj_outgrad,
    proj_hidden,
    proj_gate,
    proj_up,
):
    t = lax.axis_index("tensor")
    d = lax.axis_index("dp")
    x, core, upper = d // 2, d % 2, t // 2
    at_home = x == upper
    inner_chip = (t == 1) | (t == 2)
    near_code = jnp.where(at_home, 0, jnp.where(inner_chip, 1, 2))
    first_parity = jnp.where(at_home, t % 2, upper)
    near_slot = first_parity ^ core
    far_slot = jnp.where(inner_chip & ~at_home, 1 - near_slot, near_slot)
    flags = jnp.stack([near_code, near_slot, far_slot]).astype(jnp.int32)
    place = jnp.stack([d]).astype(jnp.int32)

    to_core = functools.partial(lax.ppermute, axis_name="dp", perm=[(i, i ^ 1) for i in range(4)])
    to_chip = functools.partial(lax.ppermute, axis_name="dp", perm=[(i, i ^ 2) for i in range(4)])
    to_other = functools.partial(lax.ppermute, axis_name="dp", perm=[(i, i ^ 3) for i in range(4)])
    outer = functools.partial(
        lax.ppermute, axis_name="tensor", perm=[(i, i ^ 1) for i in range(4)]
    )
    across = functools.partial(
        lax.ppermute, axis_name="tensor", perm=[(i, i ^ 2) for i in range(4)]
    )
    opposite = functools.partial(
        lax.ppermute, axis_name="tensor", perm=[(i, 3 - i) for i in range(4)]
    )
    middle = functools.partial(
        lax.ppermute,
        axis_name=("tensor", "dp"),
        perm=[
            (4 * i + j, 4 * (3 - i) + j) if i in (1, 2) else (4 * i + j, 4 * i + (j ^ 1))
            for i in range(4)
            for j in range(4)
        ],
    )

    def tensor_sum(values):
        return values + outer(values) + across(values) + opposite(values)

    def last_hops(own, one, two):
        mid = middle(after(own, two))
        return own, one, mid, two, two, outer(after(two, one))

    def crossing_first(own, two):
        return jnp.where(at_home, two, own)

    def crossing_second(one, mid, last):
        return jnp.where(at_home, jnp.where(inner_chip, mid, last), one)

    q_input, q_gate, q_up, q_outgrad = [
        flatten(a) for a in (query_input, query_gate, query_up, query_outgrad)
    ]
    t_input, t_gate, t_up, t_outgrad = [
        flatten(a) for a in (train_input, train_gate, train_up, train_outgrad)
    ]
    examples = train_lengths.shape[0] // 2
    cut = examples * SEQ

    def first_hops(own):
        return own, outer(own), across(own)

    def last_hops(own, one, two):
        mid = middle(after(own, two))
        return own, one, mid, two, two, outer(after(two, one))

    def crossing_pair(own, one, second_inner, third_inner, second_outer, third_outer):
        def choose(within, beyond_inner, beyond_outer):
            beyond = jnp.where(inner_chip, beyond_inner, beyond_outer)
            return jnp.where(at_home, beyond, within)

        return jnp.stack(
            [choose(own, second_inner, second_outer), choose(one, third_inner, third_outer)]
        )

    def first_hops(own):
        return own, outer(own), across(own)

    weight_own, weight_sib = down_weight, to_core(down_weight)
    q_own, q_one, q_two = first_hops(q_outgrad)
    far_gate = to_chip(t_gate[cut:])
    own_in_out, hidden = early_sides(
        t_input, q_input, t_outgrad, q_outgrad, proj_input, proj_outgrad, t_gate, t_up, q_gate,
        q_up, proj_hidden,
    )
    q_blocks = last_hops(q_own, q_one, after(q_two, own_in_out))
    q_first = to_chip(crossing_first(q_own, q_blocks[3]))
    a_own, a_one, a_two = first_hops(after(t_outgrad[:cut], q_two, far_gate))
    far_up = to_chip(after(t_up[cut:], far_gate, weight_sib))
    q_send = after(crossing_second(q_one, q_blocks[2], q_blocks[5]), far_up)
    q_far = (q_first, to_chip(q_send))

    b_own, b_one, b_two = first_hops(after(t_outgrad[cut:], a_two))
    a_two = after(a_two, q_send)
    a_first = to_chip(crossing_first(a_own, a_two))
    a_blocks = last_hops(a_own, a_one, a_two)
    gates, ups = turned(t_gate, t_up, far_gate, far_up)
    a_send = crossing_second(a_one, a_blocks[2], after(a_blocks[5], *q_far, gates))
    a_far = (a_first, to_chip(a_send))
    q_near_sum, q_far_sum = partial_sums(
        after(flags, a_send), q_blocks, q_far, weight_own, weight_sib
    )
    q_returned = to_chip(after(q_far_sum, *a_far))

    b_two = after(b_two, q_far_sum)
    b_cross = crossing_first(b_own, b_two)
    b_first = to_chip(b_cross)
    b_blocks = last_hops(b_own, b_one, b_two)
    a_near_sum, a_far_sum = partial_sums(
        after(flags, b_cross), a_blocks, a_far, weight_own, weight_sib
    )
    b_send = crossing_second(b_one, b_blocks[2], after(b_blocks[5], a_far_sum))
    b_far = (b_first, to_chip(b_send))
    a_returned = to_chip(after(a_far_sum, *b_far))
    in_out = own_in_out + outer(after(own_in_out, b_send))
    q_gradient = finished_sides(
        q_near_sum, after(q_returned, b_send), q_gate, q_up, proj_gate, proj_up
    )
    pair = jnp.concatenate([q_gradient, hidden[2 * cut :]], axis=1)
    pair = pair + outer(pair)
    b_near, b_away = lent_sides(
        after(flags, pair, in_out), b_blocks, b_far, weight_own, weight_sib, gates, ups,
        proj_gate, proj_up,
    )
    b_far_sides = to_chip(b_away)
    in_out = in_out + after(across(in_out), b_near)
    pair = pair + after(across(pair), b_near)
    own_found = query_features(
        query_lengths, jnp.concatenate([pair, in_out[2 * cut :]], axis=1)
    )
    found = (own_found, to_core(own_found), to_chip(own_found), to_other(own_found))
    a_gradient = finished_sides(
        a_near_sum, after(a_returned, b_far_sides), t_gate, t_up, proj_gate, proj_up
    )
    own_scores = partial_scores(
        train_lengths, place, in_out[: 2 * cut], hidden[: 2 * cut], a_gradient, b_near,
        b_far_sides, found,
    )
    return tensor_sum(own_scores) / (RANK * SEQ)


def solution(mesh):
    tensor, dp = mesh.shape["tensor"], mesh.shape["dp"]

    def per_device(*arguments):
        if tensor == 4 and dp == 4:
            return moving_plan(*arguments)
        return gathering_plan(*arguments)

    in_specs = (
        P(("parts", "dp"), None, "tensor"),
        P(("parts", "dp"), None, "tensor"),
        P(("parts", "dp"), None, "tensor"),
        P(("parts", "dp"), None, "tensor"),
        P(("parts", "dp")),
        P(("parts", "dp"), None, "tensor"),
        P(("parts", "dp"), None, "tensor"),
        P(("parts", "dp"), None, "tensor"),
        P(("parts", "dp"), None, "tensor"),
        P(("parts", "dp")),
        P("tensor", "dp"),
        P(None, "tensor"),
        P(None, "tensor"),
        P(None, "tensor"),
        P(None, "tensor"),
        P(None, "tensor"),
    )
    out_specs = P(("parts", "dp"), None)
    return jax.shard_map(
        per_device, mesh=mesh, in_specs=in_specs, out_specs=out_specs, check_vma=False
    )
```

```python
import functools

import jax
import jax.numpy as jnp
from jax import lax
from jax.experimental import pallas as pl
from jax.experimental.pallas import tpu as pltpu
from jax.sharding import PartitionSpec as P

RANK = 64
SEQ = 64
TILE = 512
WIDE = 1792
VMEM_BYTES = 40 * 1024 * 1024
BIG_VMEM_BYTES = 58 * 1024 * 1024


def flatten(array):
    return array.reshape(-1, array.shape[-1])


def project(rows, table):
    return lax.dot_general(
        rows, table, (((1,), (1,)), ((), ())), preferred_element_type=jnp.float32
    )


def inner(left_side, right_side):
    return lax.dot_general(
        left_side,
        right_side,
        (((1,), (1,)), ((), ())),
        precision=lax.Precision.HIGHEST,
        preferred_element_type=jnp.float32,
    )


def gated_hidden(gate, up):
    gate_wide = gate.astype(jnp.float32)
    up_wide = up.astype(jnp.float32)
    return (gate_wide * jax.nn.sigmoid(gate_wide) * up_wide).astype(jnp.bfloat16)


def gradients(gate, up, hidden_grad):
    gate_wide = gate.astype(jnp.float32)
    up_wide = up.astype(jnp.float32)
    sigmoid_gate = jax.nn.sigmoid(gate_wide)
    silu_gate = gate_wide * sigmoid_gate
    gate_grad = (
        hidden_grad * up_wide * sigmoid_gate * (1.0 + gate_wide * (1.0 - sigmoid_gate))
    ).astype(jnp.bfloat16)
    up_grad = (hidden_grad * silu_gate).astype(jnp.bfloat16)
    return gate_grad, up_grad


def gradient_sides(gate, up, hidden_grad, proj_gate, proj_up):
    gate_grad, up_grad = gradients(gate, up, hidden_grad)
    return project(gate_grad, proj_gate), project(up_grad, proj_up)


def outer_sums(left_side, right_side, lengths):
    number = lengths.shape[0]
    length = left_side.shape[0] // number
    positions = lax.broadcasted_iota(jnp.int32, (number, length), 1)
    weights = (positions < lengths[:, None]).astype(jnp.float32)
    left_rows = left_side.reshape(number, length, left_side.shape[1]) * weights[:, :, None]
    right_rows = right_side.reshape(number, length, right_side.shape[1])
    summed = jnp.einsum("est,esu->etu", left_rows, right_rows, precision=lax.Precision.HIGHEST)
    return summed.reshape(number, -1)


def features(in_side, hidden_side, gate_side, up_side, out_side, lengths):
    return jnp.concatenate(
        [
            outer_sums(in_side, gate_side, lengths),
            outer_sums(in_side, up_side, lengths),
            outer_sums(hidden_side, out_side, lengths),
        ],
        axis=1,
    )


def gathering_plan(
    train_input,
    train_gate,
    train_up,
    train_outgrad,
    train_lengths,
    query_input,
    query_gate,
    query_up,
    query_outgrad,
    query_lengths,
    down_weight,
    proj_input,
    proj_outgrad,
    proj_hidden,
    proj_gate,
    proj_up,
):
    weight = lax.all_gather(down_weight, "dp", axis=1, tiled=True)

    def full_features(inputs, gate, up, outgrad, lengths):
        inputs, gate, up, outgrad = [flatten(a) for a in (inputs, gate, up, outgrad)]
        rows = lax.all_gather(outgrad, "tensor", axis=1, tiled=True)
        gate_side, up_side = gradient_sides(gate, up, project(rows, weight), proj_gate, proj_up)
        hidden_side = project(gated_hidden(gate, up), proj_hidden)
        sides = (
            project(inputs, proj_input),
            hidden_side,
            gate_side,
            up_side,
            project(outgrad, proj_outgrad),
        )
        return features(*lax.psum(sides, "tensor"), lengths)

    train_features = full_features(
        train_input, train_gate, train_up, train_outgrad, train_lengths
    )
    query_features = full_features(
        query_input, query_gate, query_up, query_outgrad, query_lengths
    )
    gathered = lax.all_gather(query_features, "dp", axis=0, tiled=True)
    return inner(train_features, gathered) / (RANK * SEQ)


ANYWHERE = pl.BlockSpec(memory_space=pl.ANY)
SCALARS = pl.BlockSpec(memory_space=pltpu.SMEM)
IN_VMEM = pl.BlockSpec(memory_space=pltpu.VMEM)


def params(limit=VMEM_BYTES):
    return pltpu.CompilerParams(vmem_limit_bytes=limit)


def cost(flops, arrays):
    return pl.CostEstimate(flops=1024, bytes_accessed=1024, transcendentals=0)


def tile_columns(number, block=0, tile=TILE):
    return pl.BlockSpec((number, tile), lambda i: (block, i))


def tile_rows(width, tile=TILE):
    return pl.BlockSpec((tile, width), lambda i: (i, 0))


def whole(shape):
    return pl.BlockSpec(shape, lambda i: tuple(0 for _ in shape))


def stacked_products(
    flags, pairs, far, weight_own, weight_sib, stacked, semaphores, held, weight_sems
):
    number = far[0].shape[0]
    step = pl.program_id(0)
    tiles = weight_own.shape[0] // TILE

    def weight_copies(tile):
        part = pl.ds(pl.multiple_of(tile * TILE, TILE), TILE)
        slot = lax.rem(tile, 3)
        return [
            pltpu.make_async_copy(
                weight.at[part], held.at[slot, side], weight_sems.at[slot, side]
            )
            for side, weight in enumerate((weight_own, weight_sib))
        ]

    def row_copies(pair, slot, row, first):
        return [
            pltpu.make_async_copy(
                pair[i], stacked.at[jnp.bitwise_xor(slot, i), pl.ds(row, number)],
                semaphores.at[first + i],
            )
            for i in range(2)
        ]

    @pl.when(step == 0)
    def _():
        far_copies = row_copies(far, flags[2], number, 2)
        for copy in far_copies:
            copy.start()
        for code, pair in enumerate(pairs):

            @pl.when(flags[0] == code)
            def _():
                copies = row_copies(pair, flags[1], 0, 0)
                for copy in copies:
                    copy.start()
                for tile in range(2):
                    for copy in weight_copies(tile):
                        copy.start()
                for copy in copies:
                    copy.wait()

        for copy in far_copies:
            copy.wait()

    @pl.when(step + 2 < tiles)
    def _():
        for copy in weight_copies(step + 2):
            copy.start()

    for copy in weight_copies(step):
        copy.wait()
    slot = lax.rem(step, 3)
    return project(held[slot, 0], stacked[0]) + project(held[slot, 1], stacked[1])


def add_sides(hidden_grad, gate, up, proj_gate, proj_up, sides):
    gate_part, up_part = gradient_sides(gate, up, hidden_grad, proj_gate, proj_up)
    part = jnp.concatenate([gate_part, up_part], axis=1)
    first = pl.program_id(0) == 0

    @pl.when(first)
    def _():
        sides[...] = part

    @pl.when(jnp.logical_not(first))
    def _():
        sides[...] += part


def partial_kernel(
    flags, b0, b1, b2, b3, b4, b5, far_a, far_b, weight_own, weight_sib, near_sum, far_sum,
    *scratch,
):
    pairs = ((b0, b1), (b2, b3), (b4, b5))
    far = (far_a, far_b)
    total = stacked_products(flags, pairs, far, weight_own, weight_sib, *scratch)
    number = far_a.shape[0]
    near_sum[...] = total[:, :number]
    far_sum[...] = total[:, number:].astype(jnp.bfloat16)


def product_scratch(number, half):
    return [
        pltpu.VMEM((2, 2 * number, half), jnp.bfloat16),
        pltpu.SemaphoreType.DMA((4,)),
        pltpu.VMEM((3, 2, TILE, half), jnp.bfloat16),
        pltpu.SemaphoreType.DMA((3, 2)),
    ]


def partial_sums(flags, blocks, far, weight_own, weight_sib):
    number, half = blocks[0].shape
    units = weight_own.shape[0]
    return pl.pallas_call(
        partial_kernel,
        grid=(units // TILE,),
        in_specs=[SCALARS] + [ANYWHERE] * 10,
        out_specs=[tile_rows(number)] * 2,
        out_shape=[
            jax.ShapeDtypeStruct((units, number), jnp.float32),
            jax.ShapeDtypeStruct((units, number), jnp.bfloat16),
        ],
        scratch_shapes=product_scratch(number, half),
        compiler_params=params(BIG_VMEM_BYTES),
        cost_estimate=cost(8 * number * half * units, (weight_own, weight_sib)),
    )(flags, *blocks, *far, weight_own, weight_sib)


def finish_kernel(near_sum, returned, gate, up, proj_gate, proj_up, sides):
    hidden_grad = (near_sum[...] + returned[...].astype(jnp.float32)).T
    add_sides(hidden_grad, gate[...], up[...], proj_gate[...], proj_up[...], sides)


def finished_sides(near_sum, returned, gate, up, proj_gate, proj_up):
    units, number = near_sum.shape
    return pl.pallas_call(
        finish_kernel,
        grid=(units // WIDE,),
        in_specs=[tile_rows(number, WIDE)] * 2
        + [tile_columns(number, 0, WIDE)] * 2
        + [tile_columns(RANK, 0, WIDE)] * 2,
        out_specs=whole((number, 2 * RANK)),
        out_shape=jax.ShapeDtypeStruct((number, 2 * RANK), jnp.float32),
        compiler_params=params(),
        cost_estimate=cost(4 * number * RANK * units, (near_sum, returned, gate, up)),
    )(near_sum, returned, gate, up, proj_gate, proj_up)


def turn_kernel(gate, up, far_gate, far_up, gates, ups):
    number = gate.shape[0]
    for source, target, part in (
        (gate, gates, slice(0, number)),
        (up, ups, slice(0, number)),
        (far_gate, gates, slice(number, None)),
        (far_up, ups, slice(number, None)),
    ):
        target[:, part] = source[...].astype(jnp.float32).T.astype(jnp.bfloat16)


def turned(gate, up, far_gate, far_up):
    number, units = far_gate.shape
    shape = jax.ShapeDtypeStruct((units, 2 * number), jnp.bfloat16)
    return pl.pallas_call(
        turn_kernel,
        grid=(units // TILE,),
        in_specs=[tile_columns(number, 1)] * 2 + [tile_columns(number)] * 2,
        out_specs=[tile_rows(2 * number)] * 2,
        out_shape=[shape] * 2,
        compiler_params=params(),
        cost_estimate=cost(0, (gate, up)),
    )(gate, up, far_gate, far_up)


def lent_kernel(
    flags, b0, b1, b2, b3, b4, b5, far_a, far_b, weight_own, weight_sib, gates, ups, proj_gate,
    proj_up, near, away, *scratch,
):
    pairs = ((b0, b1), (b2, b3), (b4, b5))
    far = (far_a, far_b)
    hidden_grad = stacked_products(flags, pairs, far, weight_own, weight_sib, *scratch)
    gate_grad, up_grad = gradients(gates[...], ups[...], hidden_grad)
    part = jnp.concatenate(
        [
            jnp.dot(proj_gate[...], gate_grad, preferred_element_type=jnp.float32),
            jnp.dot(proj_up[...], up_grad, preferred_element_type=jnp.float32),
        ],
        axis=0,
    )
    number = near.shape[1]
    first = pl.program_id(0) == 0

    @pl.when(first)
    def _():
        near[...] = part[:, :number]
        away[...] = part[:, number:]

    @pl.when(jnp.logical_not(first))
    def _():
        near[...] += part[:, :number]
        away[...] += part[:, number:]


def lent_sides(flags, blocks, far, weight_own, weight_sib, gates, ups, proj_gate, proj_up):
    number, half = blocks[0].shape
    units = weight_own.shape[0]
    side = jax.ShapeDtypeStruct((2 * RANK, number), jnp.float32)
    return pl.pallas_call(
        lent_kernel,
        grid=(units // TILE,),
        in_specs=[SCALARS]
        + [ANYWHERE] * 10
        + [tile_rows(2 * number)] * 2
        + [tile_columns(RANK)] * 2,
        out_specs=[whole(side.shape)] * 2,
        out_shape=[side] * 2,
        scratch_shapes=product_scratch(number, half),
        compiler_params=params(BIG_VMEM_BYTES),
        cost_estimate=cost(8 * number * half * units, (weight_own, weight_sib)),
    )(flags, *blocks, *far, weight_own, weight_sib, gates, ups, proj_gate, proj_up)


def early_kernel(
    t_input, q_input, t_outgrad, q_outgrad, proj_input, proj_outgrad, t_gate, t_up, q_gate, q_up,
    proj_hidden, in_out, hidden,
):
    number = t_input.shape[0]
    t_hidden = project(gated_hidden(t_gate[...], t_up[...]), proj_hidden[...])
    q_hidden = project(gated_hidden(q_gate[...], q_up[...]), proj_hidden[...])
    first = pl.program_id(0) == 0

    @pl.when(first)
    def _():
        for inputs, outgrad, part in (
            (t_input, t_outgrad, slice(0, number)),
            (q_input, q_outgrad, slice(number, None)),
        ):
            in_out[part, :] = jnp.concatenate(
                [
                    project(inputs[...], proj_input[...]),
                    project(outgrad[...], proj_outgrad[...]),
                ],
                axis=1,
            )
        hidden[:number, :] = t_hidden
        hidden[number:, :] = q_hidden

    @pl.when(jnp.logical_not(first))
    def _():
        hidden[:number, :] += t_hidden
        hidden[number:, :] += q_hidden


def early_sides(
    t_input, q_input, t_outgrad, q_outgrad, proj_input, proj_outgrad, t_gate, t_up, q_gate, q_up,
    proj_hidden,
):
    total, units = t_gate.shape[0] + q_gate.shape[0], t_gate.shape[1]
    wide = (t_input, q_input, t_outgrad, q_outgrad, proj_input, proj_outgrad)
    tiled = (t_gate, t_up, q_gate, q_up, proj_hidden)
    shapes = ((total, 2 * RANK), (total, RANK))
    return pl.pallas_call(
        early_kernel,
        grid=(units // TILE,),
        in_specs=[whole(a.shape) for a in wide] + [tile_columns(a.shape[0]) for a in tiled],
        out_specs=[whole(shape) for shape in shapes],
        out_shape=[jax.ShapeDtypeStruct(shape, jnp.float32) for shape in shapes],
        compiler_params=params(),
        cost_estimate=cost(2 * total * RANK * units, wide + tiled),
    )(*wide, *tiled)


def outer_sum(left_side, right_side, weight):
    return lax.dot_general(
        left_side * weight,
        right_side,
        (((0,), (0,)), ((), ())),
        precision=lax.Precision.HIGHEST,
        preferred_element_type=jnp.float32,
    )


def example_features(in_side, hidden_side, gate_side, up_side, out_side, length):
    positions = lax.broadcasted_iota(jnp.int32, (SEQ, RANK), 0)
    weight = (positions < length).astype(jnp.float32)
    return (
        outer_sum(in_side, gate_side, weight),
        outer_sum(in_side, up_side, weight),
        outer_sum(hidden_side, out_side, weight),
    )


def query_kernel(lengths, sums, found):
    for e in range(found.shape[0]):
        part = slice(e * SEQ, (e + 1) * SEQ)
        gate_side, up_side, hidden_side, in_side, out_side = [
            sums[part, i * RANK : (i + 1) * RANK] for i in range(5)
        ]
        three = example_features(
            in_side, hidden_side, gate_side, up_side, out_side, lengths[e]
        )
        for segment in range(3):
            found[e, segment * RANK : (segment + 1) * RANK, :] = three[segment]


def query_features(lengths, sums):
    return pl.pallas_call(
        query_kernel,
        in_specs=[SCALARS, IN_VMEM],
        out_specs=IN_VMEM,
        out_shape=jax.ShapeDtypeStruct((lengths.shape[0], 3 * RANK, RANK), jnp.float32),
        compiler_params=params(),
    )(lengths, sums)


def score_kernel(
    lengths, place, in_out, hidden, early, near, far, q0, q1, q2, q3, scores
):
    queries = q0.shape[0]
    shape = scores.shape
    row = lax.broadcasted_iota(jnp.int32, shape, 0)
    column = lax.broadcasted_iota(jnp.int32, shape, 1)
    gradient = jnp.concatenate([early[...], (near[...] + far[...]).T], axis=0)
    total = jnp.zeros(shape, jnp.float32)
    for e in range(shape[0]):
        part = slice(e * SEQ, (e + 1) * SEQ)
        three = jnp.concatenate(
            example_features(
                in_out[part, :RANK],
                hidden[part, :],
                gradient[part, :RANK],
                gradient[part, RANK:],
                in_out[part, RANK:],
                lengths[e],
            ),
            axis=0,
        )
        for step, found in enumerate((q0, q1, q2, q3)):
            for j in range(queries):
                value = jnp.sum(three * found[j], keepdims=True)
                here = (row == e) & (
                    column == queries * jnp.bitwise_xor(place[0], step) + j
                )
                total = total + jnp.where(here, value, 0.0)
    scores[...] = total


def partial_scores(lengths, place, in_out, hidden, early, near, far, found):
    number = lengths.shape[0]
    return pl.pallas_call(
        score_kernel,
        in_specs=[SCALARS] * 2 + [IN_VMEM] * 9,
        out_specs=IN_VMEM,
        out_shape=jax.ShapeDtypeStruct((number, 4 * found[0].shape[0]), jnp.float32),
        compiler_params=params(),
    )(lengths, place, in_out, hidden, early, near, far, *found)


def after(value, *others):
    return lax.optimization_barrier((value, *others))[0]


def moving_plan(
    train_input,
    train_gate,
    train_up,
    train_outgrad,
    train_lengths,
    query_input,
    query_gate,
    query_up,
    query_outgrad,
    query_lengths,
    down_weight,
    proj_input,
    proj_outgrad,
    proj_hidden,
    proj_gate,
    proj_up,
):
    t = lax.axis_index("tensor")
    d = lax.axis_index("dp")
    x, core, upper = d // 2, d % 2, t // 2
    at_home = x == upper
    inner_chip = (t == 1) | (t == 2)
    near_code = jnp.where(at_home, 0, jnp.where(inner_chip, 1, 2))
    first_parity = jnp.where(at_home, t % 2, upper)
    near_slot = first_parity ^ core
    far_slot = jnp.where(inner_chip & ~at_home, 1 - near_slot, near_slot)
    flags = jnp.stack([near_code, near_slot, far_slot]).astype(jnp.int32)
    place = jnp.stack([d]).astype(jnp.int32)

    to_core = functools.partial(lax.ppermute, axis_name="dp", perm=[(i, i ^ 1) for i in range(4)])
    to_chip = functools.partial(lax.ppermute, axis_name="dp", perm=[(i, i ^ 2) for i in range(4)])
    to_other = functools.partial(lax.ppermute, axis_name="dp", perm=[(i, i ^ 3) for i in range(4)])
    outer = functools.partial(
        lax.ppermute, axis_name="tensor", perm=[(i, i ^ 1) for i in range(4)]
    )
    across = functools.partial(
        lax.ppermute, axis_name="tensor", perm=[(i, i ^ 2) for i in range(4)]
    )
    opposite = functools.partial(
        lax.ppermute, axis_name="tensor", perm=[(i, 3 - i) for i in range(4)]
    )
    middle = functools.partial(
        lax.ppermute,
        axis_name=("tensor", "dp"),
        perm=[
            (4 * i + j, 4 * (3 - i) + j) if i in (1, 2) else (4 * i + j, 4 * i + (j ^ 1))
            for i in range(4)
            for j in range(4)
        ],
    )

    def tensor_sum(values):
        return values + outer(values) + across(values) + opposite(values)

    def last_hops(own, one, two):
        mid = middle(after(own, two))
        return own, one, mid, two, two, outer(after(two, one))

    def crossing_first(own, two):
        return jnp.where(at_home, two, own)

    def crossing_second(one, mid, last):
        return jnp.where(at_home, jnp.where(inner_chip, mid, last), one)

    q_input, q_gate, q_up, q_outgrad = [
        flatten(a) for a in (query_input, query_gate, query_up, query_outgrad)
    ]
    t_input, t_gate, t_up, t_outgrad = [
        flatten(a) for a in (train_input, train_gate, train_up, train_outgrad)
    ]
    examples = train_lengths.shape[0] // 2
    cut = examples * SEQ

    def first_hops(own):
        return own, outer(own), across(own)

    def last_hops(own, one, two):
        mid = middle(after(own, two))
        return own, one, mid, two, two, outer(after(two, one))

    def crossing_pair(own, one, second_inner, third_inner, second_outer, third_outer):
        def choose(within, beyond_inner, beyond_outer):
            beyond = jnp.where(inner_chip, beyond_inner, beyond_outer)
            return jnp.where(at_home, beyond, within)

        return jnp.stack(
            [choose(own, second_inner, second_outer), choose(one, third_inner, third_outer)]
        )

    def first_hops(own):
        return own, outer(own), across(own)

    weight_own, weight_sib = down_weight, to_core(down_weight)
    q_own, q_one, q_two = first_hops(q_outgrad)
    far_gate = to_chip(t_gate[cut:])
    own_in_out, hidden = early_sides(
        t_input, q_input, t_outgrad, q_outgrad, proj_input, proj_outgrad, t_gate, t_up, q_gate,
        q_up, proj_hidden,
    )
    q_blocks = last_hops(q_own, q_one, after(q_two, own_in_out))
    q_first = to_chip(crossing_first(q_own, q_blocks[3]))
    a_own, a_one, a_two = first_hops(after(t_outgrad[:cut], q_two, far_gate))
    far_up = to_chip(after(t_up[cut:], far_gate, weight_sib))
    q_send = after(crossing_second(q_one, q_blocks[2], q_blocks[5]), far_up)
    q_far = (q_first, to_chip(q_send))

    a_two = after(a_two, q_send)
    a_first = to_chip(crossing_first(a_own, a_two))
    a_blocks = last_hops(a_own, a_one, a_two)
    b_own, b_one, b_two = first_hops(after(t_outgrad[cut:], a_blocks[2], a_blocks[5]))
    gates, ups = turned(t_gate, t_up, far_gate, far_up)
    a_send = crossing_second(a_one, a_blocks[2], after(a_blocks[5], *q_far, gates))
    a_far = (a_first, to_chip(a_send))
    q_near_sum, q_far_sum = partial_sums(
        after(flags, a_send), q_blocks, q_far, weight_own, weight_sib
    )
    q_returned = to_chip(after(q_far_sum, *a_far))

    b_two = after(b_two, q_far_sum)
    b_cross = crossing_first(b_own, b_two)
    b_first = to_chip(b_cross)
    b_blocks = last_hops(b_own, b_one, b_two)
    a_near_sum, a_far_sum = partial_sums(
        after(flags, b_cross), a_blocks, a_far, weight_own, weight_sib
    )
    b_send = crossing_second(b_one, b_blocks[2], after(b_blocks[5], a_far_sum, b_first))
    b_far = (b_first, to_chip(b_send))
    in_out = own_in_out + outer(after(own_in_out, b_send))
    q_gradient = finished_sides(
        q_near_sum, after(q_returned, b_send), q_gate, q_up, proj_gate, proj_up
    )
    pair = jnp.concatenate([q_gradient, hidden[2 * cut :]], axis=1)
    pair = pair + outer(after(pair, in_out, *b_far))
    a_returned = to_chip(after(a_far_sum, pair))
    b_near, b_away = lent_sides(
        after(flags, pair, in_out), b_blocks, b_far, weight_own, weight_sib, gates, ups,
        proj_gate, proj_up,
    )
    b_far_sides = to_chip(b_away)
    in_out = in_out + after(across(in_out), b_near)
    pair = pair + after(across(pair), b_near)
    own_found = query_features(
        query_lengths, jnp.concatenate([pair, in_out[2 * cut :]], axis=1)
    )
    found = (own_found, to_core(own_found), to_chip(own_found), to_other(own_found))
    a_gradient = finished_sides(
        a_near_sum, after(a_returned, b_far_sides), t_gate, t_up, proj_gate, proj_up
    )
    own_scores = partial_scores(
        train_lengths, place, in_out[: 2 * cut], hidden[: 2 * cut], a_gradient, b_near,
        b_far_sides, found,
    )
    return tensor_sum(own_scores) / (RANK * SEQ)


def solution(mesh):
    tensor, dp = mesh.shape["tensor"], mesh.shape["dp"]

    def per_device(*arguments):
        if tensor == 4 and dp == 4:
            return moving_plan(*arguments)
        return gathering_plan(*arguments)

    in_specs = (
        P(("parts", "dp"), None, "tensor"),
        P(("parts", "dp"), None, "tensor"),
        P(("parts", "dp"), None, "tensor"),
        P(("parts", "dp"), None, "tensor"),
        P(("parts", "dp")),
        P(("parts", "dp"), None, "tensor"),
        P(("parts", "dp"), None, "tensor"),
        P(("parts", "dp"), None, "tensor"),
        P(("parts", "dp"), None, "tensor"),
        P(("parts", "dp")),
        P("tensor", "dp"),
        P(None, "tensor"),
        P(None, "tensor"),
        P(None, "tensor"),
        P(None, "tensor"),
        P(None, "tensor"),
    )
    out_specs = P(("parts", "dp"), None)
    return jax.shard_map(
        per_device, mesh=mesh, in_specs=in_specs, out_specs=out_specs, check_vma=False
    )
```

```python
import functools

import jax
import jax.numpy as jnp
from jax import lax
from jax.experimental import pallas as pl
from jax.experimental.pallas import tpu as pltpu
from jax.sharding import PartitionSpec as P

RANK = 64
SEQ = 64
TILE = 512
WIDE = 1792
VMEM_BYTES = 40 * 1024 * 1024
BIG_VMEM_BYTES = 58 * 1024 * 1024


def flatten(array):
    return array.reshape(-1, array.shape[-1])


def project(rows, table):
    return lax.dot_general(
        rows, table, (((1,), (1,)), ((), ())), preferred_element_type=jnp.float32
    )


def inner(left_side, right_side):
    return lax.dot_general(
        left_side,
        right_side,
        (((1,), (1,)), ((), ())),
        precision=lax.Precision.HIGHEST,
        preferred_element_type=jnp.float32,
    )


def gated_hidden(gate, up):
    gate_wide = gate.astype(jnp.float32)
    up_wide = up.astype(jnp.float32)
    return (gate_wide * jax.nn.sigmoid(gate_wide) * up_wide).astype(jnp.bfloat16)


def gradients(gate, up, hidden_grad):
    gate_wide = gate.astype(jnp.float32)
    up_wide = up.astype(jnp.float32)
    sigmoid_gate = jax.nn.sigmoid(gate_wide)
    silu_gate = gate_wide * sigmoid_gate
    gate_grad = (
        hidden_grad * up_wide * sigmoid_gate * (1.0 + gate_wide * (1.0 - sigmoid_gate))
    ).astype(jnp.bfloat16)
    up_grad = (hidden_grad * silu_gate).astype(jnp.bfloat16)
    return gate_grad, up_grad


def gradient_sides(gate, up, hidden_grad, proj_gate, proj_up):
    gate_grad, up_grad = gradients(gate, up, hidden_grad)
    return project(gate_grad, proj_gate), project(up_grad, proj_up)


def outer_sums(left_side, right_side, lengths):
    number = lengths.shape[0]
    length = left_side.shape[0] // number
    positions = lax.broadcasted_iota(jnp.int32, (number, length), 1)
    weights = (positions < lengths[:, None]).astype(jnp.float32)
    left_rows = left_side.reshape(number, length, left_side.shape[1]) * weights[:, :, None]
    right_rows = right_side.reshape(number, length, right_side.shape[1])
    summed = jnp.einsum("est,esu->etu", left_rows, right_rows, precision=lax.Precision.HIGHEST)
    return summed.reshape(number, -1)


def features(in_side, hidden_side, gate_side, up_side, out_side, lengths):
    return jnp.concatenate(
        [
            outer_sums(in_side, gate_side, lengths),
            outer_sums(in_side, up_side, lengths),
            outer_sums(hidden_side, out_side, lengths),
        ],
        axis=1,
    )


def gathering_plan(
    train_input,
    train_gate,
    train_up,
    train_outgrad,
    train_lengths,
    query_input,
    query_gate,
    query_up,
    query_outgrad,
    query_lengths,
    down_weight,
    proj_input,
    proj_outgrad,
    proj_hidden,
    proj_gate,
    proj_up,
):
    weight = lax.all_gather(down_weight, "dp", axis=1, tiled=True)

    def full_features(inputs, gate, up, outgrad, lengths):
        inputs, gate, up, outgrad = [flatten(a) for a in (inputs, gate, up, outgrad)]
        rows = lax.all_gather(outgrad, "tensor", axis=1, tiled=True)
        gate_side, up_side = gradient_sides(gate, up, project(rows, weight), proj_gate, proj_up)
        hidden_side = project(gated_hidden(gate, up), proj_hidden)
        sides = (
            project(inputs, proj_input),
            hidden_side,
            gate_side,
            up_side,
            project(outgrad, proj_outgrad),
        )
        return features(*lax.psum(sides, "tensor"), lengths)

    train_features = full_features(
        train_input, train_gate, train_up, train_outgrad, train_lengths
    )
    query_features = full_features(
        query_input, query_gate, query_up, query_outgrad, query_lengths
    )
    gathered = lax.all_gather(query_features, "dp", axis=0, tiled=True)
    return inner(train_features, gathered) / (RANK * SEQ)


ANYWHERE = pl.BlockSpec(memory_space=pl.ANY)
SCALARS = pl.BlockSpec(memory_space=pltpu.SMEM)
IN_VMEM = pl.BlockSpec(memory_space=pltpu.VMEM)


def params(limit=VMEM_BYTES):
    return pltpu.CompilerParams(vmem_limit_bytes=limit)


def cost(flops, arrays):
    return pl.CostEstimate(flops=1024, bytes_accessed=1024, transcendentals=0)


def tile_columns(number, block=0, tile=TILE):
    return pl.BlockSpec((number, tile), lambda i: (block, i))


def tile_rows(width, tile=TILE):
    return pl.BlockSpec((tile, width), lambda i: (i, 0))


def whole(shape):
    return pl.BlockSpec(shape, lambda i: tuple(0 for _ in shape))


def stacked_products(
    flags, pairs, far, weight_own, weight_sib, stacked, semaphores, held, weight_sems
):
    number = far.shape[1]
    step = pl.program_id(0)
    tiles = weight_own.shape[0] // TILE

    def weight_copies(tile):
        part = pl.ds(pl.multiple_of(tile * TILE, TILE), TILE)
        slot = lax.rem(tile, 3)
        return [
            pltpu.make_async_copy(
                weight.at[part], held.at[slot, side], weight_sems.at[slot, side]
            )
            for side, weight in enumerate((weight_own, weight_sib))
        ]

    @pl.when(step == 0)
    def _():
        slot = flags[1]
        far_copies = [
            pltpu.make_async_copy(
                far.at[i], stacked.at[jnp.bitwise_xor(slot, i), pl.ds(number, number)],
                semaphores.at[2 + i],
            )
            for i in range(2)
        ]
        for copy in far_copies:
            copy.start()
        for code, pair in enumerate(pairs):

            @pl.when(flags[0] == code)
            def _():
                copies = [
                    pltpu.make_async_copy(
                        pair[i], stacked.at[jnp.bitwise_xor(slot, i), pl.ds(0, number)],
                        semaphores.at[i],
                    )
                    for i in range(2)
                ]
                for copy in copies:
                    copy.start()
                for tile in range(2):
                    for copy in weight_copies(tile):
                        copy.start()
                for copy in copies:
                    copy.wait()

        for copy in far_copies:
            copy.wait()

    @pl.when(step + 2 < tiles)
    def _():
        for copy in weight_copies(step + 2):
            copy.start()

    for copy in weight_copies(step):
        copy.wait()
    slot = lax.rem(step, 3)
    return project(held[slot, 0], stacked[0]) + project(held[slot, 1], stacked[1])


def add_sides(hidden_grad, gate, up, proj_gate, proj_up, sides):
    gate_part, up_part = gradient_sides(gate, up, hidden_grad, proj_gate, proj_up)
    part = jnp.concatenate([gate_part, up_part], axis=1)
    first = pl.program_id(0) == 0

    @pl.when(first)
    def _():
        sides[...] = part

    @pl.when(jnp.logical_not(first))
    def _():
        sides[...] += part


def partial_kernel(
    flags, b0, b1, b2, b3, b4, b5, far, weight_own, weight_sib, near_sum, far_sum, *scratch
):
    pairs = ((b0, b1), (b2, b3), (b4, b5))
    total = stacked_products(flags, pairs, far, weight_own, weight_sib, *scratch)
    number = far.shape[1]
    near_sum[...] = total[:, :number]
    far_sum[...] = total[:, number:].astype(jnp.bfloat16)


def partial_sums(flags, blocks, far, weight_own, weight_sib):
    number, half = blocks[0].shape
    units = weight_own.shape[0]
    return pl.pallas_call(
        partial_kernel,
        grid=(units // TILE,),
        in_specs=[SCALARS] + [ANYWHERE] * 9,
        out_specs=[tile_rows(number)] * 2,
        out_shape=[
            jax.ShapeDtypeStruct((units, number), jnp.float32),
            jax.ShapeDtypeStruct((units, number), jnp.bfloat16),
        ],
        scratch_shapes=[
            pltpu.VMEM((2, 2 * number, half), jnp.bfloat16),
            pltpu.SemaphoreType.DMA((4,)),
            pltpu.VMEM((3, 2, TILE, half), jnp.bfloat16),
            pltpu.SemaphoreType.DMA((3, 2)),
        ],
        compiler_params=params(BIG_VMEM_BYTES),
        cost_estimate=cost(8 * number * half * units, (far, weight_own, weight_sib)),
    )(flags, *blocks, far, weight_own, weight_sib)


def finish_kernel(near_sum, returned, gate, up, proj_gate, proj_up, sides):
    hidden_grad = (near_sum[...] + returned[...].astype(jnp.float32)).T
    add_sides(hidden_grad, gate[...], up[...], proj_gate[...], proj_up[...], sides)


def finished_sides(near_sum, returned, gate, up, proj_gate, proj_up):
    units, number = near_sum.shape
    return pl.pallas_call(
        finish_kernel,
        grid=(units // WIDE,),
        in_specs=[tile_rows(number, WIDE)] * 2
        + [tile_columns(number, 0, WIDE)] * 2
        + [tile_columns(RANK, 0, WIDE)] * 2,
        out_specs=whole((number, 2 * RANK)),
        out_shape=jax.ShapeDtypeStruct((number, 2 * RANK), jnp.float32),
        compiler_params=params(),
        cost_estimate=cost(4 * number * RANK * units, (near_sum, returned, gate, up)),
    )(near_sum, returned, gate, up, proj_gate, proj_up)


def turn_kernel(gate, up, far_gate, far_up, gates, ups):
    number = gate.shape[0]
    for source, target, part in (
        (gate, gates, slice(0, number)),
        (up, ups, slice(0, number)),
        (far_gate, gates, slice(number, None)),
        (far_up, ups, slice(number, None)),
    ):
        target[:, part] = source[...].astype(jnp.float32).T.astype(jnp.bfloat16)


def turned(gate, up, far_gate, far_up):
    number, units = far_gate.shape
    shape = jax.ShapeDtypeStruct((units, 2 * number), jnp.bfloat16)
    return pl.pallas_call(
        turn_kernel,
        grid=(units // TILE,),
        in_specs=[tile_columns(number, 1)] * 2 + [tile_columns(number)] * 2,
        out_specs=[tile_rows(2 * number)] * 2,
        out_shape=[shape] * 2,
        compiler_params=params(),
        cost_estimate=cost(0, (gate, up)),
    )(gate, up, far_gate, far_up)


def lent_kernel(
    flags, b0, b1, b2, b3, b4, b5, far, weight_own, weight_sib, gates, ups, proj_gate, proj_up,
    near, away, *scratch,
):
    pairs = ((b0, b1), (b2, b3), (b4, b5))
    hidden_grad = stacked_products(flags, pairs, far, weight_own, weight_sib, *scratch)
    gate_grad, up_grad = gradients(gates[...], ups[...], hidden_grad)
    part = jnp.concatenate(
        [
            jnp.dot(proj_gate[...], gate_grad, preferred_element_type=jnp.float32),
            jnp.dot(proj_up[...], up_grad, preferred_element_type=jnp.float32),
        ],
        axis=0,
    )
    number = near.shape[1]
    first = pl.program_id(0) == 0

    @pl.when(first)
    def _():
        near[...] = part[:, :number]
        away[...] = part[:, number:]

    @pl.when(jnp.logical_not(first))
    def _():
        near[...] += part[:, :number]
        away[...] += part[:, number:]


def lent_sides(flags, blocks, far, weight_own, weight_sib, gates, ups, proj_gate, proj_up):
    number, half = blocks[0].shape
    units = weight_own.shape[0]
    return pl.pallas_call(
        lent_kernel,
        grid=(units // TILE,),
        in_specs=[SCALARS]
        + [ANYWHERE] * 9
        + [tile_rows(2 * number)] * 2
        + [tile_columns(RANK)] * 2,
        out_specs=[whole((2 * RANK, number))] * 2,
        out_shape=[jax.ShapeDtypeStruct((2 * RANK, number), jnp.float32)] * 2,
        scratch_shapes=[
            pltpu.VMEM((2, 2 * number, half), jnp.bfloat16),
            pltpu.SemaphoreType.DMA((4,)),
            pltpu.VMEM((3, 2, TILE, half), jnp.bfloat16),
            pltpu.SemaphoreType.DMA((3, 2)),
        ],
        compiler_params=params(BIG_VMEM_BYTES),
        cost_estimate=cost(8 * number * half * units, (far, weight_own, weight_sib)),
    )(flags, *blocks, far, weight_own, weight_sib, gates, ups, proj_gate, proj_up)


def early_kernel(
    t_input, q_input, t_outgrad, q_outgrad, proj_input, proj_outgrad, t_gate, t_up, q_gate, q_up,
    proj_hidden, in_out, hidden,
):
    number = t_input.shape[0]
    t_hidden = project(gated_hidden(t_gate[...], t_up[...]), proj_hidden[...])
    q_hidden = project(gated_hidden(q_gate[...], q_up[...]), proj_hidden[...])
    first = pl.program_id(0) == 0

    @pl.when(first)
    def _():
        for inputs, outgrad, part in (
            (t_input, t_outgrad, slice(0, number)),
            (q_input, q_outgrad, slice(number, None)),
        ):
            in_out[part, :] = jnp.concatenate(
                [
                    project(inputs[...], proj_input[...]),
                    project(outgrad[...], proj_outgrad[...]),
                ],
                axis=1,
            )
        hidden[:number, :] = t_hidden
        hidden[number:, :] = q_hidden

    @pl.when(jnp.logical_not(first))
    def _():
        hidden[:number, :] += t_hidden
        hidden[number:, :] += q_hidden


def early_sides(
    t_input, q_input, t_outgrad, q_outgrad, proj_input, proj_outgrad, t_gate, t_up, q_gate, q_up,
    proj_hidden,
):
    total, units = t_gate.shape[0] + q_gate.shape[0], t_gate.shape[1]
    wide = (t_input, q_input, t_outgrad, q_outgrad, proj_input, proj_outgrad)
    tiled = (t_gate, t_up, q_gate, q_up, proj_hidden)
    shapes = ((total, 2 * RANK), (total, RANK))
    return pl.pallas_call(
        early_kernel,
        grid=(units // TILE,),
        in_specs=[whole(a.shape) for a in wide] + [tile_columns(a.shape[0]) for a in tiled],
        out_specs=[whole(shape) for shape in shapes],
        out_shape=[jax.ShapeDtypeStruct(shape, jnp.float32) for shape in shapes],
        compiler_params=params(),
        cost_estimate=cost(2 * total * RANK * units, wide + tiled),
    )(*wide, *tiled)


def outer_sum(left_side, right_side, weight):
    return lax.dot_general(
        left_side * weight,
        right_side,
        (((0,), (0,)), ((), ())),
        precision=lax.Precision.HIGHEST,
        preferred_element_type=jnp.float32,
    )


def example_features(in_side, hidden_side, gate_side, up_side, out_side, length):
    positions = lax.broadcasted_iota(jnp.int32, (SEQ, RANK), 0)
    weight = (positions < length).astype(jnp.float32)
    return (
        outer_sum(in_side, gate_side, weight),
        outer_sum(in_side, up_side, weight),
        outer_sum(hidden_side, out_side, weight),
    )


def query_kernel(lengths, in_out, sums, found):
    for e in range(found.shape[0]):
        part = slice(e * SEQ, (e + 1) * SEQ)
        three = example_features(
            in_out[part, :RANK],
            sums[part, 2 * RANK :],
            sums[part, :RANK],
            sums[part, RANK : 2 * RANK],
            in_out[part, RANK:],
            lengths[e],
        )
        for segment in range(3):
            found[e, segment * RANK : (segment + 1) * RANK, :] = three[segment]


def query_features(lengths, in_out, sums):
    return pl.pallas_call(
        query_kernel,
        in_specs=[SCALARS, IN_VMEM, IN_VMEM],
        out_specs=IN_VMEM,
        out_shape=jax.ShapeDtypeStruct((lengths.shape[0], 3 * RANK, RANK), jnp.float32),
        compiler_params=params(),
    )(lengths, in_out, sums)


def score_kernel(
    lengths, place, in_out, hidden, early, near, far, q0, q1, q2, q3, scores
):
    queries = q0.shape[0]
    shape = scores.shape
    row = lax.broadcasted_iota(jnp.int32, shape, 0)
    column = lax.broadcasted_iota(jnp.int32, shape, 1)
    gradient = jnp.concatenate([early[...], (near[...] + far[...]).T], axis=0)
    total = jnp.zeros(shape, jnp.float32)
    for e in range(shape[0]):
        part = slice(e * SEQ, (e + 1) * SEQ)
        three = jnp.concatenate(
            example_features(
                in_out[part, :RANK],
                hidden[part, :],
                gradient[part, :RANK],
                gradient[part, RANK:],
                in_out[part, RANK:],
                lengths[e],
            ),
            axis=0,
        )
        for step, found in enumerate((q0, q1, q2, q3)):
            for j in range(queries):
                value = jnp.sum(three * found[j], keepdims=True)
                here = (row == e) & (
                    column == queries * jnp.bitwise_xor(place[0], step) + j
                )
                total = total + jnp.where(here, value, 0.0)
    scores[...] = total


def partial_scores(lengths, place, in_out, hidden, early, near, far, found):
    number = lengths.shape[0]
    return pl.pallas_call(
        score_kernel,
        in_specs=[SCALARS] * 2 + [IN_VMEM] * 9,
        out_specs=IN_VMEM,
        out_shape=jax.ShapeDtypeStruct((number, 4 * found[0].shape[0]), jnp.float32),
        compiler_params=params(),
    )(lengths, place, in_out, hidden, early, near, far, *found)


def after(value, *others):
    return lax.optimization_barrier((value, *others))[0]


def moving_plan(
    train_input,
    train_gate,
    train_up,
    train_outgrad,
    train_lengths,
    query_input,
    query_gate,
    query_up,
    query_outgrad,
    query_lengths,
    down_weight,
    proj_input,
    proj_outgrad,
    proj_hidden,
    proj_gate,
    proj_up,
):
    t = lax.axis_index("tensor")
    d = lax.axis_index("dp")
    x, core, upper = d // 2, d % 2, t // 2
    at_home = x == upper
    inner_chip = (t == 1) | (t == 2)
    near_code = jnp.where(at_home, 0, jnp.where(inner_chip, 1, 2))
    first_parity = jnp.where(at_home, t % 2, upper)
    flags = jnp.stack([near_code, first_parity ^ core]).astype(jnp.int32)
    place = jnp.stack([d]).astype(jnp.int32)

    to_core = functools.partial(lax.ppermute, axis_name="dp", perm=[(i, i ^ 1) for i in range(4)])
    to_chip = functools.partial(lax.ppermute, axis_name="dp", perm=[(i, i ^ 2) for i in range(4)])
    to_other = functools.partial(lax.ppermute, axis_name="dp", perm=[(i, i ^ 3) for i in range(4)])
    outer = functools.partial(
        lax.ppermute, axis_name="tensor", perm=[(i, i ^ 1) for i in range(4)]
    )
    across = functools.partial(
        lax.ppermute, axis_name="tensor", perm=[(i, i ^ 2) for i in range(4)]
    )
    opposite = functools.partial(
        lax.ppermute, axis_name="tensor", perm=[(i, 3 - i) for i in range(4)]
    )
    middle = functools.partial(
        lax.ppermute,
        axis_name=("tensor", "dp"),
        perm=[
            (4 * i + j, 4 * (3 - i) + j) if i in (1, 2) else (4 * i + j, 4 * i + (j ^ 1))
            for i in range(4)
            for j in range(4)
        ],
    )

    q_input, q_gate, q_up, q_outgrad = [
        flatten(a) for a in (query_input, query_gate, query_up, query_outgrad)
    ]
    t_input, t_gate, t_up, t_outgrad = [
        flatten(a) for a in (train_input, train_gate, train_up, train_outgrad)
    ]
    examples = train_lengths.shape[0] // 2
    cut = examples * SEQ

    def first_hops(own):
        return own, outer(own), across(own)

    def last_hops(own, one, two):
        mid = middle(after(own, two))
        return own, one, mid, two, two, outer(after(two, one))

    def crossing_pair(own, one, second_inner, third_inner, second_outer, third_outer):
        def choose(within, beyond_inner, beyond_outer):
            beyond = jnp.where(inner_chip, beyond_inner, beyond_outer)
            return jnp.where(at_home, beyond, within)

        return jnp.stack(
            [choose(own, second_inner, second_outer), choose(one, third_inner, third_outer)]
        )

    weight_own, weight_sib = down_weight, to_core(down_weight)
    q_hops = first_hops(q_outgrad)
    far_gate = to_chip(t_gate[cut:])
    own_in_out, hidden = early_sides(
        t_input, q_input, t_outgrad, q_outgrad, proj_input, proj_outgrad, t_gate, t_up, q_gate,
        q_up, proj_hidden,
    )

    q_blocks = last_hops(*q_hops[:2], after(q_hops[2], own_in_out))
    a_hops = first_hops(after(t_outgrad[:cut], q_hops[2], far_gate))
    far_up = to_chip(after(t_up[cut:], far_gate))
    q_send = after(crossing_pair(*q_blocks), far_up)
    q_far = to_chip(q_send)
    a_blocks = last_hops(*a_hops[:2], after(a_hops[2], q_send))

    b_hops = first_hops(after(t_outgrad[cut:], a_hops[2]))
    gates, ups = turned(t_gate, t_up, far_gate, far_up)
    a_send = crossing_pair(*a_blocks[:5], after(a_blocks[5], q_far, gates))
    a_far = to_chip(a_send)
    q_near_sum, q_far_sum = partial_sums(
        flags, q_blocks, after(q_far, a_send), weight_own, weight_sib
    )
    q_returned = to_chip(after(q_far_sum, a_far))
    b_blocks = last_hops(*b_hops[:2], after(b_hops[2], q_far_sum))
    a_near_sum, a_far_sum = partial_sums(flags, a_blocks, a_far, weight_own, weight_sib)
    b_send = crossing_pair(*b_blocks[:5], after(b_blocks[5], a_far_sum))
    b_far = to_chip(b_send)
    in_out = own_in_out + outer(after(own_in_out, b_send))
    q_gradient = finished_sides(
        q_near_sum, after(q_returned, b_send), q_gate, q_up, proj_gate, proj_up
    )
    q_sums = jnp.concatenate([after(q_gradient, in_out), hidden[2 * cut :]], axis=1)
    q_sums = q_sums + outer(q_sums)
    in_out = in_out + across(in_out)
    q_sums = q_sums + across(q_sums)
    own_found = query_features(query_lengths, in_out[2 * cut :], q_sums)
    found = (own_found, to_core(own_found), to_chip(own_found), to_other(own_found))
    a_returned = to_chip(after(a_far_sum, b_far, *found))
    b_near, b_away = lent_sides(
        flags, b_blocks, b_far, weight_own, weight_sib, gates, ups, proj_gate, proj_up
    )
    a_gradient = finished_sides(a_near_sum, a_returned, t_gate, t_up, proj_gate, proj_up)
    own_scores = partial_scores(
        train_lengths, place, in_out[: 2 * cut], hidden[: 2 * cut], a_gradient, b_near,
        to_chip(b_away), found,
    )
    scores = own_scores + outer(own_scores) + across(own_scores) + opposite(own_scores)
    return scores / (RANK * SEQ)


def solution(mesh):
    tensor, dp = mesh.shape["tensor"], mesh.shape["dp"]

    def per_device(*arguments):
        if tensor == 4 and dp == 4:
            return moving_plan(*arguments)
        return gathering_plan(*arguments)

    in_specs = (
        P(("parts", "dp"), None, "tensor"),
        P(("parts", "dp"), None, "tensor"),
        P(("parts", "dp"), None, "tensor"),
        P(("parts", "dp"), None, "tensor"),
        P(("parts", "dp")),
        P(("parts", "dp"), None, "tensor"),
        P(("parts", "dp"), None, "tensor"),
        P(("parts", "dp"), None, "tensor"),
        P(("parts", "dp"), None, "tensor"),
        P(("parts", "dp")),
        P("tensor", "dp"),
        P(None, "tensor"),
        P(None, "tensor"),
        P(None, "tensor"),
        P(None, "tensor"),
        P(None, "tensor"),
    )
    out_specs = P(("parts", "dp"), None)
    return jax.shard_map(
        per_device, mesh=mesh, in_specs=in_specs, out_specs=out_specs, check_vma=False
    )
```

```python
import functools

import jax
import jax.numpy as jnp
from jax import lax
from jax.experimental import pallas as pl
from jax.experimental.pallas import tpu as pltpu
from jax.sharding import PartitionSpec as P

RANK = 64
SEQ = 64
TILE = 512
WIDE = 1792
VMEM_BYTES = 40 * 1024 * 1024
BIG_VMEM_BYTES = 58 * 1024 * 1024


def flatten(array):
    return array.reshape(-1, array.shape[-1])


def project(rows, table):
    return lax.dot_general(
        rows, table, (((1,), (1,)), ((), ())), preferred_element_type=jnp.float32
    )


def inner(left_side, right_side):
    return lax.dot_general(
        left_side,
        right_side,
        (((1,), (1,)), ((), ())),
        precision=lax.Precision.HIGHEST,
        preferred_element_type=jnp.float32,
    )


def gated_hidden(gate, up):
    gate_wide = gate.astype(jnp.float32)
    up_wide = up.astype(jnp.float32)
    return (gate_wide * jax.nn.sigmoid(gate_wide) * up_wide).astype(jnp.bfloat16)


def gradients(gate, up, hidden_grad):
    gate_wide = gate.astype(jnp.float32)
    up_wide = up.astype(jnp.float32)
    sigmoid_gate = jax.nn.sigmoid(gate_wide)
    silu_gate = gate_wide * sigmoid_gate
    gate_grad = (
        hidden_grad * up_wide * sigmoid_gate * (1.0 + gate_wide * (1.0 - sigmoid_gate))
    ).astype(jnp.bfloat16)
    up_grad = (hidden_grad * silu_gate).astype(jnp.bfloat16)
    return gate_grad, up_grad


def gradient_sides(gate, up, hidden_grad, proj_gate, proj_up):
    gate_grad, up_grad = gradients(gate, up, hidden_grad)
    return project(gate_grad, proj_gate), project(up_grad, proj_up)


def outer_sums(left_side, right_side, lengths):
    number = lengths.shape[0]
    length = left_side.shape[0] // number
    positions = lax.broadcasted_iota(jnp.int32, (number, length), 1)
    weights = (positions < lengths[:, None]).astype(jnp.float32)
    left_rows = left_side.reshape(number, length, left_side.shape[1]) * weights[:, :, None]
    right_rows = right_side.reshape(number, length, right_side.shape[1])
    summed = jnp.einsum("est,esu->etu", left_rows, right_rows, precision=lax.Precision.HIGHEST)
    return summed.reshape(number, -1)


def features(in_side, hidden_side, gate_side, up_side, out_side, lengths):
    return jnp.concatenate(
        [
            outer_sums(in_side, gate_side, lengths),
            outer_sums(in_side, up_side, lengths),
            outer_sums(hidden_side, out_side, lengths),
        ],
        axis=1,
    )


def gathering_plan(
    train_input,
    train_gate,
    train_up,
    train_outgrad,
    train_lengths,
    query_input,
    query_gate,
    query_up,
    query_outgrad,
    query_lengths,
    down_weight,
    proj_input,
    proj_outgrad,
    proj_hidden,
    proj_gate,
    proj_up,
):
    weight = lax.all_gather(down_weight, "dp", axis=1, tiled=True)

    def full_features(inputs, gate, up, outgrad, lengths):
        inputs, gate, up, outgrad = [flatten(a) for a in (inputs, gate, up, outgrad)]
        rows = lax.all_gather(outgrad, "tensor", axis=1, tiled=True)
        gate_side, up_side = gradient_sides(gate, up, project(rows, weight), proj_gate, proj_up)
        hidden_side = project(gated_hidden(gate, up), proj_hidden)
        sides = (
            project(inputs, proj_input),
            hidden_side,
            gate_side,
            up_side,
            project(outgrad, proj_outgrad),
        )
        return features(*lax.psum(sides, "tensor"), lengths)

    train_features = full_features(
        train_input, train_gate, train_up, train_outgrad, train_lengths
    )
    query_features = full_features(
        query_input, query_gate, query_up, query_outgrad, query_lengths
    )
    gathered = lax.all_gather(query_features, "dp", axis=0, tiled=True)
    return inner(train_features, gathered) / (RANK * SEQ)


ANYWHERE = pl.BlockSpec(memory_space=pl.ANY)
SCALARS = pl.BlockSpec(memory_space=pltpu.SMEM)
IN_VMEM = pl.BlockSpec(memory_space=pltpu.VMEM)


def params(limit=VMEM_BYTES):
    return pltpu.CompilerParams(vmem_limit_bytes=limit)


def cost(flops, arrays):
    return pl.CostEstimate(flops=1024, bytes_accessed=1024, transcendentals=0)


def tile_columns(number, block=0, tile=TILE):
    return pl.BlockSpec((number, tile), lambda i: (block, i))


def tile_rows(width, tile=TILE):
    return pl.BlockSpec((tile, width), lambda i: (i, 0))


def whole(shape):
    return pl.BlockSpec(shape, lambda i: tuple(0 for _ in shape))


def stacked_products(
    flags, pairs, far, weight_own, weight_sib, stacked, semaphores, held, weight_sems
):
    number = far.shape[1]
    step = pl.program_id(0)
    tiles = weight_own.shape[0] // TILE

    def weight_copies(tile):
        part = pl.ds(pl.multiple_of(tile * TILE, TILE), TILE)
        slot = lax.rem(tile, 3)
        return [
            pltpu.make_async_copy(
                weight.at[part], held.at[slot, side], weight_sems.at[slot, side]
            )
            for side, weight in enumerate((weight_own, weight_sib))
        ]

    @pl.when(step == 0)
    def _():
        slot = flags[1]
        far_copies = [
            pltpu.make_async_copy(
                far.at[i], stacked.at[jnp.bitwise_xor(slot, i), pl.ds(number, number)],
                semaphores.at[2 + i],
            )
            for i in range(2)
        ]
        for copy in far_copies:
            copy.start()
        for code, pair in enumerate(pairs):

            @pl.when(flags[0] == code)
            def _():
                copies = [
                    pltpu.make_async_copy(
                        pair[i], stacked.at[jnp.bitwise_xor(slot, i), pl.ds(0, number)],
                        semaphores.at[i],
                    )
                    for i in range(2)
                ]
                for copy in copies:
                    copy.start()
                for tile in range(2):
                    for copy in weight_copies(tile):
                        copy.start()
                for copy in copies:
                    copy.wait()

        for copy in far_copies:
            copy.wait()

    @pl.when(step + 2 < tiles)
    def _():
        for copy in weight_copies(step + 2):
            copy.start()

    for copy in weight_copies(step):
        copy.wait()
    slot = lax.rem(step, 3)
    return project(held[slot, 0], stacked[0]) + project(held[slot, 1], stacked[1])


def add_sides(hidden_grad, gate, up, proj_gate, proj_up, sides):
    gate_part, up_part = gradient_sides(gate, up, hidden_grad, proj_gate, proj_up)
    part = jnp.concatenate([gate_part, up_part], axis=1)
    first = pl.program_id(0) == 0

    @pl.when(first)
    def _():
        sides[...] = part

    @pl.when(jnp.logical_not(first))
    def _():
        sides[...] += part


def partial_kernel(
    flags, b0, b1, b2, b3, b4, b5, far, weight_own, weight_sib, near_sum, far_sum, *scratch
):
    pairs = ((b0, b1), (b2, b3), (b4, b5))
    total = stacked_products(flags, pairs, far, weight_own, weight_sib, *scratch)
    number = far.shape[1]
    near_sum[...] = total[:, :number]
    far_sum[...] = total[:, number:].astype(jnp.bfloat16)


def partial_sums(flags, blocks, far, weight_own, weight_sib):
    number, half = blocks[0].shape
    units = weight_own.shape[0]
    return pl.pallas_call(
        partial_kernel,
        grid=(units // TILE,),
        in_specs=[SCALARS] + [ANYWHERE] * 9,
        out_specs=[tile_rows(number)] * 2,
        out_shape=[
            jax.ShapeDtypeStruct((units, number), jnp.float32),
            jax.ShapeDtypeStruct((units, number), jnp.bfloat16),
        ],
        scratch_shapes=[
            pltpu.VMEM((2, 2 * number, half), jnp.bfloat16),
            pltpu.SemaphoreType.DMA((4,)),
            pltpu.VMEM((3, 2, TILE, half), jnp.bfloat16),
            pltpu.SemaphoreType.DMA((3, 2)),
        ],
        compiler_params=params(BIG_VMEM_BYTES),
        cost_estimate=cost(8 * number * half * units, (far, weight_own, weight_sib)),
    )(flags, *blocks, far, weight_own, weight_sib)


def finish_kernel(near_sum, returned, gate, up, proj_gate, proj_up, sides):
    hidden_grad = (near_sum[...] + returned[...].astype(jnp.float32)).T
    add_sides(hidden_grad, gate[...], up[...], proj_gate[...], proj_up[...], sides)


def finished_sides(near_sum, returned, gate, up, proj_gate, proj_up):
    units, number = near_sum.shape
    return pl.pallas_call(
        finish_kernel,
        grid=(units // WIDE,),
        in_specs=[tile_rows(number, WIDE)] * 2
        + [tile_columns(number, 0, WIDE)] * 2
        + [tile_columns(RANK, 0, WIDE)] * 2,
        out_specs=whole((number, 2 * RANK)),
        out_shape=jax.ShapeDtypeStruct((number, 2 * RANK), jnp.float32),
        compiler_params=params(),
        cost_estimate=cost(4 * number * RANK * units, (near_sum, returned, gate, up)),
    )(near_sum, returned, gate, up, proj_gate, proj_up)


def turn_kernel(gate, up, far_gate, far_up, gates, ups):
    number = gate.shape[0]
    for source, target, part in (
        (gate, gates, slice(0, number)),
        (up, ups, slice(0, number)),
        (far_gate, gates, slice(number, None)),
        (far_up, ups, slice(number, None)),
    ):
        target[:, part] = source[...].astype(jnp.float32).T.astype(jnp.bfloat16)


def turned(gate, up, far_gate, far_up):
    number, units = far_gate.shape
    shape = jax.ShapeDtypeStruct((units, 2 * number), jnp.bfloat16)
    return pl.pallas_call(
        turn_kernel,
        grid=(units // TILE,),
        in_specs=[tile_columns(number, 1)] * 2 + [tile_columns(number)] * 2,
        out_specs=[tile_rows(2 * number)] * 2,
        out_shape=[shape] * 2,
        compiler_params=params(),
        cost_estimate=cost(0, (gate, up)),
    )(gate, up, far_gate, far_up)


def lent_kernel(
    flags, b0, b1, b2, b3, b4, b5, far, weight_own, weight_sib, gates, ups, proj_gate, proj_up,
    near, away, *scratch,
):
    pairs = ((b0, b1), (b2, b3), (b4, b5))
    hidden_grad = stacked_products(flags, pairs, far, weight_own, weight_sib, *scratch)
    gate_grad, up_grad = gradients(gates[...], ups[...], hidden_grad)
    part = jnp.concatenate(
        [
            jnp.dot(proj_gate[...], gate_grad, preferred_element_type=jnp.float32),
            jnp.dot(proj_up[...], up_grad, preferred_element_type=jnp.float32),
        ],
        axis=0,
    )
    number = near.shape[1]
    first = pl.program_id(0) == 0

    @pl.when(first)
    def _():
        near[...] = part[:, :number]
        away[...] = part[:, number:]

    @pl.when(jnp.logical_not(first))
    def _():
        near[...] += part[:, :number]
        away[...] += part[:, number:]


def lent_sides(flags, blocks, far, weight_own, weight_sib, gates, ups, proj_gate, proj_up):
    number, half = blocks[0].shape
    units = weight_own.shape[0]
    return pl.pallas_call(
        lent_kernel,
        grid=(units // TILE,),
        in_specs=[SCALARS]
        + [ANYWHERE] * 9
        + [tile_rows(2 * number)] * 2
        + [tile_columns(RANK)] * 2,
        out_specs=[whole((2 * RANK, number))] * 2,
        out_shape=[jax.ShapeDtypeStruct((2 * RANK, number), jnp.float32)] * 2,
        scratch_shapes=[
            pltpu.VMEM((2, 2 * number, half), jnp.bfloat16),
            pltpu.SemaphoreType.DMA((4,)),
            pltpu.VMEM((3, 2, TILE, half), jnp.bfloat16),
            pltpu.SemaphoreType.DMA((3, 2)),
        ],
        compiler_params=params(BIG_VMEM_BYTES),
        cost_estimate=cost(8 * number * half * units, (far, weight_own, weight_sib)),
    )(flags, *blocks, far, weight_own, weight_sib, gates, ups, proj_gate, proj_up)


def early_kernel(
    t_input, q_input, t_outgrad, q_outgrad, proj_input, proj_outgrad, t_gate, t_up, q_gate, q_up,
    proj_hidden, in_out, hidden,
):
    number = t_input.shape[0]
    t_hidden = project(gated_hidden(t_gate[...], t_up[...]), proj_hidden[...])
    q_hidden = project(gated_hidden(q_gate[...], q_up[...]), proj_hidden[...])
    first = pl.program_id(0) == 0

    @pl.when(first)
    def _():
        for inputs, outgrad, part in (
            (t_input, t_outgrad, slice(0, number)),
            (q_input, q_outgrad, slice(number, None)),
        ):
            in_out[part, :] = jnp.concatenate(
                [
                    project(inputs[...], proj_input[...]),
                    project(outgrad[...], proj_outgrad[...]),
                ],
                axis=1,
            )
        hidden[:number, :] = t_hidden
        hidden[number:, :] = q_hidden

    @pl.when(jnp.logical_not(first))
    def _():
        hidden[:number, :] += t_hidden
        hidden[number:, :] += q_hidden


def early_sides(
    t_input, q_input, t_outgrad, q_outgrad, proj_input, proj_outgrad, t_gate, t_up, q_gate, q_up,
    proj_hidden,
):
    total, units = t_gate.shape[0] + q_gate.shape[0], t_gate.shape[1]
    wide = (t_input, q_input, t_outgrad, q_outgrad, proj_input, proj_outgrad)
    tiled = (t_gate, t_up, q_gate, q_up, proj_hidden)
    shapes = ((total, 2 * RANK), (total, RANK))
    return pl.pallas_call(
        early_kernel,
        grid=(units // TILE,),
        in_specs=[whole(a.shape) for a in wide] + [tile_columns(a.shape[0]) for a in tiled],
        out_specs=[whole(shape) for shape in shapes],
        out_shape=[jax.ShapeDtypeStruct(shape, jnp.float32) for shape in shapes],
        compiler_params=params(),
        cost_estimate=cost(2 * total * RANK * units, wide + tiled),
    )(*wide, *tiled)


def outer_sum(left_side, right_side, weight):
    return lax.dot_general(
        left_side * weight,
        right_side,
        (((0,), (0,)), ((), ())),
        precision=lax.Precision.HIGHEST,
        preferred_element_type=jnp.float32,
    )


def example_features(in_side, hidden_side, gate_side, up_side, out_side, length):
    positions = lax.broadcasted_iota(jnp.int32, (SEQ, RANK), 0)
    weight = (positions < length).astype(jnp.float32)
    return (
        outer_sum(in_side, gate_side, weight),
        outer_sum(in_side, up_side, weight),
        outer_sum(hidden_side, out_side, weight),
    )


def query_kernel(lengths, in_out, sums, found):
    for e in range(found.shape[0]):
        part = slice(e * SEQ, (e + 1) * SEQ)
        three = example_features(
            in_out[part, :RANK],
            sums[part, 2 * RANK :],
            sums[part, :RANK],
            sums[part, RANK : 2 * RANK],
            in_out[part, RANK:],
            lengths[e],
        )
        for segment in range(3):
            found[e, segment * RANK : (segment + 1) * RANK, :] = three[segment]


def query_features(lengths, in_out, sums):
    return pl.pallas_call(
        query_kernel,
        in_specs=[SCALARS, IN_VMEM, IN_VMEM],
        out_specs=IN_VMEM,
        out_shape=jax.ShapeDtypeStruct((lengths.shape[0], 3 * RANK, RANK), jnp.float32),
        compiler_params=params(),
    )(lengths, in_out, sums)


def score_kernel(
    lengths, place, in_out, hidden, early, near, far, q0, q1, q2, q3, scores
):
    queries = q0.shape[0]
    shape = scores.shape
    row = lax.broadcasted_iota(jnp.int32, shape, 0)
    column = lax.broadcasted_iota(jnp.int32, shape, 1)
    gradient = jnp.concatenate([early[...], (near[...] + far[...]).T], axis=0)
    total = jnp.zeros(shape, jnp.float32)
    for e in range(shape[0]):
        part = slice(e * SEQ, (e + 1) * SEQ)
        three = jnp.concatenate(
            example_features(
                in_out[part, :RANK],
                hidden[part, :],
                gradient[part, :RANK],
                gradient[part, RANK:],
                in_out[part, RANK:],
                lengths[e],
            ),
            axis=0,
        )
        for step, found in enumerate((q0, q1, q2, q3)):
            for j in range(queries):
                value = jnp.sum(three * found[j], keepdims=True)
                here = (row == e) & (
                    column == queries * jnp.bitwise_xor(place[0], step) + j
                )
                total = total + jnp.where(here, value, 0.0)
    scores[...] = total


def partial_scores(lengths, place, in_out, hidden, early, near, far, found):
    number = lengths.shape[0]
    return pl.pallas_call(
        score_kernel,
        in_specs=[SCALARS] * 2 + [IN_VMEM] * 9,
        out_specs=IN_VMEM,
        out_shape=jax.ShapeDtypeStruct((number, 4 * found[0].shape[0]), jnp.float32),
        compiler_params=params(),
    )(lengths, place, in_out, hidden, early, near, far, *found)


def after(value, *others):
    return lax.optimization_barrier((value, *others))[0]


def moving_plan(
    train_input,
    train_gate,
    train_up,
    train_outgrad,
    train_lengths,
    query_input,
    query_gate,
    query_up,
    query_outgrad,
    query_lengths,
    down_weight,
    proj_input,
    proj_outgrad,
    proj_hidden,
    proj_gate,
    proj_up,
):
    t = lax.axis_index("tensor")
    d = lax.axis_index("dp")
    x, core, upper = d // 2, d % 2, t // 2
    at_home = x == upper
    inner_chip = (t == 1) | (t == 2)
    near_code = jnp.where(at_home, 0, jnp.where(inner_chip, 1, 2))
    first_parity = jnp.where(at_home, t % 2, upper)
    flags = jnp.stack([near_code, first_parity ^ core]).astype(jnp.int32)
    place = jnp.stack([d]).astype(jnp.int32)

    to_core = functools.partial(lax.ppermute, axis_name="dp", perm=[(i, i ^ 1) for i in range(4)])
    to_chip = functools.partial(lax.ppermute, axis_name="dp", perm=[(i, i ^ 2) for i in range(4)])
    to_other = functools.partial(lax.ppermute, axis_name="dp", perm=[(i, i ^ 3) for i in range(4)])
    outer = functools.partial(
        lax.ppermute, axis_name="tensor", perm=[(i, i ^ 1) for i in range(4)]
    )
    across = functools.partial(
        lax.ppermute, axis_name="tensor", perm=[(i, i ^ 2) for i in range(4)]
    )
    opposite = functools.partial(
        lax.ppermute, axis_name="tensor", perm=[(i, 3 - i) for i in range(4)]
    )
    middle = functools.partial(
        lax.ppermute,
        axis_name=("tensor", "dp"),
        perm=[
            (4 * i + j, 4 * (3 - i) + j) if i in (1, 2) else (4 * i + j, 4 * i + (j ^ 1))
            for i in range(4)
            for j in range(4)
        ],
    )

    q_input, q_gate, q_up, q_outgrad = [
        flatten(a) for a in (query_input, query_gate, query_up, query_outgrad)
    ]
    t_input, t_gate, t_up, t_outgrad = [
        flatten(a) for a in (train_input, train_gate, train_up, train_outgrad)
    ]
    examples = train_lengths.shape[0] // 2
    cut = examples * SEQ

    def first_hops(own):
        return own, outer(own), across(own)

    def last_hops(own, one, two):
        mid = middle(after(own, two))
        return own, one, mid, two, two, outer(after(two, one))

    def crossing_pair(own, one, second_inner, third_inner, second_outer, third_outer):
        def choose(within, beyond_inner, beyond_outer):
            beyond = jnp.where(inner_chip, beyond_inner, beyond_outer)
            return jnp.where(at_home, beyond, within)

        return jnp.stack(
            [choose(own, second_inner, second_outer), choose(one, third_inner, third_outer)]
        )

    weight_own, weight_sib = down_weight, to_core(down_weight)
    q_hops = first_hops(q_outgrad)
    far_gate = to_chip(t_gate[cut:])
    own_in_out, hidden = early_sides(
        t_input, q_input, t_outgrad, q_outgrad, proj_input, proj_outgrad, t_gate, t_up, q_gate,
        q_up, proj_hidden,
    )

    q_blocks = last_hops(*q_hops[:2], after(q_hops[2], own_in_out))
    a_hops = first_hops(after(t_outgrad[:cut], q_hops[2], far_gate))
    far_up = to_chip(after(t_up[cut:], far_gate))
    q_send = after(crossing_pair(*q_blocks), far_up)
    q_far = to_chip(q_send)
    a_blocks = last_hops(*a_hops[:2], after(a_hops[2], q_send))

    b_hops = first_hops(after(t_outgrad[cut:], a_blocks[2], a_blocks[5]))
    gates, ups = turned(t_gate, t_up, far_gate, far_up)
    a_send = crossing_pair(*a_blocks[:5], after(a_blocks[5], q_far, gates))
    a_far = to_chip(a_send)
    q_near_sum, q_far_sum = partial_sums(
        flags, q_blocks, after(q_far, a_send), weight_own, weight_sib
    )
    q_returned = to_chip(after(q_far_sum, a_far))
    b_blocks = last_hops(*b_hops[:2], after(b_hops[2], q_far_sum))
    b_send = crossing_pair(*b_blocks)
    b_far = to_chip(b_send)
    a_near_sum, a_far_sum = partial_sums(
        flags, a_blocks, after(a_far, b_send), weight_own, weight_sib
    )
    a_returned = to_chip(a_far_sum)
    in_out = own_in_out + outer(after(own_in_out, b_send))
    q_gradient = finished_sides(
        q_near_sum, after(q_returned, a_far_sum), q_gate, q_up, proj_gate, proj_up
    )
    q_sums = jnp.concatenate([q_gradient, hidden[2 * cut :]], axis=1)
    q_sums = q_sums + outer(q_sums)
    b_near, b_away = lent_sides(
        after(flags, q_sums, in_out), b_blocks, b_far, weight_own, weight_sib, gates, ups,
        proj_gate, proj_up,
    )
    in_out = in_out + across(after(in_out, b_near))
    q_sums = q_sums + across(after(q_sums, b_near))
    own_found = query_features(query_lengths, in_out[2 * cut :], q_sums)
    found = (own_found, to_core(own_found), to_chip(own_found), to_other(own_found))
    a_gradient = finished_sides(a_near_sum, a_returned, t_gate, t_up, proj_gate, proj_up)
    own_scores = partial_scores(
        train_lengths, place, in_out[: 2 * cut], hidden[: 2 * cut], a_gradient, b_near,
        to_chip(b_away), found,
    )
    scores = own_scores + outer(own_scores) + across(own_scores) + opposite(own_scores)
    return scores / (RANK * SEQ)


def solution(mesh):
    tensor, dp = mesh.shape["tensor"], mesh.shape["dp"]

    def per_device(*arguments):
        if tensor == 4 and dp == 4:
            return moving_plan(*arguments)
        return gathering_plan(*arguments)

    in_specs = (
        P(("parts", "dp"), None, "tensor"),
        P(("parts", "dp"), None, "tensor"),
        P(("parts", "dp"), None, "tensor"),
        P(("parts", "dp"), None, "tensor"),
        P(("parts", "dp")),
        P(("parts", "dp"), None, "tensor"),
        P(("parts", "dp"), None, "tensor"),
        P(("parts", "dp"), None, "tensor"),
        P(("parts", "dp"), None, "tensor"),
        P(("parts", "dp")),
        P("tensor", "dp"),
        P(None, "tensor"),
        P(None, "tensor"),
        P(None, "tensor"),
        P(None, "tensor"),
        P(None, "tensor"),
    )
    out_specs = P(("parts", "dp"), None)
    return jax.shard_map(
        per_device, mesh=mesh, in_specs=in_specs, out_specs=out_specs, check_vma=False
    )
```

```python
import functools

import jax
import jax.numpy as jnp
from jax import lax
from jax.experimental import pallas as pl
from jax.experimental.pallas import tpu as pltpu
from jax.sharding import PartitionSpec as P

RANK = 64
SEQ = 64
TILE = 512
WIDE = 1792
VMEM_BYTES = 40 * 1024 * 1024
BIG_VMEM_BYTES = 58 * 1024 * 1024


def flatten(array):
    return array.reshape(-1, array.shape[-1])


def project(rows, table):
    return lax.dot_general(
        rows, table, (((1,), (1,)), ((), ())), preferred_element_type=jnp.float32
    )


def inner(left_side, right_side):
    return lax.dot_general(
        left_side,
        right_side,
        (((1,), (1,)), ((), ())),
        precision=lax.Precision.HIGHEST,
        preferred_element_type=jnp.float32,
    )


def gated_hidden(gate, up):
    gate_wide = gate.astype(jnp.float32)
    up_wide = up.astype(jnp.float32)
    return (gate_wide * jax.nn.sigmoid(gate_wide) * up_wide).astype(jnp.bfloat16)


def gradients(gate, up, hidden_grad):
    gate_wide = gate.astype(jnp.float32)
    up_wide = up.astype(jnp.float32)
    sigmoid_gate = jax.nn.sigmoid(gate_wide)
    silu_gate = gate_wide * sigmoid_gate
    gate_grad = (
        hidden_grad * up_wide * sigmoid_gate * (1.0 + gate_wide * (1.0 - sigmoid_gate))
    ).astype(jnp.bfloat16)
    up_grad = (hidden_grad * silu_gate).astype(jnp.bfloat16)
    return gate_grad, up_grad


def gradient_sides(gate, up, hidden_grad, proj_gate, proj_up):
    gate_grad, up_grad = gradients(gate, up, hidden_grad)
    return project(gate_grad, proj_gate), project(up_grad, proj_up)


def outer_sums(left_side, right_side, lengths):
    number = lengths.shape[0]
    length = left_side.shape[0] // number
    positions = lax.broadcasted_iota(jnp.int32, (number, length), 1)
    weights = (positions < lengths[:, None]).astype(jnp.float32)
    left_rows = left_side.reshape(number, length, left_side.shape[1]) * weights[:, :, None]
    right_rows = right_side.reshape(number, length, right_side.shape[1])
    summed = jnp.einsum("est,esu->etu", left_rows, right_rows, precision=lax.Precision.HIGHEST)
    return summed.reshape(number, -1)


def features(in_side, hidden_side, gate_side, up_side, out_side, lengths):
    return jnp.concatenate(
        [
            outer_sums(in_side, gate_side, lengths),
            outer_sums(in_side, up_side, lengths),
            outer_sums(hidden_side, out_side, lengths),
        ],
        axis=1,
    )


def gathering_plan(
    train_input,
    train_gate,
    train_up,
    train_outgrad,
    train_lengths,
    query_input,
    query_gate,
    query_up,
    query_outgrad,
    query_lengths,
    down_weight,
    proj_input,
    proj_outgrad,
    proj_hidden,
    proj_gate,
    proj_up,
):
    weight = lax.all_gather(down_weight, "dp", axis=1, tiled=True)

    def full_features(inputs, gate, up, outgrad, lengths):
        inputs, gate, up, outgrad = [flatten(a) for a in (inputs, gate, up, outgrad)]
        rows = lax.all_gather(outgrad, "tensor", axis=1, tiled=True)
        gate_side, up_side = gradient_sides(gate, up, project(rows, weight), proj_gate, proj_up)
        hidden_side = project(gated_hidden(gate, up), proj_hidden)
        sides = (
            project(inputs, proj_input),
            hidden_side,
            gate_side,
            up_side,
            project(outgrad, proj_outgrad),
        )
        return features(*lax.psum(sides, "tensor"), lengths)

    train_features = full_features(
        train_input, train_gate, train_up, train_outgrad, train_lengths
    )
    query_features = full_features(
        query_input, query_gate, query_up, query_outgrad, query_lengths
    )
    gathered = lax.all_gather(query_features, "dp", axis=0, tiled=True)
    return inner(train_features, gathered) / (RANK * SEQ)


ANYWHERE = pl.BlockSpec(memory_space=pl.ANY)
SCALARS = pl.BlockSpec(memory_space=pltpu.SMEM)
IN_VMEM = pl.BlockSpec(memory_space=pltpu.VMEM)


def params(limit=VMEM_BYTES):
    return pltpu.CompilerParams(vmem_limit_bytes=limit)


def cost(flops, arrays):
    return pl.CostEstimate(flops=1024, bytes_accessed=1024, transcendentals=0)


def tile_columns(number, block=0, tile=TILE):
    return pl.BlockSpec((number, tile), lambda i: (block, i))


def tile_rows(width, tile=TILE):
    return pl.BlockSpec((tile, width), lambda i: (i, 0))


def whole(shape):
    return pl.BlockSpec(shape, lambda i: tuple(0 for _ in shape))


def stacked_products(
    flags, pairs, far, weight_own, weight_sib, stacked, semaphores, held, weight_sems
):
    number = far.shape[1]
    step = pl.program_id(0)
    tiles = weight_own.shape[0] // TILE

    def weight_copies(tile):
        part = pl.ds(pl.multiple_of(tile * TILE, TILE), TILE)
        slot = lax.rem(tile, 3)
        return [
            pltpu.make_async_copy(
                weight.at[part], held.at[slot, side], weight_sems.at[slot, side]
            )
            for side, weight in enumerate((weight_own, weight_sib))
        ]

    @pl.when(step == 0)
    def _():
        slot = flags[1]
        far_copies = [
            pltpu.make_async_copy(
                far.at[i], stacked.at[jnp.bitwise_xor(slot, i), pl.ds(number, number)],
                semaphores.at[2 + i],
            )
            for i in range(2)
        ]
        for copy in far_copies:
            copy.start()
        for code, pair in enumerate(pairs):

            @pl.when(flags[0] == code)
            def _():
                copies = [
                    pltpu.make_async_copy(
                        pair[i], stacked.at[jnp.bitwise_xor(slot, i), pl.ds(0, number)],
                        semaphores.at[i],
                    )
                    for i in range(2)
                ]
                for copy in copies:
                    copy.start()
                for tile in range(2):
                    for copy in weight_copies(tile):
                        copy.start()
                for copy in copies:
                    copy.wait()

        for copy in far_copies:
            copy.wait()

    @pl.when(step + 2 < tiles)
    def _():
        for copy in weight_copies(step + 2):
            copy.start()

    for copy in weight_copies(step):
        copy.wait()
    slot = lax.rem(step, 3)
    return project(held[slot, 0], stacked[0]) + project(held[slot, 1], stacked[1])


def add_sides(hidden_grad, gate, up, proj_gate, proj_up, sides):
    gate_part, up_part = gradient_sides(gate, up, hidden_grad, proj_gate, proj_up)
    part = jnp.concatenate([gate_part, up_part], axis=1)
    first = pl.program_id(0) == 0

    @pl.when(first)
    def _():
        sides[...] = part

    @pl.when(jnp.logical_not(first))
    def _():
        sides[...] += part


def partial_kernel(
    flags, b0, b1, b2, b3, b4, b5, far, weight_own, weight_sib, near_sum, far_sum, *scratch
):
    pairs = ((b0, b1), (b2, b3), (b4, b5))
    total = stacked_products(flags, pairs, far, weight_own, weight_sib, *scratch)
    number = far.shape[1]
    near_sum[...] = total[:, :number]
    far_sum[...] = total[:, number:].astype(jnp.bfloat16)


def partial_sums(flags, blocks, far, weight_own, weight_sib):
    number, half = blocks[0].shape
    units = weight_own.shape[0]
    return pl.pallas_call(
        partial_kernel,
        grid=(units // TILE,),
        in_specs=[SCALARS] + [ANYWHERE] * 9,
        out_specs=[tile_rows(number)] * 2,
        out_shape=[
            jax.ShapeDtypeStruct((units, number), jnp.float32),
            jax.ShapeDtypeStruct((units, number), jnp.bfloat16),
        ],
        scratch_shapes=[
            pltpu.VMEM((2, 2 * number, half), jnp.bfloat16),
            pltpu.SemaphoreType.DMA((4,)),
            pltpu.VMEM((3, 2, TILE, half), jnp.bfloat16),
            pltpu.SemaphoreType.DMA((3, 2)),
        ],
        compiler_params=params(BIG_VMEM_BYTES),
        cost_estimate=cost(8 * number * half * units, (far, weight_own, weight_sib)),
    )(flags, *blocks, far, weight_own, weight_sib)


def finish_kernel(near_sum, returned, gate, up, proj_gate, proj_up, sides):
    hidden_grad = (near_sum[...] + returned[...].astype(jnp.float32)).T
    add_sides(hidden_grad, gate[...], up[...], proj_gate[...], proj_up[...], sides)


def finished_sides(near_sum, returned, gate, up, proj_gate, proj_up):
    units, number = near_sum.shape
    return pl.pallas_call(
        finish_kernel,
        grid=(units // WIDE,),
        in_specs=[tile_rows(number, WIDE)] * 2
        + [tile_columns(number, 0, WIDE)] * 2
        + [tile_columns(RANK, 0, WIDE)] * 2,
        out_specs=whole((number, 2 * RANK)),
        out_shape=jax.ShapeDtypeStruct((number, 2 * RANK), jnp.float32),
        compiler_params=params(),
        cost_estimate=cost(4 * number * RANK * units, (near_sum, returned, gate, up)),
    )(near_sum, returned, gate, up, proj_gate, proj_up)


def turn_kernel(gate, up, far_gate, far_up, gates, ups):
    number = gate.shape[0]
    for source, target, part in (
        (gate, gates, slice(0, number)),
        (up, ups, slice(0, number)),
        (far_gate, gates, slice(number, None)),
        (far_up, ups, slice(number, None)),
    ):
        target[:, part] = source[...].astype(jnp.float32).T.astype(jnp.bfloat16)


def turned(gate, up, far_gate, far_up):
    number, units = far_gate.shape
    shape = jax.ShapeDtypeStruct((units, 2 * number), jnp.bfloat16)
    return pl.pallas_call(
        turn_kernel,
        grid=(units // TILE,),
        in_specs=[tile_columns(number, 1)] * 2 + [tile_columns(number)] * 2,
        out_specs=[tile_rows(2 * number)] * 2,
        out_shape=[shape] * 2,
        compiler_params=params(),
        cost_estimate=cost(0, (gate, up)),
    )(gate, up, far_gate, far_up)


def lent_kernel(
    flags, b0, b1, b2, b3, b4, b5, far, weight_own, weight_sib, gates, ups, proj_gate, proj_up,
    near, away, *scratch,
):
    pairs = ((b0, b1), (b2, b3), (b4, b5))
    hidden_grad = stacked_products(flags, pairs, far, weight_own, weight_sib, *scratch)
    gate_grad, up_grad = gradients(gates[...], ups[...], hidden_grad)
    part = jnp.concatenate(
        [
            jnp.dot(proj_gate[...], gate_grad, preferred_element_type=jnp.float32),
            jnp.dot(proj_up[...], up_grad, preferred_element_type=jnp.float32),
        ],
        axis=0,
    )
    number = near.shape[1]
    first = pl.program_id(0) == 0

    @pl.when(first)
    def _():
        near[...] = part[:, :number]
        away[...] = part[:, number:]

    @pl.when(jnp.logical_not(first))
    def _():
        near[...] += part[:, :number]
        away[...] += part[:, number:]


def lent_sides(flags, blocks, far, weight_own, weight_sib, gates, ups, proj_gate, proj_up):
    number, half = blocks[0].shape
    units = weight_own.shape[0]
    return pl.pallas_call(
        lent_kernel,
        grid=(units // TILE,),
        in_specs=[SCALARS]
        + [ANYWHERE] * 9
        + [tile_rows(2 * number)] * 2
        + [tile_columns(RANK)] * 2,
        out_specs=[whole((2 * RANK, number))] * 2,
        out_shape=[jax.ShapeDtypeStruct((2 * RANK, number), jnp.float32)] * 2,
        scratch_shapes=[
            pltpu.VMEM((2, 2 * number, half), jnp.bfloat16),
            pltpu.SemaphoreType.DMA((4,)),
            pltpu.VMEM((3, 2, TILE, half), jnp.bfloat16),
            pltpu.SemaphoreType.DMA((3, 2)),
        ],
        compiler_params=params(BIG_VMEM_BYTES),
        cost_estimate=cost(8 * number * half * units, (far, weight_own, weight_sib)),
    )(flags, *blocks, far, weight_own, weight_sib, gates, ups, proj_gate, proj_up)


def early_kernel(
    t_input, q_input, t_outgrad, q_outgrad, proj_input, proj_outgrad, t_gate, t_up, q_gate, q_up,
    proj_hidden, in_out, hidden,
):
    number = t_input.shape[0]
    t_hidden = project(gated_hidden(t_gate[...], t_up[...]), proj_hidden[...])
    q_hidden = project(gated_hidden(q_gate[...], q_up[...]), proj_hidden[...])
    first = pl.program_id(0) == 0

    @pl.when(first)
    def _():
        for inputs, outgrad, part in (
            (t_input, t_outgrad, slice(0, number)),
            (q_input, q_outgrad, slice(number, None)),
        ):
            in_out[part, :] = jnp.concatenate(
                [
                    project(inputs[...], proj_input[...]),
                    project(outgrad[...], proj_outgrad[...]),
                ],
                axis=1,
            )
        hidden[:number, :] = t_hidden
        hidden[number:, :] = q_hidden

    @pl.when(jnp.logical_not(first))
    def _():
        hidden[:number, :] += t_hidden
        hidden[number:, :] += q_hidden


def early_sides(
    t_input, q_input, t_outgrad, q_outgrad, proj_input, proj_outgrad, t_gate, t_up, q_gate, q_up,
    proj_hidden,
):
    total, units = t_gate.shape[0] + q_gate.shape[0], t_gate.shape[1]
    wide = (t_input, q_input, t_outgrad, q_outgrad, proj_input, proj_outgrad)
    tiled = (t_gate, t_up, q_gate, q_up, proj_hidden)
    shapes = ((total, 2 * RANK), (total, RANK))
    return pl.pallas_call(
        early_kernel,
        grid=(units // TILE,),
        in_specs=[whole(a.shape) for a in wide] + [tile_columns(a.shape[0]) for a in tiled],
        out_specs=[whole(shape) for shape in shapes],
        out_shape=[jax.ShapeDtypeStruct(shape, jnp.float32) for shape in shapes],
        compiler_params=params(),
        cost_estimate=cost(2 * total * RANK * units, wide + tiled),
    )(*wide, *tiled)


def outer_sum(left_side, right_side, weight):
    return lax.dot_general(
        left_side * weight,
        right_side,
        (((0,), (0,)), ((), ())),
        precision=lax.Precision.HIGHEST,
        preferred_element_type=jnp.float32,
    )


def example_features(in_side, hidden_side, gate_side, up_side, out_side, length):
    positions = lax.broadcasted_iota(jnp.int32, (SEQ, RANK), 0)
    weight = (positions < length).astype(jnp.float32)
    return (
        outer_sum(in_side, gate_side, weight),
        outer_sum(in_side, up_side, weight),
        outer_sum(hidden_side, out_side, weight),
    )


def query_kernel(lengths, in_out, sums, found):
    for e in range(found.shape[0]):
        part = slice(e * SEQ, (e + 1) * SEQ)
        three = example_features(
            in_out[part, :RANK],
            sums[part, 2 * RANK :],
            sums[part, :RANK],
            sums[part, RANK : 2 * RANK],
            in_out[part, RANK:],
            lengths[e],
        )
        for segment in range(3):
            found[e, segment * RANK : (segment + 1) * RANK, :] = three[segment]


def query_features(lengths, in_out, sums):
    return pl.pallas_call(
        query_kernel,
        in_specs=[SCALARS, IN_VMEM, IN_VMEM],
        out_specs=IN_VMEM,
        out_shape=jax.ShapeDtypeStruct((lengths.shape[0], 3 * RANK, RANK), jnp.float32),
        compiler_params=params(),
    )(lengths, in_out, sums)


def score_kernel(
    lengths, place, in_out, hidden, early, near, far, q0, q1, q2, q3, scores
):
    queries = q0.shape[0]
    shape = scores.shape
    row = lax.broadcasted_iota(jnp.int32, shape, 0)
    column = lax.broadcasted_iota(jnp.int32, shape, 1)
    gradient = jnp.concatenate([early[...], (near[...] + far[...]).T], axis=0)
    total = jnp.zeros(shape, jnp.float32)
    for e in range(shape[0]):
        part = slice(e * SEQ, (e + 1) * SEQ)
        three = jnp.concatenate(
            example_features(
                in_out[part, :RANK],
                hidden[part, :],
                gradient[part, :RANK],
                gradient[part, RANK:],
                in_out[part, RANK:],
                lengths[e],
            ),
            axis=0,
        )
        for step, found in enumerate((q0, q1, q2, q3)):
            for j in range(queries):
                value = jnp.sum(three * found[j], keepdims=True)
                here = (row == e) & (
                    column == queries * jnp.bitwise_xor(place[0], step) + j
                )
                total = total + jnp.where(here, value, 0.0)
    scores[...] = total


def partial_scores(lengths, place, in_out, hidden, early, near, far, found):
    number = lengths.shape[0]
    return pl.pallas_call(
        score_kernel,
        in_specs=[SCALARS] * 2 + [IN_VMEM] * 9,
        out_specs=IN_VMEM,
        out_shape=jax.ShapeDtypeStruct((number, 4 * found[0].shape[0]), jnp.float32),
        compiler_params=params(),
    )(lengths, place, in_out, hidden, early, near, far, *found)


def after(value, *others):
    return lax.optimization_barrier((value, *others))[0]


def moving_plan(
    train_input,
    train_gate,
    train_up,
    train_outgrad,
    train_lengths,
    query_input,
    query_gate,
    query_up,
    query_outgrad,
    query_lengths,
    down_weight,
    proj_input,
    proj_outgrad,
    proj_hidden,
    proj_gate,
    proj_up,
):
    t = lax.axis_index("tensor")
    d = lax.axis_index("dp")
    x, core, upper = d // 2, d % 2, t // 2
    at_home = x == upper
    inner_chip = (t == 1) | (t == 2)
    near_code = jnp.where(at_home, 0, jnp.where(inner_chip, 1, 2))
    first_parity = jnp.where(at_home, t % 2, upper)
    flags = jnp.stack([near_code, first_parity ^ core]).astype(jnp.int32)
    place = jnp.stack([d]).astype(jnp.int32)

    to_core = functools.partial(lax.ppermute, axis_name="dp", perm=[(i, i ^ 1) for i in range(4)])
    to_chip = functools.partial(lax.ppermute, axis_name="dp", perm=[(i, i ^ 2) for i in range(4)])
    to_other = functools.partial(lax.ppermute, axis_name="dp", perm=[(i, i ^ 3) for i in range(4)])
    outer = functools.partial(
        lax.ppermute, axis_name="tensor", perm=[(i, i ^ 1) for i in range(4)]
    )
    across = functools.partial(
        lax.ppermute, axis_name="tensor", perm=[(i, i ^ 2) for i in range(4)]
    )
    opposite = functools.partial(
        lax.ppermute, axis_name="tensor", perm=[(i, 3 - i) for i in range(4)]
    )
    middle = functools.partial(
        lax.ppermute,
        axis_name=("tensor", "dp"),
        perm=[
            (4 * i + j, 4 * (3 - i) + j) if i in (1, 2) else (4 * i + j, 4 * i + (j ^ 1))
            for i in range(4)
            for j in range(4)
        ],
    )

    q_input, q_gate, q_up, q_outgrad = [
        flatten(a) for a in (query_input, query_gate, query_up, query_outgrad)
    ]
    t_input, t_gate, t_up, t_outgrad = [
        flatten(a) for a in (train_input, train_gate, train_up, train_outgrad)
    ]
    examples = train_lengths.shape[0] // 2
    cut = examples * SEQ

    def first_hops(own):
        return own, outer(own), across(own)

    def last_hops(own, one, two):
        mid = middle(after(own, two))
        return own, one, mid, two, two, outer(after(two, one))

    def crossing_pair(own, one, second_inner, third_inner, second_outer, third_outer):
        def choose(within, beyond_inner, beyond_outer):
            beyond = jnp.where(inner_chip, beyond_inner, beyond_outer)
            return jnp.where(at_home, beyond, within)

        return jnp.stack(
            [choose(own, second_inner, second_outer), choose(one, third_inner, third_outer)]
        )

    weight_own, weight_sib = down_weight, to_core(down_weight)
    q_hops = first_hops(q_outgrad)
    own_in_out, hidden = early_sides(
        t_input, q_input, t_outgrad, q_outgrad, proj_input, proj_outgrad, t_gate, t_up, q_gate,
        q_up, proj_hidden,
    )

    far_gate = to_chip(after(t_gate[cut:], own_in_out))
    q_blocks = last_hops(*q_hops[:2], after(q_hops[2], own_in_out))
    a_hops = first_hops(after(t_outgrad[:cut], q_hops[2]))
    far_up = to_chip(after(t_up[cut:], far_gate))
    q_send = crossing_pair(*q_blocks)
    q_far = to_chip(q_send)
    a_blocks = last_hops(*a_hops[:2], after(a_hops[2], q_send, far_up))

    b_hops = first_hops(after(t_outgrad[cut:], a_hops[2]))
    gates, ups = turned(t_gate, t_up, far_gate, far_up)
    a_send = crossing_pair(*a_blocks[:5], after(a_blocks[5], q_far, gates))
    a_far = to_chip(a_send)
    q_near_sum, q_far_sum = partial_sums(
        flags, q_blocks, after(q_far, a_send), weight_own, weight_sib
    )
    q_returned = to_chip(after(q_far_sum, a_far))
    b_blocks = last_hops(*b_hops[:2], after(b_hops[2], q_far_sum))
    b_send = crossing_pair(*b_blocks)
    b_far = to_chip(b_send)
    a_near_sum, a_far_sum = partial_sums(
        flags, a_blocks, after(a_far, b_send), weight_own, weight_sib
    )
    a_returned = to_chip(a_far_sum)
    in_out = own_in_out + outer(after(own_in_out, b_send))
    q_gradient = finished_sides(
        q_near_sum, after(q_returned, a_far_sum), q_gate, q_up, proj_gate, proj_up
    )
    q_sums = jnp.concatenate([q_gradient, hidden[2 * cut :]], axis=1)
    q_sums = q_sums + outer(q_sums)
    b_near, b_away = lent_sides(
        after(flags, q_sums, in_out), b_blocks, b_far, weight_own, weight_sib, gates, ups,
        proj_gate, proj_up,
    )
    in_out = in_out + after(across(in_out), b_near)
    q_sums = q_sums + after(across(q_sums), b_near)
    own_found = query_features(query_lengths, in_out[2 * cut :], q_sums)
    found = (own_found, to_core(own_found), to_chip(own_found), to_other(own_found))
    a_gradient = finished_sides(a_near_sum, a_returned, t_gate, t_up, proj_gate, proj_up)
    own_scores = partial_scores(
        train_lengths, place, in_out[: 2 * cut], hidden[: 2 * cut], a_gradient, b_near,
        to_chip(b_away), found,
    )
    scores = own_scores + outer(own_scores) + across(own_scores) + opposite(own_scores)
    return scores / (RANK * SEQ)


def solution(mesh):
    tensor, dp = mesh.shape["tensor"], mesh.shape["dp"]

    def per_device(*arguments):
        if tensor == 4 and dp == 4:
            return moving_plan(*arguments)
        return gathering_plan(*arguments)

    in_specs = (
        P(("parts", "dp"), None, "tensor"),
        P(("parts", "dp"), None, "tensor"),
        P(("parts", "dp"), None, "tensor"),
        P(("parts", "dp"), None, "tensor"),
        P(("parts", "dp")),
        P(("parts", "dp"), None, "tensor"),
        P(("parts", "dp"), None, "tensor"),
        P(("parts", "dp"), None, "tensor"),
        P(("parts", "dp"), None, "tensor"),
        P(("parts", "dp")),
        P("tensor", "dp"),
        P(None, "tensor"),
        P(None, "tensor"),
        P(None, "tensor"),
        P(None, "tensor"),
        P(None, "tensor"),
    )
    out_specs = P(("parts", "dp"), None)
    return jax.shard_map(
        per_device, mesh=mesh, in_specs=in_specs, out_specs=out_specs, check_vma=False
    )
```

```python
import functools

import jax
import jax.numpy as jnp
from jax import lax
from jax.experimental import pallas as pl
from jax.experimental.pallas import tpu as pltpu
from jax.sharding import PartitionSpec as P

RANK = 64
SEQ = 64
TILE = 512
WIDE = 1792
VMEM_BYTES = 40 * 1024 * 1024
BIG_VMEM_BYTES = 58 * 1024 * 1024


def flatten(array):
    return array.reshape(-1, array.shape[-1])


def project(rows, table):
    return lax.dot_general(
        rows, table, (((1,), (1,)), ((), ())), preferred_element_type=jnp.float32
    )


def inner(left_side, right_side):
    return lax.dot_general(
        left_side,
        right_side,
        (((1,), (1,)), ((), ())),
        precision=lax.Precision.HIGHEST,
        preferred_element_type=jnp.float32,
    )


def gated_hidden(gate, up):
    gate_wide = gate.astype(jnp.float32)
    up_wide = up.astype(jnp.float32)
    return (gate_wide * jax.nn.sigmoid(gate_wide) * up_wide).astype(jnp.bfloat16)


def gradients(gate, up, hidden_grad):
    gate_wide = gate.astype(jnp.float32)
    up_wide = up.astype(jnp.float32)
    sigmoid_gate = jax.nn.sigmoid(gate_wide)
    silu_gate = gate_wide * sigmoid_gate
    gate_grad = (
        hidden_grad * up_wide * sigmoid_gate * (1.0 + gate_wide * (1.0 - sigmoid_gate))
    ).astype(jnp.bfloat16)
    up_grad = (hidden_grad * silu_gate).astype(jnp.bfloat16)
    return gate_grad, up_grad


def gradient_sides(gate, up, hidden_grad, proj_gate, proj_up):
    gate_grad, up_grad = gradients(gate, up, hidden_grad)
    return project(gate_grad, proj_gate), project(up_grad, proj_up)


def outer_sums(left_side, right_side, lengths):
    number = lengths.shape[0]
    length = left_side.shape[0] // number
    positions = lax.broadcasted_iota(jnp.int32, (number, length), 1)
    weights = (positions < lengths[:, None]).astype(jnp.float32)
    left_rows = left_side.reshape(number, length, left_side.shape[1]) * weights[:, :, None]
    right_rows = right_side.reshape(number, length, right_side.shape[1])
    summed = jnp.einsum("est,esu->etu", left_rows, right_rows, precision=lax.Precision.HIGHEST)
    return summed.reshape(number, -1)


def features(in_side, hidden_side, gate_side, up_side, out_side, lengths):
    return jnp.concatenate(
        [
            outer_sums(in_side, gate_side, lengths),
            outer_sums(in_side, up_side, lengths),
            outer_sums(hidden_side, out_side, lengths),
        ],
        axis=1,
    )


def gathering_plan(
    train_input,
    train_gate,
    train_up,
    train_outgrad,
    train_lengths,
    query_input,
    query_gate,
    query_up,
    query_outgrad,
    query_lengths,
    down_weight,
    proj_input,
    proj_outgrad,
    proj_hidden,
    proj_gate,
    proj_up,
):
    weight = lax.all_gather(down_weight, "dp", axis=1, tiled=True)

    def full_features(inputs, gate, up, outgrad, lengths):
        inputs, gate, up, outgrad = [flatten(a) for a in (inputs, gate, up, outgrad)]
        rows = lax.all_gather(outgrad, "tensor", axis=1, tiled=True)
        gate_side, up_side = gradient_sides(gate, up, project(rows, weight), proj_gate, proj_up)
        hidden_side = project(gated_hidden(gate, up), proj_hidden)
        sides = (
            project(inputs, proj_input),
            hidden_side,
            gate_side,
            up_side,
            project(outgrad, proj_outgrad),
        )
        return features(*lax.psum(sides, "tensor"), lengths)

    train_features = full_features(
        train_input, train_gate, train_up, train_outgrad, train_lengths
    )
    query_features = full_features(
        query_input, query_gate, query_up, query_outgrad, query_lengths
    )
    gathered = lax.all_gather(query_features, "dp", axis=0, tiled=True)
    return inner(train_features, gathered) / (RANK * SEQ)


ANYWHERE = pl.BlockSpec(memory_space=pl.ANY)
SCALARS = pl.BlockSpec(memory_space=pltpu.SMEM)
IN_VMEM = pl.BlockSpec(memory_space=pltpu.VMEM)


def params(limit=VMEM_BYTES):
    return pltpu.CompilerParams(vmem_limit_bytes=limit)


def cost(flops, arrays):
    return pl.CostEstimate(flops=1024, bytes_accessed=1024, transcendentals=0)


def tile_columns(number, block=0, tile=TILE):
    return pl.BlockSpec((number, tile), lambda i: (block, i))


def tile_rows(width, tile=TILE):
    return pl.BlockSpec((tile, width), lambda i: (i, 0))


def whole(shape):
    return pl.BlockSpec(shape, lambda i: tuple(0 for _ in shape))


def stacked_products(
    flags, pairs, far, weight_own, weight_sib, stacked, semaphores, held, weight_sems
):
    number = far.shape[1]
    step = pl.program_id(0)
    tiles = weight_own.shape[0] // TILE

    def weight_copies(tile):
        part = pl.ds(pl.multiple_of(tile * TILE, TILE), TILE)
        slot = lax.rem(tile, 3)
        return [
            pltpu.make_async_copy(
                weight.at[part], held.at[slot, side], weight_sems.at[slot, side]
            )
            for side, weight in enumerate((weight_own, weight_sib))
        ]

    @pl.when(step == 0)
    def _():
        slot = flags[1]
        far_copies = [
            pltpu.make_async_copy(
                far.at[i], stacked.at[jnp.bitwise_xor(slot, i), pl.ds(number, number)],
                semaphores.at[2 + i],
            )
            for i in range(2)
        ]
        for copy in far_copies:
            copy.start()
        for code, pair in enumerate(pairs):

            @pl.when(flags[0] == code)
            def _():
                copies = [
                    pltpu.make_async_copy(
                        pair[i], stacked.at[jnp.bitwise_xor(slot, i), pl.ds(0, number)],
                        semaphores.at[i],
                    )
                    for i in range(2)
                ]
                for copy in copies:
                    copy.start()
                for tile in range(2):
                    for copy in weight_copies(tile):
                        copy.start()
                for copy in copies:
                    copy.wait()

        for copy in far_copies:
            copy.wait()

    @pl.when(step + 2 < tiles)
    def _():
        for copy in weight_copies(step + 2):
            copy.start()

    for copy in weight_copies(step):
        copy.wait()
    slot = lax.rem(step, 3)
    return project(held[slot, 0], stacked[0]) + project(held[slot, 1], stacked[1])


def add_sides(hidden_grad, gate, up, proj_gate, proj_up, sides):
    gate_part, up_part = gradient_sides(gate, up, hidden_grad, proj_gate, proj_up)
    part = jnp.concatenate([gate_part, up_part], axis=1)
    first = pl.program_id(0) == 0

    @pl.when(first)
    def _():
        sides[...] = part

    @pl.when(jnp.logical_not(first))
    def _():
        sides[...] += part


def partial_kernel(
    flags, b0, b1, b2, b3, b4, b5, far, weight_own, weight_sib, near_sum, far_sum, *scratch
):
    pairs = ((b0, b1), (b2, b3), (b4, b5))
    total = stacked_products(flags, pairs, far, weight_own, weight_sib, *scratch)
    number = far.shape[1]
    near_sum[...] = total[:, :number]
    far_sum[...] = total[:, number:].astype(jnp.bfloat16)


def partial_sums(flags, blocks, far, weight_own, weight_sib):
    number, half = blocks[0].shape
    units = weight_own.shape[0]
    return pl.pallas_call(
        partial_kernel,
        grid=(units // TILE,),
        in_specs=[SCALARS] + [ANYWHERE] * 9,
        out_specs=[tile_rows(number)] * 2,
        out_shape=[
            jax.ShapeDtypeStruct((units, number), jnp.float32),
            jax.ShapeDtypeStruct((units, number), jnp.bfloat16),
        ],
        scratch_shapes=[
            pltpu.VMEM((2, 2 * number, half), jnp.bfloat16),
            pltpu.SemaphoreType.DMA((4,)),
            pltpu.VMEM((3, 2, TILE, half), jnp.bfloat16),
            pltpu.SemaphoreType.DMA((3, 2)),
        ],
        compiler_params=params(BIG_VMEM_BYTES),
        cost_estimate=cost(8 * number * half * units, (far, weight_own, weight_sib)),
    )(flags, *blocks, far, weight_own, weight_sib)


def finish_kernel(near_sum, returned, gate, up, proj_gate, proj_up, sides):
    hidden_grad = (near_sum[...] + returned[...].astype(jnp.float32)).T
    add_sides(hidden_grad, gate[...], up[...], proj_gate[...], proj_up[...], sides)


def finished_sides(near_sum, returned, gate, up, proj_gate, proj_up):
    units, number = near_sum.shape
    return pl.pallas_call(
        finish_kernel,
        grid=(units // WIDE,),
        in_specs=[tile_rows(number, WIDE)] * 2
        + [tile_columns(number, 0, WIDE)] * 2
        + [tile_columns(RANK, 0, WIDE)] * 2,
        out_specs=whole((number, 2 * RANK)),
        out_shape=jax.ShapeDtypeStruct((number, 2 * RANK), jnp.float32),
        compiler_params=params(),
        cost_estimate=cost(4 * number * RANK * units, (near_sum, returned, gate, up)),
    )(near_sum, returned, gate, up, proj_gate, proj_up)


def turn_kernel(gate, up, far_gate, far_up, gates, ups):
    number = gate.shape[0]
    for source, target, part in (
        (gate, gates, slice(0, number)),
        (up, ups, slice(0, number)),
        (far_gate, gates, slice(number, None)),
        (far_up, ups, slice(number, None)),
    ):
        target[:, part] = source[...].astype(jnp.float32).T.astype(jnp.bfloat16)


def turned(gate, up, far_gate, far_up):
    number, units = far_gate.shape
    shape = jax.ShapeDtypeStruct((units, 2 * number), jnp.bfloat16)
    return pl.pallas_call(
        turn_kernel,
        grid=(units // TILE,),
        in_specs=[tile_columns(number, 1)] * 2 + [tile_columns(number)] * 2,
        out_specs=[tile_rows(2 * number)] * 2,
        out_shape=[shape] * 2,
        compiler_params=params(),
        cost_estimate=cost(0, (gate, up)),
    )(gate, up, far_gate, far_up)


def lent_kernel(
    flags, b0, b1, b2, b3, b4, b5, far, weight_own, weight_sib, gates, ups, proj_gate, proj_up,
    near, away, *scratch,
):
    pairs = ((b0, b1), (b2, b3), (b4, b5))
    hidden_grad = stacked_products(flags, pairs, far, weight_own, weight_sib, *scratch)
    gate_grad, up_grad = gradients(gates[...], ups[...], hidden_grad)
    part = jnp.concatenate(
        [
            jnp.dot(proj_gate[...], gate_grad, preferred_element_type=jnp.float32),
            jnp.dot(proj_up[...], up_grad, preferred_element_type=jnp.float32),
        ],
        axis=0,
    )
    number = near.shape[1]
    first = pl.program_id(0) == 0

    @pl.when(first)
    def _():
        near[...] = part[:, :number]
        away[...] = part[:, number:]

    @pl.when(jnp.logical_not(first))
    def _():
        near[...] += part[:, :number]
        away[...] += part[:, number:]


def lent_sides(flags, blocks, far, weight_own, weight_sib, gates, ups, proj_gate, proj_up):
    number, half = blocks[0].shape
    units = weight_own.shape[0]
    return pl.pallas_call(
        lent_kernel,
        grid=(units // TILE,),
        in_specs=[SCALARS]
        + [ANYWHERE] * 9
        + [tile_rows(2 * number)] * 2
        + [tile_columns(RANK)] * 2,
        out_specs=[whole((2 * RANK, number))] * 2,
        out_shape=[jax.ShapeDtypeStruct((2 * RANK, number), jnp.float32)] * 2,
        scratch_shapes=[
            pltpu.VMEM((2, 2 * number, half), jnp.bfloat16),
            pltpu.SemaphoreType.DMA((4,)),
            pltpu.VMEM((3, 2, TILE, half), jnp.bfloat16),
            pltpu.SemaphoreType.DMA((3, 2)),
        ],
        compiler_params=params(BIG_VMEM_BYTES),
        cost_estimate=cost(8 * number * half * units, (far, weight_own, weight_sib)),
    )(flags, *blocks, far, weight_own, weight_sib, gates, ups, proj_gate, proj_up)


def early_kernel(
    t_input, q_input, t_outgrad, q_outgrad, proj_input, proj_outgrad, t_gate, t_up, q_gate, q_up,
    proj_hidden, in_out, hidden,
):
    number = t_input.shape[0]
    t_hidden = project(gated_hidden(t_gate[...], t_up[...]), proj_hidden[...])
    q_hidden = project(gated_hidden(q_gate[...], q_up[...]), proj_hidden[...])
    first = pl.program_id(0) == 0

    @pl.when(first)
    def _():
        for inputs, outgrad, part in (
            (t_input, t_outgrad, slice(0, number)),
            (q_input, q_outgrad, slice(number, None)),
        ):
            in_out[part, :] = jnp.concatenate(
                [
                    project(inputs[...], proj_input[...]),
                    project(outgrad[...], proj_outgrad[...]),
                ],
                axis=1,
            )
        hidden[:number, :] = t_hidden
        hidden[number:, :] = q_hidden

    @pl.when(jnp.logical_not(first))
    def _():
        hidden[:number, :] += t_hidden
        hidden[number:, :] += q_hidden


def early_sides(
    t_input, q_input, t_outgrad, q_outgrad, proj_input, proj_outgrad, t_gate, t_up, q_gate, q_up,
    proj_hidden,
):
    total, units = t_gate.shape[0] + q_gate.shape[0], t_gate.shape[1]
    wide = (t_input, q_input, t_outgrad, q_outgrad, proj_input, proj_outgrad)
    tiled = (t_gate, t_up, q_gate, q_up, proj_hidden)
    shapes = ((total, 2 * RANK), (total, RANK))
    return pl.pallas_call(
        early_kernel,
        grid=(units // TILE,),
        in_specs=[whole(a.shape) for a in wide] + [tile_columns(a.shape[0]) for a in tiled],
        out_specs=[whole(shape) for shape in shapes],
        out_shape=[jax.ShapeDtypeStruct(shape, jnp.float32) for shape in shapes],
        compiler_params=params(),
        cost_estimate=cost(2 * total * RANK * units, wide + tiled),
    )(*wide, *tiled)


def outer_sum(left_side, right_side, weight):
    return lax.dot_general(
        left_side * weight,
        right_side,
        (((0,), (0,)), ((), ())),
        precision=lax.Precision.HIGHEST,
        preferred_element_type=jnp.float32,
    )


def example_features(in_side, hidden_side, gate_side, up_side, out_side, length):
    positions = lax.broadcasted_iota(jnp.int32, (SEQ, RANK), 0)
    weight = (positions < length).astype(jnp.float32)
    return (
        outer_sum(in_side, gate_side, weight),
        outer_sum(in_side, up_side, weight),
        outer_sum(hidden_side, out_side, weight),
    )


def query_kernel(lengths, in_out, sums, found):
    for e in range(found.shape[0]):
        part = slice(e * SEQ, (e + 1) * SEQ)
        three = example_features(
            in_out[part, :RANK],
            sums[part, 2 * RANK :],
            sums[part, :RANK],
            sums[part, RANK : 2 * RANK],
            in_out[part, RANK:],
            lengths[e],
        )
        for segment in range(3):
            found[e, segment * RANK : (segment + 1) * RANK, :] = three[segment]


def query_features(lengths, in_out, sums):
    return pl.pallas_call(
        query_kernel,
        in_specs=[SCALARS, IN_VMEM, IN_VMEM],
        out_specs=IN_VMEM,
        out_shape=jax.ShapeDtypeStruct((lengths.shape[0], 3 * RANK, RANK), jnp.float32),
        compiler_params=params(),
    )(lengths, in_out, sums)


def score_kernel(
    lengths, place, in_out, hidden, early, near, far, q0, q1, q2, q3, scores
):
    queries = q0.shape[0]
    shape = scores.shape
    row = lax.broadcasted_iota(jnp.int32, shape, 0)
    column = lax.broadcasted_iota(jnp.int32, shape, 1)
    gradient = jnp.concatenate([early[...], (near[...] + far[...]).T], axis=0)
    total = jnp.zeros(shape, jnp.float32)
    for e in range(shape[0]):
        part = slice(e * SEQ, (e + 1) * SEQ)
        three = jnp.concatenate(
            example_features(
                in_out[part, :RANK],
                hidden[part, :],
                gradient[part, :RANK],
                gradient[part, RANK:],
                in_out[part, RANK:],
                lengths[e],
            ),
            axis=0,
        )
        for step, found in enumerate((q0, q1, q2, q3)):
            for j in range(queries):
                value = jnp.sum(three * found[j], keepdims=True)
                here = (row == e) & (
                    column == queries * jnp.bitwise_xor(place[0], step) + j
                )
                total = total + jnp.where(here, value, 0.0)
    scores[...] = total


def partial_scores(lengths, place, in_out, hidden, early, near, far, found):
    number = lengths.shape[0]
    return pl.pallas_call(
        score_kernel,
        in_specs=[SCALARS] * 2 + [IN_VMEM] * 9,
        out_specs=IN_VMEM,
        out_shape=jax.ShapeDtypeStruct((number, 4 * found[0].shape[0]), jnp.float32),
        compiler_params=params(),
    )(lengths, place, in_out, hidden, early, near, far, *found)


def after(value, *others):
    return lax.optimization_barrier((value, *others))[0]


def moving_plan(
    train_input,
    train_gate,
    train_up,
    train_outgrad,
    train_lengths,
    query_input,
    query_gate,
    query_up,
    query_outgrad,
    query_lengths,
    down_weight,
    proj_input,
    proj_outgrad,
    proj_hidden,
    proj_gate,
    proj_up,
):
    t = lax.axis_index("tensor")
    d = lax.axis_index("dp")
    x, core, upper = d // 2, d % 2, t // 2
    at_home = x == upper
    inner_chip = (t == 1) | (t == 2)
    near_code = jnp.where(at_home, 0, jnp.where(inner_chip, 1, 2))
    first_parity = jnp.where(at_home, t % 2, upper)
    flags = jnp.stack([near_code, first_parity ^ core]).astype(jnp.int32)
    place = jnp.stack([d]).astype(jnp.int32)

    to_core = functools.partial(lax.ppermute, axis_name="dp", perm=[(i, i ^ 1) for i in range(4)])
    to_chip = functools.partial(lax.ppermute, axis_name="dp", perm=[(i, i ^ 2) for i in range(4)])
    to_other = functools.partial(lax.ppermute, axis_name="dp", perm=[(i, i ^ 3) for i in range(4)])
    outer = functools.partial(
        lax.ppermute, axis_name="tensor", perm=[(i, i ^ 1) for i in range(4)]
    )
    across = functools.partial(
        lax.ppermute, axis_name="tensor", perm=[(i, i ^ 2) for i in range(4)]
    )
    opposite = functools.partial(
        lax.ppermute, axis_name="tensor", perm=[(i, 3 - i) for i in range(4)]
    )
    middle = functools.partial(
        lax.ppermute,
        axis_name=("tensor", "dp"),
        perm=[
            (4 * i + j, 4 * (3 - i) + j) if i in (1, 2) else (4 * i + j, 4 * i + (j ^ 1))
            for i in range(4)
            for j in range(4)
        ],
    )

    q_input, q_gate, q_up, q_outgrad = [
        flatten(a) for a in (query_input, query_gate, query_up, query_outgrad)
    ]
    t_input, t_gate, t_up, t_outgrad = [
        flatten(a) for a in (train_input, train_gate, train_up, train_outgrad)
    ]
    examples = train_lengths.shape[0] // 2
    cut = examples * SEQ

    def first_hops(own):
        return own, outer(own), across(own)

    def last_hops(own, one, two):
        mid = middle(after(own, two))
        return own, one, mid, two, two, outer(after(two, one))

    def crossing_pair(own, one, second_inner, third_inner, second_outer, third_outer):
        def choose(within, beyond_inner, beyond_outer):
            beyond = jnp.where(inner_chip, beyond_inner, beyond_outer)
            return jnp.where(at_home, beyond, within)

        return jnp.stack(
            [choose(own, second_inner, second_outer), choose(one, third_inner, third_outer)]
        )

    weight_own, weight_sib = down_weight, to_core(down_weight)
    q_hops = first_hops(q_outgrad)
    far_gate = to_chip(t_gate[cut:])
    own_in_out, hidden = early_sides(
        t_input, q_input, t_outgrad, q_outgrad, proj_input, proj_outgrad, t_gate, t_up, q_gate,
        q_up, proj_hidden,
    )

    q_blocks = last_hops(*q_hops[:2], after(q_hops[2], own_in_out))
    a_hops = first_hops(after(t_outgrad[:cut], q_hops[2], far_gate))
    far_up = to_chip(after(t_up[cut:], far_gate))
    q_send = after(crossing_pair(*q_blocks), far_up)
    q_far = to_chip(q_send)
    a_blocks = last_hops(*a_hops[:2], after(a_hops[2], q_send))

    b_hops = first_hops(after(t_outgrad[cut:], a_hops[2]))
    gates, ups = turned(t_gate, t_up, far_gate, far_up)
    a_send = crossing_pair(*a_blocks[:5], after(a_blocks[5], q_far, gates))
    a_far = to_chip(a_send)
    q_near_sum, q_far_sum = partial_sums(
        flags, q_blocks, after(q_far, a_send), weight_own, weight_sib
    )
    q_returned = to_chip(after(q_far_sum, a_far))
    b_blocks = last_hops(*b_hops[:2], after(b_hops[2], q_far_sum))
    b_send = crossing_pair(*b_blocks)
    b_far = to_chip(b_send)
    a_near_sum, a_far_sum = partial_sums(
        flags, a_blocks, after(a_far, b_send), weight_own, weight_sib
    )
    a_returned = to_chip(a_far_sum)
    in_out = own_in_out + outer(after(own_in_out, b_send))
    q_gradient = finished_sides(
        q_near_sum, after(q_returned, a_far_sum), q_gate, q_up, proj_gate, proj_up
    )
    q_sums = jnp.concatenate([q_gradient, hidden[2 * cut :]], axis=1)
    q_sums = q_sums + outer(q_sums)
    b_near, b_away = lent_sides(
        after(flags, q_sums, in_out), b_blocks, b_far, weight_own, weight_sib, gates, ups,
        proj_gate, proj_up,
    )
    in_out = in_out + after(across(in_out), b_near)
    q_sums = q_sums + after(across(q_sums), b_near)
    own_found = query_features(query_lengths, in_out[2 * cut :], q_sums)
    found = (own_found, to_core(own_found), to_chip(own_found), to_other(own_found))
    a_gradient = finished_sides(a_near_sum, a_returned, t_gate, t_up, proj_gate, proj_up)
    own_scores = partial_scores(
        train_lengths, place, in_out[: 2 * cut], hidden[: 2 * cut], a_gradient, b_near,
        to_chip(b_away), found,
    )
    scores = own_scores + outer(own_scores) + across(own_scores) + opposite(own_scores)
    return scores / (RANK * SEQ)


def solution(mesh):
    tensor, dp = mesh.shape["tensor"], mesh.shape["dp"]

    def per_device(*arguments):
        if tensor == 4 and dp == 4:
            return moving_plan(*arguments)
        return gathering_plan(*arguments)

    in_specs = (
        P(("parts", "dp"), None, "tensor"),
        P(("parts", "dp"), None, "tensor"),
        P(("parts", "dp"), None, "tensor"),
        P(("parts", "dp"), None, "tensor"),
        P(("parts", "dp")),
        P(("parts", "dp"), None, "tensor"),
        P(("parts", "dp"), None, "tensor"),
        P(("parts", "dp"), None, "tensor"),
        P(("parts", "dp"), None, "tensor"),
        P(("parts", "dp")),
        P("tensor", "dp"),
        P(None, "tensor"),
        P(None, "tensor"),
        P(None, "tensor"),
        P(None, "tensor"),
        P(None, "tensor"),
    )
    out_specs = P(("parts", "dp"), None)
    return jax.shard_map(
        per_device, mesh=mesh, in_specs=in_specs, out_specs=out_specs, check_vma=False
    )
```

```python
import functools

import jax
import jax.numpy as jnp
from jax import lax
from jax.experimental import pallas as pl
from jax.experimental.pallas import tpu as pltpu
from jax.sharding import PartitionSpec as P

RANK = 64
SEQ = 64
TILE = 512
WIDE = 1792
VMEM_BYTES = 40 * 1024 * 1024
BIG_VMEM_BYTES = 58 * 1024 * 1024


def flatten(array):
    return array.reshape(-1, array.shape[-1])


def project(rows, table):
    return lax.dot_general(
        rows, table, (((1,), (1,)), ((), ())), preferred_element_type=jnp.float32
    )


def inner(left_side, right_side):
    return lax.dot_general(
        left_side,
        right_side,
        (((1,), (1,)), ((), ())),
        precision=lax.Precision.HIGHEST,
        preferred_element_type=jnp.float32,
    )


def gated_hidden(gate, up):
    gate_wide = gate.astype(jnp.float32)
    up_wide = up.astype(jnp.float32)
    return (gate_wide * jax.nn.sigmoid(gate_wide) * up_wide).astype(jnp.bfloat16)


def gradients(gate, up, hidden_grad):
    gate_wide = gate.astype(jnp.float32)
    up_wide = up.astype(jnp.float32)
    sigmoid_gate = jax.nn.sigmoid(gate_wide)
    silu_gate = gate_wide * sigmoid_gate
    gate_grad = (
        hidden_grad * up_wide * sigmoid_gate * (1.0 + gate_wide * (1.0 - sigmoid_gate))
    ).astype(jnp.bfloat16)
    up_grad = (hidden_grad * silu_gate).astype(jnp.bfloat16)
    return gate_grad, up_grad


def gradient_sides(gate, up, hidden_grad, proj_gate, proj_up):
    gate_grad, up_grad = gradients(gate, up, hidden_grad)
    return project(gate_grad, proj_gate), project(up_grad, proj_up)


def outer_sums(left_side, right_side, lengths):
    number = lengths.shape[0]
    length = left_side.shape[0] // number
    positions = lax.broadcasted_iota(jnp.int32, (number, length), 1)
    weights = (positions < lengths[:, None]).astype(jnp.float32)
    left_rows = left_side.reshape(number, length, left_side.shape[1]) * weights[:, :, None]
    right_rows = right_side.reshape(number, length, right_side.shape[1])
    summed = jnp.einsum("est,esu->etu", left_rows, right_rows, precision=lax.Precision.HIGHEST)
    return summed.reshape(number, -1)


def features(in_side, hidden_side, gate_side, up_side, out_side, lengths):
    return jnp.concatenate(
        [
            outer_sums(in_side, gate_side, lengths),
            outer_sums(in_side, up_side, lengths),
            outer_sums(hidden_side, out_side, lengths),
        ],
        axis=1,
    )


def gathering_plan(
    train_input,
    train_gate,
    train_up,
    train_outgrad,
    train_lengths,
    query_input,
    query_gate,
    query_up,
    query_outgrad,
    query_lengths,
    down_weight,
    proj_input,
    proj_outgrad,
    proj_hidden,
    proj_gate,
    proj_up,
):
    weight = lax.all_gather(down_weight, "dp", axis=1, tiled=True)

    def full_features(inputs, gate, up, outgrad, lengths):
        inputs, gate, up, outgrad = [flatten(a) for a in (inputs, gate, up, outgrad)]
        rows = lax.all_gather(outgrad, "tensor", axis=1, tiled=True)
        gate_side, up_side = gradient_sides(gate, up, project(rows, weight), proj_gate, proj_up)
        hidden_side = project(gated_hidden(gate, up), proj_hidden)
        sides = (
            project(inputs, proj_input),
            hidden_side,
            gate_side,
            up_side,
            project(outgrad, proj_outgrad),
        )
        return features(*lax.psum(sides, "tensor"), lengths)

    train_features = full_features(
        train_input, train_gate, train_up, train_outgrad, train_lengths
    )
    query_features = full_features(
        query_input, query_gate, query_up, query_outgrad, query_lengths
    )
    gathered = lax.all_gather(query_features, "dp", axis=0, tiled=True)
    return inner(train_features, gathered) / (RANK * SEQ)


ANYWHERE = pl.BlockSpec(memory_space=pl.ANY)
SCALARS = pl.BlockSpec(memory_space=pltpu.SMEM)
IN_VMEM = pl.BlockSpec(memory_space=pltpu.VMEM)


def params(limit=VMEM_BYTES):
    return pltpu.CompilerParams(vmem_limit_bytes=limit)


def cost(flops, arrays):
    return pl.CostEstimate(flops=1024, bytes_accessed=1024, transcendentals=0)


def tile_columns(number, block=0, tile=TILE):
    return pl.BlockSpec((number, tile), lambda i: (block, i))


def tile_rows(width, tile=TILE):
    return pl.BlockSpec((tile, width), lambda i: (i, 0))


def whole(shape):
    return pl.BlockSpec(shape, lambda i: tuple(0 for _ in shape))


def stacked_products(
    flags, pairs, far, weight_own, weight_sib, stacked, semaphores, held, weight_sems
):
    number = far.shape[1]
    step = pl.program_id(0)
    tiles = weight_own.shape[0] // TILE

    def weight_copies(tile):
        part = pl.ds(pl.multiple_of(tile * TILE, TILE), TILE)
        slot = lax.rem(tile, 3)
        return [
            pltpu.make_async_copy(
                weight.at[part], held.at[slot, side], weight_sems.at[slot, side]
            )
            for side, weight in enumerate((weight_own, weight_sib))
        ]

    @pl.when(step == 0)
    def _():
        slot = flags[1]
        far_copies = [
            pltpu.make_async_copy(
                far.at[i], stacked.at[jnp.bitwise_xor(slot, i), pl.ds(number, number)],
                semaphores.at[2 + i],
            )
            for i in range(2)
        ]
        for copy in far_copies:
            copy.start()
        for code, pair in enumerate(pairs):

            @pl.when(flags[0] == code)
            def _():
                copies = [
                    pltpu.make_async_copy(
                        pair[i], stacked.at[jnp.bitwise_xor(slot, i), pl.ds(0, number)],
                        semaphores.at[i],
                    )
                    for i in range(2)
                ]
                for copy in copies:
                    copy.start()
                for tile in range(2):
                    for copy in weight_copies(tile):
                        copy.start()
                for copy in copies:
                    copy.wait()

        for copy in far_copies:
            copy.wait()

    @pl.when(step + 2 < tiles)
    def _():
        for copy in weight_copies(step + 2):
            copy.start()

    for copy in weight_copies(step):
        copy.wait()
    slot = lax.rem(step, 3)
    return project(held[slot, 0], stacked[0]) + project(held[slot, 1], stacked[1])


def add_sides(hidden_grad, gate, up, proj_gate, proj_up, sides):
    gate_part, up_part = gradient_sides(gate, up, hidden_grad, proj_gate, proj_up)
    part = jnp.concatenate([gate_part, up_part], axis=1)
    first = pl.program_id(0) == 0

    @pl.when(first)
    def _():
        sides[...] = part

    @pl.when(jnp.logical_not(first))
    def _():
        sides[...] += part


def partial_kernel(
    flags, b0, b1, b2, b3, b4, b5, far, weight_own, weight_sib, near_sum, far_sum, *scratch
):
    pairs = ((b0, b1), (b2, b3), (b4, b5))
    total = stacked_products(flags, pairs, far, weight_own, weight_sib, *scratch)
    number = far.shape[1]
    near_sum[...] = total[:, :number]
    far_sum[...] = total[:, number:].astype(jnp.bfloat16)


def partial_sums(flags, blocks, far, weight_own, weight_sib):
    number, half = blocks[0].shape
    units = weight_own.shape[0]
    return pl.pallas_call(
        partial_kernel,
        grid=(units // TILE,),
        in_specs=[SCALARS] + [ANYWHERE] * 9,
        out_specs=[tile_rows(number)] * 2,
        out_shape=[
            jax.ShapeDtypeStruct((units, number), jnp.float32),
            jax.ShapeDtypeStruct((units, number), jnp.bfloat16),
        ],
        scratch_shapes=[
            pltpu.VMEM((2, 2 * number, half), jnp.bfloat16),
            pltpu.SemaphoreType.DMA((4,)),
            pltpu.VMEM((3, 2, TILE, half), jnp.bfloat16),
            pltpu.SemaphoreType.DMA((3, 2)),
        ],
        compiler_params=params(BIG_VMEM_BYTES),
        cost_estimate=cost(8 * number * half * units, (far, weight_own, weight_sib)),
    )(flags, *blocks, far, weight_own, weight_sib)


def finish_kernel(near_sum, returned, gate, up, proj_gate, proj_up, sides):
    hidden_grad = (near_sum[...] + returned[...].astype(jnp.float32)).T
    add_sides(hidden_grad, gate[...], up[...], proj_gate[...], proj_up[...], sides)


def finished_sides(near_sum, returned, gate, up, proj_gate, proj_up):
    units, number = near_sum.shape
    return pl.pallas_call(
        finish_kernel,
        grid=(units // WIDE,),
        in_specs=[tile_rows(number, WIDE)] * 2
        + [tile_columns(number, 0, WIDE)] * 2
        + [tile_columns(RANK, 0, WIDE)] * 2,
        out_specs=whole((number, 2 * RANK)),
        out_shape=jax.ShapeDtypeStruct((number, 2 * RANK), jnp.float32),
        compiler_params=params(),
        cost_estimate=cost(4 * number * RANK * units, (near_sum, returned, gate, up)),
    )(near_sum, returned, gate, up, proj_gate, proj_up)


def turn_kernel(gate, up, far_gate, far_up, gates, ups):
    number = gate.shape[0]
    for source, target, part in (
        (gate, gates, slice(0, number)),
        (up, ups, slice(0, number)),
        (far_gate, gates, slice(number, None)),
        (far_up, ups, slice(number, None)),
    ):
        target[:, part] = source[...].astype(jnp.float32).T.astype(jnp.bfloat16)


def turned(gate, up, far_gate, far_up):
    number, units = far_gate.shape
    shape = jax.ShapeDtypeStruct((units, 2 * number), jnp.bfloat16)
    return pl.pallas_call(
        turn_kernel,
        grid=(units // TILE,),
        in_specs=[tile_columns(number, 1)] * 2 + [tile_columns(number)] * 2,
        out_specs=[tile_rows(2 * number)] * 2,
        out_shape=[shape] * 2,
        compiler_params=params(),
        cost_estimate=cost(0, (gate, up)),
    )(gate, up, far_gate, far_up)


def lent_kernel(
    flags, b0, b1, b2, b3, b4, b5, far, weight_own, weight_sib, gates, ups, proj_gate, proj_up,
    near, away, *scratch,
):
    pairs = ((b0, b1), (b2, b3), (b4, b5))
    hidden_grad = stacked_products(flags, pairs, far, weight_own, weight_sib, *scratch)
    gate_grad, up_grad = gradients(gates[...], ups[...], hidden_grad)
    part = jnp.concatenate(
        [
            jnp.dot(proj_gate[...], gate_grad, preferred_element_type=jnp.float32),
            jnp.dot(proj_up[...], up_grad, preferred_element_type=jnp.float32),
        ],
        axis=0,
    )
    number = near.shape[1]
    first = pl.program_id(0) == 0

    @pl.when(first)
    def _():
        near[...] = part[:, :number]
        away[...] = part[:, number:]

    @pl.when(jnp.logical_not(first))
    def _():
        near[...] += part[:, :number]
        away[...] += part[:, number:]


def lent_sides(flags, blocks, far, weight_own, weight_sib, gates, ups, proj_gate, proj_up):
    number, half = blocks[0].shape
    units = weight_own.shape[0]
    return pl.pallas_call(
        lent_kernel,
        grid=(units // TILE,),
        in_specs=[SCALARS]
        + [ANYWHERE] * 9
        + [tile_rows(2 * number)] * 2
        + [tile_columns(RANK)] * 2,
        out_specs=[whole((2 * RANK, number))] * 2,
        out_shape=[jax.ShapeDtypeStruct((2 * RANK, number), jnp.float32)] * 2,
        scratch_shapes=[
            pltpu.VMEM((2, 2 * number, half), jnp.bfloat16),
            pltpu.SemaphoreType.DMA((4,)),
            pltpu.VMEM((3, 2, TILE, half), jnp.bfloat16),
            pltpu.SemaphoreType.DMA((3, 2)),
        ],
        compiler_params=params(BIG_VMEM_BYTES),
        cost_estimate=cost(8 * number * half * units, (far, weight_own, weight_sib)),
    )(flags, *blocks, far, weight_own, weight_sib, gates, ups, proj_gate, proj_up)


def early_kernel(
    t_input, q_input, t_outgrad, q_outgrad, proj_input, proj_outgrad, t_gate, t_up, q_gate, q_up,
    proj_hidden, in_out, hidden,
):
    number = t_input.shape[0]
    t_hidden = project(gated_hidden(t_gate[...], t_up[...]), proj_hidden[...])
    q_hidden = project(gated_hidden(q_gate[...], q_up[...]), proj_hidden[...])
    first = pl.program_id(0) == 0

    @pl.when(first)
    def _():
        for inputs, outgrad, part in (
            (t_input, t_outgrad, slice(0, number)),
            (q_input, q_outgrad, slice(number, None)),
        ):
            in_out[part, :] = jnp.concatenate(
                [
                    project(inputs[...], proj_input[...]),
                    project(outgrad[...], proj_outgrad[...]),
                ],
                axis=1,
            )
        hidden[:number, :] = t_hidden
        hidden[number:, :] = q_hidden

    @pl.when(jnp.logical_not(first))
    def _():
        hidden[:number, :] += t_hidden
        hidden[number:, :] += q_hidden


def early_sides(
    t_input, q_input, t_outgrad, q_outgrad, proj_input, proj_outgrad, t_gate, t_up, q_gate, q_up,
    proj_hidden,
):
    total, units = t_gate.shape[0] + q_gate.shape[0], t_gate.shape[1]
    wide = (t_input, q_input, t_outgrad, q_outgrad, proj_input, proj_outgrad)
    tiled = (t_gate, t_up, q_gate, q_up, proj_hidden)
    shapes = ((total, 2 * RANK), (total, RANK))
    return pl.pallas_call(
        early_kernel,
        grid=(units // TILE,),
        in_specs=[whole(a.shape) for a in wide] + [tile_columns(a.shape[0]) for a in tiled],
        out_specs=[whole(shape) for shape in shapes],
        out_shape=[jax.ShapeDtypeStruct(shape, jnp.float32) for shape in shapes],
        compiler_params=params(),
        cost_estimate=cost(2 * total * RANK * units, wide + tiled),
    )(*wide, *tiled)


def outer_sum(left_side, right_side, weight):
    return lax.dot_general(
        left_side * weight,
        right_side,
        (((0,), (0,)), ((), ())),
        precision=lax.Precision.HIGHEST,
        preferred_element_type=jnp.float32,
    )


def example_features(in_side, hidden_side, gate_side, up_side, out_side, length):
    positions = lax.broadcasted_iota(jnp.int32, (SEQ, RANK), 0)
    weight = (positions < length).astype(jnp.float32)
    return (
        outer_sum(in_side, gate_side, weight),
        outer_sum(in_side, up_side, weight),
        outer_sum(hidden_side, out_side, weight),
    )


def query_kernel(lengths, in_out, sums, found):
    for e in range(found.shape[0]):
        part = slice(e * SEQ, (e + 1) * SEQ)
        three = example_features(
            in_out[part, :RANK],
            sums[part, 2 * RANK :],
            sums[part, :RANK],
            sums[part, RANK : 2 * RANK],
            in_out[part, RANK:],
            lengths[e],
        )
        for segment in range(3):
            found[e, segment * RANK : (segment + 1) * RANK, :] = three[segment]


def query_features(lengths, in_out, sums):
    return pl.pallas_call(
        query_kernel,
        in_specs=[SCALARS, IN_VMEM, IN_VMEM],
        out_specs=IN_VMEM,
        out_shape=jax.ShapeDtypeStruct((lengths.shape[0], 3 * RANK, RANK), jnp.float32),
        compiler_params=params(),
    )(lengths, in_out, sums)


def score_kernel(
    lengths, place, in_out, hidden, early, near, far, q0, q1, q2, q3, scores
):
    queries = q0.shape[0]
    shape = scores.shape
    row = lax.broadcasted_iota(jnp.int32, shape, 0)
    column = lax.broadcasted_iota(jnp.int32, shape, 1)
    gradient = jnp.concatenate([early[...], (near[...] + far[...]).T], axis=0)
    total = jnp.zeros(shape, jnp.float32)
    for e in range(shape[0]):
        part = slice(e * SEQ, (e + 1) * SEQ)
        three = jnp.concatenate(
            example_features(
                in_out[part, :RANK],
                hidden[part, :],
                gradient[part, :RANK],
                gradient[part, RANK:],
                in_out[part, RANK:],
                lengths[e],
            ),
            axis=0,
        )
        for step, found in enumerate((q0, q1, q2, q3)):
            for j in range(queries):
                value = jnp.sum(three * found[j], keepdims=True)
                here = (row == e) & (
                    column == queries * jnp.bitwise_xor(place[0], step) + j
                )
                total = total + jnp.where(here, value, 0.0)
    scores[...] = total


def partial_scores(lengths, place, in_out, hidden, early, near, far, found):
    number = lengths.shape[0]
    return pl.pallas_call(
        score_kernel,
        in_specs=[SCALARS] * 2 + [IN_VMEM] * 9,
        out_specs=IN_VMEM,
        out_shape=jax.ShapeDtypeStruct((number, 4 * found[0].shape[0]), jnp.float32),
        compiler_params=params(),
    )(lengths, place, in_out, hidden, early, near, far, *found)


def after(value, *others):
    return lax.optimization_barrier((value, *others))[0]


def moving_plan(
    train_input,
    train_gate,
    train_up,
    train_outgrad,
    train_lengths,
    query_input,
    query_gate,
    query_up,
    query_outgrad,
    query_lengths,
    down_weight,
    proj_input,
    proj_outgrad,
    proj_hidden,
    proj_gate,
    proj_up,
):
    t = lax.axis_index("tensor")
    d = lax.axis_index("dp")
    x, core, upper = d // 2, d % 2, t // 2
    at_home = x == upper
    inner_chip = (t == 1) | (t == 2)
    near_code = jnp.where(at_home, 0, jnp.where(inner_chip, 1, 2))
    first_parity = jnp.where(at_home, t % 2, upper)
    flags = jnp.stack([near_code, first_parity ^ core]).astype(jnp.int32)
    place = jnp.stack([d]).astype(jnp.int32)

    to_core = functools.partial(lax.ppermute, axis_name="dp", perm=[(i, i ^ 1) for i in range(4)])
    to_chip = functools.partial(lax.ppermute, axis_name="dp", perm=[(i, i ^ 2) for i in range(4)])
    outer = functools.partial(
        lax.ppermute, axis_name="tensor", perm=[(i, i ^ 1) for i in range(4)]
    )
    across = functools.partial(
        lax.ppermute, axis_name="tensor", perm=[(i, i ^ 2) for i in range(4)]
    )
    opposite = functools.partial(
        lax.ppermute, axis_name="tensor", perm=[(i, 3 - i) for i in range(4)]
    )
    middle = functools.partial(
        lax.ppermute,
        axis_name=("tensor", "dp"),
        perm=[
            (4 * i + j, 4 * (3 - i) + j) if i in (1, 2) else (4 * i + j, 4 * i + (j ^ 1))
            for i in range(4)
            for j in range(4)
        ],
    )

    q_input, q_gate, q_up, q_outgrad = [
        flatten(a) for a in (query_input, query_gate, query_up, query_outgrad)
    ]
    t_input, t_gate, t_up, t_outgrad = [
        flatten(a) for a in (train_input, train_gate, train_up, train_outgrad)
    ]
    examples = train_lengths.shape[0] // 2
    cut = examples * SEQ

    def first_hops(own):
        return own, outer(own), across(own)

    def last_hops(own, one, two):
        mid = middle(after(own, two))
        return own, one, mid, two, two, outer(after(two, one))

    def crossing_pair(own, one, second_inner, third_inner, second_outer, third_outer):
        def choose(within, beyond_inner, beyond_outer):
            beyond = jnp.where(inner_chip, beyond_inner, beyond_outer)
            return jnp.where(at_home, beyond, within)

        return jnp.stack(
            [choose(own, second_inner, second_outer), choose(one, third_inner, third_outer)]
        )

    weight_own, weight_sib = down_weight, to_core(down_weight)
    q_hops = first_hops(q_outgrad)
    far_gate = to_chip(t_gate[cut:])
    own_in_out, hidden = early_sides(
        t_input, q_input, t_outgrad, q_outgrad, proj_input, proj_outgrad, t_gate, t_up, q_gate,
        q_up, proj_hidden,
    )

    q_blocks = last_hops(*q_hops[:2], after(q_hops[2], own_in_out))
    a_hops = first_hops(after(t_outgrad[:cut], q_hops[2], far_gate))
    far_up = to_chip(after(t_up[cut:], far_gate))
    q_send = after(crossing_pair(*q_blocks), far_up)
    q_far = to_chip(q_send)
    a_blocks = last_hops(*a_hops[:2], after(a_hops[2], q_send))

    b_hops = first_hops(after(t_outgrad[cut:], a_hops[2]))
    gates, ups = turned(t_gate, t_up, far_gate, far_up)
    a_send = crossing_pair(*a_blocks[:5], after(a_blocks[5], q_far, gates))
    a_far = to_chip(a_send)
    q_near_sum, q_far_sum = partial_sums(
        flags, q_blocks, after(q_far, a_send), weight_own, weight_sib
    )
    q_returned = to_chip(after(q_far_sum, a_far))
    b_blocks = last_hops(*b_hops[:2], after(b_hops[2], q_far_sum))
    b_send = crossing_pair(*b_blocks)
    b_far = to_chip(b_send)
    a_near_sum, a_far_sum = partial_sums(
        flags, a_blocks, after(a_far, b_send), weight_own, weight_sib
    )
    a_returned = to_chip(a_far_sum)
    in_out = own_in_out + outer(after(own_in_out, b_send))
    q_gradient = finished_sides(
        q_near_sum, after(q_returned, a_far_sum), q_gate, q_up, proj_gate, proj_up
    )
    q_sums = jnp.concatenate([q_gradient, hidden[2 * cut :]], axis=1)
    q_sums = q_sums + outer(q_sums)
    b_near, b_away = lent_sides(
        after(flags, q_sums, in_out), b_blocks, b_far, weight_own, weight_sib, gates, ups,
        proj_gate, proj_up,
    )
    b_far_sides = to_chip(b_away)
    in_out = in_out + after(across(in_out), b_near)
    q_sums = q_sums + after(across(q_sums), b_near)
    own_found = query_features(query_lengths, in_out[2 * cut :], q_sums)
    chip_found = to_chip(own_found)
    found = (own_found, to_core(own_found), chip_found, to_core(after(chip_found, b_far_sides)))
    a_gradient = finished_sides(a_near_sum, a_returned, t_gate, t_up, proj_gate, proj_up)
    own_scores = partial_scores(
        train_lengths, place, in_out[: 2 * cut], hidden[: 2 * cut], a_gradient, b_near,
        b_far_sides, found,
    )
    scores = own_scores + outer(own_scores) + across(own_scores) + opposite(own_scores)
    return scores / (RANK * SEQ)


def solution(mesh):
    tensor, dp = mesh.shape["tensor"], mesh.shape["dp"]

    def per_device(*arguments):
        if tensor == 4 and dp == 4:
            return moving_plan(*arguments)
        return gathering_plan(*arguments)

    in_specs = (
        P(("parts", "dp"), None, "tensor"),
        P(("parts", "dp"), None, "tensor"),
        P(("parts", "dp"), None, "tensor"),
        P(("parts", "dp"), None, "tensor"),
        P(("parts", "dp")),
        P(("parts", "dp"), None, "tensor"),
        P(("parts", "dp"), None, "tensor"),
        P(("parts", "dp"), None, "tensor"),
        P(("parts", "dp"), None, "tensor"),
        P(("parts", "dp")),
        P("tensor", "dp"),
        P(None, "tensor"),
        P(None, "tensor"),
        P(None, "tensor"),
        P(None, "tensor"),
        P(None, "tensor"),
    )
    out_specs = P(("parts", "dp"), None)
    return jax.shard_map(
        per_device, mesh=mesh, in_specs=in_specs, out_specs=out_specs, check_vma=False
    )
```

```python
import functools

import jax
import jax.numpy as jnp
from jax import lax
from jax.experimental import pallas as pl
from jax.experimental.pallas import tpu as pltpu
from jax.sharding import PartitionSpec as P

RANK = 64
SEQ = 64
TILE = 512
WIDE = 1792
NARROW = 256
SLOTS = 5
VMEM_BYTES = 40 * 1024 * 1024
BIG_VMEM_BYTES = 58 * 1024 * 1024


def flatten(array):
    return array.reshape(-1, array.shape[-1])


def project(rows, table):
    return lax.dot_general(
        rows, table, (((1,), (1,)), ((), ())), preferred_element_type=jnp.float32
    )


def inner(left_side, right_side):
    return lax.dot_general(
        left_side,
        right_side,
        (((1,), (1,)), ((), ())),
        precision=lax.Precision.HIGHEST,
        preferred_element_type=jnp.float32,
    )


def gated_hidden(gate, up):
    gate_wide = gate.astype(jnp.float32)
    up_wide = up.astype(jnp.float32)
    return (gate_wide * jax.nn.sigmoid(gate_wide) * up_wide).astype(jnp.bfloat16)


def gradients(gate, up, hidden_grad):
    gate_wide = gate.astype(jnp.float32)
    up_wide = up.astype(jnp.float32)
    sigmoid_gate = jax.nn.sigmoid(gate_wide)
    silu_gate = gate_wide * sigmoid_gate
    gate_grad = (
        hidden_grad * up_wide * sigmoid_gate * (1.0 + gate_wide * (1.0 - sigmoid_gate))
    ).astype(jnp.bfloat16)
    up_grad = (hidden_grad * silu_gate).astype(jnp.bfloat16)
    return gate_grad, up_grad


def gradient_sides(gate, up, hidden_grad, proj_gate, proj_up):
    gate_grad, up_grad = gradients(gate, up, hidden_grad)
    return project(gate_grad, proj_gate), project(up_grad, proj_up)


def outer_sums(left_side, right_side, lengths):
    number = lengths.shape[0]
    length = left_side.shape[0] // number
    positions = lax.broadcasted_iota(jnp.int32, (number, length), 1)
    weights = (positions < lengths[:, None]).astype(jnp.float32)
    left_rows = left_side.reshape(number, length, left_side.shape[1]) * weights[:, :, None]
    right_rows = right_side.reshape(number, length, right_side.shape[1])
    summed = jnp.einsum("est,esu->etu", left_rows, right_rows, precision=lax.Precision.HIGHEST)
    return summed.reshape(number, -1)


def features(in_side, hidden_side, gate_side, up_side, out_side, lengths):
    return jnp.concatenate(
        [
            outer_sums(in_side, gate_side, lengths),
            outer_sums(in_side, up_side, lengths),
            outer_sums(hidden_side, out_side, lengths),
        ],
        axis=1,
    )


def gathering_plan(
    train_input,
    train_gate,
    train_up,
    train_outgrad,
    train_lengths,
    query_input,
    query_gate,
    query_up,
    query_outgrad,
    query_lengths,
    down_weight,
    proj_input,
    proj_outgrad,
    proj_hidden,
    proj_gate,
    proj_up,
):
    weight = lax.all_gather(down_weight, "dp", axis=1, tiled=True)

    def full_features(inputs, gate, up, outgrad, lengths):
        inputs, gate, up, outgrad = [flatten(a) for a in (inputs, gate, up, outgrad)]
        rows = lax.all_gather(outgrad, "tensor", axis=1, tiled=True)
        gate_side, up_side = gradient_sides(gate, up, project(rows, weight), proj_gate, proj_up)
        hidden_side = project(gated_hidden(gate, up), proj_hidden)
        sides = (
            project(inputs, proj_input),
            hidden_side,
            gate_side,
            up_side,
            project(outgrad, proj_outgrad),
        )
        return features(*lax.psum(sides, "tensor"), lengths)

    train_features = full_features(
        train_input, train_gate, train_up, train_outgrad, train_lengths
    )
    query_features = full_features(
        query_input, query_gate, query_up, query_outgrad, query_lengths
    )
    gathered = lax.all_gather(query_features, "dp", axis=0, tiled=True)
    return inner(train_features, gathered) / (RANK * SEQ)


ANYWHERE = pl.BlockSpec(memory_space=pl.ANY)
SCALARS = pl.BlockSpec(memory_space=pltpu.SMEM)
IN_VMEM = pl.BlockSpec(memory_space=pltpu.VMEM)


def params(limit=VMEM_BYTES):
    return pltpu.CompilerParams(vmem_limit_bytes=limit)


def cost(flops, arrays):
    return pl.CostEstimate(flops=1024, bytes_accessed=1024, transcendentals=0)


def tile_columns(number, block=0, tile=TILE):
    return pl.BlockSpec((number, tile), lambda i: (block, i))


def tile_rows(width, tile=TILE):
    return pl.BlockSpec((tile, width), lambda i: (i, 0))


def whole(shape):
    return pl.BlockSpec(shape, lambda i: tuple(0 for _ in shape))


def stacked_products(
    flags, pairs, far, weight_own, weight_sib, stacked, semaphores, held, weight_sems
):
    number = far.shape[1]
    step = pl.program_id(0)
    tiles = weight_own.shape[0] // NARROW

    def weight_copies(tile):
        part = pl.ds(pl.multiple_of(tile * NARROW, NARROW), NARROW)
        slot = lax.rem(tile, SLOTS)
        return [
            pltpu.make_async_copy(
                weight.at[part], held.at[slot, side], weight_sems.at[slot, side]
            )
            for side, weight in enumerate((weight_own, weight_sib))
        ]

    @pl.when(step == 0)
    def _():
        slot = flags[1]
        far_copies = [
            pltpu.make_async_copy(
                far.at[i], stacked.at[jnp.bitwise_xor(slot, i), pl.ds(number, number)],
                semaphores.at[2 + i],
            )
            for i in range(2)
        ]
        for copy in far_copies:
            copy.start()
        for code, pair in enumerate(pairs):

            @pl.when(flags[0] == code)
            def _():
                copies = [
                    pltpu.make_async_copy(
                        pair[i], stacked.at[jnp.bitwise_xor(slot, i), pl.ds(0, number)],
                        semaphores.at[i],
                    )
                    for i in range(2)
                ]
                for copy in copies:
                    copy.start()
                for tile in range(SLOTS - 1):
                    for copy in weight_copies(tile):
                        copy.start()
                for copy in copies:
                    copy.wait()

        for copy in far_copies:
            copy.wait()

    @pl.when(step + SLOTS - 1 < tiles)
    def _():
        for copy in weight_copies(step + SLOTS - 1):
            copy.start()

    for copy in weight_copies(step):
        copy.wait()
    slot = lax.rem(step, SLOTS)
    return project(held[slot, 0], stacked[0]) + project(held[slot, 1], stacked[1])


def add_sides(hidden_grad, gate, up, proj_gate, proj_up, sides):
    gate_part, up_part = gradient_sides(gate, up, hidden_grad, proj_gate, proj_up)
    part = jnp.concatenate([gate_part, up_part], axis=1)
    first = pl.program_id(0) == 0

    @pl.when(first)
    def _():
        sides[...] = part

    @pl.when(jnp.logical_not(first))
    def _():
        sides[...] += part


def partial_kernel(
    flags, b0, b1, b2, b3, b4, b5, far, weight_own, weight_sib, near_sum, far_sum, *scratch
):
    pairs = ((b0, b1), (b2, b3), (b4, b5))
    total = stacked_products(flags, pairs, far, weight_own, weight_sib, *scratch)
    number = far.shape[1]
    near_sum[...] = total[:, :number]
    far_sum[...] = total[:, number:].astype(jnp.bfloat16)


def partial_sums(flags, blocks, far, weight_own, weight_sib):
    number, half = blocks[0].shape
    units = weight_own.shape[0]
    return pl.pallas_call(
        partial_kernel,
        grid=(units // NARROW,),
        in_specs=[SCALARS] + [ANYWHERE] * 9,
        out_specs=[tile_rows(number, NARROW)] * 2,
        out_shape=[
            jax.ShapeDtypeStruct((units, number), jnp.float32),
            jax.ShapeDtypeStruct((units, number), jnp.bfloat16),
        ],
        scratch_shapes=[
            pltpu.VMEM((2, 2 * number, half), jnp.bfloat16),
            pltpu.SemaphoreType.DMA((4,)),
            pltpu.VMEM((SLOTS, 2, NARROW, half), jnp.bfloat16),
            pltpu.SemaphoreType.DMA((SLOTS, 2)),
        ],
        compiler_params=params(BIG_VMEM_BYTES),
        cost_estimate=cost(8 * number * half * units, (far, weight_own, weight_sib)),
    )(flags, *blocks, far, weight_own, weight_sib)


def finish_kernel(near_sum, returned, gate, up, proj_gate, proj_up, sides):
    hidden_grad = (near_sum[...] + returned[...].astype(jnp.float32)).T
    add_sides(hidden_grad, gate[...], up[...], proj_gate[...], proj_up[...], sides)


def finished_sides(near_sum, returned, gate, up, proj_gate, proj_up):
    units, number = near_sum.shape
    return pl.pallas_call(
        finish_kernel,
        grid=(units // WIDE,),
        in_specs=[tile_rows(number, WIDE)] * 2
        + [tile_columns(number, 0, WIDE)] * 2
        + [tile_columns(RANK, 0, WIDE)] * 2,
        out_specs=whole((number, 2 * RANK)),
        out_shape=jax.ShapeDtypeStruct((number, 2 * RANK), jnp.float32),
        compiler_params=params(),
        cost_estimate=cost(4 * number * RANK * units, (near_sum, returned, gate, up)),
    )(near_sum, returned, gate, up, proj_gate, proj_up)


def turn_kernel(gate, up, far_gate, far_up, gates, ups):
    number = gate.shape[0]
    for source, target, part in (
        (gate, gates, slice(0, number)),
        (up, ups, slice(0, number)),
        (far_gate, gates, slice(number, None)),
        (far_up, ups, slice(number, None)),
    ):
        target[:, part] = source[...].astype(jnp.float32).T.astype(jnp.bfloat16)


def turned(gate, up, far_gate, far_up):
    number, units = far_gate.shape
    shape = jax.ShapeDtypeStruct((units, 2 * number), jnp.bfloat16)
    return pl.pallas_call(
        turn_kernel,
        grid=(units // TILE,),
        in_specs=[tile_columns(number, 1)] * 2 + [tile_columns(number)] * 2,
        out_specs=[tile_rows(2 * number)] * 2,
        out_shape=[shape] * 2,
        compiler_params=params(),
        cost_estimate=cost(0, (gate, up)),
    )(gate, up, far_gate, far_up)


def lent_kernel(
    flags, b0, b1, b2, b3, b4, b5, far, weight_own, weight_sib, gates, ups, proj_gate, proj_up,
    near, away, *scratch,
):
    pairs = ((b0, b1), (b2, b3), (b4, b5))
    hidden_grad = stacked_products(flags, pairs, far, weight_own, weight_sib, *scratch)
    gate_grad, up_grad = gradients(gates[...], ups[...], hidden_grad)
    part = jnp.concatenate(
        [
            jnp.dot(proj_gate[...], gate_grad, preferred_element_type=jnp.float32),
            jnp.dot(proj_up[...], up_grad, preferred_element_type=jnp.float32),
        ],
        axis=0,
    )
    number = near.shape[1]
    first = pl.program_id(0) == 0

    @pl.when(first)
    def _():
        near[...] = part[:, :number]
        away[...] = part[:, number:]

    @pl.when(jnp.logical_not(first))
    def _():
        near[...] += part[:, :number]
        away[...] += part[:, number:]


def lent_sides(flags, blocks, far, weight_own, weight_sib, gates, ups, proj_gate, proj_up):
    number, half = blocks[0].shape
    units = weight_own.shape[0]
    return pl.pallas_call(
        lent_kernel,
        grid=(units // NARROW,),
        in_specs=[SCALARS]
        + [ANYWHERE] * 9
        + [tile_rows(2 * number, NARROW)] * 2
        + [tile_columns(RANK, 0, NARROW)] * 2,
        out_specs=[whole((2 * RANK, number))] * 2,
        out_shape=[jax.ShapeDtypeStruct((2 * RANK, number), jnp.float32)] * 2,
        scratch_shapes=[
            pltpu.VMEM((2, 2 * number, half), jnp.bfloat16),
            pltpu.SemaphoreType.DMA((4,)),
            pltpu.VMEM((SLOTS, 2, NARROW, half), jnp.bfloat16),
            pltpu.SemaphoreType.DMA((SLOTS, 2)),
        ],
        compiler_params=params(BIG_VMEM_BYTES),
        cost_estimate=cost(8 * number * half * units, (far, weight_own, weight_sib)),
    )(flags, *blocks, far, weight_own, weight_sib, gates, ups, proj_gate, proj_up)


def early_kernel(
    t_input, q_input, t_outgrad, q_outgrad, proj_input, proj_outgrad, t_gate, t_up, q_gate, q_up,
    proj_hidden, in_out, hidden,
):
    number = t_input.shape[0]
    t_hidden = project(gated_hidden(t_gate[...], t_up[...]), proj_hidden[...])
    q_hidden = project(gated_hidden(q_gate[...], q_up[...]), proj_hidden[...])
    first = pl.program_id(0) == 0

    @pl.when(first)
    def _():
        for inputs, outgrad, part in (
            (t_input, t_outgrad, slice(0, number)),
            (q_input, q_outgrad, slice(number, None)),
        ):
            in_out[part, :] = jnp.concatenate(
                [
                    project(inputs[...], proj_input[...]),
                    project(outgrad[...], proj_outgrad[...]),
                ],
                axis=1,
            )
        hidden[:number, :] = t_hidden
        hidden[number:, :] = q_hidden

    @pl.when(jnp.logical_not(first))
    def _():
        hidden[:number, :] += t_hidden
        hidden[number:, :] += q_hidden


def early_sides(
    t_input, q_input, t_outgrad, q_outgrad, proj_input, proj_outgrad, t_gate, t_up, q_gate, q_up,
    proj_hidden,
):
    total, units = t_gate.shape[0] + q_gate.shape[0], t_gate.shape[1]
    wide = (t_input, q_input, t_outgrad, q_outgrad, proj_input, proj_outgrad)
    tiled = (t_gate, t_up, q_gate, q_up, proj_hidden)
    shapes = ((total, 2 * RANK), (total, RANK))
    return pl.pallas_call(
        early_kernel,
        grid=(units // TILE,),
        in_specs=[whole(a.shape) for a in wide] + [tile_columns(a.shape[0]) for a in tiled],
        out_specs=[whole(shape) for shape in shapes],
        out_shape=[jax.ShapeDtypeStruct(shape, jnp.float32) for shape in shapes],
        compiler_params=params(),
        cost_estimate=cost(2 * total * RANK * units, wide + tiled),
    )(*wide, *tiled)


def outer_sum(left_side, right_side, weight):
    return lax.dot_general(
        left_side * weight,
        right_side,
        (((0,), (0,)), ((), ())),
        precision=lax.Precision.HIGHEST,
        preferred_element_type=jnp.float32,
    )


def example_features(in_side, hidden_side, gate_side, up_side, out_side, length):
    positions = lax.broadcasted_iota(jnp.int32, (SEQ, RANK), 0)
    weight = (positions < length).astype(jnp.float32)
    return (
        outer_sum(in_side, gate_side, weight),
        outer_sum(in_side, up_side, weight),
        outer_sum(hidden_side, out_side, weight),
    )


def query_kernel(lengths, in_out, sums, found):
    for e in range(found.shape[0]):
        part = slice(e * SEQ, (e + 1) * SEQ)
        three = example_features(
            in_out[part, :RANK],
            sums[part, 2 * RANK :],
            sums[part, :RANK],
            sums[part, RANK : 2 * RANK],
            in_out[part, RANK:],
            lengths[e],
        )
        for segment in range(3):
            found[e, segment * RANK : (segment + 1) * RANK, :] = three[segment]


def query_features(lengths, in_out, sums):
    return pl.pallas_call(
        query_kernel,
        in_specs=[SCALARS, IN_VMEM, IN_VMEM],
        out_specs=IN_VMEM,
        out_shape=jax.ShapeDtypeStruct((lengths.shape[0], 3 * RANK, RANK), jnp.float32),
        compiler_params=params(),
    )(lengths, in_out, sums)


def score_kernel(
    lengths, place, in_out, hidden, early, near, far, q0, q1, q2, q3, scores
):
    queries = q0.shape[0]
    shape = scores.shape
    row = lax.broadcasted_iota(jnp.int32, shape, 0)
    column = lax.broadcasted_iota(jnp.int32, shape, 1)
    gradient = jnp.concatenate([early[...], (near[...] + far[...]).T], axis=0)
    total = jnp.zeros(shape, jnp.float32)
    for e in range(shape[0]):
        part = slice(e * SEQ, (e + 1) * SEQ)
        three = jnp.concatenate(
            example_features(
                in_out[part, :RANK],
                hidden[part, :],
                gradient[part, :RANK],
                gradient[part, RANK:],
                in_out[part, RANK:],
                lengths[e],
            ),
            axis=0,
        )
        for step, found in enumerate((q0, q1, q2, q3)):
            for j in range(queries):
                value = jnp.sum(three * found[j], keepdims=True)
                here = (row == e) & (
                    column == queries * jnp.bitwise_xor(place[0], step) + j
                )
                total = total + jnp.where(here, value, 0.0)
    scores[...] = total


def partial_scores(lengths, place, in_out, hidden, early, near, far, found):
    number = lengths.shape[0]
    return pl.pallas_call(
        score_kernel,
        in_specs=[SCALARS] * 2 + [IN_VMEM] * 9,
        out_specs=IN_VMEM,
        out_shape=jax.ShapeDtypeStruct((number, 4 * found[0].shape[0]), jnp.float32),
        compiler_params=params(),
    )(lengths, place, in_out, hidden, early, near, far, *found)


def after(value, *others):
    return lax.optimization_barrier((value, *others))[0]


def moving_plan(
    train_input,
    train_gate,
    train_up,
    train_outgrad,
    train_lengths,
    query_input,
    query_gate,
    query_up,
    query_outgrad,
    query_lengths,
    down_weight,
    proj_input,
    proj_outgrad,
    proj_hidden,
    proj_gate,
    proj_up,
):
    t = lax.axis_index("tensor")
    d = lax.axis_index("dp")
    x, core, upper = d // 2, d % 2, t // 2
    at_home = x == upper
    inner_chip = (t == 1) | (t == 2)
    near_code = jnp.where(at_home, 0, jnp.where(inner_chip, 1, 2))
    first_parity = jnp.where(at_home, t % 2, upper)
    flags = jnp.stack([near_code, first_parity ^ core]).astype(jnp.int32)
    place = jnp.stack([d]).astype(jnp.int32)

    to_core = functools.partial(lax.ppermute, axis_name="dp", perm=[(i, i ^ 1) for i in range(4)])
    to_chip = functools.partial(lax.ppermute, axis_name="dp", perm=[(i, i ^ 2) for i in range(4)])
    outer = functools.partial(
        lax.ppermute, axis_name="tensor", perm=[(i, i ^ 1) for i in range(4)]
    )
    across = functools.partial(
        lax.ppermute, axis_name="tensor", perm=[(i, i ^ 2) for i in range(4)]
    )
    opposite = functools.partial(
        lax.ppermute, axis_name="tensor", perm=[(i, 3 - i) for i in range(4)]
    )
    middle = functools.partial(
        lax.ppermute,
        axis_name=("tensor", "dp"),
        perm=[
            (4 * i + j, 4 * (3 - i) + j) if i in (1, 2) else (4 * i + j, 4 * i + (j ^ 1))
            for i in range(4)
            for j in range(4)
        ],
    )

    q_input, q_gate, q_up, q_outgrad = [
        flatten(a) for a in (query_input, query_gate, query_up, query_outgrad)
    ]
    t_input, t_gate, t_up, t_outgrad = [
        flatten(a) for a in (train_input, train_gate, train_up, train_outgrad)
    ]
    examples = train_lengths.shape[0] // 2
    cut = examples * SEQ

    def first_hops(own):
        return own, outer(own), across(own)

    def last_hops(own, one, two):
        mid = middle(after(own, two))
        return own, one, mid, two, two, outer(after(two, one))

    def crossing_pair(own, one, second_inner, third_inner, second_outer, third_outer):
        def choose(within, beyond_inner, beyond_outer):
            beyond = jnp.where(inner_chip, beyond_inner, beyond_outer)
            return jnp.where(at_home, beyond, within)

        return jnp.stack(
            [choose(own, second_inner, second_outer), choose(one, third_inner, third_outer)]
        )

    weight_own, weight_sib = down_weight, to_core(down_weight)
    q_hops = first_hops(q_outgrad)
    far_gate = to_chip(t_gate[cut:])
    own_in_out, hidden = early_sides(
        t_input, q_input, t_outgrad, q_outgrad, proj_input, proj_outgrad, t_gate, t_up, q_gate,
        q_up, proj_hidden,
    )

    q_blocks = last_hops(*q_hops[:2], after(q_hops[2], own_in_out))
    a_hops = first_hops(after(t_outgrad[:cut], q_hops[2], far_gate))
    far_up = to_chip(after(t_up[cut:], far_gate))
    q_send = after(crossing_pair(*q_blocks), far_up)
    q_far = to_chip(q_send)
    a_blocks = last_hops(*a_hops[:2], after(a_hops[2], q_send))

    b_hops = first_hops(after(t_outgrad[cut:], a_hops[2]))
    gates, ups = turned(t_gate, t_up, far_gate, far_up)
    a_send = crossing_pair(*a_blocks[:5], after(a_blocks[5], q_far, gates))
    a_far = to_chip(a_send)
    q_near_sum, q_far_sum = partial_sums(
        flags, q_blocks, after(q_far, a_send), weight_own, weight_sib
    )
    q_returned = to_chip(after(q_far_sum, a_far))
    b_blocks = last_hops(*b_hops[:2], after(b_hops[2], q_far_sum))
    b_send = crossing_pair(*b_blocks)
    b_far = to_chip(b_send)
    a_near_sum, a_far_sum = partial_sums(
        flags, a_blocks, after(a_far, b_send), weight_own, weight_sib
    )
    a_returned = to_chip(a_far_sum)
    in_out = own_in_out + outer(after(own_in_out, b_send))
    q_gradient = finished_sides(
        q_near_sum, after(q_returned, a_far_sum), q_gate, q_up, proj_gate, proj_up
    )
    q_sums = jnp.concatenate([q_gradient, hidden[2 * cut :]], axis=1)
    q_sums = q_sums + outer(q_sums)
    b_near, b_away = lent_sides(
        after(flags, q_sums, in_out), b_blocks, b_far, weight_own, weight_sib, gates, ups,
        proj_gate, proj_up,
    )
    b_far_sides = to_chip(b_away)
    in_out = in_out + after(across(in_out), b_near)
    q_sums = q_sums + after(across(q_sums), b_near)
    own_found = query_features(query_lengths, in_out[2 * cut :], q_sums)
    chip_found = to_chip(own_found)
    found = (own_found, to_core(own_found), chip_found, to_core(after(chip_found, b_far_sides)))
    a_gradient = finished_sides(a_near_sum, a_returned, t_gate, t_up, proj_gate, proj_up)
    own_scores = partial_scores(
        train_lengths, place, in_out[: 2 * cut], hidden[: 2 * cut], a_gradient, b_near,
        b_far_sides, found,
    )
    scores = own_scores + outer(own_scores) + across(own_scores) + opposite(own_scores)
    return scores / (RANK * SEQ)


def solution(mesh):
    tensor, dp = mesh.shape["tensor"], mesh.shape["dp"]

    def per_device(*arguments):
        if tensor == 4 and dp == 4:
            return moving_plan(*arguments)
        return gathering_plan(*arguments)

    in_specs = (
        P(("parts", "dp"), None, "tensor"),
        P(("parts", "dp"), None, "tensor"),
        P(("parts", "dp"), None, "tensor"),
        P(("parts", "dp"), None, "tensor"),
        P(("parts", "dp")),
        P(("parts", "dp"), None, "tensor"),
        P(("parts", "dp"), None, "tensor"),
        P(("parts", "dp"), None, "tensor"),
        P(("parts", "dp"), None, "tensor"),
        P(("parts", "dp")),
        P("tensor", "dp"),
        P(None, "tensor"),
        P(None, "tensor"),
        P(None, "tensor"),
        P(None, "tensor"),
        P(None, "tensor"),
    )
    out_specs = P(("parts", "dp"), None)
    return jax.shard_map(
        per_device, mesh=mesh, in_specs=in_specs, out_specs=out_specs, check_vma=False
    )
```

```python
import functools

import jax
import jax.numpy as jnp
from jax import lax
from jax.experimental import pallas as pl
from jax.experimental.pallas import tpu as pltpu
from jax.sharding import PartitionSpec as P

RANK = 64
SEQ = 64
TILE = 512
WIDE = 1792
VMEM_BYTES = 40 * 1024 * 1024
BIG_VMEM_BYTES = 58 * 1024 * 1024


def flatten(array):
    return array.reshape(-1, array.shape[-1])


def project(rows, table):
    return lax.dot_general(
        rows, table, (((1,), (1,)), ((), ())), preferred_element_type=jnp.float32
    )


def inner(left_side, right_side):
    return lax.dot_general(
        left_side,
        right_side,
        (((1,), (1,)), ((), ())),
        precision=lax.Precision.HIGHEST,
        preferred_element_type=jnp.float32,
    )


def gated_hidden(gate, up):
    gate_wide = gate.astype(jnp.float32)
    up_wide = up.astype(jnp.float32)
    return (gate_wide * jax.nn.sigmoid(gate_wide) * up_wide).astype(jnp.bfloat16)


def gradients(gate, up, hidden_grad):
    gate_wide = gate.astype(jnp.float32)
    up_wide = up.astype(jnp.float32)
    sigmoid_gate = jax.nn.sigmoid(gate_wide)
    silu_gate = gate_wide * sigmoid_gate
    gate_grad = (
        hidden_grad * up_wide * sigmoid_gate * (1.0 + gate_wide * (1.0 - sigmoid_gate))
    ).astype(jnp.bfloat16)
    up_grad = (hidden_grad * silu_gate).astype(jnp.bfloat16)
    return gate_grad, up_grad


def gradient_sides(gate, up, hidden_grad, proj_gate, proj_up):
    gate_grad, up_grad = gradients(gate, up, hidden_grad)
    return project(gate_grad, proj_gate), project(up_grad, proj_up)


def outer_sums(left_side, right_side, lengths):
    number = lengths.shape[0]
    length = left_side.shape[0] // number
    positions = lax.broadcasted_iota(jnp.int32, (number, length), 1)
    weights = (positions < lengths[:, None]).astype(jnp.float32)
    left_rows = left_side.reshape(number, length, left_side.shape[1]) * weights[:, :, None]
    right_rows = right_side.reshape(number, length, right_side.shape[1])
    summed = jnp.einsum("est,esu->etu", left_rows, right_rows, precision=lax.Precision.HIGHEST)
    return summed.reshape(number, -1)


def features(in_side, hidden_side, gate_side, up_side, out_side, lengths):
    return jnp.concatenate(
        [
            outer_sums(in_side, gate_side, lengths),
            outer_sums(in_side, up_side, lengths),
            outer_sums(hidden_side, out_side, lengths),
        ],
        axis=1,
    )


def gathering_plan(
    train_input,
    train_gate,
    train_up,
    train_outgrad,
    train_lengths,
    query_input,
    query_gate,
    query_up,
    query_outgrad,
    query_lengths,
    down_weight,
    proj_input,
    proj_outgrad,
    proj_hidden,
    proj_gate,
    proj_up,
):
    weight = lax.all_gather(down_weight, "dp", axis=1, tiled=True)

    def full_features(inputs, gate, up, outgrad, lengths):
        inputs, gate, up, outgrad = [flatten(a) for a in (inputs, gate, up, outgrad)]
        rows = lax.all_gather(outgrad, "tensor", axis=1, tiled=True)
        gate_side, up_side = gradient_sides(gate, up, project(rows, weight), proj_gate, proj_up)
        hidden_side = project(gated_hidden(gate, up), proj_hidden)
        sides = (
            project(inputs, proj_input),
            hidden_side,
            gate_side,
            up_side,
            project(outgrad, proj_outgrad),
        )
        return features(*lax.psum(sides, "tensor"), lengths)

    train_features = full_features(
        train_input, train_gate, train_up, train_outgrad, train_lengths
    )
    query_features = full_features(
        query_input, query_gate, query_up, query_outgrad, query_lengths
    )
    gathered = lax.all_gather(query_features, "dp", axis=0, tiled=True)
    return inner(train_features, gathered) / (RANK * SEQ)


ANYWHERE = pl.BlockSpec(memory_space=pl.ANY)
SCALARS = pl.BlockSpec(memory_space=pltpu.SMEM)
IN_VMEM = pl.BlockSpec(memory_space=pltpu.VMEM)


def params(limit=VMEM_BYTES):
    return pltpu.CompilerParams(vmem_limit_bytes=limit)


def cost(flops, arrays):
    return pl.CostEstimate(flops=1024, bytes_accessed=1024, transcendentals=0)


def tile_columns(number, block=0, tile=TILE):
    return pl.BlockSpec((number, tile), lambda i: (block, i))


def tile_rows(width, tile=TILE):
    return pl.BlockSpec((tile, width), lambda i: (i, 0))


def whole(shape):
    return pl.BlockSpec(shape, lambda i: tuple(0 for _ in shape))


def stacked_products(
    flags, pairs, far, weight_own, weight_sib, stacked, semaphores, held, weight_sems
):
    number = far.shape[1]
    step = pl.program_id(0)
    tiles = weight_own.shape[0] // TILE

    def weight_copies(tile):
        part = pl.ds(pl.multiple_of(tile * TILE, TILE), TILE)
        slot = lax.rem(tile, 3)
        return [
            pltpu.make_async_copy(
                weight.at[part], held.at[slot, side], weight_sems.at[slot, side]
            )
            for side, weight in enumerate((weight_own, weight_sib))
        ]

    @pl.when(step == 0)
    def _():
        slot = flags[1]
        far_copies = [
            pltpu.make_async_copy(
                far.at[i], stacked.at[jnp.bitwise_xor(slot, i), pl.ds(number, number)],
                semaphores.at[2 + i],
            )
            for i in range(2)
        ]
        for copy in far_copies:
            copy.start()
        for code, pair in enumerate(pairs):

            @pl.when(flags[0] == code)
            def _():
                copies = [
                    pltpu.make_async_copy(
                        pair[i], stacked.at[jnp.bitwise_xor(slot, i), pl.ds(0, number)],
                        semaphores.at[i],
                    )
                    for i in range(2)
                ]
                for copy in copies:
                    copy.start()
                for copy in weight_copies(0):
                    copy.start()
                for copy in copies:
                    copy.wait()

        for copy in far_copies:
            copy.wait()

    own_copy, sib_copy = weight_copies(step)
    own_copy.wait()

    @pl.when(step == 0)
    def _():
        for copy in weight_copies(1):
            copy.start()

    @pl.when(step + 2 < tiles)
    def _():
        for copy in weight_copies(step + 2):
            copy.start()

    slot = lax.rem(step, 3)
    own_product = project(held[slot, 0], stacked[0])
    sib_copy.wait()
    return own_product + project(held[slot, 1], stacked[1])


def add_sides(hidden_grad, gate, up, proj_gate, proj_up, sides):
    gate_part, up_part = gradient_sides(gate, up, hidden_grad, proj_gate, proj_up)
    part = jnp.concatenate([gate_part, up_part], axis=1)
    first = pl.program_id(0) == 0

    @pl.when(first)
    def _():
        sides[...] = part

    @pl.when(jnp.logical_not(first))
    def _():
        sides[...] += part


def partial_kernel(
    flags, b0, b1, b2, b3, b4, b5, far, weight_own, weight_sib, near_sum, far_sum, *scratch
):
    pairs = ((b0, b1), (b2, b3), (b4, b5))
    total = stacked_products(flags, pairs, far, weight_own, weight_sib, *scratch)
    number = far.shape[1]
    near_sum[...] = total[:, :number]
    far_sum[...] = total[:, number:].astype(jnp.bfloat16)


def partial_sums(flags, blocks, far, weight_own, weight_sib):
    number, half = blocks[0].shape
    units = weight_own.shape[0]
    return pl.pallas_call(
        partial_kernel,
        grid=(units // TILE,),
        in_specs=[SCALARS] + [ANYWHERE] * 9,
        out_specs=[tile_rows(number)] * 2,
        out_shape=[
            jax.ShapeDtypeStruct((units, number), jnp.float32),
            jax.ShapeDtypeStruct((units, number), jnp.bfloat16),
        ],
        scratch_shapes=[
            pltpu.VMEM((2, 2 * number, half), jnp.bfloat16),
            pltpu.SemaphoreType.DMA((4,)),
            pltpu.VMEM((3, 2, TILE, half), jnp.bfloat16),
            pltpu.SemaphoreType.DMA((3, 2)),
        ],
        compiler_params=params(BIG_VMEM_BYTES),
        cost_estimate=cost(8 * number * half * units, (far, weight_own, weight_sib)),
    )(flags, *blocks, far, weight_own, weight_sib)


def finish_kernel(near_sum, returned, gate, up, proj_gate, proj_up, sides):
    hidden_grad = (near_sum[...] + returned[...].astype(jnp.float32)).T
    add_sides(hidden_grad, gate[...], up[...], proj_gate[...], proj_up[...], sides)


def finished_sides(near_sum, returned, gate, up, proj_gate, proj_up):
    units, number = near_sum.shape
    return pl.pallas_call(
        finish_kernel,
        grid=(units // WIDE,),
        in_specs=[tile_rows(number, WIDE)] * 2
        + [tile_columns(number, 0, WIDE)] * 2
        + [tile_columns(RANK, 0, WIDE)] * 2,
        out_specs=whole((number, 2 * RANK)),
        out_shape=jax.ShapeDtypeStruct((number, 2 * RANK), jnp.float32),
        compiler_params=params(),
        cost_estimate=cost(4 * number * RANK * units, (near_sum, returned, gate, up)),
    )(near_sum, returned, gate, up, proj_gate, proj_up)


def turn_kernel(gate, up, far_gate, far_up, gates, ups):
    number = gate.shape[0]
    for source, target, part in (
        (gate, gates, slice(0, number)),
        (up, ups, slice(0, number)),
        (far_gate, gates, slice(number, None)),
        (far_up, ups, slice(number, None)),
    ):
        target[:, part] = source[...].astype(jnp.float32).T.astype(jnp.bfloat16)


def turned(gate, up, far_gate, far_up):
    number, units = far_gate.shape
    shape = jax.ShapeDtypeStruct((units, 2 * number), jnp.bfloat16)
    return pl.pallas_call(
        turn_kernel,
        grid=(units // TILE,),
        in_specs=[tile_columns(number, 1)] * 2 + [tile_columns(number)] * 2,
        out_specs=[tile_rows(2 * number)] * 2,
        out_shape=[shape] * 2,
        compiler_params=params(),
        cost_estimate=cost(0, (gate, up)),
    )(gate, up, far_gate, far_up)


def lent_kernel(
    flags, b0, b1, b2, b3, b4, b5, far, weight_own, weight_sib, gates, ups, proj_gate, proj_up,
    near, away, *scratch,
):
    pairs = ((b0, b1), (b2, b3), (b4, b5))
    hidden_grad = stacked_products(flags, pairs, far, weight_own, weight_sib, *scratch)
    gate_grad, up_grad = gradients(gates[...], ups[...], hidden_grad)
    part = jnp.concatenate(
        [
            jnp.dot(proj_gate[...], gate_grad, preferred_element_type=jnp.float32),
            jnp.dot(proj_up[...], up_grad, preferred_element_type=jnp.float32),
        ],
        axis=0,
    )
    number = near.shape[1]
    first = pl.program_id(0) == 0

    @pl.when(first)
    def _():
        near[...] = part[:, :number]
        away[...] = part[:, number:]

    @pl.when(jnp.logical_not(first))
    def _():
        near[...] += part[:, :number]
        away[...] += part[:, number:]


def lent_sides(flags, blocks, far, weight_own, weight_sib, gates, ups, proj_gate, proj_up):
    number, half = blocks[0].shape
    units = weight_own.shape[0]
    return pl.pallas_call(
        lent_kernel,
        grid=(units // TILE,),
        in_specs=[SCALARS]
        + [ANYWHERE] * 9
        + [tile_rows(2 * number)] * 2
        + [tile_columns(RANK)] * 2,
        out_specs=[whole((2 * RANK, number))] * 2,
        out_shape=[jax.ShapeDtypeStruct((2 * RANK, number), jnp.float32)] * 2,
        scratch_shapes=[
            pltpu.VMEM((2, 2 * number, half), jnp.bfloat16),
            pltpu.SemaphoreType.DMA((4,)),
            pltpu.VMEM((3, 2, TILE, half), jnp.bfloat16),
            pltpu.SemaphoreType.DMA((3, 2)),
        ],
        compiler_params=params(BIG_VMEM_BYTES),
        cost_estimate=cost(8 * number * half * units, (far, weight_own, weight_sib)),
    )(flags, *blocks, far, weight_own, weight_sib, gates, ups, proj_gate, proj_up)


def early_kernel(
    t_input, q_input, t_outgrad, q_outgrad, proj_input, proj_outgrad, t_gate, t_up, q_gate, q_up,
    proj_hidden, in_out, hidden,
):
    number = t_input.shape[0]
    t_hidden = project(gated_hidden(t_gate[...], t_up[...]), proj_hidden[...])
    q_hidden = project(gated_hidden(q_gate[...], q_up[...]), proj_hidden[...])
    first = pl.program_id(0) == 0

    @pl.when(first)
    def _():
        for inputs, outgrad, part in (
            (t_input, t_outgrad, slice(0, number)),
            (q_input, q_outgrad, slice(number, None)),
        ):
            in_out[part, :] = jnp.concatenate(
                [
                    project(inputs[...], proj_input[...]),
                    project(outgrad[...], proj_outgrad[...]),
                ],
                axis=1,
            )
        hidden[:number, :] = t_hidden
        hidden[number:, :] = q_hidden

    @pl.when(jnp.logical_not(first))
    def _():
        hidden[:number, :] += t_hidden
        hidden[number:, :] += q_hidden


def early_sides(
    t_input, q_input, t_outgrad, q_outgrad, proj_input, proj_outgrad, t_gate, t_up, q_gate, q_up,
    proj_hidden,
):
    total, units = t_gate.shape[0] + q_gate.shape[0], t_gate.shape[1]
    wide = (t_input, q_input, t_outgrad, q_outgrad, proj_input, proj_outgrad)
    tiled = (t_gate, t_up, q_gate, q_up, proj_hidden)
    shapes = ((total, 2 * RANK), (total, RANK))
    return pl.pallas_call(
        early_kernel,
        grid=(units // TILE,),
        in_specs=[whole(a.shape) for a in wide] + [tile_columns(a.shape[0]) for a in tiled],
        out_specs=[whole(shape) for shape in shapes],
        out_shape=[jax.ShapeDtypeStruct(shape, jnp.float32) for shape in shapes],
        compiler_params=params(),
        cost_estimate=cost(2 * total * RANK * units, wide + tiled),
    )(*wide, *tiled)


def outer_sum(left_side, right_side, weight):
    return lax.dot_general(
        left_side * weight,
        right_side,
        (((0,), (0,)), ((), ())),
        precision=lax.Precision.HIGHEST,
        preferred_element_type=jnp.float32,
    )


def example_features(in_side, hidden_side, gate_side, up_side, out_side, length):
    positions = lax.broadcasted_iota(jnp.int32, (SEQ, RANK), 0)
    weight = (positions < length).astype(jnp.float32)
    return (
        outer_sum(in_side, gate_side, weight),
        outer_sum(in_side, up_side, weight),
        outer_sum(hidden_side, out_side, weight),
    )


def query_kernel(lengths, in_out, sums, found):
    for e in range(found.shape[0]):
        part = slice(e * SEQ, (e + 1) * SEQ)
        three = example_features(
            in_out[part, :RANK],
            sums[part, 2 * RANK :],
            sums[part, :RANK],
            sums[part, RANK : 2 * RANK],
            in_out[part, RANK:],
            lengths[e],
        )
        for segment in range(3):
            found[e, segment * RANK : (segment + 1) * RANK, :] = three[segment]


def query_features(lengths, in_out, sums):
    return pl.pallas_call(
        query_kernel,
        in_specs=[SCALARS, IN_VMEM, IN_VMEM],
        out_specs=IN_VMEM,
        out_shape=jax.ShapeDtypeStruct((lengths.shape[0], 3 * RANK, RANK), jnp.float32),
        compiler_params=params(),
    )(lengths, in_out, sums)


def score_kernel(
    lengths, place, in_out, hidden, early, near, far, q0, q1, q2, q3, scores
):
    queries = q0.shape[0]
    shape = scores.shape
    row = lax.broadcasted_iota(jnp.int32, shape, 0)
    column = lax.broadcasted_iota(jnp.int32, shape, 1)
    gradient = jnp.concatenate([early[...], (near[...] + far[...]).T], axis=0)
    total = jnp.zeros(shape, jnp.float32)
    for e in range(shape[0]):
        part = slice(e * SEQ, (e + 1) * SEQ)
        three = jnp.concatenate(
            example_features(
                in_out[part, :RANK],
                hidden[part, :],
                gradient[part, :RANK],
                gradient[part, RANK:],
                in_out[part, RANK:],
                lengths[e],
            ),
            axis=0,
        )
        for step, found in enumerate((q0, q1, q2, q3)):
            for j in range(queries):
                value = jnp.sum(three * found[j], keepdims=True)
                here = (row == e) & (
                    column == queries * jnp.bitwise_xor(place[0], step) + j
                )
                total = total + jnp.where(here, value, 0.0)
    scores[...] = total


def partial_scores(lengths, place, in_out, hidden, early, near, far, found):
    number = lengths.shape[0]
    return pl.pallas_call(
        score_kernel,
        in_specs=[SCALARS] * 2 + [IN_VMEM] * 9,
        out_specs=IN_VMEM,
        out_shape=jax.ShapeDtypeStruct((number, 4 * found[0].shape[0]), jnp.float32),
        compiler_params=params(),
    )(lengths, place, in_out, hidden, early, near, far, *found)


def after(value, *others):
    return lax.optimization_barrier((value, *others))[0]


def moving_plan(
    train_input,
    train_gate,
    train_up,
    train_outgrad,
    train_lengths,
    query_input,
    query_gate,
    query_up,
    query_outgrad,
    query_lengths,
    down_weight,
    proj_input,
    proj_outgrad,
    proj_hidden,
    proj_gate,
    proj_up,
):
    t = lax.axis_index("tensor")
    d = lax.axis_index("dp")
    x, core, upper = d // 2, d % 2, t // 2
    at_home = x == upper
    inner_chip = (t == 1) | (t == 2)
    near_code = jnp.where(at_home, 0, jnp.where(inner_chip, 1, 2))
    first_parity = jnp.where(at_home, t % 2, upper)
    flags = jnp.stack([near_code, first_parity ^ core]).astype(jnp.int32)
    place = jnp.stack([d]).astype(jnp.int32)

    to_core = functools.partial(lax.ppermute, axis_name="dp", perm=[(i, i ^ 1) for i in range(4)])
    to_chip = functools.partial(lax.ppermute, axis_name="dp", perm=[(i, i ^ 2) for i in range(4)])
    outer = functools.partial(
        lax.ppermute, axis_name="tensor", perm=[(i, i ^ 1) for i in range(4)]
    )
    across = functools.partial(
        lax.ppermute, axis_name="tensor", perm=[(i, i ^ 2) for i in range(4)]
    )
    opposite = functools.partial(
        lax.ppermute, axis_name="tensor", perm=[(i, 3 - i) for i in range(4)]
    )
    middle = functools.partial(
        lax.ppermute,
        axis_name=("tensor", "dp"),
        perm=[
            (4 * i + j, 4 * (3 - i) + j) if i in (1, 2) else (4 * i + j, 4 * i + (j ^ 1))
            for i in range(4)
            for j in range(4)
        ],
    )

    q_input, q_gate, q_up, q_outgrad = [
        flatten(a) for a in (query_input, query_gate, query_up, query_outgrad)
    ]
    t_input, t_gate, t_up, t_outgrad = [
        flatten(a) for a in (train_input, train_gate, train_up, train_outgrad)
    ]
    examples = train_lengths.shape[0] // 2
    cut = examples * SEQ

    def first_hops(own):
        return own, outer(own), across(own)

    def last_hops(own, one, two):
        mid = middle(after(own, two))
        return own, one, mid, two, two, outer(after(two, one))

    def crossing_pair(own, one, second_inner, third_inner, second_outer, third_outer):
        def choose(within, beyond_inner, beyond_outer):
            beyond = jnp.where(inner_chip, beyond_inner, beyond_outer)
            return jnp.where(at_home, beyond, within)

        return jnp.stack(
            [choose(own, second_inner, second_outer), choose(one, third_inner, third_outer)]
        )

    weight_own, weight_sib = down_weight, to_core(down_weight)
    q_hops = first_hops(q_outgrad)
    far_gate = to_chip(t_gate[cut:])
    own_in_out, hidden = early_sides(
        t_input, q_input, t_outgrad, q_outgrad, proj_input, proj_outgrad, t_gate, t_up, q_gate,
        q_up, proj_hidden,
    )

    q_blocks = last_hops(*q_hops[:2], after(q_hops[2], own_in_out))
    a_hops = first_hops(after(t_outgrad[:cut], q_hops[2], far_gate))
    far_up = to_chip(after(t_up[cut:], far_gate))
    q_send = after(crossing_pair(*q_blocks), far_up)
    q_far = to_chip(q_send)
    a_blocks = last_hops(*a_hops[:2], after(a_hops[2], q_send))

    b_hops = first_hops(after(t_outgrad[cut:], a_hops[2]))
    gates, ups = turned(t_gate, t_up, far_gate, far_up)
    a_send = crossing_pair(*a_blocks[:5], after(a_blocks[5], q_far, gates))
    a_far = to_chip(a_send)
    q_near_sum, q_far_sum = partial_sums(
        flags, q_blocks, after(q_far, a_send), weight_own, weight_sib
    )
    q_returned = to_chip(after(q_far_sum, a_far))
    b_blocks = last_hops(*b_hops[:2], after(b_hops[2], q_far_sum))
    b_send = crossing_pair(*b_blocks)
    b_far = to_chip(b_send)
    a_near_sum, a_far_sum = partial_sums(
        flags, a_blocks, after(a_far, b_send), weight_own, weight_sib
    )
    a_returned = to_chip(a_far_sum)
    in_out = own_in_out + outer(after(own_in_out, b_send))
    q_gradient = finished_sides(
        q_near_sum, after(q_returned, a_far_sum), q_gate, q_up, proj_gate, proj_up
    )
    q_sums = jnp.concatenate([q_gradient, hidden[2 * cut :]], axis=1)
    q_sums = q_sums + outer(q_sums)
    b_near, b_away = lent_sides(
        after(flags, q_sums, in_out), b_blocks, b_far, weight_own, weight_sib, gates, ups,
        proj_gate, proj_up,
    )
    b_far_sides = to_chip(b_away)
    in_out = in_out + after(across(in_out), b_near)
    q_sums = q_sums + after(across(q_sums), b_near)
    own_found = query_features(query_lengths, in_out[2 * cut :], q_sums)
    chip_found = to_chip(own_found)
    found = (own_found, to_core(own_found), chip_found, to_core(after(chip_found, b_far_sides)))
    a_gradient = finished_sides(a_near_sum, a_returned, t_gate, t_up, proj_gate, proj_up)
    own_scores = partial_scores(
        train_lengths, place, in_out[: 2 * cut], hidden[: 2 * cut], a_gradient, b_near,
        b_far_sides, found,
    )
    scores = own_scores + outer(own_scores) + across(own_scores) + opposite(own_scores)
    return scores / (RANK * SEQ)


def solution(mesh):
    tensor, dp = mesh.shape["tensor"], mesh.shape["dp"]

    def per_device(*arguments):
        if tensor == 4 and dp == 4:
            return moving_plan(*arguments)
        return gathering_plan(*arguments)

    in_specs = (
        P(("parts", "dp"), None, "tensor"),
        P(("parts", "dp"), None, "tensor"),
        P(("parts", "dp"), None, "tensor"),
        P(("parts", "dp"), None, "tensor"),
        P(("parts", "dp")),
        P(("parts", "dp"), None, "tensor"),
        P(("parts", "dp"), None, "tensor"),
        P(("parts", "dp"), None, "tensor"),
        P(("parts", "dp"), None, "tensor"),
        P(("parts", "dp")),
        P("tensor", "dp"),
        P(None, "tensor"),
        P(None, "tensor"),
        P(None, "tensor"),
        P(None, "tensor"),
        P(None, "tensor"),
    )
    out_specs = P(("parts", "dp"), None)
    return jax.shard_map(
        per_device, mesh=mesh, in_specs=in_specs, out_specs=out_specs, check_vma=False
    )
```

```python
import functools

import jax
import jax.numpy as jnp
from jax import lax
from jax.experimental import pallas as pl
from jax.experimental.pallas import tpu as pltpu
from jax.sharding import PartitionSpec as P

RANK = 64
SEQ = 64
TILE = 512
WIDE = 1792
VMEM_BYTES = 40 * 1024 * 1024
BIG_VMEM_BYTES = 58 * 1024 * 1024


def flatten(array):
    return array.reshape(-1, array.shape[-1])


def project(rows, table):
    return lax.dot_general(
        rows, table, (((1,), (1,)), ((), ())), preferred_element_type=jnp.float32
    )


def inner(left_side, right_side):
    return lax.dot_general(
        left_side,
        right_side,
        (((1,), (1,)), ((), ())),
        precision=lax.Precision.HIGHEST,
        preferred_element_type=jnp.float32,
    )


def gated_hidden(gate, up):
    gate_wide = gate.astype(jnp.float32)
    up_wide = up.astype(jnp.float32)
    return (gate_wide * jax.nn.sigmoid(gate_wide) * up_wide).astype(jnp.bfloat16)


def gradients(gate, up, hidden_grad):
    gate_wide = gate.astype(jnp.float32)
    up_wide = up.astype(jnp.float32)
    sigmoid_gate = jax.nn.sigmoid(gate_wide)
    silu_gate = gate_wide * sigmoid_gate
    gate_grad = (
        hidden_grad * up_wide * sigmoid_gate * (1.0 + gate_wide * (1.0 - sigmoid_gate))
    ).astype(jnp.bfloat16)
    up_grad = (hidden_grad * silu_gate).astype(jnp.bfloat16)
    return gate_grad, up_grad


def gradient_sides(gate, up, hidden_grad, proj_gate, proj_up):
    gate_grad, up_grad = gradients(gate, up, hidden_grad)
    return project(gate_grad, proj_gate), project(up_grad, proj_up)


def outer_sums(left_side, right_side, lengths):
    number = lengths.shape[0]
    length = left_side.shape[0] // number
    positions = lax.broadcasted_iota(jnp.int32, (number, length), 1)
    weights = (positions < lengths[:, None]).astype(jnp.float32)
    left_rows = left_side.reshape(number, length, left_side.shape[1]) * weights[:, :, None]
    right_rows = right_side.reshape(number, length, right_side.shape[1])
    summed = jnp.einsum("est,esu->etu", left_rows, right_rows, precision=lax.Precision.HIGHEST)
    return summed.reshape(number, -1)


def features(in_side, hidden_side, gate_side, up_side, out_side, lengths):
    return jnp.concatenate(
        [
            outer_sums(in_side, gate_side, lengths),
            outer_sums(in_side, up_side, lengths),
            outer_sums(hidden_side, out_side, lengths),
        ],
        axis=1,
    )


def gathering_plan(
    train_input,
    train_gate,
    train_up,
    train_outgrad,
    train_lengths,
    query_input,
    query_gate,
    query_up,
    query_outgrad,
    query_lengths,
    down_weight,
    proj_input,
    proj_outgrad,
    proj_hidden,
    proj_gate,
    proj_up,
):
    weight = lax.all_gather(down_weight, "dp", axis=1, tiled=True)

    def full_features(inputs, gate, up, outgrad, lengths):
        inputs, gate, up, outgrad = [flatten(a) for a in (inputs, gate, up, outgrad)]
        rows = lax.all_gather(outgrad, "tensor", axis=1, tiled=True)
        gate_side, up_side = gradient_sides(gate, up, project(rows, weight), proj_gate, proj_up)
        hidden_side = project(gated_hidden(gate, up), proj_hidden)
        sides = (
            project(inputs, proj_input),
            hidden_side,
            gate_side,
            up_side,
            project(outgrad, proj_outgrad),
        )
        return features(*lax.psum(sides, "tensor"), lengths)

    train_features = full_features(
        train_input, train_gate, train_up, train_outgrad, train_lengths
    )
    query_features = full_features(
        query_input, query_gate, query_up, query_outgrad, query_lengths
    )
    gathered = lax.all_gather(query_features, "dp", axis=0, tiled=True)
    return inner(train_features, gathered) / (RANK * SEQ)


ANYWHERE = pl.BlockSpec(memory_space=pl.ANY)
SCALARS = pl.BlockSpec(memory_space=pltpu.SMEM)
IN_VMEM = pl.BlockSpec(memory_space=pltpu.VMEM)


def params(limit=VMEM_BYTES):
    return pltpu.CompilerParams(vmem_limit_bytes=limit)


def cost(flops, arrays):
    return pl.CostEstimate(flops=1024, bytes_accessed=1024, transcendentals=0)


def tile_columns(number, block=0, tile=TILE):
    return pl.BlockSpec((number, tile), lambda i: (block, i))


def tile_rows(width, tile=TILE):
    return pl.BlockSpec((tile, width), lambda i: (i, 0))


def whole(shape):
    return pl.BlockSpec(shape, lambda i: tuple(0 for _ in shape))


def stacked_products(
    flags, pairs, far, weight_own, weight_sib, stacked, semaphores, held, weight_sems
):
    number = far.shape[1]
    step = pl.program_id(0)
    tiles = weight_own.shape[0] // TILE

    def weight_copies(tile):
        part = pl.ds(pl.multiple_of(tile * TILE, TILE), TILE)
        slot = lax.rem(tile, 3)
        return [
            pltpu.make_async_copy(
                weight.at[part], held.at[slot, side], weight_sems.at[slot, side]
            )
            for side, weight in enumerate((weight_own, weight_sib))
        ]

    @pl.when(step == 0)
    def _():
        slot = flags[1]
        far_copies = [
            pltpu.make_async_copy(
                far.at[i], stacked.at[jnp.bitwise_xor(slot, i), pl.ds(number, number)],
                semaphores.at[2 + i],
            )
            for i in range(2)
        ]
        for copy in far_copies:
            copy.start()
        for code, pair in enumerate(pairs):

            @pl.when(flags[0] == code)
            def _():
                copies = [
                    pltpu.make_async_copy(
                        pair[i], stacked.at[jnp.bitwise_xor(slot, i), pl.ds(0, number)],
                        semaphores.at[i],
                    )
                    for i in range(2)
                ]
                for copy in copies:
                    copy.start()
                for tile in range(2):
                    for copy in weight_copies(tile):
                        copy.start()
                for copy in copies:
                    copy.wait()

        for copy in far_copies:
            copy.wait()

    @pl.when(step + 2 < tiles)
    def _():
        for copy in weight_copies(step + 2):
            copy.start()

    for copy in weight_copies(step):
        copy.wait()
    slot = lax.rem(step, 3)
    return project(held[slot, 0], stacked[0]) + project(held[slot, 1], stacked[1])


def add_sides(hidden_grad, gate, up, proj_gate, proj_up, sides):
    gate_part, up_part = gradient_sides(gate, up, hidden_grad, proj_gate, proj_up)
    part = jnp.concatenate([gate_part, up_part], axis=1)
    first = pl.program_id(0) == 0

    @pl.when(first)
    def _():
        sides[...] = part

    @pl.when(jnp.logical_not(first))
    def _():
        sides[...] += part


def partial_kernel(
    flags, b0, b1, b2, b3, b4, b5, far, weight_own, weight_sib, near_sum, far_sum, *scratch
):
    pairs = ((b0, b1), (b2, b3), (b4, b5))
    total = stacked_products(flags, pairs, far, weight_own, weight_sib, *scratch)
    number = far.shape[1]
    near_sum[...] = total[:, :number]
    far_sum[...] = total[:, number:].astype(jnp.bfloat16)


def partial_sums(flags, blocks, far, weight_own, weight_sib):
    number, half = blocks[0].shape
    units = weight_own.shape[0]
    return pl.pallas_call(
        partial_kernel,
        grid=(units // TILE,),
        in_specs=[SCALARS] + [ANYWHERE] * 9,
        out_specs=[tile_rows(number)] * 2,
        out_shape=[
            jax.ShapeDtypeStruct((units, number), jnp.float32),
            jax.ShapeDtypeStruct((units, number), jnp.bfloat16),
        ],
        scratch_shapes=[
            pltpu.VMEM((2, 2 * number, half), jnp.bfloat16),
            pltpu.SemaphoreType.DMA((4,)),
            pltpu.VMEM((3, 2, TILE, half), jnp.bfloat16),
            pltpu.SemaphoreType.DMA((3, 2)),
        ],
        compiler_params=params(BIG_VMEM_BYTES),
        cost_estimate=cost(8 * number * half * units, (far, weight_own, weight_sib)),
    )(flags, *blocks, far, weight_own, weight_sib)


def finish_kernel(near_sum, returned, gate, up, proj_gate, proj_up, sides):
    hidden_grad = (near_sum[...] + returned[...].astype(jnp.float32)).T
    add_sides(hidden_grad, gate[...], up[...], proj_gate[...], proj_up[...], sides)


def finished_sides(near_sum, returned, gate, up, proj_gate, proj_up):
    units, number = near_sum.shape
    return pl.pallas_call(
        finish_kernel,
        grid=(units // WIDE,),
        in_specs=[tile_rows(number, WIDE)] * 2
        + [tile_columns(number, 0, WIDE)] * 2
        + [tile_columns(RANK, 0, WIDE)] * 2,
        out_specs=whole((number, 2 * RANK)),
        out_shape=jax.ShapeDtypeStruct((number, 2 * RANK), jnp.float32),
        compiler_params=params(),
        cost_estimate=cost(4 * number * RANK * units, (near_sum, returned, gate, up)),
    )(near_sum, returned, gate, up, proj_gate, proj_up)


def turn_kernel(gate, up, far_gate, far_up, gates, ups):
    number = gate.shape[0]
    for source, target, part in (
        (gate, gates, slice(0, number)),
        (up, ups, slice(0, number)),
        (far_gate, gates, slice(number, None)),
        (far_up, ups, slice(number, None)),
    ):
        target[:, part] = source[...].astype(jnp.float32).T.astype(jnp.bfloat16)


def turned(gate, up, far_gate, far_up):
    number, units = far_gate.shape
    shape = jax.ShapeDtypeStruct((units, 2 * number), jnp.bfloat16)
    return pl.pallas_call(
        turn_kernel,
        grid=(units // TILE,),
        in_specs=[tile_columns(number, 1)] * 2 + [tile_columns(number)] * 2,
        out_specs=[tile_rows(2 * number)] * 2,
        out_shape=[shape] * 2,
        compiler_params=params(),
        cost_estimate=cost(0, (gate, up)),
    )(gate, up, far_gate, far_up)


def lent_kernel(
    flags, b0, b1, b2, b3, b4, b5, far, weight_own, weight_sib, gates, ups, proj_gate, proj_up,
    near, away, *scratch,
):
    pairs = ((b0, b1), (b2, b3), (b4, b5))
    hidden_grad = stacked_products(flags, pairs, far, weight_own, weight_sib, *scratch)
    gate_grad, up_grad = gradients(gates[...], ups[...], hidden_grad)
    part = jnp.concatenate(
        [
            jnp.dot(proj_gate[...], gate_grad, preferred_element_type=jnp.float32),
            jnp.dot(proj_up[...], up_grad, preferred_element_type=jnp.float32),
        ],
        axis=0,
    )
    number = near.shape[1]
    first = pl.program_id(0) == 0

    @pl.when(first)
    def _():
        near[...] = part[:, :number]
        away[...] = part[:, number:]

    @pl.when(jnp.logical_not(first))
    def _():
        near[...] += part[:, :number]
        away[...] += part[:, number:]


def lent_sides(flags, blocks, far, weight_own, weight_sib, gates, ups, proj_gate, proj_up):
    number, half = blocks[0].shape
    units = weight_own.shape[0]
    return pl.pallas_call(
        lent_kernel,
        grid=(units // TILE,),
        in_specs=[SCALARS]
        + [ANYWHERE] * 9
        + [tile_rows(2 * number)] * 2
        + [tile_columns(RANK)] * 2,
        out_specs=[whole((2 * RANK, number))] * 2,
        out_shape=[jax.ShapeDtypeStruct((2 * RANK, number), jnp.float32)] * 2,
        scratch_shapes=[
            pltpu.VMEM((2, 2 * number, half), jnp.bfloat16),
            pltpu.SemaphoreType.DMA((4,)),
            pltpu.VMEM((3, 2, TILE, half), jnp.bfloat16),
            pltpu.SemaphoreType.DMA((3, 2)),
        ],
        compiler_params=params(BIG_VMEM_BYTES),
        cost_estimate=cost(8 * number * half * units, (far, weight_own, weight_sib)),
    )(flags, *blocks, far, weight_own, weight_sib, gates, ups, proj_gate, proj_up)


def early_kernel(
    t_input, q_input, t_outgrad, q_outgrad, proj_input, proj_outgrad, t_gate, t_up, q_gate, q_up,
    proj_hidden, in_out, hidden,
):
    number = t_input.shape[0]
    t_hidden = project(gated_hidden(t_gate[...], t_up[...]), proj_hidden[...])
    q_hidden = project(gated_hidden(q_gate[...], q_up[...]), proj_hidden[...])
    first = pl.program_id(0) == 0

    @pl.when(first)
    def _():
        for inputs, outgrad, part in (
            (t_input, t_outgrad, slice(0, number)),
            (q_input, q_outgrad, slice(number, None)),
        ):
            in_out[part, :] = jnp.concatenate(
                [
                    project(inputs[...], proj_input[...]),
                    project(outgrad[...], proj_outgrad[...]),
                ],
                axis=1,
            )
        hidden[:number, :] = t_hidden
        hidden[number:, :] = q_hidden

    @pl.when(jnp.logical_not(first))
    def _():
        hidden[:number, :] += t_hidden
        hidden[number:, :] += q_hidden


def early_sides(
    t_input, q_input, t_outgrad, q_outgrad, proj_input, proj_outgrad, t_gate, t_up, q_gate, q_up,
    proj_hidden,
):
    total, units = t_gate.shape[0] + q_gate.shape[0], t_gate.shape[1]
    wide = (t_input, q_input, t_outgrad, q_outgrad, proj_input, proj_outgrad)
    tiled = (t_gate, t_up, q_gate, q_up, proj_hidden)
    shapes = ((total, 2 * RANK), (total, RANK))
    return pl.pallas_call(
        early_kernel,
        grid=(units // TILE,),
        in_specs=[whole(a.shape) for a in wide] + [tile_columns(a.shape[0]) for a in tiled],
        out_specs=[whole(shape) for shape in shapes],
        out_shape=[jax.ShapeDtypeStruct(shape, jnp.float32) for shape in shapes],
        compiler_params=params(),
        cost_estimate=cost(2 * total * RANK * units, wide + tiled),
    )(*wide, *tiled)


def outer_sum(left_side, right_side, weight):
    return lax.dot_general(
        left_side * weight,
        right_side,
        (((0,), (0,)), ((), ())),
        precision=lax.Precision.HIGHEST,
        preferred_element_type=jnp.float32,
    )


def example_features(in_side, hidden_side, gate_side, up_side, out_side, length):
    positions = lax.broadcasted_iota(jnp.int32, (SEQ, RANK), 0)
    weight = (positions < length).astype(jnp.float32)
    return (
        outer_sum(in_side, gate_side, weight),
        outer_sum(in_side, up_side, weight),
        outer_sum(hidden_side, out_side, weight),
    )


def query_kernel(lengths, in_out, sums, found):
    for e in range(found.shape[0]):
        part = slice(e * SEQ, (e + 1) * SEQ)
        three = example_features(
            in_out[part, :RANK],
            sums[part, 2 * RANK :],
            sums[part, :RANK],
            sums[part, RANK : 2 * RANK],
            in_out[part, RANK:],
            lengths[e],
        )
        for segment in range(3):
            found[e, segment * RANK : (segment + 1) * RANK, :] = three[segment]


def query_features(lengths, in_out, sums):
    return pl.pallas_call(
        query_kernel,
        in_specs=[SCALARS, IN_VMEM, IN_VMEM],
        out_specs=IN_VMEM,
        out_shape=jax.ShapeDtypeStruct((lengths.shape[0], 3 * RANK, RANK), jnp.float32),
        compiler_params=params(),
    )(lengths, in_out, sums)


def score_kernel(
    lengths, place, in_out, hidden, early, near, far, q0, q1, q2, q3, scores
):
    queries = q0.shape[0]
    shape = scores.shape
    row = lax.broadcasted_iota(jnp.int32, shape, 0)
    column = lax.broadcasted_iota(jnp.int32, shape, 1)
    gradient = jnp.concatenate([early[...], (near[...] + far[...]).T], axis=0)
    total = jnp.zeros(shape, jnp.float32)
    for e in range(shape[0]):
        part = slice(e * SEQ, (e + 1) * SEQ)
        three = jnp.concatenate(
            example_features(
                in_out[part, :RANK],
                hidden[part, :],
                gradient[part, :RANK],
                gradient[part, RANK:],
                in_out[part, RANK:],
                lengths[e],
            ),
            axis=0,
        )
        for step, found in enumerate((q0, q1, q2, q3)):
            for j in range(queries):
                value = jnp.sum(three * found[j], keepdims=True)
                here = (row == e) & (
                    column == queries * jnp.bitwise_xor(place[0], step) + j
                )
                total = total + jnp.where(here, value, 0.0)
    scores[...] = total


def partial_scores(lengths, place, in_out, hidden, early, near, far, found):
    number = lengths.shape[0]
    return pl.pallas_call(
        score_kernel,
        in_specs=[SCALARS] * 2 + [IN_VMEM] * 9,
        out_specs=IN_VMEM,
        out_shape=jax.ShapeDtypeStruct((number, 4 * found[0].shape[0]), jnp.float32),
        compiler_params=params(),
    )(lengths, place, in_out, hidden, early, near, far, *found)


def after(value, *others):
    return lax.optimization_barrier((value, *others))[0]


def moving_plan(
    train_input,
    train_gate,
    train_up,
    train_outgrad,
    train_lengths,
    query_input,
    query_gate,
    query_up,
    query_outgrad,
    query_lengths,
    down_weight,
    proj_input,
    proj_outgrad,
    proj_hidden,
    proj_gate,
    proj_up,
):
    t = lax.axis_index("tensor")
    d = lax.axis_index("dp")
    x, core, upper = d // 2, d % 2, t // 2
    at_home = x == upper
    inner_chip = (t == 1) | (t == 2)
    near_code = jnp.where(at_home, 0, jnp.where(inner_chip, 1, 2))
    first_parity = jnp.where(at_home, t % 2, upper)
    flags = jnp.stack([near_code, first_parity ^ core]).astype(jnp.int32)
    place = jnp.stack([d]).astype(jnp.int32)

    to_core = functools.partial(lax.ppermute, axis_name="dp", perm=[(i, i ^ 1) for i in range(4)])
    to_chip = functools.partial(lax.ppermute, axis_name="dp", perm=[(i, i ^ 2) for i in range(4)])
    outer = functools.partial(
        lax.ppermute, axis_name="tensor", perm=[(i, i ^ 1) for i in range(4)]
    )
    across = functools.partial(
        lax.ppermute, axis_name="tensor", perm=[(i, i ^ 2) for i in range(4)]
    )
    opposite = functools.partial(
        lax.ppermute, axis_name="tensor", perm=[(i, 3 - i) for i in range(4)]
    )
    middle = functools.partial(
        lax.ppermute,
        axis_name=("tensor", "dp"),
        perm=[
            (4 * i + j, 4 * (3 - i) + j) if i in (1, 2) else (4 * i + j, 4 * i + (j ^ 1))
            for i in range(4)
            for j in range(4)
        ],
    )

    q_input, q_gate, q_up, q_outgrad = [
        flatten(a) for a in (query_input, query_gate, query_up, query_outgrad)
    ]
    t_input, t_gate, t_up, t_outgrad = [
        flatten(a) for a in (train_input, train_gate, train_up, train_outgrad)
    ]
    examples = train_lengths.shape[0] // 2
    cut = examples * SEQ

    def first_hops(own):
        return own, outer(own), across(own)

    def last_hops(own, one, two):
        mid = middle(after(own, two))
        return own, one, mid, two, two, outer(after(two, one))

    def crossing_pair(own, one, second_inner, third_inner, second_outer, third_outer):
        def choose(within, beyond_inner, beyond_outer):
            beyond = jnp.where(inner_chip, beyond_inner, beyond_outer)
            return jnp.where(at_home, beyond, within)

        return jnp.stack(
            [choose(own, second_inner, second_outer), choose(one, third_inner, third_outer)]
        )

    weight_own, weight_sib = down_weight, to_core(down_weight)
    q_hops = first_hops(q_outgrad)
    far_gate = to_chip(t_gate[cut:])
    own_in_out, hidden = early_sides(
        t_input, q_input, t_outgrad, q_outgrad, proj_input, proj_outgrad, t_gate, t_up, q_gate,
        q_up, proj_hidden,
    )

    q_blocks = last_hops(*q_hops[:2], after(q_hops[2], own_in_out))
    a_hops = first_hops(after(t_outgrad[:cut], q_hops[2], far_gate))
    far_up = to_chip(after(t_up[cut:], far_gate))
    q_send = after(crossing_pair(*q_blocks), far_up)
    q_far = to_chip(q_send)
    a_blocks = last_hops(*a_hops[:2], after(a_hops[2], q_send))

    b_hops = first_hops(after(t_outgrad[cut:], a_hops[2]))
    gates, ups = turned(t_gate, t_up, far_gate, far_up)
    a_send = crossing_pair(*a_blocks[:5], after(a_blocks[5], q_far, gates))
    a_far = to_chip(a_send)
    q_near_sum, q_far_sum = partial_sums(
        flags, q_blocks, after(q_far, a_send), weight_own, weight_sib
    )
    q_returned = to_chip(after(q_far_sum, a_far))
    b_blocks = last_hops(*b_hops[:2], after(b_hops[2], q_far_sum))
    b_send = crossing_pair(*b_blocks)
    b_far = to_chip(b_send)
    a_near_sum, a_far_sum = partial_sums(
        flags, a_blocks, after(a_far, b_send), weight_own, weight_sib
    )
    in_out = own_in_out + outer(after(own_in_out, b_send))
    q_gradient = finished_sides(
        q_near_sum, after(q_returned, a_far_sum), q_gate, q_up, proj_gate, proj_up
    )
    a_returned = to_chip(after(a_far_sum, q_gradient))
    q_sums = jnp.concatenate([q_gradient, hidden[2 * cut :]], axis=1)
    q_sums = q_sums + outer(q_sums)
    b_near, b_away = lent_sides(
        after(flags, q_sums, in_out), b_blocks, b_far, weight_own, weight_sib, gates, ups,
        proj_gate, proj_up,
    )
    b_far_sides = to_chip(b_away)
    in_out = in_out + after(across(in_out), b_near)
    q_sums = q_sums + after(across(q_sums), b_near)
    own_found = query_features(query_lengths, in_out[2 * cut :], q_sums)
    chip_found = to_chip(own_found)
    found = (own_found, to_core(own_found), chip_found, to_core(after(chip_found, b_far_sides)))
    a_gradient = finished_sides(a_near_sum, a_returned, t_gate, t_up, proj_gate, proj_up)
    own_scores = partial_scores(
        train_lengths, place, in_out[: 2 * cut], hidden[: 2 * cut], a_gradient, b_near,
        b_far_sides, found,
    )
    scores = own_scores + outer(own_scores) + across(own_scores) + opposite(own_scores)
    return scores / (RANK * SEQ)


def solution(mesh):
    tensor, dp = mesh.shape["tensor"], mesh.shape["dp"]

    def per_device(*arguments):
        if tensor == 4 and dp == 4:
            return moving_plan(*arguments)
        return gathering_plan(*arguments)

    in_specs = (
        P(("parts", "dp"), None, "tensor"),
        P(("parts", "dp"), None, "tensor"),
        P(("parts", "dp"), None, "tensor"),
        P(("parts", "dp"), None, "tensor"),
        P(("parts", "dp")),
        P(("parts", "dp"), None, "tensor"),
        P(("parts", "dp"), None, "tensor"),
        P(("parts", "dp"), None, "tensor"),
        P(("parts", "dp"), None, "tensor"),
        P(("parts", "dp")),
        P("tensor", "dp"),
        P(None, "tensor"),
        P(None, "tensor"),
        P(None, "tensor"),
        P(None, "tensor"),
        P(None, "tensor"),
    )
    out_specs = P(("parts", "dp"), None)
    return jax.shard_map(
        per_device, mesh=mesh, in_specs=in_specs, out_specs=out_specs, check_vma=False
    )
```
